128 devices in a mesh: lat: 16 (over y, z_lo, core), mp: 8 (over x, z_hi).
Axes of the slice: x: 4, y: 4, z: 4 (z_hi: 2, z_lo: 2; z = z_hi * 2 + z_lo), core: 2. Of those that a mesh axis runs over, the one named last changes fastest.
Arguments:
- fields: bfloat16 [192, 288, 512], P('lat', None, 'mp'), may hold values from -16 to 16
- first_gain: float32 [512], P('mp'), may hold values from 0.1 to 1.9
- qkv_weight: bfloat16 [512, 3, 512], P(None, None, 'mp'), may hold values from -1 to 1
- proj_weight: bfloat16 [512, 512], P(None, 'mp'), may hold values from -0.25 to 0.25
- merge_gain: float32 [4, 512], P(None, 'mp'), may hold values from 0.1 to 1.9
- merge_weight: bfloat16 [4, 512, 1024], P(None, 'mp'), may hold values from -0.125 to 0.125
- mlp_gain: float32 [1024], replicated, may hold values from 0.1 to 1.9
- up_weight: bfloat16 [1024, 4096], P(None, 'mp'), may hold values from -0.1875 to 0.1875
- down_weight: bfloat16 [1024, 4096], P(None, 'mp'), may hold values from -0.09375 to 0.09375
- expand_weight: bfloat16 [1024, 4, 512], P(None, None, 'mp'), may hold values from -0.1875 to 0.1875
- lat_shift: int32 [1], replicated, may hold values from 1 to 5
- lon_shift: int32 [1], replicated, may hold values from 1 to 11
- cotangent: bfloat16 [192, 288, 512], P('lat', None, 'mp'), may hold values from -6 to 6
Outputs:
- decoded: bfloat16 [192, 288, 512], P('lat', None, 'mp')
- grad_input: float32 [192, 288, 512], P('lat', None, 'mp')
- grad_qkv: float32 [512, 3, 512], P('lat', None, 'mp')
- grad_proj: float32 [512, 512], P('lat', 'mp')
- grad_up: float32 [1024, 4096], P('lat', 'mp')
- grad_down: float32 [1024, 4096], P('lat', 'mp')
The draws below stay inside these ranges and needn't reach their ends.
All inputs are finite; a program needn't handle non-finite values.
Results may differ from the reference program's by a relative error of at most 0.035.
Values may be sent and summed in bfloat16 or wider, within the bound.
A program may use at most 128 MiB of HBM per device.

```python
import jax
import jax.numpy as jnp
from jax import lax

D1 = 512
D2 = 1024
HEADS = 8
FF = 4096
WIN_H = 6
WIN_W = 12
LON = 288
HDIM = 64
LAT = 192
N_MP = 8


def draw_fields(key, part):
    key = jax.random.fold_in(key, 3)
    base_key = jax.random.fold_in(key, 0)
    base = jax.random.normal(base_key, (LAT, LON, D1), jnp.float32)
    return jnp.clip(base, -6.0, 6.0).astype(jnp.bfloat16)


def draw_qkv_weight(key, part):
    key = jax.random.fold_in(key, 5)
    base_key = jax.random.fold_in(key, 0)
    scale = D1 ** (-0.5)
    base = jax.random.normal(base_key, (D1, 3, D1), jnp.float32)
    return (jnp.clip(base, -6.0, 6.0) * scale).astype(jnp.bfloat16)


def block_scale(key, extent, cuts, smallest, top_value):
    level = 1.0
    for axis_at, blocks in cuts:
        draws = jax.random.uniform(jax.random.fold_in(jax.random.fold_in(key, 6), axis_at), (blocks,), jnp.float32, smallest / len(cuts), top_value / len(cuts))
        level = level * jnp.repeat(jnp.exp(draws), extent[axis_at] // blocks).reshape((-1,) + (1,) * (len(extent) - 1 - axis_at))
    return level


def noise(key, shape, scale, most, cuts=(), kind=jnp.bfloat16):
    entries = scale * jax.random.normal(key, shape, jnp.float32)
    if cuts:
        entries = entries * block_scale(key, shape, cuts, -0.22, 0.18)
    return jnp.clip(entries, -most, most).astype(kind)


def setup_inputs(seed: int = 0) -> dict:
    splits = jax.random.split(jax.random.key(seed), 14)
    return {
        "fields": draw_fields(jax.random.fold_in(splits[13], 71), 0),
        "first_gain": jnp.clip(1.0 + 0.18 * jax.random.normal(splits[1], (D1,), jnp.float32), 0.1, 1.9),
        "qkv_weight": draw_qkv_weight(jax.random.fold_in(splits[13], 71), 0),
        "proj_weight": noise(splits[3], (D1, D1), D1 ** -0.5, 0.25, ((1, 8),)),
        "merge_gain": jnp.clip(1.0 + 0.18 * jax.random.normal(splits[4], (4, D1), jnp.float32), 0.1, 1.9),
        "merge_weight": noise(splits[5], (4, D1, D2), (4 * D1) ** -0.5, 0.125, ((1, 8),)),
        "mlp_gain": jnp.clip(1.0 + 0.18 * jax.random.normal(splits[6], (D2,), jnp.float32), 0.1, 1.9),
        "up_weight": noise(splits[7], (D2, FF), D2 ** -0.5, 0.1875, ((1, 8),)),
        "down_weight": noise(splits[8], (D2, FF), FF ** -0.5, 0.09375, ((1, 8),)),
        "expand_weight": noise(splits[9], (D2, 4, D1), D2 ** -0.5, 0.1875, ((2, 8),)),
        "lat_shift": jax.random.randint(splits[10], (1,), 1, WIN_H).astype(jnp.int32),
        "lon_shift": jax.random.randint(splits[11], (1,), 1, WIN_W).astype(jnp.int32),
        "cotangent": noise(splits[12], (LAT, LON, D1), 1.0, 6.0, ((0, 16), (2, 8))),
    }


EPSILON = 1e-05
MASKED = -1e+30

def widen(value):
    return lax.optimization_barrier(value).astype(jnp.float32)

def keep_rounded(value):
    return widen(value.astype(jnp.bfloat16))

def rounded_sum(term, count):
    total = keep_rounded(term(0))
    for index in range(1, count):
        total = total + keep_rounded(term(index))
    return total

def to_windows(grid):
    row_count, lon_count = (grid.shape[0], grid.shape[1])
    trailing = grid.shape[2:]
    view = grid.reshape((row_count // WIN_H, WIN_H, lon_count // WIN_W, WIN_W) + trailing)
    view = jnp.swapaxes(view, 1, 2)
    return view.reshape((row_count // WIN_H, lon_count // WIN_W, WIN_H * WIN_W) + trailing)

def from_windows(windows):
    bands, columns = (windows.shape[0], windows.shape[1])
    trailing = windows.shape[3:]
    view = windows.reshape((bands, columns, WIN_H, WIN_W) + trailing)
    view = jnp.swapaxes(view, 1, 2)
    return view.reshape((bands * WIN_H, columns * WIN_W) + trailing)

def merge_patches(grid):
    row_count, lon_count, features = grid.shape
    view = grid.reshape(row_count // 2, 2, lon_count // 2, 2, features)
    view = view.transpose(0, 2, 1, 3, 4)
    return view.reshape(row_count // 2, lon_count // 2, 4, features)

def split_patches(patches):
    half_rows, half_lon, _, features = patches.shape
    view = patches.reshape(half_rows, half_lon, 2, 2, features).transpose(0, 2, 1, 3, 4)
    return view.reshape(half_rows * 2, half_lon * 2, features)

def norm_forward(values, gain, axes):
    count = 1
    for axis in axes:
        count = count * values.shape[axis]
    center = lax.optimization_barrier(jnp.sum(values, axis=axes, keepdims=True)) / count
    second = lax.optimization_barrier(jnp.sum(values * values, axis=axes, keepdims=True)) / count
    scale_inv = lax.rsqrt(second - center * center + EPSILON)
    unit = (values - center) * scale_inv
    return (unit * gain, unit, scale_inv)

def norm_backward(grad, gain, unit, scale_inv, axes):
    count = 1
    for axis in axes:
        count = count * grad.shape[axis]
    scaled = grad * gain
    first = lax.optimization_barrier(jnp.sum(scaled, axis=axes, keepdims=True)) / count
    second = lax.optimization_barrier(jnp.sum(scaled * unit, axis=axes, keepdims=True)) / count
    return scale_inv * (scaled - first - unit * second)

def attend(packed, labels):
    allow = labels[:, :, None] == labels[:, None, :]
    query = widen(packed[:, :, 0])
    keys = widen(packed[:, :, 1])
    values = widen(packed[:, :, 2])
    factor = packed.shape[-1] ** (-0.5)
    scores = jnp.einsum('wqhe,wkhe->whqk', query, keys) * factor
    scores = jnp.where(allow[:, None], scores, MASKED)
    highest = lax.optimization_barrier(jnp.max(scores, axis=-1, keepdims=True))
    weights = jnp.exp(scores - highest)
    probs = weights / lax.optimization_barrier(jnp.sum(weights, axis=-1, keepdims=True))
    context = jnp.einsum('whqk,wkhe->wqhe', keep_rounded(probs), values).astype(jnp.bfloat16)
    return (context, probs)

def attend_back(packed, probs, grad_context):
    query = widen(packed[:, :, 0])
    keys = widen(packed[:, :, 1])
    values = widen(packed[:, :, 2])
    factor = packed.shape[-1] ** (-0.5)
    grad_wide = widen(grad_context)
    grad_probs = jnp.einsum('wqhe,wkhe->whqk', grad_wide, values)
    grad_values = jnp.einsum('whqk,wqhe->wkhe', keep_rounded(probs), grad_wide).astype(jnp.bfloat16)
    grad_scores = probs * (grad_probs - lax.optimization_barrier(jnp.sum(grad_probs * probs, axis=-1, keepdims=True))) * factor
    grad_scores = keep_rounded(grad_scores)
    grad_query = jnp.einsum('whqk,wkhe->wqhe', grad_scores, keys).astype(jnp.bfloat16)
    grad_keys = jnp.einsum('whqk,wqhe->wkhe', grad_scores, query).astype(jnp.bfloat16)
    return jnp.stack([grad_query, grad_keys, grad_values], axis=2)

def reference(fields, first_gain, qkv_weight, proj_weight, merge_gain, merge_weight, mlp_gain, up_weight, down_weight, expand_weight, lat_shift, lon_shift, cotangent):
    lat_offset = lat_shift[0].astype(jnp.int32)
    lon_offset = lon_shift[0].astype(jnp.int32)
    row_count, lon_count = (fields.shape[0], fields.shape[1])
    width = D1 // N_MP
    span = FF // N_MP

    def forward_frame(grid):
        moved = jnp.roll(grid, -lat_offset, axis=0)
        return jnp.roll(moved, -lon_offset, axis=1)

    def backward_frame(grid):
        moved = jnp.roll(grid, lat_offset, axis=0)
        return jnp.roll(moved, lon_offset, axis=1)
    row_index = jnp.arange(row_count, dtype=jnp.int32)
    region = (row_index >= jnp.int32(row_count) - lat_offset).astype(jnp.int32)
    region_grid = jnp.broadcast_to(region[:, None], (row_count, lon_count))
    fields_wide = fields.astype(jnp.float32)
    normed, unit_one, inv_one = norm_forward(fields_wide, first_gain, (2,))
    framed = forward_frame(normed.astype(jnp.bfloat16))
    packed = jnp.einsum('rld,dce->rlce', widen(framed), qkv_weight.astype(jnp.float32)).astype(jnp.bfloat16)
    windows = to_windows(packed.reshape(row_count, lon_count, 3, HEADS, HDIM))
    label_windows = to_windows(region_grid)

    def band_forward(items):
        return attend(items[0], items[1])[0]
    context_win = lax.map(band_forward, (windows, label_windows))
    context = from_windows(context_win).reshape(row_count, lon_count, D1)

    def proj_term(index):
        return jnp.einsum('rle,oe->rlo', widen(context[:, :, index * width:(index + 1) * width]), proj_weight[:, index * width:(index + 1) * width].astype(jnp.float32))
    attention_framed = rounded_sum(proj_term, N_MP).astype(jnp.bfloat16)
    attention = backward_frame(attention_framed)
    hidden = (fields_wide + widen(attention)).astype(jnp.bfloat16)
    patches = merge_patches(hidden)
    normed_two, unit_two, inv_two = norm_forward(widen(patches), merge_gain, (2, 3))
    patch_norm = normed_two.astype(jnp.bfloat16)

    def merge_term(index):
        return jnp.einsum('abkd,kde->abe', widen(patch_norm[..., index * width:(index + 1) * width]), merge_weight[:, index * width:(index + 1) * width].astype(jnp.float32))
    merged = rounded_sum(merge_term, N_MP).astype(jnp.bfloat16)
    merged_wide = widen(merged)
    normed_three, unit_three, inv_three = norm_forward(merged_wide, mlp_gain, (2,))
    mlp_in = normed_three.astype(jnp.bfloat16)
    hidden_up = jnp.einsum('abe,ef->abf', widen(mlp_in), up_weight.astype(jnp.float32))
    activated = jax.nn.gelu(hidden_up).astype(jnp.bfloat16)

    def down_term(index):
        return jnp.einsum('abf,ef->abe', widen(activated[..., index * span:(index + 1) * span]), down_weight[:, index * span:(index + 1) * span].astype(jnp.float32))
    mlp_out = rounded_sum(down_term, N_MP)
    bottom = (merged_wide + mlp_out).astype(jnp.bfloat16)
    expanded = jnp.einsum('abo,okd->abkd', widen(bottom), expand_weight.astype(jnp.float32))
    decoded = (widen(hidden) + split_patches(expanded)).astype(jnp.bfloat16)
    cot_patches = merge_patches(cotangent)

    def expand_term(index):
        return jnp.einsum('abkd,okd->abo', cot_patches[..., index * width:(index + 1) * width].astype(jnp.float32), expand_weight[:, :, index * width:(index + 1) * width].astype(jnp.float32))
    grad_bottom = rounded_sum(expand_term, N_MP)
    bottom_grad = grad_bottom.astype(jnp.bfloat16)
    grad_act = jnp.einsum('abo,of->abf', widen(bottom_grad), down_weight.astype(jnp.float32))
    gelu_back = jax.vjp(jax.nn.gelu, hidden_up)[1]
    grad_pre = gelu_back(grad_act)[0].astype(jnp.bfloat16)
    grad_down = jnp.einsum('abo,abf->of', widen(bottom_grad), widen(activated))
    grad_up = jnp.einsum('abe,abf->ef', widen(mlp_in), widen(grad_pre))

    def up_term(index):
        return jnp.einsum('abf,ef->abe', widen(grad_pre[..., index * span:(index + 1) * span]), up_weight[:, index * span:(index + 1) * span].astype(jnp.float32))
    grad_mlp_in = rounded_sum(up_term, N_MP)
    grad_merged = grad_bottom + norm_backward(grad_mlp_in, mlp_gain, unit_three, inv_three, (2,))
    grad_patch_norm = jnp.einsum('abe,kde->abkd', keep_rounded(grad_merged), merge_weight.astype(jnp.float32))
    grad_hidden = cotangent.astype(jnp.float32) + split_patches(norm_backward(grad_patch_norm, merge_gain, unit_two, inv_two, (2, 3)))
    grad_framed = forward_frame(grad_hidden.astype(jnp.bfloat16))
    grad_context = jnp.einsum('rlo,oe->rle', widen(grad_framed), proj_weight.astype(jnp.float32)).astype(jnp.bfloat16)
    grad_proj = jnp.einsum('rlo,rle->oe', widen(grad_framed), widen(context))
    grad_ctx_win = to_windows(grad_context.reshape(row_count, lon_count, HEADS, HDIM))

    def band_backward(items):
        probs = attend(items[0], items[1])[1]
        return attend_back(items[0], probs, items[2])
    grad_win = lax.map(band_backward, (windows, label_windows, grad_ctx_win))
    grad_packed = from_windows(grad_win).reshape(row_count, lon_count, 3, D1)
    grad_qkv = jnp.einsum('rld,rlce->dce', widen(framed), widen(grad_packed))

    def qkv_term(index):
        return jnp.einsum('rlce,dce->rld', widen(grad_packed[..., index * width:(index + 1) * width]), qkv_weight[:, :, index * width:(index + 1) * width].astype(jnp.float32))
    grad_norm_framed = rounded_sum(qkv_term, N_MP)
    grad_normed = backward_frame(grad_norm_framed)
    grad_input = grad_hidden + norm_backward(grad_normed, first_gain, unit_one, inv_one, (2,))
    return (decoded, grad_input, grad_qkv, grad_proj, grad_up, grad_down)
```

```python
import jax
import jax.numpy as jnp
from jax import lax
from jax.experimental import pallas as pl
from jax.experimental.pallas import tpu as pltpu
from jax.sharding import PartitionSpec as P

WIN_H = 6
WIN_W = 12
HDIM = 64
EPSILON = 1e-05
MASKED = -1e30
BF16 = jnp.bfloat16
F32 = jnp.float32


def exchange(collective, inputs, outputs, moves):
    n_lat, n_mp = lax.axis_size("lat"), lax.axis_size("mp")
    steps = sorted({(move[4] % n_lat, move[5] % n_mp) for move in moves} - {(0, 0)})

    def body(*refs):
        sources = refs[: len(inputs)]
        landings = refs[len(inputs) : len(inputs) + len(outputs)]
        send, receive = refs[-2:]
        here = {"lat": lax.axis_index("lat"), "mp": lax.axis_index("mp")}
        barrier = pltpu.get_barrier_semaphore()
        for down, right in steps:
            pl.semaphore_signal(
                barrier,
                inc=1,
                device_id=(
                    lax.rem(here["lat"] + n_lat - down, n_lat),
                    lax.rem(here["mp"] + n_mp - right, n_mp),
                ),
                device_id_type=pl.DeviceIdType.MESH,
            )
        pl.semaphore_wait(barrier, len(steps))
        copies = []
        for index, (source, source_slot, landing, landing_slot, down, right) in enumerate(moves):
            down, right = down % n_lat, right % n_mp
            target = {
                "lat": lax.rem(here["lat"] + down, n_lat),
                "mp": lax.rem(here["mp"] + right, n_mp),
            }
            source_ref = sources[source]
            if source_slot is not None:
                source_ref = source_ref.at[target[source_slot]]
            landing_ref = landings[landing]
            if landing_slot is not None:
                landing_ref = landing_ref.at[here[landing_slot]]
            if (down, right) == (0, 0):
                copy = pltpu.make_async_copy(source_ref, landing_ref, receive.at[index])
            else:
                copy = pltpu.make_async_remote_copy(
                    src_ref=source_ref,
                    dst_ref=landing_ref,
                    send_sem=send.at[index],
                    recv_sem=receive.at[index],
                    device_id=(target["lat"], target["mp"]),
                    device_id_type=pl.DeviceIdType.MESH,
                )
            copy.start()
            copies.append(copy)
        for copy in copies:
            copy.wait()

    return pl.pallas_call(
        body,
        out_shape=[jax.ShapeDtypeStruct(shape, dtype) for shape, dtype in outputs],
        in_specs=[pl.BlockSpec(memory_space=pl.ANY)] * len(inputs),
        out_specs=[pl.BlockSpec(memory_space=pl.ANY)] * len(outputs),
        scratch_shapes=[
            pltpu.SemaphoreType.DMA((len(moves),)),
            pltpu.SemaphoreType.DMA((len(moves),)),
        ],
        compiler_params=pltpu.CompilerParams(collective_id=collective, has_side_effects=True),
    )(*inputs)


def halves_beside(values):
    half = values.shape[-2] // 2
    return jnp.concatenate([values[..., :half, :], values[..., half:, :]], axis=-1)


def groups_joined(slabs):
    count, half, _ = slabs.shape
    view = slabs.reshape(count, half, 2, HDIM).transpose(2, 1, 0, 3)
    return view.reshape(2 * half, count * HDIM)


def to_windows(grid):
    row_count, lon_count = (grid.shape[0], grid.shape[1])
    trailing = grid.shape[2:]
    view = grid.reshape((row_count // WIN_H, WIN_H, lon_count // WIN_W, WIN_W) + trailing)
    view = jnp.swapaxes(view, 1, 2)
    return view.reshape(((row_count // WIN_H) * (lon_count // WIN_W), WIN_H * WIN_W) + trailing)


def from_windows(windows, bands, columns):
    trailing = windows.shape[2:]
    view = windows.reshape((bands, columns, WIN_H, WIN_W) + trailing)
    view = jnp.swapaxes(view, 1, 2)
    return view.reshape((bands * WIN_H, columns * WIN_W) + trailing)


def merge_patches(grid):
    row_count, lon_count, features = grid.shape
    view = grid.reshape(row_count // 2, 2, lon_count // 2, 2, features)
    view = view.transpose(0, 2, 1, 3, 4)
    return view.reshape(row_count * lon_count // 4, 4, features)


def split_patches(patches, row_count, lon_count):
    features = patches.shape[-1]
    view = patches.reshape(row_count // 2, lon_count // 2, 2, 2, features)
    return view.transpose(0, 2, 1, 3, 4).reshape(row_count, lon_count, features)


def norm_forward(values, gain, axes):
    center = jnp.mean(values, axis=axes, keepdims=True)
    second = jnp.mean(values * values, axis=axes, keepdims=True)
    scale_inv = lax.rsqrt(second - center * center + EPSILON)
    unit = (values - center) * scale_inv
    return (unit * gain, unit, scale_inv)


def norm_backward(grad, gain, unit, scale_inv, axes):
    scaled = grad * gain
    first = jnp.mean(scaled, axis=axes, keepdims=True)
    second = jnp.mean(scaled * unit, axis=axes, keepdims=True)
    return scale_inv * (scaled - first - unit * second)


def attend(packed, labels):
    allow = labels[:, :, None] == labels[:, None, :]
    query, keys, values = packed[..., 0, :], packed[..., 1, :], packed[..., 2, :]
    factor = packed.shape[-1] ** (-0.5)
    scores = jnp.einsum("wqhe,wkhe->whqk", query, keys, preferred_element_type=F32) * factor
    scores = jnp.where(allow[:, None], scores, MASKED)
    weights = jnp.exp(scores - jnp.max(scores, axis=-1, keepdims=True))
    probs = weights / jnp.sum(weights, axis=-1, keepdims=True)
    context = jnp.einsum("whqk,wkhe->wqhe", probs.astype(BF16), values, preferred_element_type=F32)
    return (context.astype(BF16), probs)


def attend_back(packed, probs, grad_context):
    query, keys, values = packed[..., 0, :], packed[..., 1, :], packed[..., 2, :]
    factor = packed.shape[-1] ** (-0.5)
    grad_probs = jnp.einsum("wqhe,wkhe->whqk", grad_context, values, preferred_element_type=F32)
    grad_values = jnp.einsum(
        "whqk,wqhe->wkhe", probs.astype(BF16), grad_context, preferred_element_type=F32
    ).astype(BF16)
    grad_scores = (
        probs * (grad_probs - jnp.sum(grad_probs * probs, axis=-1, keepdims=True)) * factor
    ).astype(BF16)
    grad_query = jnp.einsum(
        "whqk,wkhe->wqhe", grad_scores, keys, preferred_element_type=F32
    ).astype(BF16)
    grad_keys = jnp.einsum(
        "whqk,wqhe->wkhe", grad_scores, query, preferred_element_type=F32
    ).astype(BF16)
    return jnp.stack([grad_query, grad_keys, grad_values], axis=3)


def shards(
    fields,
    first_gain,
    qkv_weight,
    proj_weight,
    merge_gain,
    merge_weight,
    mlp_gain,
    up_weight,
    down_weight,
    expand_weight,
    lat_shift,
    lon_shift,
    cotangent,
):
    n_lat, n_mp = lax.axis_size("lat"), lax.axis_size("mp")
    lat_offset = lat_shift[0]
    lon_offset = lon_shift[0]
    rows, lon_count, group = fields.shape
    width = group * n_mp
    block = lon_count // n_mp
    wide = block + WIN_W
    tall = rows + WIN_H
    bands, columns = rows // WIN_H, block // WIN_W
    tokens = rows * block
    width_two = merge_weight.shape[2]
    span = up_weight.shape[1]
    merged_count = tokens // 4
    padded = -(-merged_count // 16) * 16
    others = range(n_mp)

    def column_blocks(values, extent):
        ring = jnp.concatenate([values, values[:, : extent - block]], axis=1)
        return jnp.stack(
            [ring[:, block * at : block * at + extent] for at in range(n_mp)], axis=0
        )

    field_blocks = column_blocks(fields, wide)
    body_slab = halves_beside(field_blocks.reshape(n_mp, rows * wide, group))
    cot_slab = halves_beside(column_blocks(cotangent, block).reshape(n_mp, tokens, group))
    slabs = jnp.concatenate([body_slab, cot_slab], axis=1)
    edge_slab = halves_beside(field_blocks[:, :WIN_H].reshape(n_mp, WIN_H * wide, group))
    weights = jnp.concatenate(
        [qkv_weight.reshape(width, 3 * group), proj_weight], axis=1
    )
    gains = jnp.pad(jnp.concatenate([first_gain[None], merge_gain], axis=0), ((0, 3), (0, 64)))
    merge_all = lax.all_gather(merge_weight, "mp", axis=1, tiled=True)
    expand_all = lax.all_gather(expand_weight, "mp", axis=0)
    got, got_edge, weights_all, gains_all = exchange(
        1,
        [slabs, edge_slab, weights, gains],
        [
            (slabs.shape, BF16),
            (edge_slab.shape, BF16),
            ((n_mp,) + weights.shape, BF16),
            ((n_mp,) + gains.shape, F32),
        ],
        [(2, None, 2, "mp", 0, step) for step in others]
        + [(3, None, 3, "mp", 0, step) for step in others]
        + [(0, "mp", 0, "mp", 0, step) for step in others]
        + [(1, "mp", 1, "mp", -1, step) for step in others],
    )
    body_half = rows * wide // 2
    body = groups_joined(got[:, :body_half]).reshape(rows, wide, width)
    edge = groups_joined(got_edge).reshape(WIN_H, wide, width)
    cot = groups_joined(got[:, body_half:]).reshape(rows, block, width)
    first_all = gains_all[:, 0, :group].reshape(width)
    merge_gain_all = gains_all[:, 1:5, :group].transpose(1, 0, 2).reshape(4, width)
    qkv_all = weights_all[:, :, : 3 * group].reshape(n_mp, width, 3, group)
    proj_all = weights_all[:, :, 3 * group :]

    def into_frame(whole):
        return lax.dynamic_slice(
            whole, (lat_offset, lon_offset, jnp.int32(0)), (rows, block, width)
        )

    own_fields = body[:, :block].astype(F32)
    framed_fields = to_windows(into_frame(jnp.concatenate([body, edge], axis=0)))
    normed, unit_one, inv_one = norm_forward(framed_fields.astype(F32), first_all, (2,))
    framed = normed.astype(BF16)
    packed = jnp.einsum("wtd,mdce->wtmce", framed, qkv_all, preferred_element_type=F32).astype(BF16)
    row_index = lax.axis_index("lat") * rows + jnp.arange(rows, dtype=jnp.int32)
    region = (row_index >= jnp.int32(rows) * n_lat - lat_offset).astype(jnp.int32)
    labels = to_windows(jnp.broadcast_to(region[:, None], (rows, block)))
    context, probs = attend(packed, labels)
    attention_framed = jnp.einsum(
        "wtme,moe->wto", context, proj_all, preferred_element_type=F32
    ).astype(BF16)
    attention_grid = from_windows(attention_framed, bands, columns)
    from_above, from_left, from_corner = exchange(
        2,
        [
            attention_grid[-WIN_H:].reshape(WIN_H * block, width),
            attention_grid[:, -WIN_W:].reshape(rows * WIN_W, width),
            attention_grid[-WIN_H:, -WIN_W:].reshape(WIN_H * WIN_W, width),
        ],
        [
            ((WIN_H * block, width), BF16),
            ((rows * WIN_W, width), BF16),
            ((WIN_H * WIN_W, width), BF16),
        ],
        [(0, None, 0, None, 1, 0), (1, None, 1, None, 0, 1), (2, None, 2, None, 1, 1)],
    )
    top = jnp.concatenate(
        [from_corner.reshape(WIN_H, WIN_W, width), from_above.reshape(WIN_H, block, width)], axis=1
    )
    low = jnp.concatenate([from_left.reshape(rows, WIN_W, width), attention_grid], axis=1)
    attention = lax.dynamic_slice(
        jnp.concatenate([top, low], axis=0),
        (WIN_H - lat_offset, WIN_W - lon_offset, jnp.int32(0)),
        (rows, block, width),
    )
    hidden = merge_patches((own_fields + attention.astype(F32)).astype(BF16))
    hidden_wide = hidden.astype(F32)
    normed_two, unit_two, inv_two = norm_forward(hidden_wide, merge_gain_all, (1, 2))
    merged = jnp.einsum(
        "akd,kde->ae", normed_two.astype(BF16), merge_all, preferred_element_type=F32
    ).astype(BF16)
    merged_wide = merged.astype(F32)
    normed_three, unit_three, inv_three = norm_forward(merged_wide, mlp_gain, (1,))
    cot_patches = merge_patches(cot)
    grad_bottom = jnp.einsum(
        "akmd,mokd->ao",
        cot_patches.reshape(merged_count, 4, n_mp, group),
        expand_all,
        preferred_element_type=F32,
    )
    pair = jnp.concatenate([normed_three.astype(BF16), grad_bottom.astype(BF16)], axis=1)
    pair = jnp.pad(pair, ((0, padded - merged_count), (0, 0)))
    (pairs,) = exchange(
        3,
        [pair],
        [((n_mp,) + pair.shape, BF16)],
        [(0, None, 0, "mp", 0, step) for step in others],
    )
    pairs = pairs.reshape(n_mp * padded, 2 * width_two)
    mlp_in, bottom_grad = pairs[:, :width_two], pairs[:, width_two:]
    hidden_up = jnp.dot(mlp_in, up_weight, preferred_element_type=F32)
    activated = jax.nn.gelu(hidden_up).astype(BF16)
    grad_act = jnp.dot(bottom_grad, down_weight, preferred_element_type=F32)
    gelu_back = jax.vjp(jax.nn.gelu, hidden_up)[1]
    grad_pre = gelu_back(grad_act)[0].astype(BF16)
    terms = jnp.concatenate(
        [
            jnp.einsum("af,ef->ae", activated, down_weight, preferred_element_type=F32),
            jnp.einsum("af,ef->ae", grad_pre, up_weight, preferred_element_type=F32),
        ],
        axis=1,
    ).astype(BF16)
    (parts,) = exchange(
        4,
        [terms.reshape(n_mp, padded, 2 * width_two)],
        [((n_mp, padded, 2 * width_two), BF16)],
        [(0, "mp", 0, "mp", 0, step) for step in others],
    )
    down_local = jnp.einsum("ao,af->of", bottom_grad, activated, preferred_element_type=F32)
    up_local = jnp.einsum("ae,af->ef", mlp_in, grad_pre, preferred_element_type=F32)
    grad_up, grad_down = (
        lax.psum_scatter(part.astype(BF16), "lat", scatter_dimension=0, tiled=True).astype(F32)
        for part in (up_local, down_local)
    )
    totals = jnp.sum(parts[:, :merged_count].astype(F32), axis=0)
    bottom = (merged_wide + totals[:, :width_two]).astype(BF16)
    expanded = jnp.einsum("ao,mokd->akmd", bottom, expand_all, preferred_element_type=F32)
    decoded = (hidden_wide + expanded.reshape(merged_count, 4, width)).astype(BF16)
    grad_merged = grad_bottom + norm_backward(
        totals[:, width_two:], mlp_gain, unit_three, inv_three, (1,)
    )
    grad_patch_norm = jnp.einsum(
        "ae,kde->akd", grad_merged.astype(BF16), merge_all, preferred_element_type=F32
    )
    grad_patches = norm_backward(grad_patch_norm, merge_gain_all, unit_two, inv_two, (1, 2))
    grad_hidden = split_patches(
        (cot_patches.astype(F32) + grad_patches).astype(BF16), rows, block
    )

    def group_slabs(grid):
        count = grid.shape[0] * grid.shape[1]
        view = grid.reshape(count, n_mp, group).transpose(1, 0, 2)
        return halves_beside(view)

    decoded_slab = group_slabs(split_patches(decoded, rows, block))
    from_below, from_right, from_corner, decoded_got = exchange(
        5,
        [
            grad_hidden[:WIN_H].reshape(WIN_H * block, width),
            grad_hidden[:, :WIN_W].reshape(rows * WIN_W, width),
            grad_hidden[:WIN_H, :WIN_W].reshape(WIN_H * WIN_W, width),
            decoded_slab,
        ],
        [
            ((WIN_H * block, width), BF16),
            ((rows * WIN_W, width), BF16),
            ((WIN_H * WIN_W, width), BF16),
            (decoded_slab.shape, BF16),
        ],
        [(0, None, 0, None, -1, 0), (1, None, 1, None, 0, -1), (2, None, 2, None, -1, -1)]
        + [(3, "mp", 3, "mp", 0, step) for step in others],
    )

    def columns_joined(slabs, row_count):
        count = slabs.shape[0]
        view = jnp.concatenate([slabs[..., :group], slabs[..., group:]], axis=1)
        view = view.reshape(count, row_count, block, group).transpose(1, 0, 2, 3)
        return view.reshape(row_count, count * block, group)

    decoded_out = columns_joined(decoded_got, rows)
    high = jnp.concatenate([grad_hidden, from_right.reshape(rows, WIN_W, width)], axis=1)
    bottom_rows = jnp.concatenate(
        [from_below.reshape(WIN_H, block, width), from_corner.reshape(WIN_H, WIN_W, width)], axis=1
    )
    grad_framed = to_windows(into_frame(jnp.concatenate([high, bottom_rows], axis=0)))
    grad_context = jnp.einsum(
        "wto,moe->wtme", grad_framed, proj_all, preferred_element_type=F32
    ).astype(BF16)
    grad_proj_part = jnp.einsum("wto,wtme->moe", grad_framed, context, preferred_element_type=F32)
    grad_packed = attend_back(packed, probs, grad_context)
    grad_qkv_part = jnp.einsum("wtd,wtmce->mdce", framed, grad_packed, preferred_element_type=F32)
    grad_normed = jnp.einsum("wtmce,mdce->wtd", grad_packed, qkv_all, preferred_element_type=F32)
    grad_input_framed = grad_framed.astype(F32) + norm_backward(
        grad_normed, first_all, unit_one, inv_one, (2,)
    )
    grad_grid = from_windows(grad_input_framed.astype(BF16), bands, columns)
    grad_slab = group_slabs(grad_grid)
    grad_edge = jnp.pad(group_slabs(grad_grid[-WIN_H:]), ((0, 0), (0, 4), (0, 0)))
    weight_slab = jnp.concatenate(
        [grad_qkv_part.reshape(n_mp, width, 3 * group), grad_proj_part], axis=2
    ).astype(BF16)
    grad_got, edge_got, weight_got = exchange(
        6,
        [grad_slab, grad_edge, weight_slab],
        [(grad_slab.shape, BF16), (grad_edge.shape, BF16), (weight_slab.shape, BF16)],
        [(2, "mp", 2, "mp", 0, step) for step in others]
        + [(0, "mp", 0, "mp", 0, step) for step in others]
        + [(1, "mp", 1, "mp", 1, step) for step in others],
    )
    weight_sum = jnp.sum(weight_got.astype(F32), axis=0).astype(BF16)
    (lat_got,) = exchange(
        7,
        [weight_sum.reshape(n_lat, width // n_lat, 4 * group)],
        [((n_lat, width // n_lat, 4 * group), BF16)],
        [(0, "lat", 0, "lat", step, 0) for step in range(n_lat)],
    )
    weight_total = jnp.sum(lat_got.astype(F32), axis=0)
    grad_qkv = weight_total[:, : 3 * group].reshape(width // n_lat, 3, group)
    grad_proj = weight_total[:, 3 * group :]
    edge_half = WIN_H * block // 2
    grad_rows = jnp.concatenate(
        [columns_joined(edge_got[:, :edge_half], WIN_H), columns_joined(grad_got, rows)], axis=0
    )
    grad_rows = jnp.concatenate([grad_rows[:, -WIN_W:], grad_rows], axis=1)
    grad_input = lax.dynamic_slice(
        grad_rows,
        (WIN_H - lat_offset, WIN_W - lon_offset, jnp.int32(0)),
        (rows, lon_count, group),
    ).astype(F32)
    return (decoded_out, grad_input, grad_qkv, grad_proj, grad_up, grad_down)


def solution(mesh):
    return jax.shard_map(
        shards,
        mesh=mesh,
        in_specs=(
            P("lat", None, "mp"),
            P("mp"),
            P(None, None, "mp"),
            P(None, "mp"),
            P(None, "mp"),
            P(None, "mp", None),
            P(),
            P(None, "mp"),
            P(None, "mp"),
            P(None, None, "mp"),
            P(),
            P(),
            P("lat", None, "mp"),
        ),
        out_specs=(
            P("lat", None, "mp"),
            P("lat", None, "mp"),
            P("lat", None, "mp"),
            P("lat", "mp"),
            P("lat", "mp"),
            P("lat", "mp"),
        ),
        check_vma=False,
    )
```

```python
import jax
import jax.numpy as jnp
from jax import lax
from jax.experimental import pallas as pl
from jax.experimental.pallas import tpu as pltpu
from jax.sharding import PartitionSpec as P

WIN_H = 6
WIN_W = 12
HDIM = 64
EPSILON = 1e-05
MASKED = -1e30
BF16 = jnp.bfloat16
F32 = jnp.float32


def exchange(collective, inputs, outputs, moves):
    n_lat, n_mp = lax.axis_size("lat"), lax.axis_size("mp")
    steps = []
    for move in moves:
        if move[4:] != (0, 0) and move[4:] not in steps:
            steps.append(move[4:])

    def part_of(ref, part, place):
        if part is None:
            return ref
        if part == "core":
            half = ref.shape[2] // 2
            return ref.at[:, :, pl.ds(pl.multiple_of(place["core"] * half, half), half)]
        if isinstance(part, str):
            return ref.at[place[part]]
        if isinstance(part[0], str):
            axis, size = part
            return ref.at[:, pl.ds(pl.multiple_of(place[axis] * size, size), size)]
        return ref.at[part]

    def body(*refs):
        sources = refs[: len(inputs)]
        landings = refs[len(inputs) : len(inputs) + len(outputs)]
        send, receive = refs[-2:]
        lat, mp = lax.axis_index("lat"), lax.axis_index("mp")
        here = {"lat": lat, "mp": mp, "core": lax.rem(lat, 2)}

        def reached(down, right):
            if down == "sibling":
                return {"lat": lat + 1 - 2 * here["core"], "mp": mp}
            return {
                "lat": lax.rem(lat + n_lat + down, n_lat),
                "mp": lax.rem(mp + n_mp + right, n_mp),
            }

        barrier = pltpu.get_barrier_semaphore()
        for down, right in steps:
            source = reached(down if down == "sibling" else -down, -right)
            pl.semaphore_signal(
                barrier,
                inc=1,
                device_id=(source["lat"], source["mp"]),
                device_id_type=pl.DeviceIdType.MESH,
            )
        pl.semaphore_wait(barrier, len(steps))
        copies = []
        for index, (source, source_part, landing, landing_part, down, right) in enumerate(moves):
            target = reached(down, right)
            source_ref = part_of(sources[source], source_part, target)
            landing_ref = part_of(landings[landing], landing_part, here)
            if (down, right) == (0, 0):
                copy = pltpu.make_async_copy(source_ref, landing_ref, receive.at[index])
            else:
                copy = pltpu.make_async_remote_copy(
                    src_ref=source_ref,
                    dst_ref=landing_ref,
                    send_sem=send.at[index],
                    recv_sem=receive.at[index],
                    device_id=(target["lat"], target["mp"]),
                    device_id_type=pl.DeviceIdType.MESH,
                )
            copy.start()
            copies.append(copy)
        for copy in copies:
            copy.wait()

    return pl.pallas_call(
        body,
        out_shape=[jax.ShapeDtypeStruct(shape, dtype) for shape, dtype in outputs],
        in_specs=[pl.BlockSpec(memory_space=pl.ANY)] * len(inputs),
        out_specs=[pl.BlockSpec(memory_space=pl.ANY)] * len(outputs),
        scratch_shapes=[
            pltpu.SemaphoreType.DMA((len(moves),)),
            pltpu.SemaphoreType.DMA((len(moves),)),
        ],
        compiler_params=pltpu.CompilerParams(collective_id=collective, has_side_effects=True),
    )(*inputs)


def local_kernel(body, operands, outputs, scratch=(), scalars=0):
    spaces = [pltpu.SMEM] * scalars + [pltpu.VMEM] * (len(operands) - scalars)
    return pl.pallas_call(
        body,
        out_shape=[jax.ShapeDtypeStruct(shape, dtype) for shape, dtype in outputs],
        in_specs=[pl.BlockSpec(memory_space=space) for space in spaces],
        out_specs=[pl.BlockSpec(memory_space=pltpu.VMEM)] * len(outputs),
        scratch_shapes=list(scratch),
        compiler_params=pltpu.CompilerParams(vmem_limit_bytes=48 * 1024 * 1024),
    )(*operands)


def dot_nn(left, right):
    return lax.dot_general(left, right, (((1,), (0,)), ((), ())), preferred_element_type=F32)


def dot_nt(left, right):
    return lax.dot_general(left, right, (((1,), (1,)), ((), ())), preferred_element_type=F32)


def dot_tn(left, right):
    return lax.dot_general(left, right, (((0,), (0,)), ((), ())), preferred_element_type=F32)


def halves_beside(values):
    half = values.shape[-2] // 2
    return jnp.concatenate([values[..., :half, :], values[..., half:, :]], axis=-1)


def groups_joined(slabs):
    count, half, _ = slabs.shape
    view = slabs.reshape(count, half, 2, HDIM).transpose(2, 1, 0, 3)
    return view.reshape(2 * half, count * HDIM)


def to_windows(grid):
    row_count, lon_count = (grid.shape[0], grid.shape[1])
    trailing = grid.shape[2:]
    view = grid.reshape((row_count // WIN_H, WIN_H, lon_count // WIN_W, WIN_W) + trailing)
    view = jnp.swapaxes(view, 1, 2)
    return view.reshape(((row_count // WIN_H) * (lon_count // WIN_W), WIN_H * WIN_W) + trailing)


def from_windows(windows):
    bands, columns, _, width = windows.shape
    view = windows.reshape((bands, columns, WIN_H, WIN_W, width))
    view = jnp.swapaxes(view, 1, 2)
    return view.reshape((bands * WIN_H, columns * WIN_W, width))


def merge_patches(grid, padded):
    row_count, lon_count, features = grid.shape
    view = grid.reshape(row_count // 2, 2, lon_count // 2, 2, features)
    view = view.transpose(1, 3, 0, 2, 4).reshape(4, row_count * lon_count // 4, features)
    return jnp.pad(view, ((0, 0), (0, padded - view.shape[1]), (0, 0)))


def norm_stats(values, count):
    center = sum(jnp.sum(value, axis=1, keepdims=True) for value in values) / count
    second = sum(jnp.sum(value * value, axis=1, keepdims=True) for value in values) / count
    return (center, lax.rsqrt(second - center * center + EPSILON))


def norm_backward(grads, gains, units, scale_inv, count):
    scaled = [grad * gain for grad, gain in zip(grads, gains)]
    first = sum(jnp.sum(value, axis=1, keepdims=True) for value in scaled) / count
    second = (
        sum(jnp.sum(value * unit, axis=1, keepdims=True) for value, unit in zip(scaled, units))
        / count
    )
    return [scale_inv * (value - first - unit * second) for value, unit in zip(scaled, units)]


def pair_slabs(upper, lower, out_ref, first_rows):
    low = lax.broadcasted_iota(jnp.int32, (upper.shape[0], 2 * HDIM), 1) < HDIM
    rows = pl.ds(first_rows, upper.shape[0])
    for pair in range(upper.shape[1] // (2 * HDIM)):
        lanes = slice(2 * HDIM * pair, 2 * HDIM * (pair + 1))
        one, two = upper[:, lanes], lower[:, lanes]
        swapped_one = jnp.concatenate([one[:, HDIM:], one[:, :HDIM]], axis=1)
        swapped_two = jnp.concatenate([two[:, HDIM:], two[:, :HDIM]], axis=1)
        out_ref[2 * pair, rows, :] = jnp.where(low, one, swapped_two).astype(BF16)
        out_ref[2 * pair + 1, rows, :] = jnp.where(low, swapped_one, two).astype(BF16)


WIN = WIN_H * WIN_W
FACTOR = HDIM ** (-0.5)


def heads_apart(values):
    low = lax.broadcasted_iota(jnp.int32, values.shape, 1) < HDIM
    zero = jnp.zeros_like(values)
    both = [jnp.where(low, values, zero), jnp.where(low, zero, values)]
    return jnp.concatenate(both, axis=0).astype(BF16)


def heads_together(values):
    low = lax.broadcasted_iota(jnp.int32, (WIN, 2 * HDIM), 1) < HDIM
    return jnp.where(low, values[:WIN], values[WIN:])


def window_probs(cut, window, query, keys):
    scores = dot_nt(query, keys) * FACTOR
    spot = lax.broadcasted_iota(jnp.int32, scores.shape, 0)
    spot = jnp.where(spot >= WIN, spot - WIN, spot)
    other = lax.broadcasted_iota(jnp.int32, scores.shape, 1)
    edge = cut * WIN_W - jnp.where(window >= 3, WIN, 0)
    same = (spot >= edge) == (other >= edge)
    scores = jnp.where(same, scores, MASKED)
    weights = jnp.exp(scores - jnp.max(scores, axis=1, keepdims=True))
    return weights / jnp.sum(weights, axis=1, keepdims=True)


def framed_packed(fields_ref, gain_ref, weights_ref, packed):
    values = fields_ref[...].astype(F32)
    center, scale_inv = norm_stats([values], values.shape[1])
    unit = (values - center) * scale_inv
    framed = (unit * gain_ref[...]).astype(BF16)
    for kind in range(3):
        packed[kind] = dot_nt(framed, weights_ref[kind]).astype(BF16).astype(F32)
    return (framed, unit, scale_inv)


def window_parts(refs, window, pair):
    rows = pl.ds(pl.multiple_of(window * WIN, 8), WIN)
    lanes = slice(2 * HDIM * pair, 2 * HDIM * (pair + 1))
    return [ref[rows, lanes] for ref in refs]


def attention_forward(cut_ref, fields_ref, gain_ref, weights_ref, out_ref, context_ref, packed, held):
    framed_packed(fields_ref, gain_ref, weights_ref, packed)
    cut = cut_ref[0]
    windows = fields_ref.shape[0] // WIN

    def step(window, carry):
        rows = pl.ds(pl.multiple_of(window * WIN, 8), WIN)
        for pair in range(fields_ref.shape[1] // (2 * HDIM)):
            query, keys, values = window_parts([packed.at[kind] for kind in range(3)], window, pair)
            probs = window_probs(cut, window, heads_apart(query), keys.astype(BF16))
            joined = dot_nn(probs.astype(BF16), values.astype(BF16))
            held[rows, 2 * HDIM * pair : 2 * HDIM * (pair + 1)] = heads_together(joined)
        return carry

    lax.fori_loop(0, windows, step, 0)
    context = held[...].astype(BF16)
    context_ref[...] = context
    out_ref[...] = dot_nn(context, weights_ref[3]).astype(BF16)


def attention_backward(
    cut_ref, fields_ref, gain_ref, weights_ref, context_ref, grad_ref, slab_ref, weight_ref,
    packed, grads, held,
):
    framed, unit, scale_inv = framed_packed(fields_ref, gain_ref, weights_ref, packed)
    cut = cut_ref[0]
    windows = fields_ref.shape[0] // WIN
    grad_framed = grad_ref[...]
    held[...] = dot_nt(grad_framed, weights_ref[3]).astype(BF16).astype(F32)

    def step(window, carry):
        rows = pl.ds(pl.multiple_of(window * WIN, 8), WIN)
        for pair in range(fields_ref.shape[1] // (2 * HDIM)):
            lanes = slice(2 * HDIM * pair, 2 * HDIM * (pair + 1))
            query, keys, values, grad = window_parts(
                [packed.at[kind] for kind in range(3)] + [held], window, pair
            )
            query, grad = heads_apart(query), heads_apart(grad)
            keys, values = keys.astype(BF16), values.astype(BF16)
            probs = window_probs(cut, window, query, keys)
            grad_probs = dot_nt(grad, values)
            inner = jnp.sum(grad_probs * probs, axis=1, keepdims=True)
            grad_scores = (probs * (grad_probs - inner) * FACTOR).astype(BF16)
            grads[0, rows, lanes] = heads_together(dot_nn(grad_scores, keys))
            grads[1, rows, lanes] = dot_tn(grad_scores, query)
            grads[2, rows, lanes] = dot_tn(probs.astype(BF16), grad)
        return carry

    lax.fori_loop(0, windows, step, 0)
    grad_normed = jnp.zeros(fields_ref.shape, F32)
    for kind in range(3):
        grad_kind = grads[kind].astype(BF16)
        weight_ref[kind] = dot_tn(grad_kind, framed).astype(BF16)
        grad_normed = grad_normed + dot_nn(grad_kind, weights_ref[kind])
    weight_ref[3] = dot_tn(context_ref[...], grad_framed).astype(BF16)
    (back,) = norm_backward([grad_normed], [gain_ref[...]], [unit], scale_inv, unit.shape[1])
    result = grad_framed.astype(F32) + back
    half = result.shape[0] // 2
    pair_slabs(result[:half], result[half:], slab_ref, 0)


def merge_forward(
    fields_ref, attention_ref, cot_ref, gain_ref, mlp_gain_ref, weights_ref,
    pair_ref, hidden_ref, merged_ref, grad_ref,
):
    width_two = merged_ref.shape[1]
    hidden = []
    for patch in range(4):
        value = fields_ref[patch].astype(F32) + attention_ref[patch].astype(F32)
        hidden_ref[patch] = value.astype(BF16)
        hidden.append(value.astype(BF16).astype(F32))
    center, scale_inv = norm_stats(hidden, 4 * hidden[0].shape[1])
    merged = jnp.zeros(merged_ref.shape, F32)
    grad = jnp.zeros(merged_ref.shape, F32)
    for patch in range(4):
        normed = (hidden[patch] - center) * scale_inv * gain_ref[patch : patch + 1, :]
        merged = merged + dot_nn(normed.astype(BF16), weights_ref[patch])
        grad = grad + dot_nn(cot_ref[patch], weights_ref[4 + patch])
    merged_ref[...] = merged.astype(BF16)
    merged = merged.astype(BF16).astype(F32)
    center, scale_inv = norm_stats([merged], width_two)
    mlp_in = (merged - center) * scale_inv * mlp_gain_ref[...]
    pair_ref[:, :width_two] = mlp_in.astype(BF16)
    pair_ref[:, width_two:] = grad.astype(BF16)
    grad_ref[...] = grad


def merge_backward(
    parts_ref, merged_ref, grad_ref, hidden_ref, cot_ref, gain_ref, mlp_gain_ref, weights_ref,
    slab_ref, out_ref,
):
    width_two = merged_ref.shape[1]
    count = merged_ref.shape[0]
    total = parts_ref[0].astype(F32)
    for index in range(1, parts_ref.shape[0]):
        total = total + parts_ref[index].astype(F32)
    merged = merged_ref[...].astype(F32)
    bottom = (merged + total[:, :width_two]).astype(BF16)
    decoded = [
        hidden_ref[patch].astype(F32) + dot_nt(bottom, weights_ref[4 + patch])
        for patch in range(4)
    ]
    for side in range(2):
        pair_slabs(decoded[side], decoded[2 + side], slab_ref, side * count)
    center, scale_inv = norm_stats([merged], width_two)
    unit = (merged - center) * scale_inv
    (back,) = norm_backward(
        [total[:, width_two:]], [mlp_gain_ref[...]], [unit], scale_inv, width_two
    )
    grad_merged = (grad_ref[...] + back).astype(BF16)
    hidden = [hidden_ref[patch].astype(F32) for patch in range(4)]
    center, scale_inv = norm_stats(hidden, 4 * hidden[0].shape[1])
    units = [(value - center) * scale_inv for value in hidden]
    backs = norm_backward(
        [dot_nt(grad_merged, weights_ref[patch]) for patch in range(4)],
        [gain_ref[patch : patch + 1, :] for patch in range(4)],
        units,
        scale_inv,
        4 * hidden[0].shape[1],
    )
    for patch in range(4):
        out_ref[patch] = (cot_ref[patch].astype(F32) + backs[patch]).astype(BF16)


def shards(
    fields,
    first_gain,
    qkv_weight,
    proj_weight,
    merge_gain,
    merge_weight,
    mlp_gain,
    up_weight,
    down_weight,
    expand_weight,
    lat_shift,
    lon_shift,
    cotangent,
):
    n_lat, n_mp = lax.axis_size("lat"), lax.axis_size("mp")
    lat, core = lax.axis_index("lat"), lax.rem(lax.axis_index("lat"), 2)
    lat_offset = lat_shift[0]
    lon_offset = lon_shift[0]
    rows, lon_count, group = fields.shape
    width = group * n_mp
    block = lon_count // n_mp
    wide = block + WIN_W
    bands, columns = rows // WIN_H, block // WIN_W
    tokens = rows * block
    width_two = merge_weight.shape[2]
    span = up_weight.shape[1]
    merged_count = tokens // 4
    padded = -(-merged_count // 16) * 16
    others = range(n_mp)

    section = jnp.concatenate([merge_weight, expand_weight.transpose(1, 2, 0)], axis=0)
    half_section = lax.dynamic_slice_in_dim(section, core * (group // 2), group // 2, 1)
    half_all = lax.all_gather(half_section, "mp", axis=1)

    blocks = fields.reshape(rows, n_mp, block, group).transpose(1, 0, 2, 3)
    margin = jnp.roll(blocks[:, :, :WIN_W], -1, axis=0)
    field_blocks = jnp.concatenate([blocks, margin], axis=2)
    body_slab = halves_beside(field_blocks.reshape(n_mp, rows * wide, group))
    edge_slab = halves_beside(field_blocks[:, :WIN_H].reshape(n_mp, WIN_H * wide, group))
    cot_blocks = cotangent.reshape(rows, n_mp, block, group).transpose(1, 0, 2, 3)
    cot_slab = halves_beside(cot_blocks.reshape(n_mp, tokens, group))
    weights = jnp.concatenate(
        [qkv_weight.transpose(1, 2, 0), proj_weight.transpose(1, 0)[None]], axis=0
    )
    gains = jnp.pad(jnp.concatenate([first_gain[None], merge_gain], axis=0), ((0, 3), (0, 64)))
    body_got, edge_got, cot_got, weights_all, gains_all = exchange(
        1,
        [body_slab, edge_slab, cot_slab, weights, gains],
        [
            (body_slab.shape, BF16),
            (edge_slab.shape, BF16),
            (cot_slab.shape, BF16),
            ((4, width, width), BF16),
            ((n_mp,) + gains.shape, F32),
        ],
        [(4, None, 4, "mp", 0, step) for step in others]
        + [(0, "mp", 0, "mp", 0, step) for step in others]
        + [(1, "mp", 1, "mp", -1, step) for step in others]
        + [(3, None, 3, ("mp", group), 0, step) for step in others]
        + [(2, "mp", 2, "mp", 0, step) for step in others],
    )
    body = groups_joined(body_got).reshape(rows, wide, width)
    edge = groups_joined(edge_got).reshape(WIN_H, wide, width)
    cot = groups_joined(cot_got).reshape(rows, block, width)
    first_all = gains_all[:, 0, :group].reshape(1, width)
    merge_gain_all = gains_all[:, 1:5, :group].transpose(1, 0, 2).reshape(4, width)
    mlp_gain_row = mlp_gain.reshape(1, width_two)
    own_fields = merge_patches(body[:, :block], padded)
    cot_patches = merge_patches(cot, padded)

    def into_frame(whole):
        part = lax.dynamic_slice(
            whole, (lat_offset, lon_offset, jnp.int32(0)), (rows, block, width)
        )
        return to_windows(part).reshape(tokens, width)

    framed_fields = into_frame(jnp.concatenate([body, edge], axis=0))
    cut = (jnp.int32(rows) * (n_lat - lat) - lat_offset).reshape(1)
    attention_framed, context = local_kernel(
        attention_forward,
        [cut, framed_fields, first_all, weights_all],
        [((tokens, width), BF16), ((tokens, width), BF16)],
        [pltpu.VMEM((3, tokens, width), F32), pltpu.VMEM((tokens, width), F32)],
        scalars=1,
    )
    window_shape = (bands, columns, WIN, width)
    around = (bands + 1, columns + 1, WIN, width)
    halo, section_all = exchange(
        2,
        [attention_framed.reshape(window_shape), half_all],
        [(around, BF16), ((8, n_mp, group, width_two), BF16)],
        [
            (0, (bands - 1, columns - 1), 0, (0, 0), 1, 1),
            (0, (slice(0, bands), columns - 1), 0, (slice(1, bands + 1), 0), 0, 1),
            (0, (bands - 1,), 0, (0, slice(1, columns + 1)), 1, 0),
            (1, None, 1, "core", "sibling", 0),
            (1, None, 1, "core", 0, 0),
            (0, None, 0, (slice(1, bands + 1), slice(1, columns + 1)), 0, 0),
        ],
    )
    section_all = section_all.reshape(8, width, width_two)
    attention = lax.dynamic_slice(
        from_windows(halo),
        (WIN_H - lat_offset, WIN_W - lon_offset, jnp.int32(0)),
        (rows, block, width),
    )
    pair, hidden, merged, grad_bottom = local_kernel(
        merge_forward,
        [
            own_fields,
            merge_patches(attention, padded),
            cot_patches,
            merge_gain_all,
            mlp_gain_row,
            section_all,
        ],
        [
            ((padded, 2 * width_two), BF16),
            ((4, padded, width), BF16),
            ((padded, width_two), BF16),
            ((padded, width_two), F32),
        ],
    )
    (pairs,) = exchange(
        3,
        [pair],
        [((n_mp,) + pair.shape, BF16)],
        [(0, None, 0, "mp", 0, step) for step in others],
    )
    pairs = pairs.reshape(n_mp * padded, 2 * width_two)
    mlp_in, bottom_grad = pairs[:, :width_two], pairs[:, width_two:]
    hidden_up = jnp.dot(mlp_in, up_weight, preferred_element_type=F32)
    activated = jax.nn.gelu(hidden_up).astype(BF16)
    grad_act = jnp.dot(bottom_grad, down_weight, preferred_element_type=F32)
    gelu_back = jax.vjp(jax.nn.gelu, hidden_up)[1]
    grad_pre = gelu_back(grad_act)[0].astype(BF16)
    terms = jnp.concatenate(
        [
            jnp.einsum("af,ef->ae", activated, down_weight, preferred_element_type=F32),
            jnp.einsum("af,ef->ae", grad_pre, up_weight, preferred_element_type=F32),
        ],
        axis=1,
    ).astype(BF16)
    (parts,) = exchange(
        4,
        [terms.reshape(n_mp, padded, 2 * width_two)],
        [((n_mp, padded, 2 * width_two), BF16)],
        [(0, "mp", 0, "mp", 0, step) for step in others],
    )
    down_local = jnp.einsum("ao,af->of", bottom_grad, activated, preferred_element_type=F32)
    up_local = jnp.einsum("ae,af->ef", mlp_in, grad_pre, preferred_element_type=F32)
    decoded_slab, grad_hidden = local_kernel(
        merge_backward,
        [
            parts,
            merged,
            grad_bottom,
            hidden,
            cot_patches,
            merge_gain_all,
            mlp_gain_row,
            section_all,
        ],
        [((n_mp, 2 * padded, 2 * group), BF16), ((4, padded, width), BF16)],
    )
    grad_windows = grad_hidden[:, :merged_count].reshape(
        2, 2, bands, WIN_H // 2, columns, WIN_W // 2, width
    )
    grad_windows = grad_windows.transpose(2, 4, 3, 0, 5, 1, 6).reshape(window_shape)
    halo, decoded_got = exchange(
        5,
        [grad_windows, decoded_slab],
        [(around, BF16), (decoded_slab.shape, BF16)],
        [
            (0, (0, 0), 0, (bands, columns), -1, -1),
            (0, (slice(0, bands), 0), 0, (slice(0, bands), columns), 0, -1),
            (0, (0,), 0, (bands, slice(0, columns)), -1, 0),
            (0, None, 0, (slice(0, bands), slice(0, columns)), 0, 0),
        ]
        + [(1, "mp", 1, "mp", 0, step) for step in others],
    )
    grad_framed = into_frame(from_windows(halo))
    grad_slab, weight_grads = local_kernel(
        attention_backward,
        [cut, framed_fields, first_all, weights_all, context, grad_framed],
        [((n_mp, tokens // 2, 2 * group), BF16), ((4, width, width), BF16)],
        [
            pltpu.VMEM((3, tokens, width), F32),
            pltpu.VMEM((3, tokens, width), F32),
            pltpu.VMEM((tokens, width), F32),
        ],
        scalars=1,
    )
    large = (n_lat, width_two // n_lat, span)
    grad_got, edge_got, weight_got, up_got, down_got = exchange(
        6,
        [
            grad_slab,
            weight_grads,
            up_local.astype(BF16).reshape(large),
            down_local.astype(BF16).reshape(large),
        ],
        [
            (grad_slab.shape, BF16),
            (grad_slab.shape, BF16),
            ((n_mp, 4, group, width), BF16),
            (large, BF16),
            (large, BF16),
        ],
        [(1, ("mp", group), 2, "mp", 0, step) for step in others]
        + [(2, "lat", 3, "lat", step, 0) for step in range(n_lat)]
        + [(3, "lat", 4, "lat", step, 0) for step in range(n_lat)]
        + [(0, "mp", 0, "mp", 0, step) for step in others]
        + [(0, "mp", 1, "mp", 1, step) for step in others],
    )
    weight_sum = jnp.sum(weight_got.astype(F32), axis=0).astype(BF16)
    weight_sum = weight_sum.reshape(4 * group, width).transpose(1, 0)
    (lat_got,) = exchange(
        7,
        [weight_sum.reshape(n_lat, width // n_lat, 4 * group)],
        [((n_lat, width // n_lat, 4 * group), BF16)],
        [(0, "lat", 0, "lat", step, 0) for step in range(n_lat)],
    )
    grad_up = jnp.sum(up_got.astype(F32), axis=0)
    grad_down = jnp.sum(down_got.astype(F32), axis=0)
    weight_total = jnp.sum(lat_got.astype(F32), axis=0)
    grad_qkv = weight_total[:, : 3 * group].reshape(width // n_lat, 3, group)
    grad_proj = weight_total[:, 3 * group :]
    decoded_view = decoded_got.reshape(n_mp, 2, padded, 2, group)[:, :, :merged_count]
    decoded_view = decoded_view.reshape(n_mp, 2, rows // 2, block // 2, 2, group)
    decoded = decoded_view.transpose(2, 4, 0, 3, 1, 5).reshape(rows, lon_count, group)

    def columns_joined(slabs):
        view = slabs.reshape(n_mp, columns, WIN_H, WIN_W, -1, group)
        return view.transpose(4, 2, 0, 1, 3, 5).reshape(-1, lon_count, group)

    grad_rows = jnp.concatenate(
        [columns_joined(edge_got[..., group:]), columns_joined(grad_got)], axis=0
    )
    grad_rows = jnp.concatenate([grad_rows[:, -WIN_W:], grad_rows], axis=1)
    grad_input = lax.dynamic_slice(
        grad_rows,
        (WIN_H - lat_offset, WIN_W - lon_offset, jnp.int32(0)),
        (rows, lon_count, group),
    ).astype(F32)
    return (decoded, grad_input, grad_qkv, grad_proj, grad_up, grad_down)


def solution(mesh):
    return jax.shard_map(
        shards,
        mesh=mesh,
        in_specs=(
            P("lat", None, "mp"),
            P("mp"),
            P(None, None, "mp"),
            P(None, "mp"),
            P(None, "mp"),
            P(None, "mp", None),
            P(),
            P(None, "mp"),
            P(None, "mp"),
            P(None, None, "mp"),
            P(),
            P(),
            P("lat", None, "mp"),
        ),
        out_specs=(
            P("lat", None, "mp"),
            P("lat", None, "mp"),
            P("lat", None, "mp"),
            P("lat", "mp"),
            P("lat", "mp"),
            P("lat", "mp"),
        ),
        check_vma=False,
    )
```

```python
import jax
import jax.numpy as jnp
from jax import lax
from jax.experimental import pallas as pl
from jax.experimental.pallas import tpu as pltpu
from jax.sharding import PartitionSpec as P

WIN_H = 6
WIN_W = 12
HDIM = 64
EPSILON = 1e-05
MASKED = -1e30
BF16 = jnp.bfloat16
F32 = jnp.float32


def positions():
    lat, mp = lax.axis_index("lat"), lax.axis_index("mp")
    return {
        "lat": lat,
        "mp": mp,
        "core": lax.rem(lat, 2),
        "x": lax.div(mp, 2),
        "z": lax.rem(mp, 2),
    }


def reached(here, down, right):
    n_lat, n_mp = lax.axis_size("lat"), lax.axis_size("mp")
    if down == "sibling":
        return {"lat": here["lat"] + 1 - 2 * here["core"], "mp": here["mp"]}
    return {
        "lat": lax.rem(here["lat"] + n_lat + down, n_lat),
        "mp": lax.rem(here["mp"] + n_mp + right, n_mp),
    }


def device_of(target):
    return {
        "device_id": (target["lat"], target["mp"]),
        "device_id_type": pl.DeviceIdType.MESH,
    }


def greet(here, steps):
    barrier = pltpu.get_barrier_semaphore()
    for down, right in steps:
        source = reached(here, down if down == "sibling" else -down, -right)
        pl.semaphore_signal(barrier, inc=1, **device_of(source))
    pl.semaphore_wait(barrier, len(steps))


def remote(source, landing, send, receive, target):
    return pltpu.make_async_remote_copy(
        src_ref=source, dst_ref=landing, send_sem=send, recv_sem=receive, **device_of(target)
    )


def exchange(collective, inputs, outputs, moves):
    steps = []
    for move in moves:
        if move[4:6] != (0, 0) and move[4:6] not in steps:
            steps.append(move[4:6])

    def body(*refs):
        sources = refs[: len(inputs)]
        landings = refs[len(inputs) : len(inputs) + len(outputs)]
        send, receive = refs[-2:]
        here = positions()

        def part_of(ref, part, place, target):
            if part is None:
                return ref
            if isinstance(part, str):
                return ref.at[place[part]]
            if callable(part):
                return part(ref, here, target)
            return ref.at[part]

        greet(here, steps)
        copies = []
        arrived = set()
        for index, move in enumerate(moves):
            source, source_part, landing, landing_part, down, right = move[:6]
            target = reached(here, down, right)
            if len(move) > 6:
                copies[move[6]].wait_recv()
                arrived.add(move[6])
                source_ref = part_of(landings[source], source_part, target, target)
            else:
                source_ref = part_of(sources[source], source_part, target, target)
            landing_ref = part_of(landings[landing], landing_part, here, target)
            if (down, right) == (0, 0):
                copy = pltpu.make_async_copy(source_ref, landing_ref, receive.at[index])
            else:
                copy = remote(
                    source_ref, landing_ref, send.at[index], receive.at[index], target
                )
            copy.start()
            copies.append(copy)
        for index, copy in enumerate(copies):
            if moves[index][4:6] == (0, 0):
                copy.wait()
            else:
                copy.wait_send()
                if index not in arrived:
                    copy.wait_recv()

    return pl.pallas_call(
        body,
        out_shape=[jax.ShapeDtypeStruct(shape, dtype) for shape, dtype in outputs],
        in_specs=[pl.BlockSpec(memory_space=pl.ANY)] * len(inputs),
        out_specs=[pl.BlockSpec(memory_space=pl.ANY)] * len(outputs),
        scratch_shapes=[
            pltpu.SemaphoreType.DMA((len(moves),)),
            pltpu.SemaphoreType.DMA((len(moves),)),
        ],
        compiler_params=pltpu.CompilerParams(collective_id=collective, has_side_effects=True),
    )(*inputs)


X_STEPS = ((4, 2), (2, 1), (-2, 3))


def terms_back(collective, terms):
    count, _, rows, width = terms.shape

    def body(terms_ref, parts_ref, other, own, total, send, receive, fetch):
        here = positions()
        core, x = here["core"], here["x"]
        sibling = reached(here, "sibling", 0)
        greet(here, [("sibling", 0)] + [(0, right) for right, _ in X_STEPS])
        order = [lax.rem(x + step, count) for _, step in X_STEPS] + [x]
        swaps, loads = [], []
        for index, spot in enumerate(order):
            swap = remote(
                terms_ref.at[spot, 1 - core],
                other.at[index],
                send.at[index],
                receive.at[index],
                sibling,
            )
            load = pltpu.make_async_copy(terms_ref.at[spot, core], own.at[index], fetch.at[index])
            swap.start()
            load.start()
            swaps.append(swap)
            loads.append(load)
        sends = []
        for index, spot in enumerate(order):
            loads[index].wait()
            swaps[index].wait_recv()
            total[index] = (own[index].astype(F32) + other[index].astype(F32)).astype(BF16)
            if index < len(X_STEPS):
                copy = remote(
                    total.at[index],
                    parts_ref.at[x],
                    send.at[count + index],
                    receive.at[count + index],
                    reached(here, 0, X_STEPS[index][0]),
                )
            else:
                copy = pltpu.make_async_copy(total.at[index], parts_ref.at[x], fetch.at[count])
            copy.start()
            sends.append(copy)
        for swap in swaps:
            swap.wait_send()
        for copy in sends:
            copy.wait()

    return pl.pallas_call(
        body,
        out_shape=jax.ShapeDtypeStruct((count, rows, width), BF16),
        in_specs=[pl.BlockSpec(memory_space=pl.ANY)],
        out_specs=pl.BlockSpec(memory_space=pl.ANY),
        scratch_shapes=[
            pltpu.VMEM((count, rows, width), BF16),
            pltpu.VMEM((count, rows, width), BF16),
            pltpu.VMEM((count, rows, width), BF16),
            pltpu.SemaphoreType.DMA((2 * count,)),
            pltpu.SemaphoreType.DMA((2 * count,)),
            pltpu.SemaphoreType.DMA((count + 1,)),
        ],
        compiler_params=pltpu.CompilerParams(
            collective_id=collective, has_side_effects=True, vmem_limit_bytes=48 * 1024 * 1024
        ),
    )(terms)


def gradients_out(collective, weight_grads, slabs, up_grads, down_grads):
    n_lat, n_mp = lax.axis_size("lat"), lax.axis_size("mp")
    kinds, width, _ = weight_grads.shape
    pair, group, share = kinds // 2, width // n_mp, width // n_lat

    def body(
        weight_ref, slab_ref, up_ref, down_ref, out_ref, got_ref, edge_ref, up_got, down_got,
        other, total, parts, turned, landed, send, receive, large_send, large_receive,
    ):
        here = positions()
        lat, mp, core, x, z = (here[name] for name in ("lat", "mp", "core", "x", "z"))
        mine = 2 * lax.div(lat, 2) + z
        owner = z == core
        sibling = reached(here, "sibling", 0)
        barrier = pltpu.get_barrier_semaphore()
        greeted = [sibling]
        greeted += [reached(here, 0, -step) for step in range(1, n_mp)]
        greeted += [reached(here, -1, -step) for step in range(n_mp)]
        greeted += [reached(here, -step, 0) for step in range(1, n_lat)]
        for target in greeted:
            pl.semaphore_signal(barrier, inc=1, **device_of(target))
        for source in range(n_lat):

            @pl.when(jnp.logical_or(jnp.logical_not(owner), mine != source))
            def _():
                target = {"lat": 2 * (source // 2) + z, "mp": 2 * x + source % 2}
                pl.semaphore_signal(barrier, inc=1, **device_of(target))

        pl.semaphore_wait(barrier, len(greeted) + n_lat - jnp.where(owner, 1, 0))

        copies = []

        def sent(source, landing, target):
            index = len(copies)
            copy = remote(source, landing, send.at[index], receive.at[index], target)
            copy.start()
            copies.append(copy)
            return copy

        swap = sent(weight_ref.at[pl.ds(pair * (1 - core), pair)], other, sibling)
        for step in range(1, n_mp):
            target = reached(here, 0, step)
            sent(slab_ref.at[target["mp"]], got_ref.at[mp], target)
        for step in range(n_mp):
            target = reached(here, 1, step)
            sent(slab_ref.at[target["mp"]], edge_ref.at[mp], target)

        large = ((up_ref, up_got), (down_ref, down_got))
        for which, (source, landing) in enumerate(large):
            for step in range(n_lat):
                target = {"lat": lax.rem(lat + step, n_lat), "mp": 2 * x + core}

                def there():
                    return remote(
                        source.at[target["lat"]],
                        landing.at[mine],
                        large_send.at[which, step],
                        large_receive.at[which, mine],
                        target,
                    )

                if step == 0:

                    @pl.when(owner)
                    def _():
                        pltpu.make_async_copy(
                            source.at[lat], landing.at[mine], large_receive.at[which, mine]
                        ).start()

                    @pl.when(jnp.logical_not(owner))
                    def _():
                        there().start()

                else:
                    there().start()
        own_slab = pltpu.make_async_copy(slab_ref.at[mp], got_ref.at[mp], send.at[60])
        own_slab.start()

        swap.wait_recv()
        total[...] = (
            weight_ref[pl.ds(pair * core, pair)].astype(F32) + other[...].astype(F32)
        ).astype(BF16)
        scattered = []
        for step in range(1, n_mp):
            target = reached(here, 0, step)
            rows = pl.ds(pl.multiple_of(group * target["mp"], group), group)
            scattered.append(sent(total.at[:, rows], parts.at[mp], target))
        gathered = total[:, pl.ds(pl.multiple_of(group * mp, group), group), :].astype(F32)
        for step in range(1, n_mp):
            scattered[step - 1].wait_recv()
            gathered = gathered + parts[lax.rem(mp + n_mp - step, n_mp)].astype(F32)
        flat = gathered.reshape(pair * group, width).T.astype(BF16)
        for index in range(n_lat):
            turned[index] = flat[index * share : (index + 1) * share]
        spread = []
        for step in range(1, n_lat):
            target = reached(here, step, 0)
            spread.append(sent(turned.at[target["lat"]], landed.at[lat], target))
        landed[lat] = turned[lat]
        for copy in spread:
            copy.wait_recv()
        for half in range(2):
            result = landed[half].astype(F32)
            for index in range(half + 2, n_lat, 2):
                result = result + landed[index].astype(F32)
            out_ref[:, half * pair * group : (half + 1) * pair * group] = result

        done = [swap] + scattered + spread
        for copy in copies:
            copy.wait_send()
            if not any(copy is other_copy for other_copy in done):
                copy.wait_recv()
        own_slab.wait()
        for which, (source, landing) in enumerate(large):
            for step in range(n_lat):
                target = {"lat": lax.rem(lat + step, n_lat), "mp": 2 * x + core}
                wait = remote(
                    source.at[target["lat"]],
                    landing.at[step],
                    large_send.at[which, step],
                    large_receive.at[which, step],
                    target,
                )
                wait.wait_recv()
                if step == 0:

                    @pl.when(jnp.logical_not(owner))
                    def _():
                        wait.wait_send()

                else:
                    wait.wait_send()

    any_space = pl.BlockSpec(memory_space=pl.ANY)
    vmem = pl.BlockSpec(memory_space=pltpu.VMEM)
    return pl.pallas_call(
        body,
        out_shape=[
            jax.ShapeDtypeStruct((share, kinds * group), F32),
            jax.ShapeDtypeStruct(slabs.shape, BF16),
            jax.ShapeDtypeStruct(slabs.shape, BF16),
            jax.ShapeDtypeStruct(up_grads.shape, BF16),
            jax.ShapeDtypeStruct(down_grads.shape, BF16),
        ],
        in_specs=[vmem, any_space, any_space, any_space],
        out_specs=[vmem, any_space, any_space, any_space, any_space],
        scratch_shapes=[
            pltpu.VMEM((pair, width, width), BF16),
            pltpu.VMEM((pair, width, width), BF16),
            pltpu.VMEM((n_mp, pair, group, width), BF16),
            pltpu.VMEM((n_lat, share, pair * group), BF16),
            pltpu.VMEM((n_lat, share, pair * group), BF16),
            pltpu.SemaphoreType.DMA((64,)),
            pltpu.SemaphoreType.DMA((64,)),
            pltpu.SemaphoreType.DMA((2, n_lat)),
            pltpu.SemaphoreType.DMA((2, n_lat)),
        ],
        compiler_params=pltpu.CompilerParams(
            collective_id=collective, has_side_effects=True, vmem_limit_bytes=48 * 1024 * 1024
        ),
    )(weight_grads, slabs, up_grads, down_grads)


def local_kernel(body, operands, outputs, scratch=(), scalars=0, outside=0):
    spaces = [pltpu.SMEM] * scalars + [pltpu.VMEM] * (len(operands) - scalars - outside)
    spaces += [pl.ANY] * outside
    return pl.pallas_call(
        body,
        out_shape=[jax.ShapeDtypeStruct(shape, dtype) for shape, dtype in outputs],
        in_specs=[pl.BlockSpec(memory_space=space) for space in spaces],
        out_specs=[pl.BlockSpec(memory_space=pltpu.VMEM)] * len(outputs),
        scratch_shapes=list(scratch),
        compiler_params=pltpu.CompilerParams(vmem_limit_bytes=48 * 1024 * 1024),
    )(*operands)


def dot_nn(left, right):
    return lax.dot_general(left, right, (((1,), (0,)), ((), ())), preferred_element_type=F32)


def dot_nt(left, right):
    return lax.dot_general(left, right, (((1,), (1,)), ((), ())), preferred_element_type=F32)


def dot_tn(left, right):
    return lax.dot_general(left, right, (((0,), (0,)), ((), ())), preferred_element_type=F32)


def halves_beside(values):
    half = values.shape[-2] // 2
    return jnp.concatenate([values[..., :half, :], values[..., half:, :]], axis=-1)


def groups_joined(slabs):
    count, half, _ = slabs.shape
    view = slabs.reshape(count, half, 2, HDIM).transpose(2, 1, 0, 3)
    return view.reshape(2 * half, count * HDIM)


def to_windows(grid):
    row_count, lon_count = (grid.shape[0], grid.shape[1])
    trailing = grid.shape[2:]
    view = grid.reshape((row_count // WIN_H, WIN_H, lon_count // WIN_W, WIN_W) + trailing)
    view = jnp.swapaxes(view, 1, 2)
    return view.reshape(((row_count // WIN_H) * (lon_count // WIN_W), WIN_H * WIN_W) + trailing)


def from_windows(windows):
    bands, columns, _, width = windows.shape
    view = windows.reshape((bands, columns, WIN_H, WIN_W, width))
    view = jnp.swapaxes(view, 1, 2)
    return view.reshape((bands * WIN_H, columns * WIN_W, width))


def merge_patches(grid, padded):
    row_count, lon_count, features = grid.shape
    view = grid.reshape(row_count // 2, 2, lon_count // 2, 2, features)
    view = view.transpose(1, 3, 0, 2, 4).reshape(4, row_count * lon_count // 4, features)
    return jnp.pad(view, ((0, 0), (0, padded - view.shape[1]), (0, 0)))


def norm_stats(values, count):
    center = sum(jnp.sum(value, axis=1, keepdims=True) for value in values) / count
    second = sum(jnp.sum(value * value, axis=1, keepdims=True) for value in values) / count
    return (center, lax.rsqrt(second - center * center + EPSILON))


def norm_backward(grads, gains, units, scale_inv, count):
    scaled = [grad * gain for grad, gain in zip(grads, gains)]
    first = sum(jnp.sum(value, axis=1, keepdims=True) for value in scaled) / count
    second = (
        sum(jnp.sum(value * unit, axis=1, keepdims=True) for value, unit in zip(scaled, units))
        / count
    )
    return [scale_inv * (value - first - unit * second) for value, unit in zip(scaled, units)]


def pair_slabs(upper, lower, out_ref, first_rows):
    low = lax.broadcasted_iota(jnp.int32, (upper.shape[0], 2 * HDIM), 1) < HDIM
    rows = pl.ds(first_rows, upper.shape[0])
    for pair in range(upper.shape[1] // (2 * HDIM)):
        lanes = slice(2 * HDIM * pair, 2 * HDIM * (pair + 1))
        one, two = upper[:, lanes], lower[:, lanes]
        swapped_one = jnp.concatenate([one[:, HDIM:], one[:, :HDIM]], axis=1)
        swapped_two = jnp.concatenate([two[:, HDIM:], two[:, :HDIM]], axis=1)
        out_ref[2 * pair, rows, :] = jnp.where(low, one, swapped_two).astype(BF16)
        out_ref[2 * pair + 1, rows, :] = jnp.where(low, swapped_one, two).astype(BF16)


WIN = WIN_H * WIN_W
FACTOR = HDIM ** (-0.5)


def heads_apart(values):
    low = lax.broadcasted_iota(jnp.int32, values.shape, 1) < HDIM
    zero = jnp.zeros_like(values)
    both = [jnp.where(low, values, zero), jnp.where(low, zero, values)]
    return jnp.concatenate(both, axis=0).astype(BF16)


def heads_together(values):
    low = lax.broadcasted_iota(jnp.int32, (WIN, 2 * HDIM), 1) < HDIM
    return jnp.where(low, values[:WIN], values[WIN:])


def window_probs(cut, window, query, keys):
    scores = dot_nt(query, keys) * FACTOR
    spot = lax.broadcasted_iota(jnp.int32, scores.shape, 0)
    spot = jnp.where(spot >= WIN, spot - WIN, spot)
    other = lax.broadcasted_iota(jnp.int32, scores.shape, 1)
    edge = cut * WIN_W - jnp.where(window >= 3, WIN, 0)
    same = (spot >= edge) == (other >= edge)
    scores = jnp.where(same, scores, MASKED)
    weights = jnp.exp(scores - jnp.max(scores, axis=1, keepdims=True))
    return weights / jnp.sum(weights, axis=1, keepdims=True)


def framed_packed(fields_ref, gain_ref, weights_ref, packed):
    values = fields_ref[...].astype(F32)
    center, scale_inv = norm_stats([values], values.shape[1])
    unit = (values - center) * scale_inv
    framed = (unit * gain_ref[...]).astype(BF16)
    for kind in range(3):
        packed[kind] = dot_nt(framed, weights_ref[kind]).astype(BF16).astype(F32)
    return (framed, unit, scale_inv)


def window_parts(refs, window, pair):
    rows = pl.ds(pl.multiple_of(window * WIN, 8), WIN)
    lanes = slice(2 * HDIM * pair, 2 * HDIM * (pair + 1))
    return [ref[rows, lanes] for ref in refs]


def attention_forward(cut_ref, fields_ref, gain_ref, weights_ref, out_ref, context_ref, packed, held):
    framed_packed(fields_ref, gain_ref, weights_ref, packed)
    cut = cut_ref[0]
    windows = fields_ref.shape[0] // WIN

    def step(window, carry):
        rows = pl.ds(pl.multiple_of(window * WIN, 8), WIN)
        for pair in range(fields_ref.shape[1] // (2 * HDIM)):
            query, keys, values = window_parts([packed.at[kind] for kind in range(3)], window, pair)
            probs = window_probs(cut, window, heads_apart(query), keys.astype(BF16))
            joined = dot_nn(probs.astype(BF16), values.astype(BF16))
            held[rows, 2 * HDIM * pair : 2 * HDIM * (pair + 1)] = heads_together(joined)
        return carry

    lax.fori_loop(0, windows, step, 0)
    context = held[...].astype(BF16)
    context_ref[...] = context
    out_ref[...] = dot_nn(context, weights_ref[3]).astype(BF16)


def attention_backward(
    cut_ref, fields_ref, gain_ref, weights_ref, context_ref, grad_ref, slab_ref, weight_ref,
    packed, grads, held,
):
    framed, unit, scale_inv = framed_packed(fields_ref, gain_ref, weights_ref, packed)
    cut = cut_ref[0]
    windows = fields_ref.shape[0] // WIN
    grad_framed = grad_ref[...]
    held[...] = dot_nt(grad_framed, weights_ref[3]).astype(BF16).astype(F32)

    def step(window, carry):
        rows = pl.ds(pl.multiple_of(window * WIN, 8), WIN)
        for pair in range(fields_ref.shape[1] // (2 * HDIM)):
            lanes = slice(2 * HDIM * pair, 2 * HDIM * (pair + 1))
            query, keys, values, grad = window_parts(
                [packed.at[kind] for kind in range(3)] + [held], window, pair
            )
            query, grad = heads_apart(query), heads_apart(grad)
            keys, values = keys.astype(BF16), values.astype(BF16)
            probs = window_probs(cut, window, query, keys)
            grad_probs = dot_nt(grad, values)
            inner = jnp.sum(grad_probs * probs, axis=1, keepdims=True)
            grad_scores = (probs * (grad_probs - inner) * FACTOR).astype(BF16)
            grads[0, rows, lanes] = heads_together(dot_nn(grad_scores, keys))
            grads[1, rows, lanes] = dot_tn(grad_scores, query)
            grads[2, rows, lanes] = dot_tn(probs.astype(BF16), grad)
        return carry

    lax.fori_loop(0, windows, step, 0)
    grad_normed = jnp.zeros(fields_ref.shape, F32)
    for kind in range(3):
        grad_kind = grads[kind].astype(BF16)
        weight_ref[kind] = dot_tn(grad_kind, framed).astype(BF16)
        grad_normed = grad_normed + dot_nn(grad_kind, weights_ref[kind])
    weight_ref[3] = dot_tn(context_ref[...], grad_framed).astype(BF16)
    (back,) = norm_backward([grad_normed], [gain_ref[...]], [unit], scale_inv, unit.shape[1])
    result = grad_framed.astype(F32) + back
    half = result.shape[0] // 2
    pair_slabs(result[:half], result[half:], slab_ref, 0)


def section_loads(core_ref, own_ref, other_ref, weights, loaded):
    core = core_ref[0]
    loads = [
        pltpu.make_async_copy(own_ref, weights.at[core], loaded.at[0]),
        pltpu.make_async_copy(other_ref, weights.at[1 - core], loaded.at[1]),
    ]
    for load in loads:
        load.start()
    return loads


def merge_forward(
    core_ref, fields_ref, attention_ref, cot_ref, gain_ref, mlp_gain_ref, own_ref, other_ref,
    pair_ref, hidden_ref, merged_ref, grad_ref, weights, loaded,
):
    loads = section_loads(core_ref, own_ref, other_ref, weights, loaded)
    width_two = merged_ref.shape[1]
    hidden = []
    for patch in range(4):
        value = fields_ref[patch].astype(F32) + attention_ref[patch].astype(F32)
        hidden_ref[patch] = value.astype(BF16)
        hidden.append(value.astype(BF16).astype(F32))
    center, scale_inv = norm_stats(hidden, 4 * hidden[0].shape[1])
    merged = jnp.zeros(merged_ref.shape, F32)
    grad = jnp.zeros(merged_ref.shape, F32)
    for load in loads:
        load.wait()
    for patch in range(4):
        normed = (hidden[patch] - center) * scale_inv * gain_ref[patch : patch + 1, :]
        merged = merged + dot_nn(normed.astype(BF16), weights[0, patch])
        grad = grad + dot_nn(cot_ref[patch], weights[1, patch])
    merged_ref[...] = merged.astype(BF16)
    merged = merged.astype(BF16).astype(F32)
    center, scale_inv = norm_stats([merged], width_two)
    mlp_in = (merged - center) * scale_inv * mlp_gain_ref[...]
    pair_ref[:, :width_two] = mlp_in.astype(BF16)
    pair_ref[:, width_two:] = grad.astype(BF16)
    grad_ref[...] = grad


def merge_backward(
    core_ref, parts_ref, merged_ref, grad_ref, hidden_ref, cot_ref, gain_ref, mlp_gain_ref,
    own_ref, other_ref, slab_ref, out_ref, weights, loaded,
):
    loads = section_loads(core_ref, own_ref, other_ref, weights, loaded)
    width_two = merged_ref.shape[1]
    count = merged_ref.shape[0]
    total = parts_ref[0].astype(F32)
    for index in range(1, parts_ref.shape[0]):
        total = total + parts_ref[index].astype(F32)
    merged = merged_ref[...].astype(F32)
    bottom = (merged + total[:, :width_two]).astype(BF16)
    for load in loads:
        load.wait()
    decoded = [
        hidden_ref[patch].astype(F32) + dot_nt(bottom, weights[1, patch])
        for patch in range(4)
    ]
    for side in range(2):
        pair_slabs(decoded[side], decoded[2 + side], slab_ref, side * count)
    center, scale_inv = norm_stats([merged], width_two)
    unit = (merged - center) * scale_inv
    (back,) = norm_backward(
        [total[:, width_two:]], [mlp_gain_ref[...]], [unit], scale_inv, width_two
    )
    grad_merged = (grad_ref[...] + back).astype(BF16)
    hidden = [hidden_ref[patch].astype(F32) for patch in range(4)]
    center, scale_inv = norm_stats(hidden, 4 * hidden[0].shape[1])
    units = [(value - center) * scale_inv for value in hidden]
    backs = norm_backward(
        [dot_nt(grad_merged, weights[0, patch]) for patch in range(4)],
        [gain_ref[patch : patch + 1, :] for patch in range(4)],
        units,
        scale_inv,
        4 * hidden[0].shape[1],
    )
    for patch in range(4):
        out_ref[patch] = (cot_ref[patch].astype(F32) + backs[patch]).astype(BF16)


def shards(
    fields,
    first_gain,
    qkv_weight,
    proj_weight,
    merge_gain,
    merge_weight,
    mlp_gain,
    up_weight,
    down_weight,
    expand_weight,
    lat_shift,
    lon_shift,
    cotangent,
):
    n_lat, n_mp = lax.axis_size("lat"), lax.axis_size("mp")
    lat, core = lax.axis_index("lat"), lax.rem(lax.axis_index("lat"), 2)
    lat_offset = lat_shift[0]
    lon_offset = lon_shift[0]
    rows, lon_count, group = fields.shape
    width = group * n_mp
    block = lon_count // n_mp
    wide = block + WIN_W
    bands, columns = rows // WIN_H, block // WIN_W
    tokens = rows * block
    width_two = merge_weight.shape[2]
    span = up_weight.shape[1]
    merged_count = tokens // 4
    padded = -(-merged_count // 16) * 16
    others = range(n_mp)

    section = jnp.where(core == 0, merge_weight, expand_weight.transpose(1, 2, 0))
    section_own = lax.all_gather(section, "mp", axis=1, tiled=True)
    has_shard = lax.rem(lax.axis_index("mp"), 2) == core
    fetch = [
        (at * n_mp + m, at * n_mp + (m ^ 1))
        for at in range(n_lat)
        for m in range(n_mp)
        if at % 2 == m % 2
    ]
    up_shard, down_shard = (
        jnp.where(has_shard, weight, lax.ppermute(weight, ("lat", "mp"), fetch))
        for weight in (up_weight, down_weight)
    )

    blocks = fields.reshape(rows, n_mp, block, group).transpose(1, 0, 2, 3)
    margin = jnp.roll(blocks[:, :, :WIN_W], -1, axis=0)
    field_blocks = jnp.concatenate([blocks, margin], axis=2)
    body_slab = halves_beside(field_blocks.reshape(n_mp, rows * wide, group))
    edge_slab = halves_beside(field_blocks[:, :WIN_H].reshape(n_mp, WIN_H * wide, group))
    cot_blocks = cotangent.reshape(rows, n_mp, block, group).transpose(1, 0, 2, 3)
    cot_slab = halves_beside(cot_blocks.reshape(n_mp, tokens, group))
    weights = jnp.concatenate(
        [qkv_weight.transpose(1, 2, 0), proj_weight.transpose(1, 0)[None]], axis=0
    )
    gains = jnp.pad(jnp.concatenate([first_gain[None], merge_gain], axis=0), ((0, 3), (0, 64)))

    def rows_at(here, step):
        return pl.ds(pl.multiple_of(lax.rem(here["mp"] + n_mp - step, n_mp) * group, group), group)

    def core_half(ref, here, target):
        return ref.at[pl.ds(2 * here["core"], 2)]

    def core_half_rows(step):
        return lambda ref, here, target: ref.at[pl.ds(2 * here["core"], 2), rows_at(here, step)]

    def own_rows(ref, here, target):
        return ref.at[:, rows_at(here, 0)]

    body_got, edge_got, cot_got, weights_all, gains_all = exchange(
        1,
        [body_slab, edge_slab, cot_slab, weights, gains],
        [
            (body_slab.shape, BF16),
            (edge_slab.shape, BF16),
            (cot_slab.shape, BF16),
            ((4, width, width), BF16),
            ((n_mp,) + gains.shape, F32),
        ],
        [(3, core_half, 3, core_half_rows(0), 0, step) for step in range(1, n_mp)]
        + [(4, None, 4, "mp", 0, step) for step in others]
        + [(0, "mp", 0, "mp", 0, step) for step in others]
        + [(1, "mp", 1, "mp", -1, step) for step in others]
        + [(2, "mp", 2, "mp", 0, step) for step in others]
        + [(3, None, 3, own_rows, 0, 0)]
        + [
            (3, core_half_rows(step), 3, core_half_rows(step), "sibling", 0, step - 1)
            for step in range(1, n_mp)
        ],
    )
    body = groups_joined(body_got).reshape(rows, wide, width)
    edge = groups_joined(edge_got).reshape(WIN_H, wide, width)
    cot = groups_joined(cot_got).reshape(rows, block, width)
    first_all = gains_all[:, 0, :group].reshape(1, width)
    merge_gain_all = gains_all[:, 1:5, :group].transpose(1, 0, 2).reshape(4, width)
    mlp_gain_row = mlp_gain.reshape(1, width_two)
    own_fields = merge_patches(body[:, :block], padded)
    cot_patches = merge_patches(cot, padded)

    def into_frame(whole):
        part = lax.dynamic_slice(
            whole, (lat_offset, lon_offset, jnp.int32(0)), (rows, block, width)
        )
        return to_windows(part).reshape(tokens, width)

    framed_fields = into_frame(jnp.concatenate([body, edge], axis=0))
    cut = (jnp.int32(rows) * (n_lat - lat) - lat_offset).reshape(1)
    attention_framed, context = local_kernel(
        attention_forward,
        [cut, framed_fields, first_all, weights_all],
        [((tokens, width), BF16), ((tokens, width), BF16)],
        [pltpu.VMEM((3, tokens, width), F32), pltpu.VMEM((tokens, width), F32)],
        scalars=1,
    )
    window_shape = (bands, columns, WIN, width)
    around = (bands + 1, columns + 1, WIN, width)
    own_windows = attention_framed.reshape(window_shape)
    halo, section_other = exchange(
        2,
        [own_windows, section_own],
        [(around, BF16), (section_own.shape, BF16)],
        [
            (0, (bands - 1, columns - 1), 0, (0, 0), 1, 1),
            (0, (slice(0, bands), columns - 1), 0, (slice(1, bands + 1), 0), 0, 1),
            (0, (bands - 1,), 0, (0, slice(1, columns + 1)), 1, 0),
            (1, None, 1, None, "sibling", 0),
        ],
    )
    halo = halo.at[1:, 1:].set(own_windows)
    attention = lax.dynamic_slice(
        from_windows(halo),
        (WIN_H - lat_offset, WIN_W - lon_offset, jnp.int32(0)),
        (rows, block, width),
    )
    n_x = n_mp // 2
    section_scratch = [
        pltpu.VMEM((2,) + section_own.shape, BF16),
        pltpu.SemaphoreType.DMA((2,)),
    ]
    pair, hidden, merged, grad_bottom = local_kernel(
        merge_forward,
        [
            core.reshape(1),
            own_fields,
            merge_patches(attention, padded),
            cot_patches,
            merge_gain_all,
            mlp_gain_row,
            section_own,
            section_other,
        ],
        [
            ((padded, 2 * width_two), BF16),
            ((4, padded, width), BF16),
            ((padded, width_two), BF16),
            ((padded, width_two), F32),
        ],
        section_scratch,
        scalars=1,
        outside=2,
    )

    def chip_spot(step):
        def spot(ref, here, target):
            return ref.at[lax.rem(here["x"] + n_x + step, n_x), here["core"]]

        return spot

    (pairs,) = exchange(
        3,
        [pair],
        [((n_x, 2) + pair.shape, BF16)],
        [
            (0, None, 0, chip_spot(0), 0, 4),
            (0, None, 0, chip_spot(0), 0, 2),
            (0, None, 0, chip_spot(0), 0, -2),
            (0, None, 0, chip_spot(0), "sibling", 0),
            (0, None, 0, chip_spot(0), 0, 0),
            (0, chip_spot(-1), 0, chip_spot(-1), "sibling", 0, 1),
            (0, chip_spot(1), 0, chip_spot(1), "sibling", 0, 2),
            (0, chip_spot(-2), 0, chip_spot(-2), "sibling", 0, 0),
        ],
    )
    pairs = pairs.reshape(n_mp * padded, 2 * width_two)
    mlp_in, bottom_grad = pairs[:, :width_two], pairs[:, width_two:]
    hidden_up = jnp.dot(mlp_in, up_shard, preferred_element_type=F32)
    activated = jax.nn.gelu(hidden_up).astype(BF16)
    grad_act = jnp.dot(bottom_grad, down_shard, preferred_element_type=F32)
    gelu_back = jax.vjp(jax.nn.gelu, hidden_up)[1]
    grad_pre = gelu_back(grad_act)[0].astype(BF16)
    terms = jnp.concatenate(
        [
            jnp.einsum("af,ef->ae", activated, down_shard, preferred_element_type=F32),
            jnp.einsum("af,ef->ae", grad_pre, up_shard, preferred_element_type=F32),
        ],
        axis=1,
    ).astype(BF16)
    parts = terms_back(4, terms.reshape(n_x, 2, padded, 2 * width_two))
    down_local = jnp.einsum("ao,af->of", bottom_grad, activated, preferred_element_type=F32)
    up_local = jnp.einsum("ae,af->ef", mlp_in, grad_pre, preferred_element_type=F32)
    decoded_slab, grad_hidden = local_kernel(
        merge_backward,
        [
            core.reshape(1),
            parts,
            merged,
            grad_bottom,
            hidden,
            cot_patches,
            merge_gain_all,
            mlp_gain_row,
            section_own,
            section_other,
        ],
        [((n_mp, 2 * padded, 2 * group), BF16), ((4, padded, width), BF16)],
        section_scratch,
        scalars=1,
        outside=2,
    )
    grad_windows = grad_hidden[:, :merged_count].reshape(
        2, 2, bands, WIN_H // 2, columns, WIN_W // 2, width
    )
    grad_windows = grad_windows.transpose(2, 4, 3, 0, 5, 1, 6).reshape(window_shape)
    halo, decoded_got = exchange(
        5,
        [grad_windows, decoded_slab],
        [(around, BF16), (decoded_slab.shape, BF16)],
        [
            (0, (0, 0), 0, (bands, columns), -1, -1),
            (0, (slice(0, bands), 0), 0, (slice(0, bands), columns), 0, -1),
            (0, (0,), 0, (bands, slice(0, columns)), -1, 0),
        ]
        + [(1, "mp", 1, "mp", 0, step) for step in others],
    )
    halo = halo.at[:bands, :columns].set(grad_windows)
    grad_framed = into_frame(from_windows(halo))
    grad_slab, weight_grads = local_kernel(
        attention_backward,
        [cut, framed_fields, first_all, weights_all, context, grad_framed],
        [((n_mp, tokens // 2, 2 * group), BF16), ((4, width, width), BF16)],
        [
            pltpu.VMEM((3, tokens, width), F32),
            pltpu.VMEM((3, tokens, width), F32),
            pltpu.VMEM((tokens, width), F32),
        ],
        scalars=1,
    )
    large = (n_lat, width_two // n_lat, span)
    weight_total, grad_got, edge_got, up_got, down_got = gradients_out(
        6,
        weight_grads,
        grad_slab,
        up_local.astype(BF16).reshape(large),
        down_local.astype(BF16).reshape(large),
    )
    grad_up = jnp.sum(up_got.astype(F32), axis=0)
    grad_down = jnp.sum(down_got.astype(F32), axis=0)
    grad_qkv = weight_total[:, : 3 * group].reshape(width // n_lat, 3, group)
    grad_proj = weight_total[:, 3 * group :]
    decoded_view = decoded_got.reshape(n_mp, 2, padded, 2, group)[:, :, :merged_count]
    decoded_view = decoded_view.reshape(n_mp, 2, rows // 2, block // 2, 2, group)
    decoded = decoded_view.transpose(2, 4, 0, 3, 1, 5).reshape(rows, lon_count, group)

    def columns_joined(slabs):
        view = slabs.reshape(n_mp, columns, WIN_H, WIN_W, -1, group)
        return view.transpose(4, 2, 0, 1, 3, 5).reshape(-1, lon_count, group)

    grad_rows = jnp.concatenate(
        [columns_joined(edge_got[..., group:]), columns_joined(grad_got)], axis=0
    )
    grad_rows = jnp.concatenate([grad_rows[:, -WIN_W:], grad_rows], axis=1)
    grad_input = lax.dynamic_slice(
        grad_rows,
        (WIN_H - lat_offset, WIN_W - lon_offset, jnp.int32(0)),
        (rows, lon_count, group),
    ).astype(F32)
    return (decoded, grad_input, grad_qkv, grad_proj, grad_up, grad_down)


def solution(mesh):
    return jax.shard_map(
        shards,
        mesh=mesh,
        in_specs=(
            P("lat", None, "mp"),
            P("mp"),
            P(None, None, "mp"),
            P(None, "mp"),
            P(None, "mp"),
            P(None, "mp", None),
            P(),
            P(None, "mp"),
            P(None, "mp"),
            P(None, None, "mp"),
            P(),
            P(),
            P("lat", None, "mp"),
        ),
        out_specs=(
            P("lat", None, "mp"),
            P("lat", None, "mp"),
            P("lat", None, "mp"),
            P("lat", "mp"),
            P("lat", "mp"),
            P("lat", "mp"),
        ),
        check_vma=False,
    )
```

```python
import jax
import jax.numpy as jnp
from jax import lax
from jax.experimental import pallas as pl
from jax.experimental.pallas import tpu as pltpu
from jax.sharding import PartitionSpec as P

WIN_H = 6
WIN_W = 12
HDIM = 64
EPSILON = 1e-05
MASKED = -1e30
BF16 = jnp.bfloat16
F32 = jnp.float32


def positions():
    lat, mp = lax.axis_index("lat"), lax.axis_index("mp")
    return {
        "lat": lat,
        "mp": mp,
        "core": lax.rem(lat, 2),
        "x": lax.div(mp, 2),
        "z": lax.rem(mp, 2),
    }


def reached(here, down, right):
    n_lat, n_mp = lax.axis_size("lat"), lax.axis_size("mp")
    if down == "sibling":
        return {"lat": here["lat"] + 1 - 2 * here["core"], "mp": here["mp"]}
    return {
        "lat": lax.rem(here["lat"] + n_lat + down, n_lat),
        "mp": lax.rem(here["mp"] + n_mp + right, n_mp),
    }


def device_of(target):
    return {
        "device_id": (target["lat"], target["mp"]),
        "device_id_type": pl.DeviceIdType.MESH,
    }


def greet(here, steps):
    barrier = pltpu.get_barrier_semaphore()
    for down, right in steps:
        source = reached(here, down if down == "sibling" else -down, -right)
        pl.semaphore_signal(barrier, inc=1, **device_of(source))
    pl.semaphore_wait(barrier, len(steps))


def remote(source, landing, send, receive, target):
    return pltpu.make_async_remote_copy(
        src_ref=source, dst_ref=landing, send_sem=send, recv_sem=receive, **device_of(target)
    )


def exchange(collective, inputs, outputs, moves):
    steps = []
    for move in moves:
        if move[4:6] != (0, 0) and move[4:6] not in steps:
            steps.append(move[4:6])

    def body(*refs):
        sources = refs[: len(inputs)]
        landings = refs[len(inputs) : len(inputs) + len(outputs)]
        send, receive = refs[-2:]
        here = positions()

        def part_of(ref, part, place, target):
            if part is None:
                return ref
            if isinstance(part, str):
                return ref.at[place[part]]
            if callable(part):
                return part(ref, here, target)
            return ref.at[part]

        greet(here, steps)
        copies = []
        arrived = set()
        for index, move in enumerate(moves):
            source, source_part, landing, landing_part, down, right = move[:6]
            target = reached(here, down, right)
            if len(move) > 6:
                copies[move[6]].wait_recv()
                arrived.add(move[6])
                source_ref = part_of(landings[source], source_part, target, target)
            else:
                source_ref = part_of(sources[source], source_part, target, target)
            landing_ref = part_of(landings[landing], landing_part, here, target)
            if (down, right) == (0, 0):
                copy = pltpu.make_async_copy(source_ref, landing_ref, receive.at[index])
            else:
                copy = remote(
                    source_ref, landing_ref, send.at[index], receive.at[index], target
                )
            copy.start()
            copies.append(copy)
        for index, copy in enumerate(copies):
            if moves[index][4:6] == (0, 0):
                copy.wait()
            else:
                copy.wait_send()
                if index not in arrived:
                    copy.wait_recv()

    return pl.pallas_call(
        body,
        out_shape=[jax.ShapeDtypeStruct(shape, dtype) for shape, dtype in outputs],
        in_specs=[pl.BlockSpec(memory_space=pl.ANY)] * len(inputs),
        out_specs=[pl.BlockSpec(memory_space=pl.ANY)] * len(outputs),
        scratch_shapes=[
            pltpu.SemaphoreType.DMA((len(moves),)),
            pltpu.SemaphoreType.DMA((len(moves),)),
        ],
        compiler_params=pltpu.CompilerParams(collective_id=collective, has_side_effects=True),
    )(*inputs)


X_STEPS = ((4, 2), (2, 1), (-2, 3))


def terms_back(collective, terms):
    count, _, rows, width = terms.shape

    def body(terms_ref, parts_ref, other, own, total, send, receive, fetch):
        here = positions()
        core, x = here["core"], here["x"]
        sibling = reached(here, "sibling", 0)
        greet(here, [("sibling", 0)] + [(0, right) for right, _ in X_STEPS])
        order = [lax.rem(x + step, count) for _, step in X_STEPS] + [x]
        swaps, loads = [], []
        for index, spot in enumerate(order):
            swap = remote(
                terms_ref.at[spot, 1 - core],
                other.at[index],
                send.at[index],
                receive.at[index],
                sibling,
            )
            load = pltpu.make_async_copy(terms_ref.at[spot, core], own.at[index], fetch.at[index])
            swap.start()
            load.start()
            swaps.append(swap)
            loads.append(load)
        sends = []
        for index, spot in enumerate(order):
            loads[index].wait()
            swaps[index].wait_recv()
            total[index] = (own[index].astype(F32) + other[index].astype(F32)).astype(BF16)
            if index < len(X_STEPS):
                copy = remote(
                    total.at[index],
                    parts_ref.at[x],
                    send.at[count + index],
                    receive.at[count + index],
                    reached(here, 0, X_STEPS[index][0]),
                )
            else:
                copy = pltpu.make_async_copy(total.at[index], parts_ref.at[x], fetch.at[count])
            copy.start()
            sends.append(copy)
        for swap in swaps:
            swap.wait_send()
        for copy in sends:
            copy.wait()

    return pl.pallas_call(
        body,
        out_shape=jax.ShapeDtypeStruct((count, rows, width), BF16),
        in_specs=[pl.BlockSpec(memory_space=pl.ANY)],
        out_specs=pl.BlockSpec(memory_space=pl.ANY),
        scratch_shapes=[
            pltpu.VMEM((count, rows, width), BF16),
            pltpu.VMEM((count, rows, width), BF16),
            pltpu.VMEM((count, rows, width), BF16),
            pltpu.SemaphoreType.DMA((2 * count,)),
            pltpu.SemaphoreType.DMA((2 * count,)),
            pltpu.SemaphoreType.DMA((count + 1,)),
        ],
        compiler_params=pltpu.CompilerParams(
            collective_id=collective, has_side_effects=True, vmem_limit_bytes=48 * 1024 * 1024
        ),
    )(terms)


def gradients_out(collective, weight_grads, slabs):
    n_lat, n_mp = lax.axis_size("lat"), lax.axis_size("mp")
    kinds, width, _ = weight_grads.shape
    pair, group, share = kinds // 2, width // n_mp, width // n_lat

    def body(
        weight_ref, slab_ref, out_ref, got_ref, edge_ref,
        other, total, parts, turned, landed, send, receive,
    ):
        here = positions()
        lat, mp, core = here["lat"], here["mp"], here["core"]
        sibling = reached(here, "sibling", 0)
        barrier = pltpu.get_barrier_semaphore()
        greeted = [sibling]
        greeted += [reached(here, 0, -step) for step in range(1, n_mp)]
        greeted += [reached(here, -1, -step) for step in range(n_mp)]
        greeted += [reached(here, -step, 0) for step in range(1, n_lat)]
        for target in greeted:
            pl.semaphore_signal(barrier, inc=1, **device_of(target))
        pl.semaphore_wait(barrier, len(greeted))

        copies = []

        def sent(source, landing, target):
            index = len(copies)
            copy = remote(source, landing, send.at[index], receive.at[index], target)
            copy.start()
            copies.append(copy)
            return copy

        swap = sent(weight_ref.at[pl.ds(pair * (1 - core), pair)], other, sibling)
        for step in range(1, n_mp):
            target = reached(here, 0, step)
            sent(slab_ref.at[target["mp"]], got_ref.at[mp], target)
        for step in range(n_mp):
            target = reached(here, 1, step)
            sent(slab_ref.at[target["mp"]], edge_ref.at[mp], target)

        own_slab = pltpu.make_async_copy(slab_ref.at[mp], got_ref.at[mp], send.at[60])
        own_slab.start()

        swap.wait_recv()
        total[...] = (
            weight_ref[pl.ds(pair * core, pair)].astype(F32) + other[...].astype(F32)
        ).astype(BF16)
        scattered = []
        for step in range(1, n_mp):
            target = reached(here, 0, step)
            rows = pl.ds(pl.multiple_of(group * target["mp"], group), group)
            scattered.append(sent(total.at[:, rows], parts.at[mp], target))
        gathered = total[:, pl.ds(pl.multiple_of(group * mp, group), group), :].astype(F32)
        for step in range(1, n_mp):
            scattered[step - 1].wait_recv()
            gathered = gathered + parts[lax.rem(mp + n_mp - step, n_mp)].astype(F32)
        flat = gathered.reshape(pair * group, width).T.astype(BF16)
        for index in range(n_lat):
            turned[index] = flat[index * share : (index + 1) * share]
        spread = []
        for step in range(1, n_lat):
            target = reached(here, step, 0)
            spread.append(sent(turned.at[target["lat"]], landed.at[lat], target))
        landed[lat] = turned[lat]
        for copy in spread:
            copy.wait_recv()
        for half in range(2):
            result = landed[half].astype(F32)
            for index in range(half + 2, n_lat, 2):
                result = result + landed[index].astype(F32)
            out_ref[:, half * pair * group : (half + 1) * pair * group] = result

        done = [swap] + scattered + spread
        for copy in copies:
            copy.wait_send()
            if not any(copy is other_copy for other_copy in done):
                copy.wait_recv()
        own_slab.wait()

    any_space = pl.BlockSpec(memory_space=pl.ANY)
    vmem = pl.BlockSpec(memory_space=pltpu.VMEM)
    return pl.pallas_call(
        body,
        out_shape=[
            jax.ShapeDtypeStruct((share, kinds * group), F32),
            jax.ShapeDtypeStruct(slabs.shape, BF16),
            jax.ShapeDtypeStruct(slabs.shape, BF16),
        ],
        in_specs=[vmem, any_space],
        out_specs=[vmem, any_space, any_space],
        scratch_shapes=[
            pltpu.VMEM((pair, width, width), BF16),
            pltpu.VMEM((pair, width, width), BF16),
            pltpu.VMEM((n_mp, pair, group, width), BF16),
            pltpu.VMEM((n_lat, share, pair * group), BF16),
            pltpu.VMEM((n_lat, share, pair * group), BF16),
            pltpu.SemaphoreType.DMA((64,)),
            pltpu.SemaphoreType.DMA((64,)),
        ],
        compiler_params=pltpu.CompilerParams(
            collective_id=collective, has_side_effects=True, vmem_limit_bytes=48 * 1024 * 1024
        ),
    )(weight_grads, slabs)


def local_kernel(body, operands, outputs, scratch=(), scalars=0, outside=0):
    spaces = [pltpu.SMEM] * scalars + [pltpu.VMEM] * (len(operands) - scalars - outside)
    spaces += [pl.ANY] * outside
    return pl.pallas_call(
        body,
        out_shape=[jax.ShapeDtypeStruct(shape, dtype) for shape, dtype in outputs],
        in_specs=[pl.BlockSpec(memory_space=space) for space in spaces],
        out_specs=[pl.BlockSpec(memory_space=pltpu.VMEM)] * len(outputs),
        scratch_shapes=list(scratch),
        compiler_params=pltpu.CompilerParams(vmem_limit_bytes=48 * 1024 * 1024),
    )(*operands)


def dot_nn(left, right):
    return lax.dot_general(left, right, (((1,), (0,)), ((), ())), preferred_element_type=F32)


def dot_nt(left, right):
    return lax.dot_general(left, right, (((1,), (1,)), ((), ())), preferred_element_type=F32)


def dot_tn(left, right):
    return lax.dot_general(left, right, (((0,), (0,)), ((), ())), preferred_element_type=F32)


def halves_beside(values):
    half = values.shape[-2] // 2
    return jnp.concatenate([values[..., :half, :], values[..., half:, :]], axis=-1)


def groups_joined(slabs):
    count, half, _ = slabs.shape
    view = slabs.reshape(count, half, 2, HDIM).transpose(2, 1, 0, 3)
    return view.reshape(2 * half, count * HDIM)


def to_windows(grid):
    row_count, lon_count = (grid.shape[0], grid.shape[1])
    trailing = grid.shape[2:]
    view = grid.reshape((row_count // WIN_H, WIN_H, lon_count // WIN_W, WIN_W) + trailing)
    view = jnp.swapaxes(view, 1, 2)
    return view.reshape(((row_count // WIN_H) * (lon_count // WIN_W), WIN_H * WIN_W) + trailing)


def from_windows(windows):
    bands, columns, _, width = windows.shape
    view = windows.reshape((bands, columns, WIN_H, WIN_W, width))
    view = jnp.swapaxes(view, 1, 2)
    return view.reshape((bands * WIN_H, columns * WIN_W, width))


def merge_patches(grid, padded):
    row_count, lon_count, features = grid.shape
    view = grid.reshape(row_count // 2, 2, lon_count // 2, 2, features)
    view = view.transpose(1, 3, 0, 2, 4).reshape(4, row_count * lon_count // 4, features)
    return jnp.pad(view, ((0, 0), (0, padded - view.shape[1]), (0, 0)))


def norm_stats(values, count):
    center = sum(jnp.sum(value, axis=1, keepdims=True) for value in values) / count
    second = sum(jnp.sum(value * value, axis=1, keepdims=True) for value in values) / count
    return (center, lax.rsqrt(second - center * center + EPSILON))


def norm_backward(grads, gains, units, scale_inv, count):
    scaled = [grad * gain for grad, gain in zip(grads, gains)]
    first = sum(jnp.sum(value, axis=1, keepdims=True) for value in scaled) / count
    second = (
        sum(jnp.sum(value * unit, axis=1, keepdims=True) for value, unit in zip(scaled, units))
        / count
    )
    return [scale_inv * (value - first - unit * second) for value, unit in zip(scaled, units)]


def pair_slabs(upper, lower, out_ref, first_rows):
    low = lax.broadcasted_iota(jnp.int32, (upper.shape[0], 2 * HDIM), 1) < HDIM
    rows = pl.ds(first_rows, upper.shape[0])
    for pair in range(upper.shape[1] // (2 * HDIM)):
        lanes = slice(2 * HDIM * pair, 2 * HDIM * (pair + 1))
        one, two = upper[:, lanes], lower[:, lanes]
        swapped_one = jnp.concatenate([one[:, HDIM:], one[:, :HDIM]], axis=1)
        swapped_two = jnp.concatenate([two[:, HDIM:], two[:, :HDIM]], axis=1)
        out_ref[2 * pair, rows, :] = jnp.where(low, one, swapped_two).astype(BF16)
        out_ref[2 * pair + 1, rows, :] = jnp.where(low, swapped_one, two).astype(BF16)


WIN = WIN_H * WIN_W
FACTOR = HDIM ** (-0.5)


def heads_apart(values):
    low = lax.broadcasted_iota(jnp.int32, values.shape, 1) < HDIM
    zero = jnp.zeros_like(values)
    both = [jnp.where(low, values, zero), jnp.where(low, zero, values)]
    return jnp.concatenate(both, axis=0).astype(BF16)


def heads_together(values):
    low = lax.broadcasted_iota(jnp.int32, (WIN, 2 * HDIM), 1) < HDIM
    return jnp.where(low, values[:WIN], values[WIN:])


def window_probs(cut, window, query, keys):
    scores = dot_nt(query, keys) * FACTOR
    spot = lax.broadcasted_iota(jnp.int32, scores.shape, 0)
    spot = jnp.where(spot >= WIN, spot - WIN, spot)
    other = lax.broadcasted_iota(jnp.int32, scores.shape, 1)
    edge = cut * WIN_W - jnp.where(window >= 3, WIN, 0)
    same = (spot >= edge) == (other >= edge)
    scores = jnp.where(same, scores, MASKED)
    weights = jnp.exp(scores - jnp.max(scores, axis=1, keepdims=True))
    return weights / jnp.sum(weights, axis=1, keepdims=True)


def framed_packed(fields_ref, gain_ref, weights_ref, packed):
    values = fields_ref[...].astype(F32)
    center, scale_inv = norm_stats([values], values.shape[1])
    unit = (values - center) * scale_inv
    framed = (unit * gain_ref[...]).astype(BF16)
    for kind in range(3):
        packed[kind] = dot_nt(framed, weights_ref[kind]).astype(BF16).astype(F32)
    return (framed, unit, scale_inv)


def window_parts(refs, window, pair):
    rows = pl.ds(pl.multiple_of(window * WIN, 8), WIN)
    lanes = slice(2 * HDIM * pair, 2 * HDIM * (pair + 1))
    return [ref[rows, lanes] for ref in refs]


def attention_forward(cut_ref, fields_ref, gain_ref, weights_ref, out_ref, context_ref, packed, held):
    framed_packed(fields_ref, gain_ref, weights_ref, packed)
    cut = cut_ref[0]
    windows = fields_ref.shape[0] // WIN

    def step(window, carry):
        rows = pl.ds(pl.multiple_of(window * WIN, 8), WIN)
        for pair in range(fields_ref.shape[1] // (2 * HDIM)):
            query, keys, values = window_parts([packed.at[kind] for kind in range(3)], window, pair)
            probs = window_probs(cut, window, heads_apart(query), keys.astype(BF16))
            joined = dot_nn(probs.astype(BF16), values.astype(BF16))
            held[rows, 2 * HDIM * pair : 2 * HDIM * (pair + 1)] = heads_together(joined)
        return carry

    lax.fori_loop(0, windows, step, 0)
    context = held[...].astype(BF16)
    context_ref[...] = context
    out_ref[...] = dot_nn(context, weights_ref[3]).astype(BF16)


def attention_backward(
    cut_ref, fields_ref, gain_ref, weights_ref, context_ref, grad_ref, slab_ref, weight_ref,
    packed, grads, held,
):
    framed, unit, scale_inv = framed_packed(fields_ref, gain_ref, weights_ref, packed)
    cut = cut_ref[0]
    windows = fields_ref.shape[0] // WIN
    grad_framed = grad_ref[...]
    held[...] = dot_nt(grad_framed, weights_ref[3]).astype(BF16).astype(F32)

    def step(window, carry):
        rows = pl.ds(pl.multiple_of(window * WIN, 8), WIN)
        for pair in range(fields_ref.shape[1] // (2 * HDIM)):
            lanes = slice(2 * HDIM * pair, 2 * HDIM * (pair + 1))
            query, keys, values, grad = window_parts(
                [packed.at[kind] for kind in range(3)] + [held], window, pair
            )
            query, grad = heads_apart(query), heads_apart(grad)
            keys, values = keys.astype(BF16), values.astype(BF16)
            probs = window_probs(cut, window, query, keys)
            grad_probs = dot_nt(grad, values)
            inner = jnp.sum(grad_probs * probs, axis=1, keepdims=True)
            grad_scores = (probs * (grad_probs - inner) * FACTOR).astype(BF16)
            grads[0, rows, lanes] = heads_together(dot_nn(grad_scores, keys))
            grads[1, rows, lanes] = dot_tn(grad_scores, query)
            grads[2, rows, lanes] = dot_tn(probs.astype(BF16), grad)
        return carry

    lax.fori_loop(0, windows, step, 0)
    grad_normed = jnp.zeros(fields_ref.shape, F32)
    for kind in range(3):
        grad_kind = grads[kind].astype(BF16)
        weight_ref[kind] = dot_tn(grad_kind, framed).astype(BF16)
        grad_normed = grad_normed + dot_nn(grad_kind, weights_ref[kind])
    weight_ref[3] = dot_tn(context_ref[...], grad_framed).astype(BF16)
    (back,) = norm_backward([grad_normed], [gain_ref[...]], [unit], scale_inv, unit.shape[1])
    result = grad_framed.astype(F32) + back
    half = result.shape[0] // 2
    pair_slabs(result[:half], result[half:], slab_ref, 0)


def section_loads(core_ref, own_ref, other_ref, weights, loaded):
    core = core_ref[0]
    loads = [
        pltpu.make_async_copy(own_ref, weights.at[core], loaded.at[0]),
        pltpu.make_async_copy(other_ref, weights.at[1 - core], loaded.at[1]),
    ]
    for load in loads:
        load.start()
    return loads


def merge_forward(
    core_ref, fields_ref, attention_ref, cot_ref, gain_ref, mlp_gain_ref, own_ref, other_ref,
    pair_ref, hidden_ref, merged_ref, grad_ref, weights, loaded,
):
    loads = section_loads(core_ref, own_ref, other_ref, weights, loaded)
    width_two = merged_ref.shape[1]
    hidden = []
    for patch in range(4):
        value = fields_ref[patch].astype(F32) + attention_ref[patch].astype(F32)
        hidden_ref[patch] = value.astype(BF16)
        hidden.append(value.astype(BF16).astype(F32))
    center, scale_inv = norm_stats(hidden, 4 * hidden[0].shape[1])
    merged = jnp.zeros(merged_ref.shape, F32)
    grad = jnp.zeros(merged_ref.shape, F32)
    for load in loads:
        load.wait()
    for patch in range(4):
        normed = (hidden[patch] - center) * scale_inv * gain_ref[patch : patch + 1, :]
        merged = merged + dot_nn(normed.astype(BF16), weights[0, patch])
        grad = grad + dot_nn(cot_ref[patch], weights[1, patch])
    merged_ref[...] = merged.astype(BF16)
    merged = merged.astype(BF16).astype(F32)
    center, scale_inv = norm_stats([merged], width_two)
    mlp_in = (merged - center) * scale_inv * mlp_gain_ref[...]
    pair_ref[:, :width_two] = mlp_in.astype(BF16)
    pair_ref[:, width_two:] = grad.astype(BF16)
    grad_ref[...] = grad


def merge_backward(
    core_ref, parts_ref, merged_ref, grad_ref, hidden_ref, cot_ref, gain_ref, mlp_gain_ref,
    own_ref, other_ref, slab_ref, out_ref, weights, loaded,
):
    loads = section_loads(core_ref, own_ref, other_ref, weights, loaded)
    width_two = merged_ref.shape[1]
    count = merged_ref.shape[0]
    total = parts_ref[0].astype(F32)
    for index in range(1, parts_ref.shape[0]):
        total = total + parts_ref[index].astype(F32)
    merged = merged_ref[...].astype(F32)
    bottom = (merged + total[:, :width_two]).astype(BF16)
    for load in loads:
        load.wait()
    decoded = [
        hidden_ref[patch].astype(F32) + dot_nt(bottom, weights[1, patch])
        for patch in range(4)
    ]
    for side in range(2):
        pair_slabs(decoded[side], decoded[2 + side], slab_ref, side * count)
    center, scale_inv = norm_stats([merged], width_two)
    unit = (merged - center) * scale_inv
    (back,) = norm_backward(
        [total[:, width_two:]], [mlp_gain_ref[...]], [unit], scale_inv, width_two
    )
    grad_merged = (grad_ref[...] + back).astype(BF16)
    hidden = [hidden_ref[patch].astype(F32) for patch in range(4)]
    center, scale_inv = norm_stats(hidden, 4 * hidden[0].shape[1])
    units = [(value - center) * scale_inv for value in hidden]
    backs = norm_backward(
        [dot_nt(grad_merged, weights[0, patch]) for patch in range(4)],
        [gain_ref[patch : patch + 1, :] for patch in range(4)],
        units,
        scale_inv,
        4 * hidden[0].shape[1],
    )
    for patch in range(4):
        out_ref[patch] = (cot_ref[patch].astype(F32) + backs[patch]).astype(BF16)


def shards(
    fields,
    first_gain,
    qkv_weight,
    proj_weight,
    merge_gain,
    merge_weight,
    mlp_gain,
    up_weight,
    down_weight,
    expand_weight,
    lat_shift,
    lon_shift,
    cotangent,
):
    n_lat, n_mp = lax.axis_size("lat"), lax.axis_size("mp")
    lat, core = lax.axis_index("lat"), lax.rem(lax.axis_index("lat"), 2)
    lat_offset = lat_shift[0]
    lon_offset = lon_shift[0]
    rows, lon_count, group = fields.shape
    width = group * n_mp
    block = lon_count // n_mp
    wide = block + WIN_W
    bands, columns = rows // WIN_H, block // WIN_W
    tokens = rows * block
    width_two = merge_weight.shape[2]
    span = up_weight.shape[1]
    merged_count = tokens // 4
    padded = -(-merged_count // 16) * 16
    others = range(n_mp)

    section = jnp.where(core == 0, merge_weight, expand_weight.transpose(1, 2, 0))
    section_own = lax.all_gather(section, "mp", axis=1, tiled=True)
    blocks = fields.reshape(rows, n_mp, block, group).transpose(1, 0, 2, 3)
    margin = jnp.roll(blocks[:, :, :WIN_W], -1, axis=0)
    field_blocks = jnp.concatenate([blocks, margin], axis=2)
    body_slab = halves_beside(field_blocks.reshape(n_mp, rows * wide, group))
    edge_slab = halves_beside(field_blocks[:, :WIN_H].reshape(n_mp, WIN_H * wide, group))
    cot_blocks = cotangent.reshape(rows, n_mp, block, group).transpose(1, 0, 2, 3)
    cot_slab = halves_beside(cot_blocks.reshape(n_mp, tokens, group))
    weights = jnp.concatenate(
        [qkv_weight.transpose(1, 2, 0), proj_weight.transpose(1, 0)[None]], axis=0
    )
    gains = jnp.pad(jnp.concatenate([first_gain[None], merge_gain], axis=0), ((0, 3), (0, 64)))

    def rows_at(here, step):
        return pl.ds(pl.multiple_of(lax.rem(here["mp"] + n_mp - step, n_mp) * group, group), group)

    def core_half(ref, here, target):
        return ref.at[pl.ds(2 * here["core"], 2)]

    def core_half_rows(step):
        return lambda ref, here, target: ref.at[pl.ds(2 * here["core"], 2), rows_at(here, step)]

    def own_rows(ref, here, target):
        return ref.at[:, rows_at(here, 0)]

    body_got, edge_got, weights_all, gains_all = exchange(
        1,
        [body_slab, edge_slab, weights, gains],
        [
            (body_slab.shape, BF16),
            (edge_slab.shape, BF16),
            ((4, width, width), BF16),
            ((n_mp,) + gains.shape, F32),
        ],
        [(2, core_half, 2, core_half_rows(0), 0, step) for step in range(1, n_mp)]
        + [(3, None, 3, "mp", 0, step) for step in others]
        + [(0, "mp", 0, "mp", 0, step) for step in others]
        + [(1, "mp", 1, "mp", -1, step) for step in others]
        + [(2, None, 2, own_rows, 0, 0)]
        + [
            (2, core_half_rows(step), 2, core_half_rows(step), "sibling", 0, step - 1)
            for step in range(1, n_mp)
        ],
    )
    body = groups_joined(body_got).reshape(rows, wide, width)
    edge = groups_joined(edge_got).reshape(WIN_H, wide, width)
    has_shard = lax.rem(lax.axis_index("mp"), 2) == core
    fetch = [
        (at * n_mp + m, at * n_mp + (m ^ 1))
        for at in range(n_lat)
        for m in range(n_mp)
        if at % 2 == m % 2
    ]
    up_late, down_late, gains_all = lax.optimization_barrier((up_weight, down_weight, gains_all))
    up_shard, down_shard = (
        jnp.where(has_shard, weight, lax.ppermute(weight, ("lat", "mp"), fetch))
        for weight in (up_late, down_late)
    )

    first_all = gains_all[:, 0, :group].reshape(1, width)
    merge_gain_all = gains_all[:, 1:5, :group].transpose(1, 0, 2).reshape(4, width)
    mlp_gain_row = mlp_gain.reshape(1, width_two)
    own_fields = merge_patches(body[:, :block], padded)

    def into_frame(whole):
        part = lax.dynamic_slice(
            whole, (lat_offset, lon_offset, jnp.int32(0)), (rows, block, width)
        )
        return to_windows(part).reshape(tokens, width)

    framed_fields = into_frame(jnp.concatenate([body, edge], axis=0))
    cut = (jnp.int32(rows) * (n_lat - lat) - lat_offset).reshape(1)
    attention_framed, context = local_kernel(
        attention_forward,
        [cut, framed_fields, first_all, weights_all],
        [((tokens, width), BF16), ((tokens, width), BF16)],
        [pltpu.VMEM((3, tokens, width), F32), pltpu.VMEM((tokens, width), F32)],
        scalars=1,
    )
    window_shape = (bands, columns, WIN, width)
    around = (bands + 1, columns + 1, WIN, width)
    own_windows = attention_framed.reshape(window_shape)
    halo, section_other, cot_got = exchange(
        2,
        [own_windows, section_own, cot_slab],
        [(around, BF16), (section_own.shape, BF16), (cot_slab.shape, BF16)],
        [
            (0, (bands - 1, columns - 1), 0, (0, 0), 1, 1),
            (0, (slice(0, bands), columns - 1), 0, (slice(1, bands + 1), 0), 0, 1),
            (0, (bands - 1,), 0, (0, slice(1, columns + 1)), 1, 0),
            (1, None, 1, None, "sibling", 0),
        ]
        + [(2, "mp", 2, "mp", 0, step) for step in others],
    )
    cot_patches = merge_patches(groups_joined(cot_got).reshape(rows, block, width), padded)
    halo = halo.at[1:, 1:].set(own_windows)
    attention = lax.dynamic_slice(
        from_windows(halo),
        (WIN_H - lat_offset, WIN_W - lon_offset, jnp.int32(0)),
        (rows, block, width),
    )
    n_x = n_mp // 2
    section_scratch = [
        pltpu.VMEM((2,) + section_own.shape, BF16),
        pltpu.SemaphoreType.DMA((2,)),
    ]
    pair, hidden, merged, grad_bottom = local_kernel(
        merge_forward,
        [
            core.reshape(1),
            own_fields,
            merge_patches(attention, padded),
            cot_patches,
            merge_gain_all,
            mlp_gain_row,
            section_own,
            section_other,
        ],
        [
            ((padded, 2 * width_two), BF16),
            ((4, padded, width), BF16),
            ((padded, width_two), BF16),
            ((padded, width_two), F32),
        ],
        section_scratch,
        scalars=1,
        outside=2,
    )

    def chip_spot(step):
        def spot(ref, here, target):
            return ref.at[lax.rem(here["x"] + n_x + step, n_x), here["core"]]

        return spot

    (pairs,) = exchange(
        3,
        [pair],
        [((n_x, 2) + pair.shape, BF16)],
        [
            (0, None, 0, chip_spot(0), 0, 4),
            (0, None, 0, chip_spot(0), 0, 2),
            (0, None, 0, chip_spot(0), 0, -2),
            (0, None, 0, chip_spot(0), "sibling", 0),
            (0, None, 0, chip_spot(0), 0, 0),
            (0, chip_spot(-1), 0, chip_spot(-1), "sibling", 0, 1),
            (0, chip_spot(1), 0, chip_spot(1), "sibling", 0, 2),
            (0, chip_spot(-2), 0, chip_spot(-2), "sibling", 0, 0),
        ],
    )
    pairs = pairs.reshape(n_mp * padded, 2 * width_two)
    mlp_in, bottom_grad = pairs[:, :width_two], pairs[:, width_two:]
    hidden_up = jnp.dot(mlp_in, up_shard, preferred_element_type=F32)
    activated = jax.nn.gelu(hidden_up).astype(BF16)
    grad_act = jnp.dot(bottom_grad, down_shard, preferred_element_type=F32)
    gelu_back = jax.vjp(jax.nn.gelu, hidden_up)[1]
    grad_pre = gelu_back(grad_act)[0].astype(BF16)
    terms = jnp.concatenate(
        [
            jnp.einsum("af,ef->ae", activated, down_shard, preferred_element_type=F32),
            jnp.einsum("af,ef->ae", grad_pre, up_shard, preferred_element_type=F32),
        ],
        axis=1,
    ).astype(BF16)
    parts = terms_back(4, terms.reshape(n_x, 2, padded, 2 * width_two))
    shard_groups = [
        [at * n_mp + 2 * x + z for at in range(core_at, n_lat, 2) for z in range(2)]
        for x in range(n_x)
        for core_at in range(2)
    ]
    owners = [
        ((2 * spot + c) * n_mp + 2 * x + z, (2 * spot + z) * n_mp + 2 * x + c)
        for spot in range(n_lat // 2)
        for x in range(n_x)
        for c in range(2)
        for z in range(2)
    ]
    local_grads = [
        jnp.einsum("ae,af->ef", mlp_in, grad_pre, preferred_element_type=F32),
        jnp.einsum("ao,af->of", bottom_grad, activated, preferred_element_type=F32),
    ]
    grad_up, grad_down = (
        lax.ppermute(
            lax.psum_scatter(
                part.astype(BF16),
                ("lat", "mp"),
                scatter_dimension=0,
                axis_index_groups=shard_groups,
                tiled=True,
            ),
            ("lat", "mp"),
            owners,
        ).astype(F32)
        for part in local_grads
    )
    decoded_slab, grad_hidden = local_kernel(
        merge_backward,
        [
            core.reshape(1),
            parts,
            merged,
            grad_bottom,
            hidden,
            cot_patches,
            merge_gain_all,
            mlp_gain_row,
            section_own,
            section_other,
        ],
        [((n_mp, 2 * padded, 2 * group), BF16), ((4, padded, width), BF16)],
        section_scratch,
        scalars=1,
        outside=2,
    )
    grad_windows = grad_hidden[:, :merged_count].reshape(
        2, 2, bands, WIN_H // 2, columns, WIN_W // 2, width
    )
    grad_windows = grad_windows.transpose(2, 4, 3, 0, 5, 1, 6).reshape(window_shape)
    halo, decoded_got = exchange(
        5,
        [grad_windows, decoded_slab],
        [(around, BF16), (decoded_slab.shape, BF16)],
        [
            (0, (0, 0), 0, (bands, columns), -1, -1),
            (0, (slice(0, bands), 0), 0, (slice(0, bands), columns), 0, -1),
            (0, (0,), 0, (bands, slice(0, columns)), -1, 0),
        ]
        + [(1, "mp", 1, "mp", 0, step) for step in others],
    )
    halo = halo.at[:bands, :columns].set(grad_windows)
    grad_framed = into_frame(from_windows(halo))
    grad_slab, weight_grads = local_kernel(
        attention_backward,
        [cut, framed_fields, first_all, weights_all, context, grad_framed],
        [((n_mp, tokens // 2, 2 * group), BF16), ((4, width, width), BF16)],
        [
            pltpu.VMEM((3, tokens, width), F32),
            pltpu.VMEM((3, tokens, width), F32),
            pltpu.VMEM((tokens, width), F32),
        ],
        scalars=1,
    )
    weight_total, grad_got, edge_got = gradients_out(6, weight_grads, grad_slab)
    grad_qkv = weight_total[:, : 3 * group].reshape(width // n_lat, 3, group)
    grad_proj = weight_total[:, 3 * group :]
    decoded_view = decoded_got.reshape(n_mp, 2, padded, 2, group)[:, :, :merged_count]
    decoded_view = decoded_view.reshape(n_mp, 2, rows // 2, block // 2, 2, group)
    decoded = decoded_view.transpose(2, 4, 0, 3, 1, 5).reshape(rows, lon_count, group)

    def columns_joined(slabs):
        view = slabs.reshape(n_mp, columns, WIN_H, WIN_W, -1, group)
        return view.transpose(4, 2, 0, 1, 3, 5).reshape(-1, lon_count, group)

    grad_rows = jnp.concatenate(
        [columns_joined(edge_got[..., group:]), columns_joined(grad_got)], axis=0
    )
    grad_rows = jnp.concatenate([grad_rows[:, -WIN_W:], grad_rows], axis=1)
    grad_input = lax.dynamic_slice(
        grad_rows,
        (WIN_H - lat_offset, WIN_W - lon_offset, jnp.int32(0)),
        (rows, lon_count, group),
    ).astype(F32)
    return (decoded, grad_input, grad_qkv, grad_proj, grad_up, grad_down)


def solution(mesh):
    return jax.shard_map(
        shards,
        mesh=mesh,
        in_specs=(
            P("lat", None, "mp"),
            P("mp"),
            P(None, None, "mp"),
            P(None, "mp"),
            P(None, "mp"),
            P(None, "mp", None),
            P(),
            P(None, "mp"),
            P(None, "mp"),
            P(None, None, "mp"),
            P(),
            P(),
            P("lat", None, "mp"),
        ),
        out_specs=(
            P("lat", None, "mp"),
            P("lat", None, "mp"),
            P("lat", None, "mp"),
            P("lat", "mp"),
            P("lat", "mp"),
            P("lat", "mp"),
        ),
        check_vma=False,
    )
```

```python
import jax
import jax.numpy as jnp
import numpy as np
from jax import lax
from jax.experimental import pallas as pl
from jax.experimental.pallas import tpu as pltpu
from jax.sharding import PartitionSpec as P

WIN_H = 6
WIN_W = 12
HDIM = 64
EPSILON = 1e-05
MASKED = -1e30
BF16 = jnp.bfloat16
F32 = jnp.float32


def positions():
    lat, mp = lax.axis_index("lat"), lax.axis_index("mp")
    return {
        "lat": lat,
        "mp": mp,
        "core": lax.rem(lat, 2),
        "x": lax.div(mp, 2),
        "z": lax.rem(mp, 2),
    }


def reached(here, down, right):
    n_lat, n_mp = lax.axis_size("lat"), lax.axis_size("mp")
    if down == "sibling":
        return {"lat": here["lat"] + 1 - 2 * here["core"], "mp": here["mp"]}
    if down == "flip":
        return {"lat": here["lat"], "mp": 2 * here["x"] + 1 - here["z"]}
    return {
        "lat": lax.rem(here["lat"] + n_lat + down, n_lat),
        "mp": lax.rem(here["mp"] + n_mp + right, n_mp),
    }


def device_of(target):
    return {
        "device_id": (target["lat"], target["mp"]),
        "device_id_type": pl.DeviceIdType.MESH,
    }


def greet(here, steps):
    barrier = pltpu.get_barrier_semaphore()
    for down, right in steps:
        source = reached(here, down if isinstance(down, str) else -down, -right)
        pl.semaphore_signal(barrier, inc=1, **device_of(source))
    pl.semaphore_wait(barrier, len(steps))


def remote(source, landing, send, receive, target):
    return pltpu.make_async_remote_copy(
        src_ref=source, dst_ref=landing, send_sem=send, recv_sem=receive, **device_of(target)
    )


def exchange(collective, inputs, outputs, moves):
    steps = []
    for move in moves:
        if move[4:6] != (0, 0) and move[4:6] not in steps:
            steps.append(move[4:6])

    def body(*refs):
        sources = refs[: len(inputs)]
        landings = refs[len(inputs) : len(inputs) + len(outputs)]
        send, receive = refs[-2:]
        here = positions()

        def part_of(ref, part, place, target):
            if part is None:
                return ref
            if isinstance(part, str):
                return ref.at[place[part]]
            if callable(part):
                return part(ref, here, target)
            return ref.at[part]

        greet(here, steps)
        copies = []
        arrived = set()
        for index, move in enumerate(moves):
            source, source_part, landing, landing_part, down, right = move[:6]
            target = reached(here, down, right)
            if len(move) > 6:
                copies[move[6]].wait_recv()
                arrived.add(move[6])
                source_ref = part_of(landings[source], source_part, target, target)
            else:
                source_ref = part_of(sources[source], source_part, target, target)
            landing_ref = part_of(landings[landing], landing_part, here, target)
            if (down, right) == (0, 0):
                copy = pltpu.make_async_copy(source_ref, landing_ref, receive.at[index])
            else:
                copy = remote(
                    source_ref, landing_ref, send.at[index], receive.at[index], target
                )
            if down == "flip":
                pl.when(here["z"] == here["core"])(copy.start)
            else:
                copy.start()
            copies.append(copy)
        for index, copy in enumerate(copies):
            if moves[index][4:6] == (0, 0):
                copy.wait()
            elif moves[index][4] == "flip":
                pl.when(here["z"] == here["core"])(copy.wait_send)
                pl.when(here["z"] != here["core"])(copy.wait_recv)
            else:
                copy.wait_send()
                if index not in arrived:
                    copy.wait_recv()

    return pl.pallas_call(
        body,
        out_shape=[jax.ShapeDtypeStruct(shape, dtype) for shape, dtype in outputs],
        in_specs=[pl.BlockSpec(memory_space=pl.ANY)] * len(inputs),
        out_specs=[pl.BlockSpec(memory_space=pl.ANY)] * len(outputs),
        scratch_shapes=[
            pltpu.SemaphoreType.DMA((len(moves),)),
            pltpu.SemaphoreType.DMA((len(moves),)),
        ],
        compiler_params=pltpu.CompilerParams(collective_id=collective, has_side_effects=True),
    )(*inputs)


X_STEPS = ((4, 2), (2, 1), (-2, 3))


def terms_back(collective, terms, up_grads, down_grads):
    count, _, rows, width = terms.shape
    n_lat = lax.axis_size("lat")

    def body(
        terms_ref, up_ref, down_ref, parts_ref, up_got, down_got,
        other, own, total, send, receive, fetch, large_send, large_receive,
    ):
        here = positions()
        lat, core, x, z = here["lat"], here["core"], here["x"], here["z"]
        mine = 2 * lax.div(lat, 2) + z
        owner = z == core
        sibling = reached(here, "sibling", 0)
        barrier = pltpu.get_barrier_semaphore()
        greeted = [sibling] + [reached(here, 0, -right) for right, _ in X_STEPS]
        for target in greeted:
            pl.semaphore_signal(barrier, inc=1, **device_of(target))
        for source in range(n_lat):

            @pl.when(jnp.logical_or(jnp.logical_not(owner), mine != source))
            def _():
                target = {"lat": 2 * (source // 2) + z, "mp": 2 * x + source % 2}
                pl.semaphore_signal(barrier, inc=1, **device_of(target))

        pl.semaphore_wait(barrier, len(greeted) + n_lat - jnp.where(owner, 1, 0))
        order = [lax.rem(x + step, count) for _, step in X_STEPS] + [x]
        swaps, loads = [], []
        for index, spot in enumerate(order):
            swap = remote(
                terms_ref.at[spot, 1 - core],
                other.at[index],
                send.at[index],
                receive.at[index],
                sibling,
            )
            load = pltpu.make_async_copy(terms_ref.at[spot, core], own.at[index], fetch.at[index])
            swap.start()
            load.start()
            swaps.append(swap)
            loads.append(load)

        def to_owner(which, step):
            source, landing = ((up_ref, up_got), (down_ref, down_got))[which]
            target = {"lat": lax.rem(lat + step, n_lat), "mp": 2 * x + core}
            return remote(
                source.at[target["lat"]],
                landing.at[mine],
                large_send.at[which, step],
                large_receive.at[which, mine],
                target,
            )

        for which, (source, landing) in enumerate(((up_ref, up_got), (down_ref, down_got))):
            for step in range(1, n_lat):
                to_owner(which, step).start()

            @pl.when(owner)
            def _():
                pltpu.make_async_copy(
                    source.at[lat], landing.at[mine], large_receive.at[which, mine]
                ).start()

            @pl.when(jnp.logical_not(owner))
            def _():
                to_owner(which, 0).start()

        sends = []
        for index, spot in enumerate(order):
            loads[index].wait()
            swaps[index].wait_recv()
            total[index] = (own[index].astype(F32) + other[index].astype(F32)).astype(BF16)
            if index < len(X_STEPS):
                copy = remote(
                    total.at[index],
                    parts_ref.at[x],
                    send.at[count + index],
                    receive.at[count + index],
                    reached(here, 0, X_STEPS[index][0]),
                )
            else:
                copy = pltpu.make_async_copy(total.at[index], parts_ref.at[x], fetch.at[count])
            copy.start()
            sends.append(copy)
        for swap in swaps:
            swap.wait_send()
        for copy in sends:
            copy.wait()
        for which, (source, landing) in enumerate(((up_ref, up_got), (down_ref, down_got))):
            for step in range(n_lat):
                remote(
                    source.at[step],
                    landing.at[step],
                    large_send.at[which, step],
                    large_receive.at[which, step],
                    sibling,
                ).wait_recv()
            for step in range(1, n_lat):
                to_owner(which, step).wait_send()

            @pl.when(jnp.logical_not(owner))
            def _():
                to_owner(which, 0).wait_send()

    return pl.pallas_call(
        body,
        out_shape=[
            jax.ShapeDtypeStruct((count, rows, width), BF16),
            jax.ShapeDtypeStruct(up_grads.shape, BF16),
            jax.ShapeDtypeStruct(down_grads.shape, BF16),
        ],
        in_specs=[pl.BlockSpec(memory_space=pl.ANY)] * 3,
        out_specs=[pl.BlockSpec(memory_space=pl.ANY)] * 3,
        scratch_shapes=[
            pltpu.VMEM((count, rows, width), BF16),
            pltpu.VMEM((count, rows, width), BF16),
            pltpu.VMEM((count, rows, width), BF16),
            pltpu.SemaphoreType.DMA((2 * count,)),
            pltpu.SemaphoreType.DMA((2 * count,)),
            pltpu.SemaphoreType.DMA((count + 1,)),
            pltpu.SemaphoreType.DMA((2, n_lat)),
            pltpu.SemaphoreType.DMA((2, n_lat)),
        ],
        compiler_params=pltpu.CompilerParams(
            collective_id=collective, has_side_effects=True, vmem_limit_bytes=48 * 1024 * 1024
        ),
    )(terms, up_grads, down_grads)


def gradients_out(collective, weight_grads, slabs):
    n_lat, n_mp = lax.axis_size("lat"), lax.axis_size("mp")
    kinds, width, _ = weight_grads.shape
    pair, group, share = kinds // 2, width // n_mp, width // n_lat

    def body(
        weight_ref, slab_ref, out_ref, got_ref, edge_ref,
        other, total, parts, turned, landed, send, receive,
    ):
        here = positions()
        lat, mp, core = here["lat"], here["mp"], here["core"]
        sibling = reached(here, "sibling", 0)
        barrier = pltpu.get_barrier_semaphore()
        greeted = [sibling]
        greeted += [reached(here, 0, -step) for step in range(1, n_mp)]
        greeted += [reached(here, -1, -step) for step in range(n_mp)]
        greeted += [reached(here, -step, 0) for step in range(1, n_lat)]
        for target in greeted:
            pl.semaphore_signal(barrier, inc=1, **device_of(target))
        pl.semaphore_wait(barrier, len(greeted))

        copies = []

        def sent(source, landing, target):
            index = len(copies)
            copy = remote(source, landing, send.at[index], receive.at[index], target)
            copy.start()
            copies.append(copy)
            return copy

        swap = sent(weight_ref.at[pl.ds(pair * (1 - core), pair)], other, sibling)
        for step in range(1, n_mp):
            target = reached(here, 0, step)
            sent(slab_ref.at[target["mp"]], got_ref.at[mp], target)
        for step in range(n_mp):
            target = reached(here, 1, step)
            sent(slab_ref.at[target["mp"]], edge_ref.at[mp], target)

        own_slab = pltpu.make_async_copy(slab_ref.at[mp], got_ref.at[mp], send.at[60])
        own_slab.start()

        swap.wait_recv()
        total[...] = (
            weight_ref[pl.ds(pair * core, pair)].astype(F32) + other[...].astype(F32)
        ).astype(BF16)
        scattered = []
        for step in range(1, n_mp):
            target = reached(here, 0, step)
            rows = pl.ds(pl.multiple_of(group * target["mp"], group), group)
            scattered.append(sent(total.at[:, rows], parts.at[mp], target))
        gathered = total[:, pl.ds(pl.multiple_of(group * mp, group), group), :].astype(F32)
        for step in range(1, n_mp):
            scattered[step - 1].wait_recv()
            gathered = gathered + parts[lax.rem(mp + n_mp - step, n_mp)].astype(F32)
        flat = gathered.reshape(pair * group, width).T.astype(BF16)
        for index in range(n_lat):
            turned[index] = flat[index * share : (index + 1) * share]
        spread = []
        for step in range(1, n_lat):
            target = reached(here, step, 0)
            spread.append(sent(turned.at[target["lat"]], landed.at[lat], target))
        landed[lat] = turned[lat]
        for copy in spread:
            copy.wait_recv()
        for half in range(2):
            result = landed[half].astype(F32)
            for index in range(half + 2, n_lat, 2):
                result = result + landed[index].astype(F32)
            out_ref[:, half * pair * group : (half + 1) * pair * group] = result

        done = [swap] + scattered + spread
        for copy in copies:
            copy.wait_send()
            if not any(copy is other_copy for other_copy in done):
                copy.wait_recv()
        own_slab.wait()

    any_space = pl.BlockSpec(memory_space=pl.ANY)
    vmem = pl.BlockSpec(memory_space=pltpu.VMEM)
    return pl.pallas_call(
        body,
        out_shape=[
            jax.ShapeDtypeStruct((share, kinds * group), F32),
            jax.ShapeDtypeStruct(slabs.shape, BF16),
            jax.ShapeDtypeStruct(slabs.shape, BF16),
        ],
        in_specs=[vmem, any_space],
        out_specs=[vmem, any_space, any_space],
        scratch_shapes=[
            pltpu.VMEM((pair, width, width), BF16),
            pltpu.VMEM((pair, width, width), BF16),
            pltpu.VMEM((n_mp, pair, group, width), BF16),
            pltpu.VMEM((n_lat, share, pair * group), BF16),
            pltpu.VMEM((n_lat, share, pair * group), BF16),
            pltpu.SemaphoreType.DMA((64,)),
            pltpu.SemaphoreType.DMA((64,)),
        ],
        compiler_params=pltpu.CompilerParams(
            collective_id=collective, has_side_effects=True, vmem_limit_bytes=48 * 1024 * 1024
        ),
    )(weight_grads, slabs)


def local_kernel(body, operands, outputs, scratch=(), scalars=0, outside=0):
    spaces = [pltpu.SMEM] * scalars + [pltpu.VMEM] * (len(operands) - scalars - outside)
    spaces += [pl.ANY] * outside
    return pl.pallas_call(
        body,
        out_shape=[jax.ShapeDtypeStruct(shape, dtype) for shape, dtype in outputs],
        in_specs=[pl.BlockSpec(memory_space=space) for space in spaces],
        out_specs=[pl.BlockSpec(memory_space=pltpu.VMEM)] * len(outputs),
        scratch_shapes=list(scratch),
        compiler_params=pltpu.CompilerParams(vmem_limit_bytes=48 * 1024 * 1024),
    )(*operands)


def dot_nn(left, right):
    return lax.dot_general(left, right, (((1,), (0,)), ((), ())), preferred_element_type=F32)


def dot_nt(left, right):
    return lax.dot_general(left, right, (((1,), (1,)), ((), ())), preferred_element_type=F32)


def dot_tn(left, right):
    return lax.dot_general(left, right, (((0,), (0,)), ((), ())), preferred_element_type=F32)


def halves_beside(values):
    half = values.shape[-2] // 2
    return jnp.concatenate([values[..., :half, :], values[..., half:, :]], axis=-1)


def picked(places, values):
    spots = lax.broadcasted_iota(jnp.int32, (places.shape[0], values.shape[0]), 1)
    return dot_nn(jnp.where(spots == places, 1.0, 0.0).astype(BF16), values)


def spread_over(places, values, count):
    spots = lax.broadcasted_iota(jnp.int32, (places.shape[0], count), 1)
    return dot_tn(values, jnp.where(spots == places, 1.0, 0.0).astype(BF16))


def swapped(values):
    return jnp.concatenate([values[:, HDIM:], values[:, :HDIM]], axis=1)


def join_slabs(slab_ref, out_ref, first_rows, second_rows):
    half = slab_ref.shape[1]
    low = lax.broadcasted_iota(jnp.int32, (half, 2 * HDIM), 1) < HDIM
    for pair in range(slab_ref.shape[0] // 2):
        lanes = slice(2 * HDIM * pair, 2 * HDIM * (pair + 1))
        one = slab_ref[2 * pair].astype(F32)
        two = slab_ref[2 * pair + 1].astype(F32)
        first = jnp.where(low, one, swapped(two)).astype(out_ref.dtype)
        second = jnp.where(low, swapped(one), two).astype(out_ref.dtype)
        out_ref[first_rows : first_rows + half, lanes] = first
        out_ref[second_rows : second_rows + half, lanes] = second


PADDED_COLUMNS = 48
FRAME, OWN, BACK, BACK_HALO, COT, UNPATCH, GRAD, GRAD_HALO, BY_ROW, BY_ROW_PATCH, SHIFT, STAY = range(12)


def place_table(lat_offset, lon_offset, rows, block, padded, n_mp):
    columns = block // WIN_W
    size = max(rows * block, 4 * padded, n_mp * PADDED_COLUMNS)

    def window_place(row, column):
        window = (row // WIN_H) * columns + column // WIN_W
        return window * WIN + (row % WIN_H) * WIN_W + column % WIN_W

    token = np.arange(rows * block)
    window, spot = token // WIN, token % WIN
    row = (window // columns) * WIN_H + spot // WIN_W
    column = (window % columns) * WIN_W + spot % WIN_W
    patch, at = np.arange(4 * padded) // padded, np.arange(4 * padded) % padded
    real = at < rows * block // 4
    prow = np.where(real, 2 * (at // (block // 2)) + patch // 2, 0)
    pcolumn = np.where(real, 2 * (at % (block // 2)) + patch % 2, 0)
    side, spot = np.arange(WIN_H * PADDED_COLUMNS) // PADDED_COLUMNS, np.arange(WIN_H * PADDED_COLUMNS) % PADDED_COLUMNS
    shown = spot < block
    spot = np.where(shown, spot, 0)
    group = np.arange(n_mp * PADDED_COLUMNS) // PADDED_COLUMNS
    place = np.arange(n_mp * PADDED_COLUMNS) % PADDED_COLUMNS
    inside = place < block
    lon = group * block + place

    def halo(down, right, row, column):
        corner = row % WIN_H * WIN_W + column % WIN_W
        slot = jnp.where(
            down,
            jnp.where(right, 0, 3 + column // WIN_W),
            1 + row // WIN_H,
        )
        return jnp.where(jnp.logical_or(down, right), slot * WIN + corner, -1)

    wide = block + WIN_W
    back_row, back_column = prow - lat_offset, pcolumn - lon_offset
    above, left = back_row < 0, back_column < 0
    grad_row, grad_column = row + lat_offset, column + lon_offset
    below, right = grad_row >= rows, grad_column >= block
    table = {
        FRAME: (row + lat_offset) * wide + column + lon_offset,
        OWN: np.where(real, prow * wide + pcolumn, -1),
        BACK: jnp.where(
            jnp.logical_and(real, jnp.logical_not(jnp.logical_or(above, left))),
            window_place(back_row, back_column),
            -1,
        ),
        BACK_HALO: jnp.where(
            real,
            halo(
                above,
                left,
                jnp.where(above, back_row + WIN_H, back_row),
                jnp.where(left, back_column + WIN_W, back_column),
            ),
            -1,
        ),
        COT: np.where(real, prow * block + pcolumn, -1),
        UNPATCH: (2 * (row % 2) + column % 2) * padded + (row // 2) * (block // 2) + column // 2,
        GRAD: jnp.where(
            jnp.logical_or(below, right), -1, window_place(grad_row, grad_column)
        ),
        GRAD_HALO: halo(
            below,
            right,
            jnp.where(below, grad_row - rows, grad_row),
            jnp.where(right, grad_column - block, grad_column),
        ),
        BY_ROW: np.where(shown, (spot // WIN_W) * WIN + side * WIN_W + spot % WIN_W, -1),
        BY_ROW_PATCH: np.where(
            shown, (spot % 2) * padded + side * (block // 2) + spot // 2, -1
        ),
        SHIFT: jnp.where(inside, (lon + lon_offset) % (n_mp * block), -1),
        STAY: np.where(inside, lon, -1),
    }
    columns_list = [
        jnp.pad(jnp.asarray(table[key], jnp.int32), (0, size - table[key].shape[0]))
        for key in range(len(table))
    ]
    return jnp.stack(columns_list, axis=1)


def norm_stats(values, count):
    center = sum(jnp.sum(value, axis=1, keepdims=True) for value in values) / count
    second = sum(jnp.sum(value * value, axis=1, keepdims=True) for value in values) / count
    return (center, lax.rsqrt(second - center * center + EPSILON))


def norm_backward(grads, gains, units, scale_inv, count):
    scaled = [grad * gain for grad, gain in zip(grads, gains)]
    first = sum(jnp.sum(value, axis=1, keepdims=True) for value in scaled) / count
    second = (
        sum(jnp.sum(value * unit, axis=1, keepdims=True) for value, unit in zip(scaled, units))
        / count
    )
    return [scale_inv * (value - first - unit * second) for value, unit in zip(scaled, units)]


def pair_slabs(upper, lower, out_ref, first_rows):
    low = lax.broadcasted_iota(jnp.int32, (upper.shape[0], 2 * HDIM), 1) < HDIM
    rows = pl.ds(first_rows, upper.shape[0])
    for pair in range(upper.shape[1] // (2 * HDIM)):
        lanes = slice(2 * HDIM * pair, 2 * HDIM * (pair + 1))
        one, two = upper[:, lanes], lower[:, lanes]
        out_ref[2 * pair, rows, :] = jnp.where(low, one, swapped(two)).astype(BF16)
        out_ref[2 * pair + 1, rows, :] = jnp.where(low, swapped(one), two).astype(BF16)


WIN = WIN_H * WIN_W
FACTOR = HDIM ** (-0.5)


def heads_apart(values):
    low = lax.broadcasted_iota(jnp.int32, values.shape, 1) < HDIM
    zero = jnp.zeros_like(values)
    both = [jnp.where(low, values, zero), jnp.where(low, zero, values)]
    return jnp.concatenate(both, axis=0).astype(BF16)


def heads_together(values):
    low = lax.broadcasted_iota(jnp.int32, (WIN, 2 * HDIM), 1) < HDIM
    return jnp.where(low, values[:WIN], values[WIN:])


def window_probs(cut, window, query, keys):
    scores = dot_nt(query, keys) * FACTOR
    spot = lax.broadcasted_iota(jnp.int32, scores.shape, 0)
    spot = jnp.where(spot >= WIN, spot - WIN, spot)
    other = lax.broadcasted_iota(jnp.int32, scores.shape, 1)
    edge = cut * WIN_W - jnp.where(window >= 3, WIN, 0)
    same = (spot >= edge) == (other >= edge)
    scores = jnp.where(same, scores, MASKED)
    weights = jnp.exp(scores - jnp.max(scores, axis=1, keepdims=True))
    return weights / jnp.sum(weights, axis=1, keepdims=True)


def framed_packed(fields_ref, gain_ref, weights_ref, packed):
    values = fields_ref[...].astype(F32)
    center, scale_inv = norm_stats([values], values.shape[1])
    unit = (values - center) * scale_inv
    framed = (unit * gain_ref[...]).astype(BF16)
    for kind in range(3):
        packed[kind] = dot_nt(framed, weights_ref[kind]).astype(BF16).astype(F32)
    return (framed, unit, scale_inv)


def window_parts(refs, window, pair):
    rows = pl.ds(pl.multiple_of(window * WIN, 8), WIN)
    lanes = slice(2 * HDIM * pair, 2 * HDIM * (pair + 1))
    return [ref[rows, lanes] for ref in refs]


def attention_forward(
    cut_ref, body_ref, edge_ref, places_ref, gain_ref, weights_ref,
    out_ref, context_ref, fields_ref, own_ref, packed, held, grid,
):
    half, rest = body_ref.shape[1], edge_ref.shape[1]
    join_slabs(body_ref, grid, 0, half)
    join_slabs(edge_ref, grid, 2 * half, 2 * half + rest)
    tokens = fields_ref.shape[0]
    whole = grid[...]
    fields_ref[...] = picked(places_ref[:tokens, FRAME : FRAME + 1], whole).astype(BF16)
    padded = own_ref.shape[1]
    for patch in range(4):
        rows = slice(padded * patch, padded * (patch + 1))
        own_ref[patch] = picked(places_ref[rows, OWN : OWN + 1], whole).astype(BF16)
    framed_packed(fields_ref, gain_ref, weights_ref, packed)
    cut = cut_ref[0]
    windows = fields_ref.shape[0] // WIN

    def step(window, carry):
        rows = pl.ds(pl.multiple_of(window * WIN, 8), WIN)
        for pair in range(fields_ref.shape[1] // (2 * HDIM)):
            query, keys, values = window_parts([packed.at[kind] for kind in range(3)], window, pair)
            probs = window_probs(cut, window, heads_apart(query), keys.astype(BF16))
            joined = dot_nn(probs.astype(BF16), values.astype(BF16))
            held[rows, 2 * HDIM * pair : 2 * HDIM * (pair + 1)] = heads_together(joined)
        return carry

    lax.fori_loop(0, windows, step, 0)
    context = held[...].astype(BF16)
    context_ref[...] = context
    out_ref[...] = dot_nn(context, weights_ref[3]).astype(BF16)


def attention_backward(
    cut_ref, fields_ref, gain_ref, weights_ref, context_ref, grad_ref, halo_ref, places_ref,
    slab_ref, weight_ref, packed, grads, held,
):
    framed, unit, scale_inv = framed_packed(fields_ref, gain_ref, weights_ref, packed)
    cut = cut_ref[0]
    windows = fields_ref.shape[0] // WIN
    tokens = fields_ref.shape[0]
    grad_framed = (
        picked(places_ref[:tokens, GRAD : GRAD + 1], grad_ref[...])
        + picked(places_ref[:tokens, GRAD_HALO : GRAD_HALO + 1], halo_ref[...])
    ).astype(BF16)
    held[...] = dot_nt(grad_framed, weights_ref[3]).astype(BF16).astype(F32)

    def step(window, carry):
        rows = pl.ds(pl.multiple_of(window * WIN, 8), WIN)
        for pair in range(fields_ref.shape[1] // (2 * HDIM)):
            lanes = slice(2 * HDIM * pair, 2 * HDIM * (pair + 1))
            query, keys, values, grad = window_parts(
                [packed.at[kind] for kind in range(3)] + [held], window, pair
            )
            query, grad = heads_apart(query), heads_apart(grad)
            keys, values = keys.astype(BF16), values.astype(BF16)
            probs = window_probs(cut, window, query, keys)
            grad_probs = dot_nt(grad, values)
            inner = jnp.sum(grad_probs * probs, axis=1, keepdims=True)
            grad_scores = (probs * (grad_probs - inner) * FACTOR).astype(BF16)
            grads[0, rows, lanes] = heads_together(dot_nn(grad_scores, keys))
            grads[1, rows, lanes] = dot_tn(grad_scores, query)
            grads[2, rows, lanes] = dot_tn(probs.astype(BF16), grad)
        return carry

    lax.fori_loop(0, windows, step, 0)
    grad_normed = jnp.zeros(fields_ref.shape, F32)
    for kind in range(3):
        grad_kind = grads[kind].astype(BF16)
        weight_ref[kind] = dot_tn(grad_kind, framed).astype(BF16)
        grad_normed = grad_normed + dot_nn(grad_kind, weights_ref[kind])
    weight_ref[3] = dot_tn(context_ref[...], grad_framed).astype(BF16)
    (back,) = norm_backward([grad_normed], [gain_ref[...]], [unit], scale_inv, unit.shape[1])
    result = grad_framed.astype(F32) + back
    half = result.shape[0] // 2
    by_row = places_ref[: slab_ref.shape[1], BY_ROW : BY_ROW + 1]
    upper, lower = (picked(by_row, part.astype(BF16)) for part in (result[:half], result[half:]))
    pair_slabs(upper, lower, slab_ref, 0)


def section_loads(core_ref, own_ref, other_ref, weights, loaded):
    core = core_ref[0]
    loads = [
        pltpu.make_async_copy(own_ref, weights.at[core], loaded.at[0]),
        pltpu.make_async_copy(other_ref, weights.at[1 - core], loaded.at[1]),
    ]
    for load in loads:
        load.start()
    return loads


def merge_forward(
    core_ref, fields_ref, attention_ref, halo_ref, cot_got_ref, places_ref, gain_ref,
    mlp_gain_ref, own_ref, other_ref,
    pair_ref, hidden_ref, merged_ref, grad_ref, cot_ref, weights, loaded, joined,
):
    loads = section_loads(core_ref, own_ref, other_ref, weights, loaded)
    width_two = merged_ref.shape[1]
    join_slabs(cot_got_ref, joined, 0, cot_got_ref.shape[1])
    cot = joined[...].astype(BF16)
    padded = merged_ref.shape[0]
    hidden = []
    for patch in range(4):
        rows = slice(padded * patch, padded * (patch + 1))
        cot_ref[patch] = picked(places_ref[rows, COT : COT + 1], cot).astype(BF16)
        attention = picked(places_ref[rows, BACK : BACK + 1], attention_ref[...])
        attention = attention + picked(
            places_ref[rows, BACK_HALO : BACK_HALO + 1], halo_ref[...]
        )
        value = fields_ref[patch].astype(F32) + attention
        hidden_ref[patch] = value.astype(BF16)
        hidden.append(value.astype(BF16).astype(F32))
    center, scale_inv = norm_stats(hidden, 4 * hidden[0].shape[1])
    merged = jnp.zeros(merged_ref.shape, F32)
    grad = jnp.zeros(merged_ref.shape, F32)
    for load in loads:
        load.wait()
    for patch in range(4):
        normed = (hidden[patch] - center) * scale_inv * gain_ref[patch : patch + 1, :]
        merged = merged + dot_nn(normed.astype(BF16), weights[0, patch])
        grad = grad + dot_nn(cot_ref[patch], weights[1, patch])
    merged_ref[...] = merged.astype(BF16)
    merged = merged.astype(BF16).astype(F32)
    center, scale_inv = norm_stats([merged], width_two)
    mlp_in = (merged - center) * scale_inv * mlp_gain_ref[...]
    pair_ref[:, :width_two] = mlp_in.astype(BF16)
    pair_ref[:, width_two:] = grad.astype(BF16)
    grad_ref[...] = grad


def merge_backward(
    core_ref, parts_ref, merged_ref, grad_ref, hidden_ref, cot_ref, places_ref, gain_ref,
    mlp_gain_ref, own_ref, other_ref, slab_ref, out_ref, weights, loaded,
):
    loads = section_loads(core_ref, own_ref, other_ref, weights, loaded)
    width_two = merged_ref.shape[1]
    total = parts_ref[0].astype(F32)
    for index in range(1, parts_ref.shape[0]):
        total = total + parts_ref[index].astype(F32)
    merged = merged_ref[...].astype(F32)
    bottom = (merged + total[:, :width_two]).astype(BF16)
    for load in loads:
        load.wait()
    decoded = [
        hidden_ref[patch].astype(F32) + dot_nt(bottom, weights[1, patch])
        for patch in range(4)
    ]
    by_row = places_ref[: slab_ref.shape[1], BY_ROW_PATCH : BY_ROW_PATCH + 1]
    upper, lower = (
        picked(by_row, jnp.concatenate([decoded[at], decoded[at + 1]], axis=0).astype(BF16))
        for at in (0, 2)
    )
    pair_slabs(upper, lower, slab_ref, 0)
    center, scale_inv = norm_stats([merged], width_two)
    unit = (merged - center) * scale_inv
    (back,) = norm_backward(
        [total[:, width_two:]], [mlp_gain_ref[...]], [unit], scale_inv, width_two
    )
    grad_merged = (grad_ref[...] + back).astype(BF16)
    hidden = [hidden_ref[patch].astype(F32) for patch in range(4)]
    center, scale_inv = norm_stats(hidden, 4 * hidden[0].shape[1])
    units = [(value - center) * scale_inv for value in hidden]
    backs = norm_backward(
        [dot_nt(grad_merged, weights[0, patch]) for patch in range(4)],
        [gain_ref[patch : patch + 1, :] for patch in range(4)],
        units,
        scale_inv,
        4 * hidden[0].shape[1],
    )
    grads = [(cot_ref[patch].astype(F32) + backs[patch]) for patch in range(4)]
    grads = jnp.concatenate(grads, axis=0).astype(BF16)
    tokens = out_ref.shape[0]
    out_ref[...] = picked(places_ref[:tokens, UNPATCH : UNPATCH + 1], grads).astype(BF16)


def decoded_rows(got_ref, places_ref, out_ref):
    places = places_ref[: got_ref.shape[0] * PADDED_COLUMNS, STAY : STAY + 1]
    for side in range(WIN_H):
        rows = slice(side * PADDED_COLUMNS, (side + 1) * PADDED_COLUMNS)
        values = got_ref[:, rows, :].reshape(-1, 2 * HDIM)
        both = spread_over(places, values, out_ref.shape[2])
        for index in range(2):
            out_ref[2 * side + index] = both[HDIM * index : HDIM * (index + 1)].astype(BF16)


def input_rows(shift_ref, got_ref, edge_ref, places_ref, out_ref, framed):
    places = places_ref[: got_ref.shape[0] * PADDED_COLUMNS, SHIFT : SHIFT + 1]
    for side in range(WIN_H):
        rows = slice(side * PADDED_COLUMNS, (side + 1) * PADDED_COLUMNS)
        both = spread_over(places, got_ref[:, rows, :].reshape(-1, 2 * HDIM), out_ref.shape[2])
        framed[WIN_H + side] = both[:HDIM]
        framed[2 * WIN_H + side] = both[HDIM:]
        both = spread_over(places, edge_ref[:, rows, :].reshape(-1, 2 * HDIM), out_ref.shape[2])
        framed[side] = both[HDIM:]
    first = WIN_H - shift_ref[0]
    for row in range(out_ref.shape[0]):
        out_ref[row] = framed[first + row]


def shards(
    fields,
    first_gain,
    qkv_weight,
    proj_weight,
    merge_gain,
    merge_weight,
    mlp_gain,
    up_weight,
    down_weight,
    expand_weight,
    lat_shift,
    lon_shift,
    cotangent,
):
    n_lat, n_mp = lax.axis_size("lat"), lax.axis_size("mp")
    lat, core = lax.axis_index("lat"), lax.rem(lax.axis_index("lat"), 2)
    lat_offset = lat_shift[0]
    lon_offset = lon_shift[0]
    rows, lon_count, group = fields.shape
    width = group * n_mp
    block = lon_count // n_mp
    wide = block + WIN_W
    bands, columns = rows // WIN_H, block // WIN_W
    tokens = rows * block
    width_two = merge_weight.shape[2]
    span = up_weight.shape[1]
    merged_count = tokens // 4
    padded = -(-merged_count // 16) * 16
    others = range(n_mp)

    section = jnp.where(core == 0, merge_weight, expand_weight.transpose(1, 2, 0))
    section_own = lax.all_gather(section, "mp", axis=1, tiled=True)
    blocks = fields.reshape(rows, n_mp, block, group).transpose(1, 0, 2, 3)
    margin = jnp.roll(blocks[:, :, :WIN_W], -1, axis=0)
    field_blocks = jnp.concatenate([blocks, margin], axis=2)
    body_slab = halves_beside(field_blocks.reshape(n_mp, rows * wide, group))
    edge_slab = halves_beside(field_blocks[:, :WIN_H].reshape(n_mp, WIN_H * wide, group))
    cot_blocks = cotangent.reshape(rows, n_mp, block, group).transpose(1, 0, 2, 3)
    cot_slab = halves_beside(cot_blocks.reshape(n_mp, tokens, group))
    weights = jnp.concatenate(
        [qkv_weight.transpose(1, 2, 0), proj_weight.transpose(1, 0)[None]], axis=0
    )
    gains = jnp.pad(jnp.concatenate([first_gain[None], merge_gain], axis=0), ((0, 3), (0, 64)))

    def rows_at(here, step):
        return pl.ds(pl.multiple_of(lax.rem(here["mp"] + n_mp - step, n_mp) * group, group), group)

    def core_half(ref, here, target):
        return ref.at[pl.ds(2 * here["core"], 2)]

    def core_half_rows(step):
        return lambda ref, here, target: ref.at[pl.ds(2 * here["core"], 2), rows_at(here, step)]

    def own_rows(ref, here, target):
        return ref.at[:, rows_at(here, 0)]

    places = place_table(lat_offset, lon_offset, rows, block, padded, n_mp)
    body_got, edge_got, weights_all, gains_all = exchange(
        1,
        [body_slab, edge_slab, weights, gains],
        [
            (body_slab.shape, BF16),
            (edge_slab.shape, BF16),
            ((4, width, width), BF16),
            ((n_mp,) + gains.shape, F32),
        ],
        [(2, core_half, 2, core_half_rows(0), 0, step) for step in range(1, n_mp)]
        + [(3, None, 3, "mp", 0, step) for step in others]
        + [(0, "mp", 0, "mp", 0, step) for step in others]
        + [(1, "mp", 1, "mp", -1, step) for step in others]
        + [(2, None, 2, own_rows, 0, 0)]
        + [
            (2, core_half_rows(step), 2, core_half_rows(step), "sibling", 0, step - 1)
            for step in range(1, n_mp)
        ],
    )
    has_shard = lax.rem(lax.axis_index("mp"), 2) == core
    first_all = gains_all[:, 0, :group].reshape(1, width)
    merge_gain_all = gains_all[:, 1:5, :group].transpose(1, 0, 2).reshape(4, width)
    mlp_gain_row = mlp_gain.reshape(1, width_two)
    cut = (jnp.int32(rows) * (n_lat - lat) - lat_offset).reshape(1)
    attention_framed, context, framed_fields, own_fields = local_kernel(
        attention_forward,
        [cut, body_got, edge_got, places, first_all, weights_all],
        [((tokens, width), BF16)] * 3 + [((4, padded, width), BF16)],
        [
            pltpu.VMEM((3, tokens, width), F32),
            pltpu.VMEM((tokens, width), F32),
            pltpu.VMEM(((rows + WIN_H) * wide, width), BF16),
        ],
        scalars=1,
    )
    window_shape = (bands, columns, WIN, width)
    around = (2 * bands + 2, WIN, width)
    halo, cot_got = exchange(
        2,
        [attention_framed.reshape(window_shape), cot_slab],
        [(around, BF16), (cot_slab.shape, BF16)],
        [
            (0, (bands - 1, columns - 1), 0, (0,), 1, 1),
            (0, (slice(0, bands), columns - 1), 0, (slice(1, 1 + bands),), 0, 1),
            (0, (bands - 1,), 0, (slice(1 + bands, 1 + bands + columns),), 1, 0),
        ]
        + [(1, "mp", 1, "mp", 0, step) for step in others],
    )
    (section_other,) = exchange(
        7, [section_own], [(section_own.shape, BF16)], [(0, None, 0, None, "sibling", 0)]
    )
    n_x = n_mp // 2
    section_scratch = [
        pltpu.VMEM((2,) + section_own.shape, BF16),
        pltpu.SemaphoreType.DMA((2,)),
    ]
    pair, hidden, merged, grad_bottom, cot_patches = local_kernel(
        merge_forward,
        [
            core.reshape(1),
            own_fields,
            attention_framed,
            halo.reshape(-1, width),
            cot_got,
            places,
            merge_gain_all,
            mlp_gain_row,
            section_own,
            section_other,
        ],
        [
            ((padded, 2 * width_two), BF16),
            ((4, padded, width), BF16),
            ((padded, width_two), BF16),
            ((padded, width_two), F32),
            ((4, padded, width), BF16),
        ],
        section_scratch + [pltpu.VMEM((tokens, width), F32)],
        scalars=1,
        outside=2,
    )

    def chip_spot(step):
        def spot(ref, here, target):
            return ref.at[lax.rem(here["x"] + n_x + step, n_x), here["core"]]

        return spot

    pairs, up_other, down_other = exchange(
        3,
        [pair, up_weight, down_weight],
        [
            ((n_x, 2) + pair.shape, BF16),
            (up_weight.shape, BF16),
            (down_weight.shape, BF16),
        ],
        [
            (0, None, 0, chip_spot(0), 0, 4),
            (0, None, 0, chip_spot(0), 0, 2),
            (0, None, 0, chip_spot(0), 0, -2),
            (0, None, 0, chip_spot(0), "sibling", 0),
            (0, None, 0, chip_spot(0), 0, 0),
            (1, None, 1, None, "flip", 0),
            (2, None, 2, None, "flip", 0),
            (0, chip_spot(-1), 0, chip_spot(-1), "sibling", 0, 1),
            (0, chip_spot(1), 0, chip_spot(1), "sibling", 0, 2),
            (0, chip_spot(-2), 0, chip_spot(-2), "sibling", 0, 0),
        ],
    )
    up_shard = jnp.where(has_shard, up_weight, up_other)
    down_shard = jnp.where(has_shard, down_weight, down_other)
    pairs = pairs.reshape(n_mp * padded, 2 * width_two)
    mlp_in, bottom_grad = pairs[:, :width_two], pairs[:, width_two:]
    hidden_up = jnp.dot(mlp_in, up_shard, preferred_element_type=F32)
    activated = jax.nn.gelu(hidden_up).astype(BF16)
    grad_act = jnp.dot(bottom_grad, down_shard, preferred_element_type=F32)
    gelu_back = jax.vjp(jax.nn.gelu, hidden_up)[1]
    grad_pre = gelu_back(grad_act)[0].astype(BF16)
    terms = jnp.concatenate(
        [
            jnp.einsum("af,ef->ae", activated, down_shard, preferred_element_type=F32),
            jnp.einsum("af,ef->ae", grad_pre, up_shard, preferred_element_type=F32),
        ],
        axis=1,
    ).astype(BF16)
    large = (n_lat, width_two // n_lat, span)
    parts, up_got, down_got = terms_back(
        4,
        terms.reshape(n_x, 2, padded, 2 * width_two),
        jnp.einsum("ae,af->ef", mlp_in, grad_pre, preferred_element_type=F32)
        .astype(BF16)
        .reshape(large),
        jnp.einsum("ao,af->of", bottom_grad, activated, preferred_element_type=F32)
        .astype(BF16)
        .reshape(large),
    )
    grad_up = jnp.sum(up_got.astype(F32), axis=0)
    grad_down = jnp.sum(down_got.astype(F32), axis=0)
    row_slab = (n_mp, WIN_H * PADDED_COLUMNS, 2 * group)
    decoded_slab, grad_windows = local_kernel(
        merge_backward,
        [
            core.reshape(1),
            parts,
            merged,
            grad_bottom,
            hidden,
            cot_patches,
            places,
            merge_gain_all,
            mlp_gain_row,
            section_own,
            section_other,
        ],
        [(row_slab, BF16), ((tokens, width), BF16)],
        section_scratch,
        scalars=1,
        outside=2,
    )
    halo, decoded_got = exchange(
        5,
        [grad_windows.reshape(window_shape), decoded_slab],
        [(around, BF16), (decoded_slab.shape, BF16)],
        [
            (0, (0, 0), 0, (0,), -1, -1),
            (0, (slice(0, bands), 0), 0, (slice(1, 1 + bands),), 0, -1),
            (0, (0,), 0, (slice(1 + bands, 1 + bands + columns),), -1, 0),
        ]
        + [(1, "mp", 1, "mp", 0, step) for step in others],
    )
    grad_slab, weight_grads = local_kernel(
        attention_backward,
        [
            cut,
            framed_fields,
            first_all,
            weights_all,
            context,
            grad_windows,
            halo.reshape(-1, width),
            places,
        ],
        [(row_slab, BF16), ((4, width, width), BF16)],
        [
            pltpu.VMEM((3, tokens, width), F32),
            pltpu.VMEM((3, tokens, width), F32),
            pltpu.VMEM((tokens, width), F32),
        ],
        scalars=1,
    )
    weight_total, grad_got, edge_got = gradients_out(6, weight_grads, grad_slab)
    grad_qkv = weight_total[:, : 3 * group].reshape(width // n_lat, 3, group)
    grad_proj = weight_total[:, 3 * group :]
    (decoded,) = local_kernel(
        decoded_rows, [decoded_got, places], [((rows, group, lon_count), BF16)]
    )
    (grad_input,) = local_kernel(
        input_rows,
        [lat_shift, grad_got, edge_got, places],
        [((rows, group, lon_count), F32)],
        [pltpu.VMEM((rows + WIN_H, group, lon_count), F32)],
        scalars=1,
    )
    decoded, grad_input = decoded.transpose(0, 2, 1), grad_input.transpose(0, 2, 1)
    return (decoded, grad_input, grad_qkv, grad_proj, grad_up, grad_down)


def solution(mesh):
    return jax.shard_map(
        shards,
        mesh=mesh,
        in_specs=(
            P("lat", None, "mp"),
            P("mp"),
            P(None, None, "mp"),
            P(None, "mp"),
            P(None, "mp"),
            P(None, "mp", None),
            P(),
            P(None, "mp"),
            P(None, "mp"),
            P(None, None, "mp"),
            P(),
            P(),
            P("lat", None, "mp"),
        ),
        out_specs=(
            P("lat", None, "mp"),
            P("lat", None, "mp"),
            P("lat", None, "mp"),
            P("lat", "mp"),
            P("lat", "mp"),
            P("lat", "mp"),
        ),
        check_vma=False,
    )
```

```python
import jax
import jax.numpy as jnp
import numpy as np
from jax import lax
from jax.experimental import pallas as pl
from jax.experimental.pallas import tpu as pltpu
from jax.sharding import PartitionSpec as P

WIN_H = 6
WIN_W = 12
HDIM = 64
EPSILON = 1e-05
MASKED = -1e30
BF16 = jnp.bfloat16
F32 = jnp.float32


def positions():
    lat, mp = lax.axis_index("lat"), lax.axis_index("mp")
    return {
        "lat": lat,
        "mp": mp,
        "core": lax.rem(lat, 2),
        "x": lax.div(mp, 2),
        "z": lax.rem(mp, 2),
        "quarter": 2 * lax.rem(lax.div(lat, 4), 2) + lax.rem(lat, 2),
    }


def reached(here, down, right):
    n_lat, n_mp = lax.axis_size("lat"), lax.axis_size("mp")
    if down == "sibling":
        return {"lat": here["lat"] + 1 - 2 * here["core"], "mp": here["mp"]}
    if down == "flip":
        return {"lat": here["lat"], "mp": 2 * here["x"] + 1 - here["z"]}
    return {
        "lat": lax.rem(here["lat"] + n_lat + down, n_lat),
        "mp": lax.rem(here["mp"] + n_mp + right, n_mp),
    }


def device_of(target):
    return {
        "device_id": (target["lat"], target["mp"]),
        "device_id_type": pl.DeviceIdType.MESH,
    }


def greet(here, steps, owned=False):
    barrier = pltpu.get_barrier_semaphore()
    count = len(steps)
    if owned:
        n_lat, x, z = lax.axis_size("lat"), here["x"], here["z"]
        owner = z == here["core"]
        mine = 2 * lax.div(here["lat"], 2) + z
        count = count + n_lat - jnp.where(owner, 1, 0)
        for source in range(n_lat):

            @pl.when(jnp.logical_or(jnp.logical_not(owner), mine != source))
            def _():
                target = {"lat": 2 * (source // 2) + z, "mp": 2 * x + source % 2}
                pl.semaphore_signal(barrier, inc=1, **device_of(target))

    for down, right in steps:
        source = reached(here, down if isinstance(down, str) else -down, -right)
        pl.semaphore_signal(barrier, inc=1, **device_of(source))
    pl.semaphore_wait(barrier, count)


def to_owners(here, source, landing, send, receive):
    n_lat = lax.axis_size("lat")
    lat, core, x, z = here["lat"], here["core"], here["x"], here["z"]
    mine = 2 * lax.div(lat, 2) + z
    owner = z == core

    def copy_at(step):
        target = {"lat": lax.rem(lat + step, n_lat), "mp": 2 * x + core}
        rows = target["lat"]
        return remote(source.at[rows], landing.at[mine], send.at[step], receive.at[mine], target)

    def start():
        for step in range(1, n_lat):
            copy_at(step).start()

        @pl.when(owner)
        def _():
            pltpu.make_async_copy(source.at[lat], landing.at[mine], receive.at[mine]).start()

        @pl.when(jnp.logical_not(owner))
        def _():
            copy_at(0).start()

    def wait():
        sibling = reached(here, "sibling", 0)
        for slot in range(n_lat):
            remote(
                source.at[slot], landing.at[slot], send.at[slot], receive.at[slot], sibling
            ).wait_recv()
        for step in range(1, n_lat):
            copy_at(step).wait_send()

        @pl.when(jnp.logical_not(owner))
        def _():
            copy_at(0).wait_send()

    return start, wait


def remote(source, landing, send, receive, target):
    return pltpu.make_async_remote_copy(
        src_ref=source, dst_ref=landing, send_sem=send, recv_sem=receive, **device_of(target)
    )


def exchange(collective, inputs, outputs, moves, owned=()):
    n_lat = lax.axis_size("lat")
    steps = []
    for move in moves:
        if move[4:6] != (0, 0) and move[4:6] not in steps:
            steps.append(move[4:6])

    def body(*refs):
        sources = refs[: len(inputs)]
        landings = refs[len(inputs) : len(inputs) + len(outputs)]
        send, receive, owned_send, owned_receive = refs[-4:]
        here = positions()

        def part_of(ref, part, place, target):
            if part is None:
                return ref
            if isinstance(part, str):
                return ref.at[place[part]]
            if callable(part):
                return part(ref, here, target)
            return ref.at[part]

        greet(here, steps, bool(owned))
        copies = []
        arrived = set()
        scatters = [
            to_owners(
                here, sources[one], landings[two], owned_send.at[index], owned_receive.at[index]
            )
            for index, (one, two) in enumerate(owned)
        ]
        for index, move in enumerate(moves):
            source, source_part, landing, landing_part, down, right = move[:6]
            target = reached(here, down, right)
            if len(move) > 6:
                copies[move[6]].wait_recv()
                arrived.add(move[6])
                source_ref = part_of(landings[source], source_part, target, target)
            else:
                source_ref = part_of(sources[source], source_part, target, target)
            landing_ref = part_of(landings[landing], landing_part, here, target)
            if (down, right) == (0, 0):
                copy = pltpu.make_async_copy(source_ref, landing_ref, receive.at[index])
            else:
                copy = remote(
                    source_ref, landing_ref, send.at[index], receive.at[index], target
                )
            if down == "flip":
                pl.when(here["z"] == here["core"])(copy.start)
            else:
                copy.start()
            copies.append(copy)
        for start, _ in scatters:
            start()
        for _, wait in scatters:
            wait()
        for index, copy in enumerate(copies):
            if moves[index][4:6] == (0, 0):
                copy.wait()
            elif moves[index][4] == "flip":
                pl.when(here["z"] == here["core"])(copy.wait_send)
                pl.when(here["z"] != here["core"])(copy.wait_recv)
            else:
                copy.wait_send()
                if index not in arrived:
                    copy.wait_recv()

    return pl.pallas_call(
        body,
        out_shape=[jax.ShapeDtypeStruct(shape, dtype) for shape, dtype in outputs],
        in_specs=[pl.BlockSpec(memory_space=pl.ANY)] * len(inputs),
        out_specs=[pl.BlockSpec(memory_space=pl.ANY)] * len(outputs),
        scratch_shapes=[
            pltpu.SemaphoreType.DMA((len(moves),)),
            pltpu.SemaphoreType.DMA((len(moves),)),
            pltpu.SemaphoreType.DMA((max(len(owned), 1), n_lat)),
            pltpu.SemaphoreType.DMA((max(len(owned), 1), n_lat)),
        ],
        compiler_params=pltpu.CompilerParams(collective_id=collective, has_side_effects=True),
    )(*inputs)


X_STEPS = ((4, 2), (2, 1), (-2, 3))


def terms_back(collective, terms, grads):
    count, _, rows, width = terms.shape
    n_lat = lax.axis_size("lat")

    def body(
        terms_ref, grads_ref, parts_ref, grads_got,
        other, own, total, send, receive, fetch, large_send, large_receive,
    ):
        here = positions()
        core, x = here["core"], here["x"]
        sibling = reached(here, "sibling", 0)
        greet(here, [("sibling", 0)] + [(0, right) for right, _ in X_STEPS], True)
        start, wait = to_owners(here, grads_ref, grads_got, large_send, large_receive)
        order = [lax.rem(x + step, count) for _, step in X_STEPS] + [x]
        swaps, loads = [], []
        for index, spot in enumerate(order):
            swap = remote(
                terms_ref.at[spot, 1 - core],
                other.at[index],
                send.at[index],
                receive.at[index],
                sibling,
            )
            load = pltpu.make_async_copy(terms_ref.at[spot, core], own.at[index], fetch.at[index])
            swap.start()
            load.start()
            swaps.append(swap)
            loads.append(load)
        start()
        sends = []
        for index, spot in enumerate(order):
            loads[index].wait()
            swaps[index].wait_recv()
            total[index] = (own[index].astype(F32) + other[index].astype(F32)).astype(BF16)
            if index < len(X_STEPS):
                copy = remote(
                    total.at[index],
                    parts_ref.at[x],
                    send.at[count + index],
                    receive.at[count + index],
                    reached(here, 0, X_STEPS[index][0]),
                )
            else:
                copy = pltpu.make_async_copy(total.at[index], parts_ref.at[x], fetch.at[count])
            copy.start()
            sends.append(copy)
        for swap in swaps:
            swap.wait_send()
        for copy in sends:
            copy.wait()
        wait()

    return pl.pallas_call(
        body,
        out_shape=[
            jax.ShapeDtypeStruct((count, rows, width), BF16),
            jax.ShapeDtypeStruct(grads.shape, BF16),
        ],
        in_specs=[pl.BlockSpec(memory_space=pl.ANY)] * 2,
        out_specs=[pl.BlockSpec(memory_space=pl.ANY)] * 2,
        scratch_shapes=[
            pltpu.VMEM((count, rows, width), BF16),
            pltpu.VMEM((count, rows, width), BF16),
            pltpu.VMEM((count, rows, width), BF16),
            pltpu.SemaphoreType.DMA((2 * count,)),
            pltpu.SemaphoreType.DMA((2 * count,)),
            pltpu.SemaphoreType.DMA((count + 1,)),
            pltpu.SemaphoreType.DMA((n_lat,)),
            pltpu.SemaphoreType.DMA((n_lat,)),
        ],
        compiler_params=pltpu.CompilerParams(
            collective_id=collective, has_side_effects=True, vmem_limit_bytes=48 * 1024 * 1024
        ),
    )(terms, grads)


def gradients_out(collective, weight_grads, slabs, edges):
    n_lat, n_mp = lax.axis_size("lat"), lax.axis_size("mp")
    kinds, width, _ = weight_grads.shape
    pair, group, share = kinds // 2, width // n_mp, width // n_lat

    def body(
        weight_ref, slab_ref, edge_ref, out_ref, got_ref, edge_got,
        other, total, parts, turned, landed, send, receive,
    ):
        here = positions()
        lat, mp, core = here["lat"], here["mp"], here["core"]
        sibling = reached(here, "sibling", 0)
        barrier = pltpu.get_barrier_semaphore()
        greeted = [sibling]
        greeted += [reached(here, 0, -step) for step in range(1, n_mp)]
        greeted += [reached(here, -1, -step) for step in range(n_mp)]
        greeted += [reached(here, -step, 0) for step in range(1, n_lat)]
        for target in greeted:
            pl.semaphore_signal(barrier, inc=1, **device_of(target))
        pl.semaphore_wait(barrier, len(greeted))

        copies = []

        def sent(source, landing, target):
            index = len(copies)
            copy = remote(source, landing, send.at[index], receive.at[index], target)
            copy.start()
            copies.append(copy)
            return copy

        swap = sent(weight_ref.at[pl.ds(pair * (1 - core), pair)], other, sibling)
        own_slab = pltpu.make_async_copy(slab_ref.at[mp], got_ref.at[mp], send.at[60])
        own_slab.start()

        swap.wait_recv()
        total[...] = (
            weight_ref[pl.ds(pair * core, pair)].astype(F32) + other[...].astype(F32)
        ).astype(BF16)
        scattered = []
        for step in range(1, n_mp):
            target = reached(here, 0, step)
            rows = pl.ds(pl.multiple_of(group * target["mp"], group), group)
            scattered.append(sent(total.at[:, rows], parts.at[mp], target))
        for step in range(1, n_mp):
            target = reached(here, 0, step)
            sent(slab_ref.at[target["mp"]], got_ref.at[mp], target)
        for step in range(n_mp):
            target = reached(here, 1, step)
            sent(edge_ref.at[target["mp"]], edge_got.at[mp], target)
        gathered = total[:, pl.ds(pl.multiple_of(group * mp, group), group), :].astype(F32)
        for step in range(1, n_mp):
            scattered[step - 1].wait_recv()
            gathered = gathered + parts[lax.rem(mp + n_mp - step, n_mp)].astype(F32)
        flat = gathered.reshape(pair * group, width).T.astype(BF16)
        for index in range(n_lat):
            turned[index] = flat[index * share : (index + 1) * share]
        spread = []
        for step in range(1, n_lat):
            target = reached(here, step, 0)
            spread.append(sent(turned.at[target["lat"]], landed.at[lat], target))
        landed[lat] = turned[lat]
        for copy in spread:
            copy.wait_recv()
        for half in range(2):
            result = landed[half].astype(F32)
            for index in range(half + 2, n_lat, 2):
                result = result + landed[index].astype(F32)
            out_ref[:, half * pair * group : (half + 1) * pair * group] = result

        done = [swap] + scattered + spread
        for copy in copies:
            copy.wait_send()
            if not any(copy is other_copy for other_copy in done):
                copy.wait_recv()
        own_slab.wait()

    any_space = pl.BlockSpec(memory_space=pl.ANY)
    vmem = pl.BlockSpec(memory_space=pltpu.VMEM)
    return pl.pallas_call(
        body,
        out_shape=[
            jax.ShapeDtypeStruct((share, kinds * group), F32),
            jax.ShapeDtypeStruct(slabs.shape, BF16),
            jax.ShapeDtypeStruct(edges.shape, BF16),
        ],
        in_specs=[vmem, any_space, any_space],
        out_specs=[vmem, any_space, any_space],
        scratch_shapes=[
            pltpu.VMEM((pair, width, width), BF16),
            pltpu.VMEM((pair, width, width), BF16),
            pltpu.VMEM((n_mp, pair, group, width), BF16),
            pltpu.VMEM((n_lat, share, pair * group), BF16),
            pltpu.VMEM((n_lat, share, pair * group), BF16),
            pltpu.SemaphoreType.DMA((64,)),
            pltpu.SemaphoreType.DMA((64,)),
        ],
        compiler_params=pltpu.CompilerParams(
            collective_id=collective, has_side_effects=True, vmem_limit_bytes=48 * 1024 * 1024
        ),
    )(weight_grads, slabs, edges)


def local_kernel(body, operands, outputs, scratch=(), scalars=0, outside=0):
    spaces = [pltpu.SMEM] * scalars + [pltpu.VMEM] * (len(operands) - scalars - outside)
    spaces += [pl.ANY] * outside
    return pl.pallas_call(
        body,
        out_shape=[jax.ShapeDtypeStruct(shape, dtype) for shape, dtype in outputs],
        in_specs=[pl.BlockSpec(memory_space=space) for space in spaces],
        out_specs=[pl.BlockSpec(memory_space=pltpu.VMEM)] * len(outputs),
        scratch_shapes=list(scratch),
        compiler_params=pltpu.CompilerParams(vmem_limit_bytes=48 * 1024 * 1024),
    )(*operands)


def dot_nn(left, right):
    return lax.dot_general(left, right, (((1,), (0,)), ((), ())), preferred_element_type=F32)


def dot_nt(left, right):
    return lax.dot_general(left, right, (((1,), (1,)), ((), ())), preferred_element_type=F32)


def dot_tn(left, right):
    return lax.dot_general(left, right, (((0,), (0,)), ((), ())), preferred_element_type=F32)


def halves_beside(values):
    half = values.shape[-2] // 2
    return jnp.concatenate([values[..., :half, :], values[..., half:, :]], axis=-1)


def picked(places, values):
    spots = lax.broadcasted_iota(jnp.int32, (places.shape[0], values.shape[0]), 1)
    return dot_nn(jnp.where(spots == places, 1.0, 0.0).astype(BF16), values)


def spread_over(places, values, count):
    spots = lax.broadcasted_iota(jnp.int32, (places.shape[0], count), 1)
    return dot_tn(values, jnp.where(spots == places, 1.0, 0.0).astype(BF16))


def swapped(values):
    return jnp.concatenate([values[:, HDIM:], values[:, :HDIM]], axis=1)


def join_slabs(slab_ref, out_ref, first_rows, second_rows):
    half = slab_ref.shape[1]
    low = lax.broadcasted_iota(jnp.int32, (half, 2 * HDIM), 1) < HDIM
    for pair in range(slab_ref.shape[0] // 2):
        lanes = slice(2 * HDIM * pair, 2 * HDIM * (pair + 1))
        one = slab_ref[2 * pair].astype(F32)
        two = slab_ref[2 * pair + 1].astype(F32)
        first = jnp.where(low, one, swapped(two)).astype(out_ref.dtype)
        second = jnp.where(low, swapped(one), two).astype(out_ref.dtype)
        out_ref[first_rows : first_rows + half, lanes] = first
        out_ref[second_rows : second_rows + half, lanes] = second


PADDED_COLUMNS = 48
FRAME, OWN, BACK, BACK_HALO, COT, UNPATCH, GRAD, GRAD_HALO, BY_ROW, BY_ROW_PATCH, SHIFT, STAY = range(12)


def place_table(lat_offset, lon_offset, rows, block, padded, n_mp):
    columns = block // WIN_W
    size = max(rows * block, 4 * padded, n_mp * PADDED_COLUMNS)

    def window_place(row, column):
        window = (row // WIN_H) * columns + column // WIN_W
        return window * WIN + (row % WIN_H) * WIN_W + column % WIN_W

    token = np.arange(rows * block)
    window, spot = token // WIN, token % WIN
    row = (window // columns) * WIN_H + spot // WIN_W
    column = (window % columns) * WIN_W + spot % WIN_W
    patch, at = np.arange(4 * padded) // padded, np.arange(4 * padded) % padded
    real = at < rows * block // 4
    prow = np.where(real, 2 * (at // (block // 2)) + patch // 2, 0)
    pcolumn = np.where(real, 2 * (at % (block // 2)) + patch % 2, 0)
    side, spot = np.arange(WIN_H * PADDED_COLUMNS) // PADDED_COLUMNS, np.arange(WIN_H * PADDED_COLUMNS) % PADDED_COLUMNS
    shown = spot < block
    spot = np.where(shown, spot, 0)
    group = np.arange(n_mp * PADDED_COLUMNS) // PADDED_COLUMNS
    place = np.arange(n_mp * PADDED_COLUMNS) % PADDED_COLUMNS
    inside = place < block
    lon = group * block + place

    def halo(down, right, row, column):
        corner = row % WIN_H * WIN_W + column % WIN_W
        slot = jnp.where(
            down,
            jnp.where(right, 0, 3 + column // WIN_W),
            1 + row // WIN_H,
        )
        return jnp.where(jnp.logical_or(down, right), slot * WIN + corner, -1)

    wide = block + WIN_W
    back_row, back_column = prow - lat_offset, pcolumn - lon_offset
    above, left = back_row < 0, back_column < 0
    grad_row, grad_column = row + lat_offset, column + lon_offset
    below, right = grad_row >= rows, grad_column >= block
    table = {
        FRAME: (row + lat_offset) * wide + column + lon_offset,
        OWN: np.where(real, prow * wide + pcolumn, -1),
        BACK: jnp.where(
            jnp.logical_and(real, jnp.logical_not(jnp.logical_or(above, left))),
            window_place(back_row, back_column),
            -1,
        ),
        BACK_HALO: jnp.where(
            real,
            halo(
                above,
                left,
                jnp.where(above, back_row + WIN_H, back_row),
                jnp.where(left, back_column + WIN_W, back_column),
            ),
            -1,
        ),
        COT: np.where(real, prow * block + pcolumn, -1),
        UNPATCH: (2 * (row % 2) + column % 2) * padded + (row // 2) * (block // 2) + column // 2,
        GRAD: jnp.where(
            jnp.logical_or(below, right), -1, window_place(grad_row, grad_column)
        ),
        GRAD_HALO: halo(
            below,
            right,
            jnp.where(below, grad_row - rows, grad_row),
            jnp.where(right, grad_column - block, grad_column),
        ),
        BY_ROW: np.where(shown, (spot // WIN_W) * WIN + side * WIN_W + spot % WIN_W, -1),
        BY_ROW_PATCH: np.where(
            shown, (spot % 2) * padded + side * (block // 2) + spot // 2, -1
        ),
        SHIFT: jnp.where(inside, (lon + lon_offset) % (n_mp * block), -1),
        STAY: np.where(inside, lon, -1),
    }
    columns_list = [
        jnp.pad(jnp.asarray(table[key], jnp.int32), (0, size - table[key].shape[0]))
        for key in range(len(table))
    ]
    return jnp.stack(columns_list, axis=1)


def norm_stats(values, count):
    center = sum(jnp.sum(value, axis=1, keepdims=True) for value in values) / count
    second = sum(jnp.sum(value * value, axis=1, keepdims=True) for value in values) / count
    return (center, lax.rsqrt(second - center * center + EPSILON))


def norm_backward(grads, gains, units, scale_inv, count):
    scaled = [grad * gain for grad, gain in zip(grads, gains)]
    first = sum(jnp.sum(value, axis=1, keepdims=True) for value in scaled) / count
    second = (
        sum(jnp.sum(value * unit, axis=1, keepdims=True) for value, unit in zip(scaled, units))
        / count
    )
    return [scale_inv * (value - first - unit * second) for value, unit in zip(scaled, units)]


def pair_slabs(upper, lower, out_ref, first_rows):
    low = lax.broadcasted_iota(jnp.int32, (upper.shape[0], 2 * HDIM), 1) < HDIM
    rows = pl.ds(first_rows, upper.shape[0])
    for pair in range(upper.shape[1] // (2 * HDIM)):
        lanes = slice(2 * HDIM * pair, 2 * HDIM * (pair + 1))
        one, two = upper[:, lanes], lower[:, lanes]
        out_ref[2 * pair, rows, :] = jnp.where(low, one, swapped(two)).astype(BF16)
        out_ref[2 * pair + 1, rows, :] = jnp.where(low, swapped(one), two).astype(BF16)


WIN = WIN_H * WIN_W
FACTOR = HDIM ** (-0.5)


def heads_apart(values):
    low = lax.broadcasted_iota(jnp.int32, values.shape, 1) < HDIM
    zero = jnp.zeros_like(values)
    both = [jnp.where(low, values, zero), jnp.where(low, zero, values)]
    return jnp.concatenate(both, axis=0).astype(BF16)


def heads_together(values):
    low = lax.broadcasted_iota(jnp.int32, (WIN, 2 * HDIM), 1) < HDIM
    return jnp.where(low, values[:WIN], values[WIN:])


def window_probs(cut, window, query, keys):
    scores = dot_nt(query, keys) * FACTOR
    spot = lax.broadcasted_iota(jnp.int32, scores.shape, 0)
    spot = jnp.where(spot >= WIN, spot - WIN, spot)
    other = lax.broadcasted_iota(jnp.int32, scores.shape, 1)
    edge = cut * WIN_W - jnp.where(window >= 3, WIN, 0)
    same = (spot >= edge) == (other >= edge)
    scores = jnp.where(same, scores, MASKED)
    weights = jnp.exp(scores - jnp.max(scores, axis=1, keepdims=True))
    return weights / jnp.sum(weights, axis=1, keepdims=True)


def framed_packed(fields_ref, gain_ref, weights_ref, packed):
    values = fields_ref[...].astype(F32)
    center, scale_inv = norm_stats([values], values.shape[1])
    unit = (values - center) * scale_inv
    framed = (unit * gain_ref[...]).astype(BF16)
    for kind in range(3):
        packed[kind] = dot_nt(framed, weights_ref[kind]).astype(BF16).astype(F32)
    return (framed, unit, scale_inv)


def window_parts(refs, window, pair):
    rows = pl.ds(pl.multiple_of(window * WIN, 8), WIN)
    lanes = slice(2 * HDIM * pair, 2 * HDIM * (pair + 1))
    return [ref[rows, lanes] for ref in refs]


def attention_forward(
    cut_ref, body_ref, edge_ref, places_ref, gain_ref, weights_ref,
    out_ref, context_ref, fields_ref, own_ref, packed, held, grid,
):
    half, rest = body_ref.shape[1], edge_ref.shape[1]
    join_slabs(body_ref, grid, 0, half)
    join_slabs(edge_ref, grid, 2 * half, 2 * half + rest)
    tokens = fields_ref.shape[0]
    whole = grid[...]
    fields_ref[...] = picked(places_ref[:tokens, FRAME : FRAME + 1], whole).astype(BF16)
    padded = own_ref.shape[1]
    for patch in range(4):
        rows = slice(padded * patch, padded * (patch + 1))
        own_ref[patch] = picked(places_ref[rows, OWN : OWN + 1], whole).astype(BF16)
    framed_packed(fields_ref, gain_ref, weights_ref, packed)
    cut = cut_ref[0]
    windows = fields_ref.shape[0] // WIN

    def step(window, carry):
        rows = pl.ds(pl.multiple_of(window * WIN, 8), WIN)
        for pair in range(fields_ref.shape[1] // (2 * HDIM)):
            query, keys, values = window_parts([packed.at[kind] for kind in range(3)], window, pair)
            probs = window_probs(cut, window, heads_apart(query), keys.astype(BF16))
            joined = dot_nn(probs.astype(BF16), values.astype(BF16))
            held[rows, 2 * HDIM * pair : 2 * HDIM * (pair + 1)] = heads_together(joined)
        return carry

    lax.fori_loop(0, windows, step, 0)
    context = held[...].astype(BF16)
    context_ref[...] = context
    out_ref[...] = dot_nn(context, weights_ref[3]).astype(BF16)


def attention_backward(
    cut_ref, fields_ref, gain_ref, weights_ref, context_ref, grad_ref, halo_ref, places_ref,
    slab_ref, edge_ref, weight_ref, packed, grads, held,
):
    framed, unit, scale_inv = framed_packed(fields_ref, gain_ref, weights_ref, packed)
    cut = cut_ref[0]
    windows = fields_ref.shape[0] // WIN
    tokens = fields_ref.shape[0]
    grad_framed = (
        picked(places_ref[:tokens, GRAD : GRAD + 1], grad_ref[...])
        + picked(places_ref[:tokens, GRAD_HALO : GRAD_HALO + 1], halo_ref[...])
    ).astype(BF16)
    held[...] = dot_nt(grad_framed, weights_ref[3]).astype(BF16).astype(F32)

    def step(window, carry):
        rows = pl.ds(pl.multiple_of(window * WIN, 8), WIN)
        for pair in range(fields_ref.shape[1] // (2 * HDIM)):
            lanes = slice(2 * HDIM * pair, 2 * HDIM * (pair + 1))
            query, keys, values, grad = window_parts(
                [packed.at[kind] for kind in range(3)] + [held], window, pair
            )
            query, grad = heads_apart(query), heads_apart(grad)
            keys, values = keys.astype(BF16), values.astype(BF16)
            probs = window_probs(cut, window, query, keys)
            grad_probs = dot_nt(grad, values)
            inner = jnp.sum(grad_probs * probs, axis=1, keepdims=True)
            grad_scores = (probs * (grad_probs - inner) * FACTOR).astype(BF16)
            grads[0, rows, lanes] = heads_together(dot_nn(grad_scores, keys))
            grads[1, rows, lanes] = dot_tn(grad_scores, query)
            grads[2, rows, lanes] = dot_tn(probs.astype(BF16), grad)
        return carry

    lax.fori_loop(0, windows, step, 0)
    grad_normed = jnp.zeros(fields_ref.shape, F32)
    for kind in range(3):
        grad_kind = grads[kind].astype(BF16)
        weight_ref[kind] = dot_tn(grad_kind, framed).astype(BF16)
        grad_normed = grad_normed + dot_nn(grad_kind, weights_ref[kind])
    weight_ref[3] = dot_tn(context_ref[...], grad_framed).astype(BF16)
    (back,) = norm_backward([grad_normed], [gain_ref[...]], [unit], scale_inv, unit.shape[1])
    result = grad_framed.astype(F32) + back
    half = result.shape[0] // 2
    by_row = places_ref[: slab_ref.shape[1], BY_ROW : BY_ROW + 1]
    upper, lower = (picked(by_row, part.astype(BF16)) for part in (result[:half], result[half:]))
    pair_slabs(upper, lower, slab_ref, 0)
    half = edge_ref.shape[1]
    pair_slabs(lower[:half], lower[half:], edge_ref, 0)


def section_loads(quarter_ref, own_ref, got_ref, weights, loaded):
    quarter = quarter_ref[0]
    loads = []
    for step in range(4):
        place = pl.ds(2 * lax.rem(quarter + step, 4), 2)
        source = own_ref if step == 0 else got_ref.at[place]
        loads.append(pltpu.make_async_copy(source, weights.at[place], loaded.at[step]))
    for load in loads:
        load.start()
    return loads


def merge_forward(
    quarter_ref, fields_ref, attention_ref, halo_ref, cot_got_ref, places_ref, gain_ref,
    mlp_gain_ref, own_ref, got_ref,
    pair_ref, hidden_ref, merged_ref, grad_ref, cot_ref, weights, loaded, joined,
):
    loads = section_loads(quarter_ref, own_ref, got_ref, weights, loaded)
    width_two = merged_ref.shape[1]
    join_slabs(cot_got_ref, joined, 0, cot_got_ref.shape[1])
    cot = joined[...].astype(BF16)
    padded = merged_ref.shape[0]
    hidden = []
    for patch in range(4):
        rows = slice(padded * patch, padded * (patch + 1))
        cot_ref[patch] = picked(places_ref[rows, COT : COT + 1], cot).astype(BF16)
        attention = picked(places_ref[rows, BACK : BACK + 1], attention_ref[...])
        attention = attention + picked(
            places_ref[rows, BACK_HALO : BACK_HALO + 1], halo_ref[...]
        )
        value = fields_ref[patch].astype(F32) + attention
        hidden_ref[patch] = value.astype(BF16)
        hidden.append(value.astype(BF16).astype(F32))
    center, scale_inv = norm_stats(hidden, 4 * hidden[0].shape[1])
    merged = jnp.zeros(merged_ref.shape, F32)
    grad = jnp.zeros(merged_ref.shape, F32)
    for load in loads:
        load.wait()
    for patch in range(4):
        normed = (hidden[patch] - center) * scale_inv * gain_ref[patch : patch + 1, :]
        merged = merged + dot_nn(normed.astype(BF16), weights[patch])
        grad = grad + dot_nn(cot_ref[patch], weights[4 + patch])
    merged_ref[...] = merged.astype(BF16)
    merged = merged.astype(BF16).astype(F32)
    center, scale_inv = norm_stats([merged], width_two)
    mlp_in = (merged - center) * scale_inv * mlp_gain_ref[...]
    pair_ref[:, :width_two] = mlp_in.astype(BF16)
    pair_ref[:, width_two:] = grad.astype(BF16)
    grad_ref[...] = grad


def merge_backward(
    quarter_ref, parts_ref, merged_ref, grad_ref, hidden_ref, cot_ref, places_ref, gain_ref,
    mlp_gain_ref, own_ref, got_ref, slab_ref, out_ref, weights, loaded,
):
    loads = section_loads(quarter_ref, own_ref, got_ref, weights, loaded)
    width_two = merged_ref.shape[1]
    total = parts_ref[0].astype(F32)
    for index in range(1, parts_ref.shape[0]):
        total = total + parts_ref[index].astype(F32)
    merged = merged_ref[...].astype(F32)
    bottom = (merged + total[:, :width_two]).astype(BF16)
    for load in loads:
        load.wait()
    decoded = [
        hidden_ref[patch].astype(F32) + dot_nt(bottom, weights[4 + patch])
        for patch in range(4)
    ]
    by_row = places_ref[: slab_ref.shape[1], BY_ROW_PATCH : BY_ROW_PATCH + 1]
    upper, lower = (
        picked(by_row, jnp.concatenate([decoded[at], decoded[at + 1]], axis=0).astype(BF16))
        for at in (0, 2)
    )
    pair_slabs(upper, lower, slab_ref, 0)
    center, scale_inv = norm_stats([merged], width_two)
    unit = (merged - center) * scale_inv
    (back,) = norm_backward(
        [total[:, width_two:]], [mlp_gain_ref[...]], [unit], scale_inv, width_two
    )
    grad_merged = (grad_ref[...] + back).astype(BF16)
    hidden = [hidden_ref[patch].astype(F32) for patch in range(4)]
    center, scale_inv = norm_stats(hidden, 4 * hidden[0].shape[1])
    units = [(value - center) * scale_inv for value in hidden]
    backs = norm_backward(
        [dot_nt(grad_merged, weights[patch]) for patch in range(4)],
        [gain_ref[patch : patch + 1, :] for patch in range(4)],
        units,
        scale_inv,
        4 * hidden[0].shape[1],
    )
    grads = [(cot_ref[patch].astype(F32) + backs[patch]) for patch in range(4)]
    grads = jnp.concatenate(grads, axis=0).astype(BF16)
    tokens = out_ref.shape[0]
    out_ref[...] = picked(places_ref[:tokens, UNPATCH : UNPATCH + 1], grads).astype(BF16)


def decoded_rows(got_ref, places_ref, out_ref):
    places = places_ref[: got_ref.shape[0] * PADDED_COLUMNS, STAY : STAY + 1]
    for side in range(WIN_H):
        rows = slice(side * PADDED_COLUMNS, (side + 1) * PADDED_COLUMNS)
        values = got_ref[:, rows, :].reshape(-1, 2 * HDIM)
        both = spread_over(places, values, out_ref.shape[2])
        for index in range(2):
            out_ref[2 * side + index] = both[HDIM * index : HDIM * (index + 1)].astype(BF16)


def input_rows(shift_ref, got_ref, edge_ref, places_ref, out_ref, framed):
    places = places_ref[: got_ref.shape[0] * PADDED_COLUMNS, SHIFT : SHIFT + 1]
    for side in range(WIN_H):
        rows = slice(side * PADDED_COLUMNS, (side + 1) * PADDED_COLUMNS)
        both = spread_over(places, got_ref[:, rows, :].reshape(-1, 2 * HDIM), out_ref.shape[2])
        framed[WIN_H + side] = both[:HDIM]
        framed[2 * WIN_H + side] = both[HDIM:]
    for side in range(WIN_H // 2):
        rows = slice(side * PADDED_COLUMNS, (side + 1) * PADDED_COLUMNS)
        both = spread_over(places, edge_ref[:, rows, :].reshape(-1, 2 * HDIM), out_ref.shape[2])
        framed[side] = both[:HDIM]
        framed[WIN_H // 2 + side] = both[HDIM:]
    first = WIN_H - shift_ref[0]
    for row in range(out_ref.shape[0]):
        out_ref[row] = framed[first + row]


def shards(
    fields,
    first_gain,
    qkv_weight,
    proj_weight,
    merge_gain,
    merge_weight,
    mlp_gain,
    up_weight,
    down_weight,
    expand_weight,
    lat_shift,
    lon_shift,
    cotangent,
):
    n_lat, n_mp = lax.axis_size("lat"), lax.axis_size("mp")
    lat, core = lax.axis_index("lat"), lax.rem(lax.axis_index("lat"), 2)
    lat_offset = lat_shift[0]
    lon_offset = lon_shift[0]
    rows, lon_count, group = fields.shape
    width = group * n_mp
    block = lon_count // n_mp
    wide = block + WIN_W
    bands, columns = rows // WIN_H, block // WIN_W
    tokens = rows * block
    width_two = merge_weight.shape[2]
    span = up_weight.shape[1]
    merged_count = tokens // 4
    padded = -(-merged_count // 16) * 16
    others = range(n_mp)

    expand_turned = expand_weight.transpose(1, 2, 0)
    quarter = 2 * lax.rem(lax.div(lat, 4), 2) + core
    section = merge_weight[:2]
    for index, part in enumerate((merge_weight[2:], expand_turned[:2], expand_turned[2:])):
        section = jnp.where(quarter == index + 1, part, section)
    section_own = lax.all_gather(section, "mp", axis=1, tiled=True)

    blocks = fields.reshape(rows, n_mp, block, group).transpose(1, 0, 2, 3)
    margin = jnp.roll(blocks[:, :, :WIN_W], -1, axis=0)
    field_blocks = jnp.concatenate([blocks, margin], axis=2)
    body_slab = halves_beside(field_blocks.reshape(n_mp, rows * wide, group))
    edge_slab = halves_beside(field_blocks[:, :WIN_H].reshape(n_mp, WIN_H * wide, group))
    cot_blocks = cotangent.reshape(rows, n_mp, block, group).transpose(1, 0, 2, 3)
    cot_slab = halves_beside(cot_blocks.reshape(n_mp, tokens, group))
    weights = jnp.concatenate(
        [qkv_weight.transpose(1, 2, 0), proj_weight.transpose(1, 0)[None]], axis=0
    )
    gains = jnp.pad(jnp.concatenate([first_gain[None], merge_gain], axis=0), ((0, 3), (0, 64)))

    def rows_at(here, step):
        return pl.ds(pl.multiple_of(lax.rem(here["mp"] + n_mp - step, n_mp) * group, group), group)

    def core_half(ref, here, target):
        return ref.at[pl.ds(2 * here["core"], 2)]

    def core_half_rows(step):
        return lambda ref, here, target: ref.at[pl.ds(2 * here["core"], 2), rows_at(here, step)]

    def own_rows(ref, here, target):
        return ref.at[:, rows_at(here, 0)]

    places = place_table(lat_offset, lon_offset, rows, block, padded, n_mp)
    body_got, edge_got, weights_all, gains_all = exchange(
        1,
        [body_slab, edge_slab, weights, gains],
        [
            (body_slab.shape, BF16),
            (edge_slab.shape, BF16),
            ((4, width, width), BF16),
            ((n_mp,) + gains.shape, F32),
        ],
        [(2, core_half, 2, core_half_rows(0), 0, step) for step in range(1, n_mp)]
        + [(3, None, 3, "mp", 0, step) for step in others]
        + [(0, "mp", 0, "mp", 0, step) for step in others]
        + [(1, "mp", 1, "mp", -1, step) for step in others]
        + [(2, None, 2, own_rows, 0, 0)]
        + [
            (2, core_half_rows(step), 2, core_half_rows(step), "sibling", 0, step - 1)
            for step in range(1, n_mp)
        ],
    )
    has_shard = lax.rem(lax.axis_index("mp"), 2) == core
    first_all = gains_all[:, 0, :group].reshape(1, width)
    merge_gain_all = gains_all[:, 1:5, :group].transpose(1, 0, 2).reshape(4, width)
    mlp_gain_row = mlp_gain.reshape(1, width_two)
    cut = (jnp.int32(rows) * (n_lat - lat) - lat_offset).reshape(1)
    attention_framed, context, framed_fields, own_fields = local_kernel(
        attention_forward,
        [cut, body_got, edge_got, places, first_all, weights_all],
        [((tokens, width), BF16)] * 3 + [((4, padded, width), BF16)],
        [
            pltpu.VMEM((3, tokens, width), F32),
            pltpu.VMEM((tokens, width), F32),
            pltpu.VMEM(((rows + WIN_H) * wide, width), BF16),
        ],
        scalars=1,
    )
    window_shape = (bands, columns, WIN, width)
    around = (2 * bands + 2, WIN, width)

    def quarter_at(extra, half=None):
        def place(ref, here, target):
            at = 2 * lax.rem(here["quarter"] + extra, 4)
            return ref.at[pl.ds(at, 2)] if half is None else ref.at[at + half]

        return place

    halo, cot_got, section_got = exchange(
        2,
        [attention_framed.reshape(window_shape), cot_slab, section_own],
        [(around, BF16), (cot_slab.shape, BF16), ((8, width, width_two), BF16)],
        [
            (2, (0,), 2, quarter_at(0, 0), 4, 0),
            (2, (1,), 2, quarter_at(0, 1), -4, 0),
            (0, (bands - 1, columns - 1), 0, (0,), 1, 1),
            (0, (slice(0, bands), columns - 1), 0, (slice(1, 1 + bands),), 0, 1),
            (0, (bands - 1,), 0, (slice(1 + bands, 1 + bands + columns),), 1, 0),
        ]
        + [(1, "mp", 1, "mp", 0, step) for step in others]
        + [
            (2, None, 2, quarter_at(0), "sibling", 0),
            (2, quarter_at(2, 0), 2, quarter_at(2, 0), "sibling", 0, 0),
            (2, quarter_at(2, 1), 2, quarter_at(2, 1), "sibling", 0, 1),
        ],
    )
    n_x = n_mp // 2
    section_scratch = [
        pltpu.VMEM(section_got.shape, BF16),
        pltpu.SemaphoreType.DMA((4,)),
    ]
    pair, hidden, merged, grad_bottom, cot_patches = local_kernel(
        merge_forward,
        [
            quarter.reshape(1),
            own_fields,
            attention_framed,
            halo.reshape(-1, width),
            cot_got,
            places,
            merge_gain_all,
            mlp_gain_row,
            section_own,
            section_got,
        ],
        [
            ((padded, 2 * width_two), BF16),
            ((4, padded, width), BF16),
            ((padded, width_two), BF16),
            ((padded, width_two), F32),
            ((4, padded, width), BF16),
        ],
        section_scratch + [pltpu.VMEM((tokens, width), F32)],
        scalars=1,
        outside=2,
    )

    def chip_spot(step):
        def spot(ref, here, target):
            return ref.at[lax.rem(here["x"] + n_x + step, n_x), here["core"]]

        return spot

    pairs, up_other, down_other = exchange(
        3,
        [pair, up_weight, down_weight],
        [
            ((n_x, 2) + pair.shape, BF16),
            (up_weight.shape, BF16),
            (down_weight.shape, BF16),
        ],
        [
            (0, None, 0, chip_spot(0), 0, 4),
            (0, None, 0, chip_spot(0), 0, 2),
            (0, None, 0, chip_spot(0), 0, -2),
            (0, None, 0, chip_spot(0), "sibling", 0),
            (0, None, 0, chip_spot(0), 0, 0),
            (1, None, 1, None, "flip", 0),
            (2, None, 2, None, "flip", 0),
            (0, chip_spot(-1), 0, chip_spot(-1), "sibling", 0, 1),
            (0, chip_spot(1), 0, chip_spot(1), "sibling", 0, 2),
            (0, chip_spot(-2), 0, chip_spot(-2), "sibling", 0, 0),
        ],
    )
    up_shard = jnp.where(has_shard, up_weight, up_other)
    down_shard = jnp.where(has_shard, down_weight, down_other)
    pairs = pairs.reshape(n_mp * padded, 2 * width_two)
    mlp_in, bottom_grad = pairs[:, :width_two], pairs[:, width_two:]
    hidden_up = jnp.dot(mlp_in, up_shard, preferred_element_type=F32)
    activated = jax.nn.gelu(hidden_up).astype(BF16)
    grad_act = jnp.dot(bottom_grad, down_shard, preferred_element_type=F32)
    gelu_back = jax.vjp(jax.nn.gelu, hidden_up)[1]
    grad_pre = gelu_back(grad_act)[0].astype(BF16)
    terms = jnp.concatenate(
        [
            jnp.einsum("af,ef->ae", activated, down_shard, preferred_element_type=F32),
            jnp.einsum("af,ef->ae", grad_pre, up_shard, preferred_element_type=F32),
        ],
        axis=1,
    ).astype(BF16)
    large = (n_lat, width_two // n_lat, span)
    parts, up_got = terms_back(
        4,
        terms.reshape(n_x, 2, padded, 2 * width_two),
        jnp.einsum("ae,af->ef", mlp_in, grad_pre, preferred_element_type=F32)
        .astype(BF16)
        .reshape(large),
    )
    down_local = jnp.einsum("ao,af->of", bottom_grad, activated, preferred_element_type=F32)
    row_slab = (n_mp, WIN_H * PADDED_COLUMNS, 2 * group)
    decoded_slab, grad_windows = local_kernel(
        merge_backward,
        [
            quarter.reshape(1),
            parts,
            merged,
            grad_bottom,
            hidden,
            cot_patches,
            places,
            merge_gain_all,
            mlp_gain_row,
            section_own,
            section_got,
        ],
        [(row_slab, BF16), ((tokens, width), BF16)],
        section_scratch,
        scalars=1,
        outside=2,
    )
    halo, decoded_got, down_got = exchange(
        5,
        [
            grad_windows.reshape(window_shape),
            decoded_slab,
            down_local.astype(BF16).reshape(large),
        ],
        [(around, BF16), (decoded_slab.shape, BF16), (large, BF16)],
        [
            (0, (0, 0), 0, (0,), -1, -1),
            (0, (slice(0, bands), 0), 0, (slice(1, 1 + bands),), 0, -1),
            (0, (0,), 0, (slice(1 + bands, 1 + bands + columns),), -1, 0),
        ]
        + [(1, "mp", 1, "mp", 0, step) for step in others],
        owned=((2, 2),),
    )
    grad_up = jnp.sum(up_got.astype(F32), axis=0)
    grad_down = jnp.sum(down_got.astype(F32), axis=0)
    grad_slab, grad_edge, weight_grads = local_kernel(
        attention_backward,
        [
            cut,
            framed_fields,
            first_all,
            weights_all,
            context,
            grad_windows,
            halo.reshape(-1, width),
            places,
        ],
        [
            (row_slab, BF16),
            ((n_mp, WIN_H * PADDED_COLUMNS // 2, 2 * group), BF16),
            ((4, width, width), BF16),
        ],
        [
            pltpu.VMEM((3, tokens, width), F32),
            pltpu.VMEM((3, tokens, width), F32),
            pltpu.VMEM((tokens, width), F32),
        ],
        scalars=1,
    )
    weight_total, grad_got, edge_got = gradients_out(6, weight_grads, grad_slab, grad_edge)
    grad_qkv = weight_total[:, : 3 * group].reshape(width // n_lat, 3, group)
    grad_proj = weight_total[:, 3 * group :]
    (decoded,) = local_kernel(
        decoded_rows, [decoded_got, places], [((rows, group, lon_count), BF16)]
    )
    (grad_input,) = local_kernel(
        input_rows,
        [lat_shift, grad_got, edge_got, places],
        [((rows, group, lon_count), F32)],
        [pltpu.VMEM((rows + WIN_H, group, lon_count), F32)],
        scalars=1,
    )
    decoded, grad_input = decoded.transpose(0, 2, 1), grad_input.transpose(0, 2, 1)
    return (decoded, grad_input, grad_qkv, grad_proj, grad_up, grad_down)


def solution(mesh):
    return jax.shard_map(
        shards,
        mesh=mesh,
        in_specs=(
            P("lat", None, "mp"),
            P("mp"),
            P(None, None, "mp"),
            P(None, "mp"),
            P(None, "mp"),
            P(None, "mp", None),
            P(),
            P(None, "mp"),
            P(None, "mp"),
            P(None, None, "mp"),
            P(),
            P(),
            P("lat", None, "mp"),
        ),
        out_specs=(
            P("lat", None, "mp"),
            P("lat", None, "mp"),
            P("lat", None, "mp"),
            P("lat", "mp"),
            P("lat", "mp"),
            P("lat", "mp"),
        ),
        check_vma=False,
    )
```

```python
import jax
import jax.numpy as jnp
import numpy as np
from jax import lax
from jax.experimental import pallas as pl
from jax.experimental.pallas import tpu as pltpu
from jax.sharding import PartitionSpec as P

WIN_H = 6
WIN_W = 12
HDIM = 64
EPSILON = 1e-05
MASKED = -1e30
BF16 = jnp.bfloat16
F32 = jnp.float32


def positions():
    lat, mp = lax.axis_index("lat"), lax.axis_index("mp")
    return {
        "lat": lat,
        "mp": mp,
        "core": lax.rem(lat, 2),
        "x": lax.div(mp, 2),
        "z": lax.rem(mp, 2),
        "quarter": 2 * lax.rem(lax.div(lat, 4), 2) + lax.rem(lat, 2),
    }


def reached(here, down, right):
    n_lat, n_mp = lax.axis_size("lat"), lax.axis_size("mp")
    if down == "sibling":
        return {"lat": here["lat"] + 1 - 2 * here["core"], "mp": here["mp"]}
    if down == "flip":
        return {"lat": here["lat"], "mp": 2 * here["x"] + 1 - here["z"]}
    return {
        "lat": lax.rem(here["lat"] + n_lat + down, n_lat),
        "mp": lax.rem(here["mp"] + n_mp + right, n_mp),
    }


def device_of(target):
    return {
        "device_id": (target["lat"], target["mp"]),
        "device_id_type": pl.DeviceIdType.MESH,
    }


def greet(here, steps, owned=False):
    barrier = pltpu.get_barrier_semaphore()
    count = len(steps)
    if owned:
        n_lat, x, z = lax.axis_size("lat"), here["x"], here["z"]
        owner = z == here["core"]
        mine = 2 * lax.div(here["lat"], 2) + z
        count = count + n_lat - jnp.where(owner, 1, 0)
        for source in range(n_lat):

            @pl.when(jnp.logical_or(jnp.logical_not(owner), mine != source))
            def _():
                target = {"lat": 2 * (source // 2) + z, "mp": 2 * x + source % 2}
                pl.semaphore_signal(barrier, inc=1, **device_of(target))

    for down, right in steps:
        source = reached(here, down if isinstance(down, str) else -down, -right)
        pl.semaphore_signal(barrier, inc=1, **device_of(source))
    pl.semaphore_wait(barrier, count)


def to_owners(here, source, landing, send, receive):
    n_lat = lax.axis_size("lat")
    lat, core, x, z = here["lat"], here["core"], here["x"], here["z"]
    mine = 2 * lax.div(lat, 2) + z
    owner = z == core

    def copy_at(step):
        target = {"lat": lax.rem(lat + step, n_lat), "mp": 2 * x + core}
        rows = target["lat"]
        return remote(source.at[rows], landing.at[mine], send.at[step], receive.at[mine], target)

    def start():
        for step in range(1, n_lat):
            copy_at(step).start()

        @pl.when(owner)
        def _():
            pltpu.make_async_copy(source.at[lat], landing.at[mine], receive.at[mine]).start()

        @pl.when(jnp.logical_not(owner))
        def _():
            copy_at(0).start()

    def wait():
        sibling = reached(here, "sibling", 0)
        for slot in range(n_lat):
            remote(
                source.at[slot], landing.at[slot], send.at[slot], receive.at[slot], sibling
            ).wait_recv()
        for step in range(1, n_lat):
            copy_at(step).wait_send()

        @pl.when(jnp.logical_not(owner))
        def _():
            copy_at(0).wait_send()

    return start, wait


def remote(source, landing, send, receive, target):
    return pltpu.make_async_remote_copy(
        src_ref=source, dst_ref=landing, send_sem=send, recv_sem=receive, **device_of(target)
    )


def exchange(collective, inputs, outputs, moves, owned=()):
    n_lat = lax.axis_size("lat")
    steps = []
    for move in moves:
        if move[4:6] != (0, 0) and move[4:6] not in steps:
            steps.append(move[4:6])

    def body(*refs):
        sources = refs[: len(inputs)]
        landings = refs[len(inputs) : len(inputs) + len(outputs)]
        send, receive, owned_send, owned_receive = refs[-4:]
        here = positions()

        def part_of(ref, part, place, target):
            if part is None:
                return ref
            if isinstance(part, str):
                return ref.at[place[part]]
            if callable(part):
                return part(ref, here, target)
            return ref.at[part]

        greet(here, steps, bool(owned))
        copies = []
        arrived = set()
        scatters = [
            to_owners(
                here, sources[one], landings[two], owned_send.at[index], owned_receive.at[index]
            )
            for index, (one, two) in enumerate(owned)
        ]
        for index, move in enumerate(moves):
            source, source_part, landing, landing_part, down, right = move[:6]
            target = reached(here, down, right)
            if len(move) > 6:
                if move[6] not in arrived:
                    copies[move[6]].wait_recv()
                    arrived.add(move[6])
                source_ref = part_of(landings[source], source_part, target, target)
            else:
                source_ref = part_of(sources[source], source_part, target, target)
            landing_ref = part_of(landings[landing], landing_part, here, target)
            if (down, right) == (0, 0):
                copy = pltpu.make_async_copy(source_ref, landing_ref, receive.at[index])
            else:
                copy = remote(
                    source_ref, landing_ref, send.at[index], receive.at[index], target
                )
            if down == "flip":
                pl.when(here["z"] == here["core"])(copy.start)
            else:
                copy.start()
            copies.append(copy)
        for start, _ in scatters:
            start()
        for _, wait in scatters:
            wait()
        for index, copy in enumerate(copies):
            if moves[index][4:6] == (0, 0):
                copy.wait()
            elif moves[index][4] == "flip":
                pl.when(here["z"] == here["core"])(copy.wait_send)
                pl.when(here["z"] != here["core"])(copy.wait_recv)
            else:
                copy.wait_send()
                if index not in arrived:
                    copy.wait_recv()

    return pl.pallas_call(
        body,
        out_shape=[jax.ShapeDtypeStruct(shape, dtype) for shape, dtype in outputs],
        in_specs=[pl.BlockSpec(memory_space=pl.ANY)] * len(inputs),
        out_specs=[pl.BlockSpec(memory_space=pl.ANY)] * len(outputs),
        scratch_shapes=[
            pltpu.SemaphoreType.DMA((len(moves),)),
            pltpu.SemaphoreType.DMA((len(moves),)),
            pltpu.SemaphoreType.DMA((max(len(owned), 1), n_lat)),
            pltpu.SemaphoreType.DMA((max(len(owned), 1), n_lat)),
        ],
        compiler_params=pltpu.CompilerParams(collective_id=collective, has_side_effects=True),
    )(*inputs)


X_STEPS = ((4, 2), (2, 1), (-2, 3))


def terms_back(collective, terms, up_grads, down_grads):
    count, _, rows, width = terms.shape
    n_lat = lax.axis_size("lat")

    def body(
        terms_ref, up_ref, down_ref, parts_ref, up_got, down_got,
        other, own, total, send, receive, fetch, large_send, large_receive,
    ):
        here = positions()
        core, x = here["core"], here["x"]
        sibling = reached(here, "sibling", 0)
        greet(here, [("sibling", 0)] + [(0, right) for right, _ in X_STEPS], True)
        scatters = [
            to_owners(here, source, landing, large_send.at[index], large_receive.at[index])
            for index, (source, landing) in enumerate(((up_ref, up_got), (down_ref, down_got)))
        ]
        order = [lax.rem(x + step, count) for _, step in X_STEPS] + [x]
        swaps, loads = [], []
        for index, spot in enumerate(order):
            swap = remote(
                terms_ref.at[spot, 1 - core],
                other.at[index],
                send.at[index],
                receive.at[index],
                sibling,
            )
            load = pltpu.make_async_copy(terms_ref.at[spot, core], own.at[index], fetch.at[index])
            swap.start()
            load.start()
            swaps.append(swap)
            loads.append(load)
        for start, _ in scatters:
            start()
        sends = []
        for index, spot in enumerate(order):
            loads[index].wait()
            swaps[index].wait_recv()
            total[index] = (own[index].astype(F32) + other[index].astype(F32)).astype(BF16)
            if index < len(X_STEPS):
                copy = remote(
                    total.at[index],
                    parts_ref.at[x],
                    send.at[count + index],
                    receive.at[count + index],
                    reached(here, 0, X_STEPS[index][0]),
                )
            else:
                copy = pltpu.make_async_copy(total.at[index], parts_ref.at[x], fetch.at[count])
            copy.start()
            sends.append(copy)
        for swap in swaps:
            swap.wait_send()
        for copy in sends:
            copy.wait()
        for _, wait in scatters:
            wait()

    return pl.pallas_call(
        body,
        out_shape=[
            jax.ShapeDtypeStruct((count, rows, width), BF16),
            jax.ShapeDtypeStruct(up_grads.shape, BF16),
            jax.ShapeDtypeStruct(down_grads.shape, BF16),
        ],
        in_specs=[pl.BlockSpec(memory_space=pl.ANY)] * 3,
        out_specs=[pl.BlockSpec(memory_space=pl.ANY)] * 3,
        scratch_shapes=[
            pltpu.VMEM((count, rows, width), BF16),
            pltpu.VMEM((count, rows, width), BF16),
            pltpu.VMEM((count, rows, width), BF16),
            pltpu.SemaphoreType.DMA((2 * count,)),
            pltpu.SemaphoreType.DMA((2 * count,)),
            pltpu.SemaphoreType.DMA((count + 1,)),
            pltpu.SemaphoreType.DMA((2, n_lat)),
            pltpu.SemaphoreType.DMA((2, n_lat)),
        ],
        compiler_params=pltpu.CompilerParams(
            collective_id=collective, has_side_effects=True, vmem_limit_bytes=48 * 1024 * 1024
        ),
    )(terms, up_grads, down_grads)


def gradients_out(collective, weight_grads, slabs, edges):
    n_lat, n_mp = lax.axis_size("lat"), lax.axis_size("mp")
    kinds, width, _ = weight_grads.shape
    pair, group, share = kinds // 2, width // n_mp, width // n_lat

    def body(
        weight_ref, slab_ref, edge_ref, out_ref, got_ref, edge_got,
        other, total, parts, turned, landed, send, receive,
    ):
        here = positions()
        lat, mp, core = here["lat"], here["mp"], here["core"]
        sibling = reached(here, "sibling", 0)
        barrier = pltpu.get_barrier_semaphore()
        greeted = [sibling]
        greeted += [reached(here, 0, -step) for step in range(1, n_mp)]
        greeted += [reached(here, -1, -step) for step in range(n_mp)]
        greeted += [reached(here, -step, 0) for step in range(1, n_lat)]
        for target in greeted:
            pl.semaphore_signal(barrier, inc=1, **device_of(target))
        pl.semaphore_wait(barrier, len(greeted))

        copies = []

        def sent(source, landing, target):
            index = len(copies)
            copy = remote(source, landing, send.at[index], receive.at[index], target)
            copy.start()
            copies.append(copy)
            return copy

        swap = sent(weight_ref.at[pl.ds(pair * (1 - core), pair)], other, sibling)
        own_slab = pltpu.make_async_copy(slab_ref.at[mp], got_ref.at[mp], send.at[60])
        own_slab.start()

        swap.wait_recv()
        total[...] = (
            weight_ref[pl.ds(pair * core, pair)].astype(F32) + other[...].astype(F32)
        ).astype(BF16)
        scattered = []
        for step in range(1, n_mp):
            target = reached(here, 0, step)
            rows = pl.ds(pl.multiple_of(group * target["mp"], group), group)
            scattered.append(sent(total.at[:, rows], parts.at[mp], target))
        for step in range(1, n_mp):
            target = reached(here, 0, step)
            sent(slab_ref.at[target["mp"]], got_ref.at[mp], target)
        for step in range(n_mp):
            target = reached(here, 1, step)
            sent(edge_ref.at[target["mp"]], edge_got.at[mp], target)
        gathered = total[:, pl.ds(pl.multiple_of(group * mp, group), group), :].astype(F32)
        for step in range(1, n_mp):
            scattered[step - 1].wait_recv()
            gathered = gathered + parts[lax.rem(mp + n_mp - step, n_mp)].astype(F32)
        flat = gathered.reshape(pair * group, width).T.astype(BF16)
        for index in range(n_lat):
            turned[index] = flat[index * share : (index + 1) * share]
        spread = []
        for step in range(1, n_lat):
            target = reached(here, step, 0)
            spread.append(sent(turned.at[target["lat"]], landed.at[lat], target))
        landed[lat] = turned[lat]
        for copy in spread:
            copy.wait_recv()
        for half in range(2):
            result = landed[half].astype(F32)
            for index in range(half + 2, n_lat, 2):
                result = result + landed[index].astype(F32)
            out_ref[:, half * pair * group : (half + 1) * pair * group] = result

        done = [swap] + scattered + spread
        for copy in copies:
            copy.wait_send()
            if not any(copy is other_copy for other_copy in done):
                copy.wait_recv()
        own_slab.wait()

    any_space = pl.BlockSpec(memory_space=pl.ANY)
    vmem = pl.BlockSpec(memory_space=pltpu.VMEM)
    return pl.pallas_call(
        body,
        out_shape=[
            jax.ShapeDtypeStruct((share, kinds * group), F32),
            jax.ShapeDtypeStruct(slabs.shape, BF16),
            jax.ShapeDtypeStruct(edges.shape, BF16),
        ],
        in_specs=[vmem, any_space, any_space],
        out_specs=[vmem, any_space, any_space],
        scratch_shapes=[
            pltpu.VMEM((pair, width, width), BF16),
            pltpu.VMEM((pair, width, width), BF16),
            pltpu.VMEM((n_mp, pair, group, width), BF16),
            pltpu.VMEM((n_lat, share, pair * group), BF16),
            pltpu.VMEM((n_lat, share, pair * group), BF16),
            pltpu.SemaphoreType.DMA((64,)),
            pltpu.SemaphoreType.DMA((64,)),
        ],
        compiler_params=pltpu.CompilerParams(
            collective_id=collective, has_side_effects=True, vmem_limit_bytes=48 * 1024 * 1024
        ),
    )(weight_grads, slabs, edges)


def local_kernel(body, operands, outputs, scratch=(), scalars=0, outside=0):
    spaces = [pltpu.SMEM] * scalars + [pltpu.VMEM] * (len(operands) - scalars - outside)
    spaces += [pl.ANY] * outside
    return pl.pallas_call(
        body,
        out_shape=[jax.ShapeDtypeStruct(shape, dtype) for shape, dtype in outputs],
        in_specs=[pl.BlockSpec(memory_space=space) for space in spaces],
        out_specs=[pl.BlockSpec(memory_space=pltpu.VMEM)] * len(outputs),
        scratch_shapes=list(scratch),
        compiler_params=pltpu.CompilerParams(vmem_limit_bytes=48 * 1024 * 1024),
    )(*operands)


def dot_nn(left, right):
    return lax.dot_general(left, right, (((1,), (0,)), ((), ())), preferred_element_type=F32)


def dot_nt(left, right):
    return lax.dot_general(left, right, (((1,), (1,)), ((), ())), preferred_element_type=F32)


def dot_tn(left, right):
    return lax.dot_general(left, right, (((0,), (0,)), ((), ())), preferred_element_type=F32)


def halves_beside(values):
    half = values.shape[-2] // 2
    return jnp.concatenate([values[..., :half, :], values[..., half:, :]], axis=-1)


def picked(places, values):
    spots = lax.broadcasted_iota(jnp.int32, (places.shape[0], values.shape[0]), 1)
    return dot_nn(jnp.where(spots == places, 1.0, 0.0).astype(BF16), values)


def spread_over(places, values, count):
    spots = lax.broadcasted_iota(jnp.int32, (places.shape[0], count), 1)
    return dot_tn(values, jnp.where(spots == places, 1.0, 0.0).astype(BF16))


def swapped(values):
    return jnp.concatenate([values[:, HDIM:], values[:, :HDIM]], axis=1)


def join_slabs(slab_ref, out_ref, first_rows, second_rows):
    half = slab_ref.shape[1]
    low = lax.broadcasted_iota(jnp.int32, (half, 2 * HDIM), 1) < HDIM
    for pair in range(slab_ref.shape[0] // 2):
        lanes = slice(2 * HDIM * pair, 2 * HDIM * (pair + 1))
        one = slab_ref[2 * pair].astype(F32)
        two = slab_ref[2 * pair + 1].astype(F32)
        first = jnp.where(low, one, swapped(two)).astype(out_ref.dtype)
        second = jnp.where(low, swapped(one), two).astype(out_ref.dtype)
        out_ref[first_rows : first_rows + half, lanes] = first
        out_ref[second_rows : second_rows + half, lanes] = second


PADDED_COLUMNS = 48
FRAME, OWN, BACK, BACK_HALO, COT, UNPATCH, GRAD, GRAD_HALO, BY_ROW, BY_ROW_PATCH, SHIFT, STAY = range(12)


def place_table(lat_offset, lon_offset, rows, block, padded, n_mp):
    columns = block // WIN_W
    size = max(rows * block, 4 * padded, n_mp * PADDED_COLUMNS)

    def window_place(row, column):
        window = (row // WIN_H) * columns + column // WIN_W
        return window * WIN + (row % WIN_H) * WIN_W + column % WIN_W

    token = np.arange(rows * block)
    window, spot = token // WIN, token % WIN
    row = (window // columns) * WIN_H + spot // WIN_W
    column = (window % columns) * WIN_W + spot % WIN_W
    patch, at = np.arange(4 * padded) // padded, np.arange(4 * padded) % padded
    real = at < rows * block // 4
    prow = np.where(real, 2 * (at // (block // 2)) + patch // 2, 0)
    pcolumn = np.where(real, 2 * (at % (block // 2)) + patch % 2, 0)
    side, spot = np.arange(WIN_H * PADDED_COLUMNS) // PADDED_COLUMNS, np.arange(WIN_H * PADDED_COLUMNS) % PADDED_COLUMNS
    shown = spot < block
    spot = np.where(shown, spot, 0)
    group = np.arange(n_mp * PADDED_COLUMNS) // PADDED_COLUMNS
    place = np.arange(n_mp * PADDED_COLUMNS) % PADDED_COLUMNS
    inside = place < block
    lon = group * block + place

    def halo(down, right, row, column):
        corner = row % WIN_H * WIN_W + column % WIN_W
        slot = jnp.where(
            down,
            jnp.where(right, 0, 3 + column // WIN_W),
            1 + row // WIN_H,
        )
        return jnp.where(jnp.logical_or(down, right), slot * WIN + corner, -1)

    wide = block + WIN_W
    back_row, back_column = prow - lat_offset, pcolumn - lon_offset
    above, left = back_row < 0, back_column < 0
    grad_row, grad_column = row + lat_offset, column + lon_offset
    below, right = grad_row >= rows, grad_column >= block
    table = {
        FRAME: (row + lat_offset) * wide + column + lon_offset,
        OWN: np.where(real, prow * wide + pcolumn, -1),
        BACK: jnp.where(
            jnp.logical_and(real, jnp.logical_not(jnp.logical_or(above, left))),
            window_place(back_row, back_column),
            -1,
        ),
        BACK_HALO: jnp.where(
            real,
            halo(
                above,
                left,
                jnp.where(above, back_row + WIN_H, back_row),
                jnp.where(left, back_column + WIN_W, back_column),
            ),
            -1,
        ),
        COT: np.where(real, prow * block + pcolumn, -1),
        UNPATCH: (2 * (row % 2) + column % 2) * padded + (row // 2) * (block // 2) + column // 2,
        GRAD: jnp.where(
            jnp.logical_or(below, right), -1, window_place(grad_row, grad_column)
        ),
        GRAD_HALO: halo(
            below,
            right,
            jnp.where(below, grad_row - rows, grad_row),
            jnp.where(right, grad_column - block, grad_column),
        ),
        BY_ROW: np.where(shown, (spot // WIN_W) * WIN + side * WIN_W + spot % WIN_W, -1),
        BY_ROW_PATCH: np.where(
            shown, (spot % 2) * padded + side * (block // 2) + spot // 2, -1
        ),
        SHIFT: jnp.where(inside, (lon + lon_offset) % (n_mp * block), -1),
        STAY: np.where(inside, lon, -1),
    }
    columns_list = [
        jnp.pad(jnp.asarray(table[key], jnp.int32), (0, size - table[key].shape[0]))
        for key in range(len(table))
    ]
    return jnp.stack(columns_list, axis=1)


def norm_stats(values, count):
    center = sum(jnp.sum(value, axis=1, keepdims=True) for value in values) / count
    second = sum(jnp.sum(value * value, axis=1, keepdims=True) for value in values) / count
    return (center, lax.rsqrt(second - center * center + EPSILON))


def norm_backward(grads, gains, units, scale_inv, count):
    scaled = [grad * gain for grad, gain in zip(grads, gains)]
    first = sum(jnp.sum(value, axis=1, keepdims=True) for value in scaled) / count
    second = (
        sum(jnp.sum(value * unit, axis=1, keepdims=True) for value, unit in zip(scaled, units))
        / count
    )
    return [scale_inv * (value - first - unit * second) for value, unit in zip(scaled, units)]


def pair_slabs(upper, lower, out_ref, first_rows):
    low = lax.broadcasted_iota(jnp.int32, (upper.shape[0], 2 * HDIM), 1) < HDIM
    rows = pl.ds(first_rows, upper.shape[0])
    for pair in range(upper.shape[1] // (2 * HDIM)):
        lanes = slice(2 * HDIM * pair, 2 * HDIM * (pair + 1))
        one, two = upper[:, lanes], lower[:, lanes]
        out_ref[2 * pair, rows, :] = jnp.where(low, one, swapped(two)).astype(BF16)
        out_ref[2 * pair + 1, rows, :] = jnp.where(low, swapped(one), two).astype(BF16)


WIN = WIN_H * WIN_W
FACTOR = HDIM ** (-0.5)


def heads_apart(values):
    low = lax.broadcasted_iota(jnp.int32, values.shape, 1) < HDIM
    zero = jnp.zeros_like(values)
    both = [jnp.where(low, values, zero), jnp.where(low, zero, values)]
    return jnp.concatenate(both, axis=0).astype(BF16)


def heads_together(values):
    low = lax.broadcasted_iota(jnp.int32, (WIN, 2 * HDIM), 1) < HDIM
    return jnp.where(low, values[:WIN], values[WIN:])


def window_probs(cut, window, query, keys):
    scores = dot_nt(query, keys) * FACTOR
    spot = lax.broadcasted_iota(jnp.int32, scores.shape, 0)
    spot = jnp.where(spot >= WIN, spot - WIN, spot)
    other = lax.broadcasted_iota(jnp.int32, scores.shape, 1)
    edge = cut * WIN_W - jnp.where(window >= 3, WIN, 0)
    same = (spot >= edge) == (other >= edge)
    scores = jnp.where(same, scores, MASKED)
    weights = jnp.exp(scores - jnp.max(scores, axis=1, keepdims=True))
    return weights / jnp.sum(weights, axis=1, keepdims=True)


def framed_packed(fields_ref, gain_ref, weights_ref, packed):
    values = fields_ref[...].astype(F32)
    center, scale_inv = norm_stats([values], values.shape[1])
    unit = (values - center) * scale_inv
    framed = (unit * gain_ref[...]).astype(BF16)
    for kind in range(3):
        packed[kind] = dot_nt(framed, weights_ref[kind]).astype(BF16).astype(F32)
    return (framed, unit, scale_inv)


def window_parts(refs, window, pair):
    rows = pl.ds(pl.multiple_of(window * WIN, 8), WIN)
    lanes = slice(2 * HDIM * pair, 2 * HDIM * (pair + 1))
    return [ref[rows, lanes] for ref in refs]


def attention_forward(
    cut_ref, body_ref, edge_ref, places_ref, gain_ref, weights_ref,
    out_ref, context_ref, fields_ref, own_ref, packed, held, grid,
):
    half, rest = body_ref.shape[1], edge_ref.shape[1]
    join_slabs(body_ref, grid, 0, half)
    join_slabs(edge_ref, grid, 2 * half, 2 * half + rest)
    tokens = fields_ref.shape[0]
    whole = grid[...]
    fields_ref[...] = picked(places_ref[:tokens, FRAME : FRAME + 1], whole).astype(BF16)
    padded = own_ref.shape[1]
    for patch in range(4):
        rows = slice(padded * patch, padded * (patch + 1))
        own_ref[patch] = picked(places_ref[rows, OWN : OWN + 1], whole).astype(BF16)
    framed_packed(fields_ref, gain_ref, weights_ref, packed)
    cut = cut_ref[0]
    windows = fields_ref.shape[0] // WIN

    def step(window, carry):
        rows = pl.ds(pl.multiple_of(window * WIN, 8), WIN)
        for pair in range(fields_ref.shape[1] // (2 * HDIM)):
            query, keys, values = window_parts([packed.at[kind] for kind in range(3)], window, pair)
            probs = window_probs(cut, window, heads_apart(query), keys.astype(BF16))
            joined = dot_nn(probs.astype(BF16), values.astype(BF16))
            held[rows, 2 * HDIM * pair : 2 * HDIM * (pair + 1)] = heads_together(joined)
        return carry

    lax.fori_loop(0, windows, step, 0)
    context = held[...].astype(BF16)
    context_ref[...] = context
    out_ref[...] = dot_nn(context, weights_ref[3]).astype(BF16)


def attention_backward(
    cut_ref, fields_ref, gain_ref, weights_ref, context_ref, grad_ref, halo_ref, places_ref,
    slab_ref, edge_ref, weight_ref, packed, grads, held,
):
    framed, unit, scale_inv = framed_packed(fields_ref, gain_ref, weights_ref, packed)
    cut = cut_ref[0]
    windows = fields_ref.shape[0] // WIN
    tokens = fields_ref.shape[0]
    grad_framed = (
        picked(places_ref[:tokens, GRAD : GRAD + 1], grad_ref[...])
        + picked(places_ref[:tokens, GRAD_HALO : GRAD_HALO + 1], halo_ref[...])
    ).astype(BF16)
    held[...] = dot_nt(grad_framed, weights_ref[3]).astype(BF16).astype(F32)

    def step(window, carry):
        rows = pl.ds(pl.multiple_of(window * WIN, 8), WIN)
        for pair in range(fields_ref.shape[1] // (2 * HDIM)):
            lanes = slice(2 * HDIM * pair, 2 * HDIM * (pair + 1))
            query, keys, values, grad = window_parts(
                [packed.at[kind] for kind in range(3)] + [held], window, pair
            )
            query, grad = heads_apart(query), heads_apart(grad)
            keys, values = keys.astype(BF16), values.astype(BF16)
            probs = window_probs(cut, window, query, keys)
            grad_probs = dot_nt(grad, values)
            inner = jnp.sum(grad_probs * probs, axis=1, keepdims=True)
            grad_scores = (probs * (grad_probs - inner) * FACTOR).astype(BF16)
            grads[0, rows, lanes] = heads_together(dot_nn(grad_scores, keys))
            grads[1, rows, lanes] = dot_tn(grad_scores, query)
            grads[2, rows, lanes] = dot_tn(probs.astype(BF16), grad)
        return carry

    lax.fori_loop(0, windows, step, 0)
    grad_normed = jnp.zeros(fields_ref.shape, F32)
    for kind in range(3):
        grad_kind = grads[kind].astype(BF16)
        weight_ref[kind] = dot_tn(grad_kind, framed).astype(BF16)
        grad_normed = grad_normed + dot_nn(grad_kind, weights_ref[kind])
    weight_ref[3] = dot_tn(context_ref[...], grad_framed).astype(BF16)
    (back,) = norm_backward([grad_normed], [gain_ref[...]], [unit], scale_inv, unit.shape[1])
    result = grad_framed.astype(F32) + back
    half = result.shape[0] // 2
    by_row = places_ref[: slab_ref.shape[1], BY_ROW : BY_ROW + 1]
    upper, lower = (picked(by_row, part.astype(BF16)) for part in (result[:half], result[half:]))
    pair_slabs(upper, lower, slab_ref, 0)
    half = edge_ref.shape[1]
    pair_slabs(lower[:half], lower[half:], edge_ref, 0)


def section_load(place_ref, own_ref, got_ref, weights, loaded):
    whole = pltpu.make_async_copy(got_ref, weights, loaded.at[0])
    whole.start()

    def wait():
        whole.wait()
        count = own_ref.shape[1]
        rows = pl.ds(pl.multiple_of(place_ref[0] * count, count), count)
        own = pltpu.make_async_copy(own_ref, weights.at[:, rows], loaded.at[1])
        own.start()
        own.wait()

    return wait


def merge_forward(
    place_ref, fields_ref, attention_ref, halo_ref, cot_got_ref, places_ref, gain_ref,
    mlp_gain_ref, own_ref, got_ref,
    pair_ref, hidden_ref, merged_ref, grad_ref, cot_ref, weights, loaded, joined,
):
    wait = section_load(place_ref, own_ref, got_ref, weights, loaded)
    width_two = merged_ref.shape[1]
    join_slabs(cot_got_ref, joined, 0, cot_got_ref.shape[1])
    cot = joined[...].astype(BF16)
    padded = merged_ref.shape[0]
    hidden = []
    for patch in range(4):
        rows = slice(padded * patch, padded * (patch + 1))
        cot_ref[patch] = picked(places_ref[rows, COT : COT + 1], cot).astype(BF16)
        attention = picked(places_ref[rows, BACK : BACK + 1], attention_ref[...])
        attention = attention + picked(
            places_ref[rows, BACK_HALO : BACK_HALO + 1], halo_ref[...]
        )
        value = fields_ref[patch].astype(F32) + attention
        hidden_ref[patch] = value.astype(BF16)
        hidden.append(value.astype(BF16).astype(F32))
    center, scale_inv = norm_stats(hidden, 4 * hidden[0].shape[1])
    merged = jnp.zeros(merged_ref.shape, F32)
    grad = jnp.zeros(merged_ref.shape, F32)
    wait()
    for patch in range(4):
        normed = (hidden[patch] - center) * scale_inv * gain_ref[patch : patch + 1, :]
        merged = merged + dot_nn(normed.astype(BF16), weights[patch])
        grad = grad + dot_nn(cot_ref[patch], weights[4 + patch])
    merged_ref[...] = merged.astype(BF16)
    merged = merged.astype(BF16).astype(F32)
    center, scale_inv = norm_stats([merged], width_two)
    mlp_in = (merged - center) * scale_inv * mlp_gain_ref[...]
    pair_ref[:, :width_two] = mlp_in.astype(BF16)
    pair_ref[:, width_two:] = grad.astype(BF16)
    grad_ref[...] = grad


def merge_backward(
    place_ref, parts_ref, merged_ref, grad_ref, hidden_ref, cot_ref, places_ref, gain_ref,
    mlp_gain_ref, own_ref, got_ref, slab_ref, out_ref, weights, loaded,
):
    wait = section_load(place_ref, own_ref, got_ref, weights, loaded)
    width_two = merged_ref.shape[1]
    total = parts_ref[0].astype(F32)
    for index in range(1, parts_ref.shape[0]):
        total = total + parts_ref[index].astype(F32)
    merged = merged_ref[...].astype(F32)
    bottom = (merged + total[:, :width_two]).astype(BF16)
    wait()
    decoded = [
        hidden_ref[patch].astype(F32) + dot_nt(bottom, weights[4 + patch])
        for patch in range(4)
    ]
    by_row = places_ref[: slab_ref.shape[1], BY_ROW_PATCH : BY_ROW_PATCH + 1]
    upper, lower = (
        picked(by_row, jnp.concatenate([decoded[at], decoded[at + 1]], axis=0).astype(BF16))
        for at in (0, 2)
    )
    pair_slabs(upper, lower, slab_ref, 0)
    center, scale_inv = norm_stats([merged], width_two)
    unit = (merged - center) * scale_inv
    (back,) = norm_backward(
        [total[:, width_two:]], [mlp_gain_ref[...]], [unit], scale_inv, width_two
    )
    grad_merged = (grad_ref[...] + back).astype(BF16)
    hidden = [hidden_ref[patch].astype(F32) for patch in range(4)]
    center, scale_inv = norm_stats(hidden, 4 * hidden[0].shape[1])
    units = [(value - center) * scale_inv for value in hidden]
    backs = norm_backward(
        [dot_nt(grad_merged, weights[patch]) for patch in range(4)],
        [gain_ref[patch : patch + 1, :] for patch in range(4)],
        units,
        scale_inv,
        4 * hidden[0].shape[1],
    )
    grads = [(cot_ref[patch].astype(F32) + backs[patch]) for patch in range(4)]
    grads = jnp.concatenate(grads, axis=0).astype(BF16)
    tokens = out_ref.shape[0]
    out_ref[...] = picked(places_ref[:tokens, UNPATCH : UNPATCH + 1], grads).astype(BF16)


def decoded_rows(got_ref, places_ref, out_ref):
    places = places_ref[: got_ref.shape[0] * PADDED_COLUMNS, STAY : STAY + 1]
    for side in range(WIN_H):
        rows = slice(side * PADDED_COLUMNS, (side + 1) * PADDED_COLUMNS)
        values = got_ref[:, rows, :].reshape(-1, 2 * HDIM)
        both = spread_over(places, values, out_ref.shape[2])
        for index in range(2):
            out_ref[2 * side + index] = both[HDIM * index : HDIM * (index + 1)].astype(BF16)


def input_rows(shift_ref, got_ref, edge_ref, places_ref, out_ref, framed):
    places = places_ref[: got_ref.shape[0] * PADDED_COLUMNS, SHIFT : SHIFT + 1]
    for side in range(WIN_H):
        rows = slice(side * PADDED_COLUMNS, (side + 1) * PADDED_COLUMNS)
        both = spread_over(places, got_ref[:, rows, :].reshape(-1, 2 * HDIM), out_ref.shape[2])
        framed[WIN_H + side] = both[:HDIM]
        framed[2 * WIN_H + side] = both[HDIM:]
    for side in range(WIN_H // 2):
        rows = slice(side * PADDED_COLUMNS, (side + 1) * PADDED_COLUMNS)
        both = spread_over(places, edge_ref[:, rows, :].reshape(-1, 2 * HDIM), out_ref.shape[2])
        framed[side] = both[:HDIM]
        framed[WIN_H // 2 + side] = both[HDIM:]
    first = WIN_H - shift_ref[0]
    for row in range(out_ref.shape[0]):
        out_ref[row] = framed[first + row]


def shards(
    fields,
    first_gain,
    qkv_weight,
    proj_weight,
    merge_gain,
    merge_weight,
    mlp_gain,
    up_weight,
    down_weight,
    expand_weight,
    lat_shift,
    lon_shift,
    cotangent,
):
    n_lat, n_mp = lax.axis_size("lat"), lax.axis_size("mp")
    lat, core = lax.axis_index("lat"), lax.rem(lax.axis_index("lat"), 2)
    lat_offset = lat_shift[0]
    lon_offset = lon_shift[0]
    rows, lon_count, group = fields.shape
    width = group * n_mp
    block = lon_count // n_mp
    wide = block + WIN_W
    bands, columns = rows // WIN_H, block // WIN_W
    tokens = rows * block
    width_two = merge_weight.shape[2]
    span = up_weight.shape[1]
    merged_count = tokens // 4
    padded = -(-merged_count // 16) * 16
    others = range(n_mp)

    section = jnp.concatenate([merge_weight, expand_weight.transpose(1, 2, 0)], axis=0)

    blocks = fields.reshape(rows, n_mp, block, group).transpose(1, 0, 2, 3)
    margin = jnp.roll(blocks[:, :, :WIN_W], -1, axis=0)
    field_blocks = jnp.concatenate([blocks, margin], axis=2)
    body_slab = halves_beside(field_blocks.reshape(n_mp, rows * wide, group))
    edge_slab = halves_beside(field_blocks[:, :WIN_H].reshape(n_mp, WIN_H * wide, group))
    cot_blocks = cotangent.reshape(rows, n_mp, block, group).transpose(1, 0, 2, 3)
    cot_slab = halves_beside(cot_blocks.reshape(n_mp, tokens, group))
    weights = jnp.concatenate(
        [qkv_weight.transpose(1, 2, 0), proj_weight.transpose(1, 0)[None]], axis=0
    )
    gains = jnp.pad(jnp.concatenate([first_gain[None], merge_gain], axis=0), ((0, 3), (0, 64)))

    def rows_at(here, step):
        return pl.ds(pl.multiple_of(lax.rem(here["mp"] + n_mp - step, n_mp) * group, group), group)

    def own_rows(ref, here, target):
        return ref.at[:, rows_at(here, 0)]

    def own_quarter(size):
        return lambda ref, here, target: ref.at[pl.ds(size * here["quarter"], size)]

    def quarter_rows(size, step, extra, half=None):
        def part(ref, here, target):
            first = size * lax.rem(here["quarter"] + extra, 4)
            if half is None:
                return ref.at[pl.ds(first, size), rows_at(here, step)]
            if size > 1:
                return ref.at[first + half, rows_at(here, step)]
            count = group // 2
            at = lax.rem(here["mp"] + n_mp - step, n_mp) * group + half * count
            return ref.at[first, pl.ds(pl.multiple_of(at, count), count)]

        return part

    nearest_first = (2, 6, 1, 7, 4, 3, 5)
    gather_moves = [
        (source, own_quarter(size), source, quarter_rows(size, 0, 0), 0, step)
        for source, size in ((0, 2), (1, 1))
        for step in nearest_first
    ]
    relays, last_relays = [], []
    for source, size, first in ((0, 2, 0), (1, 1, n_mp - 1)):
        for index, step in enumerate(nearest_first):
            after = first + index
            for half, down in ((0, 4), (1, -4)):
                part = quarter_rows(size, step, 0, half)
                relays.append((source, part, source, part, down, 0, after))
                part = quarter_rows(size, step, 2, half)
                last_relays.append((source, part, source, part, "sibling", 0, len(relays) - 1))
            part = quarter_rows(size, step, 0)
            relays.append((source, part, source, part, "sibling", 0, after))
    places = place_table(lat_offset, lon_offset, rows, block, padded, n_mp)
    moves = (
        gather_moves
        + [(4, None, 4, "mp", 0, step) for step in others]
        + [(2, "mp", 2, "mp", 0, step) for step in others]
        + [(3, "mp", 3, "mp", -1, step) for step in others]
        + [(1, None, 1, own_rows, 0, 0)]
    )
    last_relays = [move[:6] + (move[6] + len(moves),) for move in last_relays]
    section_got, weights_all, body_got, edge_got, gains_all = exchange(
        1,
        [section, weights, body_slab, edge_slab, gains],
        [
            ((8, width, width_two), BF16),
            ((4, width, width), BF16),
            (body_slab.shape, BF16),
            (edge_slab.shape, BF16),
            ((n_mp,) + gains.shape, F32),
        ],
        moves + relays + last_relays,
    )
    has_shard = lax.rem(lax.axis_index("mp"), 2) == core
    first_all = gains_all[:, 0, :group].reshape(1, width)
    merge_gain_all = gains_all[:, 1:5, :group].transpose(1, 0, 2).reshape(4, width)
    mlp_gain_row = mlp_gain.reshape(1, width_two)
    cut = (jnp.int32(rows) * (n_lat - lat) - lat_offset).reshape(1)
    attention_framed, context, framed_fields, own_fields = local_kernel(
        attention_forward,
        [cut, body_got, edge_got, places, first_all, weights_all],
        [((tokens, width), BF16)] * 3 + [((4, padded, width), BF16)],
        [
            pltpu.VMEM((3, tokens, width), F32),
            pltpu.VMEM((tokens, width), F32),
            pltpu.VMEM(((rows + WIN_H) * wide, width), BF16),
        ],
        scalars=1,
    )
    window_shape = (bands, columns, WIN, width)
    around = (2 * bands + 2, WIN, width)

    halo, cot_got = exchange(
        2,
        [attention_framed.reshape(window_shape), cot_slab],
        [(around, BF16), (cot_slab.shape, BF16)],
        [
            (0, (bands - 1, columns - 1), 0, (0,), 1, 1),
            (0, (slice(0, bands), columns - 1), 0, (slice(1, 1 + bands),), 0, 1),
            (0, (bands - 1,), 0, (slice(1 + bands, 1 + bands + columns),), 1, 0),
        ]
        + [(1, "mp", 1, "mp", 0, step) for step in others],
    )
    n_x = n_mp // 2
    section_scratch = [
        pltpu.VMEM(section_got.shape, BF16),
        pltpu.SemaphoreType.DMA((2,)),
    ]
    pair, hidden, merged, grad_bottom, cot_patches = local_kernel(
        merge_forward,
        [
            lax.axis_index("mp").reshape(1),
            own_fields,
            attention_framed,
            halo.reshape(-1, width),
            cot_got,
            places,
            merge_gain_all,
            mlp_gain_row,
            section,
            section_got,
        ],
        [
            ((padded, 2 * width_two), BF16),
            ((4, padded, width), BF16),
            ((padded, width_two), BF16),
            ((padded, width_two), F32),
            ((4, padded, width), BF16),
        ],
        section_scratch + [pltpu.VMEM((tokens, width), F32)],
        scalars=1,
        outside=2,
    )

    def chip_spot(step):
        def spot(ref, here, target):
            return ref.at[lax.rem(here["x"] + n_x + step, n_x), here["core"]]

        return spot

    pairs, up_other, down_other = exchange(
        3,
        [pair, up_weight, down_weight],
        [
            ((n_x, 2) + pair.shape, BF16),
            (up_weight.shape, BF16),
            (down_weight.shape, BF16),
        ],
        [
            (0, None, 0, chip_spot(0), 0, 4),
            (0, None, 0, chip_spot(0), 0, 2),
            (0, None, 0, chip_spot(0), 0, -2),
            (0, None, 0, chip_spot(0), "sibling", 0),
            (0, None, 0, chip_spot(0), 0, 0),
            (1, None, 1, None, "flip", 0),
            (2, None, 2, None, "flip", 0),
            (0, chip_spot(-1), 0, chip_spot(-1), "sibling", 0, 1),
            (0, chip_spot(1), 0, chip_spot(1), "sibling", 0, 2),
            (0, chip_spot(-2), 0, chip_spot(-2), "sibling", 0, 0),
        ],
    )
    up_shard = jnp.where(has_shard, up_weight, up_other)
    down_shard = jnp.where(has_shard, down_weight, down_other)
    pairs = pairs.reshape(n_mp * padded, 2 * width_two)
    mlp_in, bottom_grad = pairs[:, :width_two], pairs[:, width_two:]
    hidden_up = jnp.dot(mlp_in, up_shard, preferred_element_type=F32)
    activated = jax.nn.gelu(hidden_up).astype(BF16)
    grad_act = jnp.dot(bottom_grad, down_shard, preferred_element_type=F32)
    gelu_back = jax.vjp(jax.nn.gelu, hidden_up)[1]
    grad_pre = gelu_back(grad_act)[0].astype(BF16)
    terms = jnp.concatenate(
        [
            jnp.einsum("af,ef->ae", activated, down_shard, preferred_element_type=F32),
            jnp.einsum("af,ef->ae", grad_pre, up_shard, preferred_element_type=F32),
        ],
        axis=1,
    ).astype(BF16)
    large = (n_lat, width_two // n_lat, span)
    parts, up_got, down_got = terms_back(
        4,
        terms.reshape(n_x, 2, padded, 2 * width_two),
        jnp.einsum("ae,af->ef", mlp_in, grad_pre, preferred_element_type=F32)
        .astype(BF16)
        .reshape(large),
        jnp.einsum("ao,af->of", bottom_grad, activated, preferred_element_type=F32)
        .astype(BF16)
        .reshape(large),
    )
    row_slab = (n_mp, WIN_H * PADDED_COLUMNS, 2 * group)
    decoded_slab, grad_windows = local_kernel(
        merge_backward,
        [
            lax.axis_index("mp").reshape(1),
            parts,
            merged,
            grad_bottom,
            hidden,
            cot_patches,
            places,
            merge_gain_all,
            mlp_gain_row,
            section,
            section_got,
        ],
        [(row_slab, BF16), ((tokens, width), BF16)],
        section_scratch,
        scalars=1,
        outside=2,
    )
    halo, decoded_got = exchange(
        5,
        [grad_windows.reshape(window_shape), decoded_slab],
        [(around, BF16), (decoded_slab.shape, BF16)],
        [
            (0, (0, 0), 0, (0,), -1, -1),
            (0, (slice(0, bands), 0), 0, (slice(1, 1 + bands),), 0, -1),
            (0, (0,), 0, (slice(1 + bands, 1 + bands + columns),), -1, 0),
        ]
        + [(1, "mp", 1, "mp", 0, step) for step in others],
    )
    grad_up = jnp.sum(up_got.astype(F32), axis=0)
    grad_down = jnp.sum(down_got.astype(F32), axis=0)
    grad_slab, grad_edge, weight_grads = local_kernel(
        attention_backward,
        [
            cut,
            framed_fields,
            first_all,
            weights_all,
            context,
            grad_windows,
            halo.reshape(-1, width),
            places,
        ],
        [
            (row_slab, BF16),
            ((n_mp, WIN_H * PADDED_COLUMNS // 2, 2 * group), BF16),
            ((4, width, width), BF16),
        ],
        [
            pltpu.VMEM((3, tokens, width), F32),
            pltpu.VMEM((3, tokens, width), F32),
            pltpu.VMEM((tokens, width), F32),
        ],
        scalars=1,
    )
    weight_total, grad_got, edge_got = gradients_out(6, weight_grads, grad_slab, grad_edge)
    grad_qkv = weight_total[:, : 3 * group].reshape(width // n_lat, 3, group)
    grad_proj = weight_total[:, 3 * group :]
    (decoded,) = local_kernel(
        decoded_rows, [decoded_got, places], [((rows, group, lon_count), BF16)]
    )
    (grad_input,) = local_kernel(
        input_rows,
        [lat_shift, grad_got, edge_got, places],
        [((rows, group, lon_count), F32)],
        [pltpu.VMEM((rows + WIN_H, group, lon_count), F32)],
        scalars=1,
    )
    decoded, grad_input = decoded.transpose(0, 2, 1), grad_input.transpose(0, 2, 1)
    return (decoded, grad_input, grad_qkv, grad_proj, grad_up, grad_down)


def solution(mesh):
    return jax.shard_map(
        shards,
        mesh=mesh,
        in_specs=(
            P("lat", None, "mp"),
            P("mp"),
            P(None, None, "mp"),
            P(None, "mp"),
            P(None, "mp"),
            P(None, "mp", None),
            P(),
            P(None, "mp"),
            P(None, "mp"),
            P(None, None, "mp"),
            P(),
            P(),
            P("lat", None, "mp"),
        ),
        out_specs=(
            P("lat", None, "mp"),
            P("lat", None, "mp"),
            P("lat", None, "mp"),
            P("lat", "mp"),
            P("lat", "mp"),
            P("lat", "mp"),
        ),
        check_vma=False,
    )
```

```python
import jax
import jax.numpy as jnp
import numpy as np
from jax import lax
from jax.experimental import pallas as pl
from jax.experimental.pallas import tpu as pltpu
from jax.sharding import PartitionSpec as P

WIN_H = 6
WIN_W = 12
HDIM = 64
EPSILON = 1e-05
MASKED = -1e30
BF16 = jnp.bfloat16
F32 = jnp.float32


def space_of(shape):
    return pltpu.VMEM if int(np.prod(shape)) <= 2 * 1024 * 1024 else pl.ANY


def positions():
    lat, mp = lax.axis_index("lat"), lax.axis_index("mp")
    return {
        "lat": lat,
        "mp": mp,
        "core": lax.rem(lat, 2),
        "x": lax.div(mp, 2),
        "z": lax.rem(mp, 2),
        "quarter": 2 * lax.rem(lax.div(lat, 4), 2) + lax.rem(lat, 2),
    }


def reached(here, down, right):
    n_lat, n_mp = lax.axis_size("lat"), lax.axis_size("mp")
    if down == "sibling":
        return {"lat": here["lat"] + 1 - 2 * here["core"], "mp": here["mp"]}
    if down == "flip":
        return {"lat": here["lat"], "mp": 2 * here["x"] + 1 - here["z"]}
    return {
        "lat": lax.rem(here["lat"] + n_lat + down, n_lat),
        "mp": lax.rem(here["mp"] + n_mp + right, n_mp),
    }


def device_of(target):
    return {
        "device_id": (target["lat"], target["mp"]),
        "device_id_type": pl.DeviceIdType.MESH,
    }


def greet(here, steps, owned=False):
    barrier = pltpu.get_barrier_semaphore()
    count = len(steps)
    if owned:
        n_lat, x, z = lax.axis_size("lat"), here["x"], here["z"]
        owner = z == here["core"]
        mine = 2 * lax.div(here["lat"], 2) + z
        count = count + n_lat - jnp.where(owner, 1, 0)
        for source in range(n_lat):

            @pl.when(jnp.logical_or(jnp.logical_not(owner), mine != source))
            def _():
                target = {"lat": 2 * (source // 2) + z, "mp": 2 * x + source % 2}
                pl.semaphore_signal(barrier, inc=1, **device_of(target))

    for down, right in steps:
        source = reached(here, down if isinstance(down, str) else -down, -right)
        pl.semaphore_signal(barrier, inc=1, **device_of(source))
    pl.semaphore_wait(barrier, count)


def to_owners(here, source, landing, send, receive):
    n_lat = lax.axis_size("lat")
    lat, core, x, z = here["lat"], here["core"], here["x"], here["z"]
    mine = 2 * lax.div(lat, 2) + z
    owner = z == core

    def copy_at(step):
        target = {"lat": lax.rem(lat + step, n_lat), "mp": 2 * x + core}
        rows = target["lat"]
        return remote(source.at[rows], landing.at[mine], send.at[step], receive.at[mine], target)

    def start():
        for step in range(1, n_lat):
            copy_at(step).start()

        @pl.when(owner)
        def _():
            pltpu.make_async_copy(source.at[lat], landing.at[mine], receive.at[mine]).start()

        @pl.when(jnp.logical_not(owner))
        def _():
            copy_at(0).start()

    def wait():
        sibling = reached(here, "sibling", 0)
        for slot in range(n_lat):
            remote(
                source.at[slot], landing.at[slot], send.at[slot], receive.at[slot], sibling
            ).wait_recv()
        for step in range(1, n_lat):
            copy_at(step).wait_send()

        @pl.when(jnp.logical_not(owner))
        def _():
            copy_at(0).wait_send()

    return start, wait


def remote(source, landing, send, receive, target):
    return pltpu.make_async_remote_copy(
        src_ref=source, dst_ref=landing, send_sem=send, recv_sem=receive, **device_of(target)
    )


def exchange(collective, inputs, outputs, moves, owned=()):
    n_lat = lax.axis_size("lat")
    steps = []
    for move in moves:
        if move[4:6] != (0, 0) and move[4:6] not in steps:
            steps.append(move[4:6])

    def body(*refs):
        sources = refs[: len(inputs)]
        landings = refs[len(inputs) : len(inputs) + len(outputs)]
        send, receive, owned_send, owned_receive = refs[-4:]
        here = positions()

        def part_of(ref, part, place, target):
            if part is None:
                return ref
            if isinstance(part, str):
                return ref.at[place[part]]
            if callable(part):
                return part(ref, here, target)
            return ref.at[part]

        greet(here, steps, bool(owned))
        copies = []
        arrived = set()
        scatters = [
            to_owners(
                here, sources[one], landings[two], owned_send.at[index], owned_receive.at[index]
            )
            for index, (one, two) in enumerate(owned)
        ]
        for index, move in enumerate(moves):
            source, source_part, landing, landing_part, down, right = move[:6]
            target = reached(here, down, right)
            if len(move) > 6:
                if move[6] not in arrived:
                    copies[move[6]].wait_recv()
                    arrived.add(move[6])
                source_ref = part_of(landings[source], source_part, target, target)
            else:
                source_ref = part_of(sources[source], source_part, target, target)
            landing_ref = part_of(landings[landing], landing_part, here, target)
            if (down, right) == (0, 0):
                copy = pltpu.make_async_copy(source_ref, landing_ref, receive.at[index])
            else:
                copy = remote(
                    source_ref, landing_ref, send.at[index], receive.at[index], target
                )
            if down == "flip":
                pl.when(here["z"] == here["core"])(copy.start)
            else:
                copy.start()
            copies.append(copy)
        for start, _ in scatters:
            start()
        for _, wait in scatters:
            wait()
        for index, copy in enumerate(copies):
            if moves[index][4:6] == (0, 0):
                copy.wait()
            elif moves[index][4] == "flip":
                pl.when(here["z"] == here["core"])(copy.wait_send)
                pl.when(here["z"] != here["core"])(copy.wait_recv)
            else:
                copy.wait_send()
                if index not in arrived:
                    copy.wait_recv()

    return pl.pallas_call(
        body,
        out_shape=[jax.ShapeDtypeStruct(shape, dtype) for shape, dtype in outputs],
        in_specs=[pl.BlockSpec(memory_space=pl.ANY)] * len(inputs),
        out_specs=[pl.BlockSpec(memory_space=space_of(shape)) for shape, _ in outputs],
        scratch_shapes=[
            pltpu.SemaphoreType.DMA((len(moves),)),
            pltpu.SemaphoreType.DMA((len(moves),)),
            pltpu.SemaphoreType.DMA((max(len(owned), 1), n_lat)),
            pltpu.SemaphoreType.DMA((max(len(owned), 1), n_lat)),
        ],
        compiler_params=pltpu.CompilerParams(
            collective_id=collective, has_side_effects=True, vmem_limit_bytes=32 * 1024 * 1024
        ),
    )(*inputs)


X_STEPS = ((4, 2), (2, 1), (-2, 3))


def terms_back(collective, terms, up_grads, down_grads):
    count, _, rows, width = terms.shape
    n_lat = lax.axis_size("lat")

    def body(
        terms_ref, up_ref, down_ref, parts_ref, up_got, down_got,
        other, own, total, send, receive, fetch, large_send, large_receive,
    ):
        here = positions()
        core, x = here["core"], here["x"]
        sibling = reached(here, "sibling", 0)
        greet(here, [("sibling", 0)] + [(0, right) for right, _ in X_STEPS], True)
        scatters = [
            to_owners(here, source, landing, large_send.at[index], large_receive.at[index])
            for index, (source, landing) in enumerate(((up_ref, up_got), (down_ref, down_got)))
        ]
        order = [lax.rem(x + step, count) for _, step in X_STEPS] + [x]
        swaps, loads = [], []
        for index, spot in enumerate(order):
            swap = remote(
                terms_ref.at[spot, 1 - core],
                other.at[index],
                send.at[index],
                receive.at[index],
                sibling,
            )
            load = pltpu.make_async_copy(terms_ref.at[spot, core], own.at[index], fetch.at[index])
            swap.start()
            load.start()
            swaps.append(swap)
            loads.append(load)
        for start, _ in scatters:
            start()
        sends = []
        for index, spot in enumerate(order):
            loads[index].wait()
            swaps[index].wait_recv()
            total[index] = (own[index].astype(F32) + other[index].astype(F32)).astype(BF16)
            if index < len(X_STEPS):
                copy = remote(
                    total.at[index],
                    parts_ref.at[x],
                    send.at[count + index],
                    receive.at[count + index],
                    reached(here, 0, X_STEPS[index][0]),
                )
            else:
                copy = pltpu.make_async_copy(total.at[index], parts_ref.at[x], fetch.at[count])
            copy.start()
            sends.append(copy)
        for swap in swaps:
            swap.wait_send()
        for copy in sends:
            copy.wait()
        for _, wait in scatters:
            wait()

    return pl.pallas_call(
        body,
        out_shape=[
            jax.ShapeDtypeStruct((count, rows, width), BF16),
            jax.ShapeDtypeStruct(up_grads.shape, BF16),
            jax.ShapeDtypeStruct(down_grads.shape, BF16),
        ],
        in_specs=[pl.BlockSpec(memory_space=pl.ANY)] * 3,
        out_specs=[
            pl.BlockSpec(memory_space=pltpu.VMEM),
            pl.BlockSpec(memory_space=pl.ANY),
            pl.BlockSpec(memory_space=pl.ANY),
        ],
        scratch_shapes=[
            pltpu.VMEM((count, rows, width), BF16),
            pltpu.VMEM((count, rows, width), BF16),
            pltpu.VMEM((count, rows, width), BF16),
            pltpu.SemaphoreType.DMA((2 * count,)),
            pltpu.SemaphoreType.DMA((2 * count,)),
            pltpu.SemaphoreType.DMA((count + 1,)),
            pltpu.SemaphoreType.DMA((2, n_lat)),
            pltpu.SemaphoreType.DMA((2, n_lat)),
        ],
        compiler_params=pltpu.CompilerParams(
            collective_id=collective, has_side_effects=True, vmem_limit_bytes=48 * 1024 * 1024
        ),
    )(terms, up_grads, down_grads)


def gradients_out(collective, weight_grads, slabs, edges):
    n_lat, n_mp = lax.axis_size("lat"), lax.axis_size("mp")
    kinds, width, _ = weight_grads.shape
    pair, group, share = kinds // 2, width // n_mp, width // n_lat

    def body(
        weight_ref, slab_ref, edge_ref, out_ref, got_ref, edge_got,
        other, total, parts, turned, landed, send, receive,
    ):
        here = positions()
        lat, mp, core = here["lat"], here["mp"], here["core"]
        sibling = reached(here, "sibling", 0)
        barrier = pltpu.get_barrier_semaphore()
        greeted = [sibling]
        greeted += [reached(here, 0, -step) for step in range(1, n_mp)]
        greeted += [reached(here, -1, -step) for step in range(n_mp)]
        greeted += [reached(here, -step, 0) for step in range(1, n_lat)]
        for target in greeted:
            pl.semaphore_signal(barrier, inc=1, **device_of(target))
        pl.semaphore_wait(barrier, len(greeted))

        copies = []

        def sent(source, landing, target):
            index = len(copies)
            copy = remote(source, landing, send.at[index], receive.at[index], target)
            copy.start()
            copies.append(copy)
            return copy

        swap = sent(weight_ref.at[pl.ds(pair * (1 - core), pair)], other, sibling)
        own_slab = pltpu.make_async_copy(slab_ref.at[mp], got_ref.at[mp], send.at[60])
        own_slab.start()

        swap.wait_recv()
        total[...] = (
            weight_ref[pl.ds(pair * core, pair)].astype(F32) + other[...].astype(F32)
        ).astype(BF16)
        scattered = []
        for step in range(1, n_mp):
            target = reached(here, 0, step)
            rows = pl.ds(pl.multiple_of(group * target["mp"], group), group)
            scattered.append(sent(total.at[:, rows], parts.at[mp], target))
        for step in range(1, n_mp):
            target = reached(here, 0, step)
            sent(slab_ref.at[target["mp"]], got_ref.at[mp], target)
        for step in range(n_mp):
            target = reached(here, 1, step)
            sent(edge_ref.at[target["mp"]], edge_got.at[mp], target)
        gathered = total[:, pl.ds(pl.multiple_of(group * mp, group), group), :].astype(F32)
        for step in range(1, n_mp):
            scattered[step - 1].wait_recv()
            gathered = gathered + parts[lax.rem(mp + n_mp - step, n_mp)].astype(F32)
        flat = gathered.reshape(pair * group, width).T.astype(BF16)
        for index in range(n_lat):
            turned[index] = flat[index * share : (index + 1) * share]
        spread = []
        for step in range(1, n_lat):
            target = reached(here, step, 0)
            spread.append(sent(turned.at[target["lat"]], landed.at[lat], target))
        landed[lat] = turned[lat]
        for copy in spread:
            copy.wait_recv()
        for half in range(2):
            result = landed[half].astype(F32)
            for index in range(half + 2, n_lat, 2):
                result = result + landed[index].astype(F32)
            out_ref[:, half * pair * group : (half + 1) * pair * group] = result

        done = [swap] + scattered + spread
        for copy in copies:
            copy.wait_send()
            if not any(copy is other_copy for other_copy in done):
                copy.wait_recv()
        own_slab.wait()

    any_space = pl.BlockSpec(memory_space=pl.ANY)
    vmem = pl.BlockSpec(memory_space=pltpu.VMEM)
    return pl.pallas_call(
        body,
        out_shape=[
            jax.ShapeDtypeStruct((share, kinds * group), F32),
            jax.ShapeDtypeStruct(slabs.shape, BF16),
            jax.ShapeDtypeStruct(edges.shape, BF16),
        ],
        in_specs=[vmem, any_space, any_space],
        out_specs=[vmem, vmem, vmem],
        scratch_shapes=[
            pltpu.VMEM((pair, width, width), BF16),
            pltpu.VMEM((pair, width, width), BF16),
            pltpu.VMEM((n_mp, pair, group, width), BF16),
            pltpu.VMEM((n_lat, share, pair * group), BF16),
            pltpu.VMEM((n_lat, share, pair * group), BF16),
            pltpu.SemaphoreType.DMA((64,)),
            pltpu.SemaphoreType.DMA((64,)),
        ],
        compiler_params=pltpu.CompilerParams(
            collective_id=collective, has_side_effects=True, vmem_limit_bytes=48 * 1024 * 1024
        ),
    )(weight_grads, slabs, edges)


def local_kernel(body, operands, outputs, scratch=(), scalars=0, outside=0):
    spaces = [pltpu.SMEM] * scalars + [pltpu.VMEM] * (len(operands) - scalars - outside)
    spaces += [pl.ANY] * outside
    return pl.pallas_call(
        body,
        out_shape=[jax.ShapeDtypeStruct(shape, dtype) for shape, dtype in outputs],
        in_specs=[pl.BlockSpec(memory_space=space) for space in spaces],
        out_specs=[pl.BlockSpec(memory_space=pltpu.VMEM)] * len(outputs),
        scratch_shapes=list(scratch),
        compiler_params=pltpu.CompilerParams(vmem_limit_bytes=48 * 1024 * 1024),
    )(*operands)


def dot_nn(left, right):
    return lax.dot_general(left, right, (((1,), (0,)), ((), ())), preferred_element_type=F32)


def dot_nt(left, right):
    return lax.dot_general(left, right, (((1,), (1,)), ((), ())), preferred_element_type=F32)


def dot_tn(left, right):
    return lax.dot_general(left, right, (((0,), (0,)), ((), ())), preferred_element_type=F32)


def halves_beside(values):
    half = values.shape[-2] // 2
    return jnp.concatenate([values[..., :half, :], values[..., half:, :]], axis=-1)


def picked(places, values):
    spots = lax.broadcasted_iota(jnp.int32, (places.shape[0], values.shape[0]), 1)
    return dot_nn(jnp.where(spots == places, 1.0, 0.0).astype(BF16), values)


def spread_over(places, values, count):
    spots = lax.broadcasted_iota(jnp.int32, (places.shape[0], count), 1)
    return dot_tn(values, jnp.where(spots == places, 1.0, 0.0).astype(BF16))


def swapped(values):
    return jnp.concatenate([values[:, HDIM:], values[:, :HDIM]], axis=1)


def join_slabs(slab_ref, out_ref, first_rows, second_rows):
    half = slab_ref.shape[1]
    low = lax.broadcasted_iota(jnp.int32, (half, 2 * HDIM), 1) < HDIM
    for pair in range(slab_ref.shape[0] // 2):
        lanes = slice(2 * HDIM * pair, 2 * HDIM * (pair + 1))
        one = slab_ref[2 * pair].astype(F32)
        two = slab_ref[2 * pair + 1].astype(F32)
        first = jnp.where(low, one, swapped(two)).astype(out_ref.dtype)
        second = jnp.where(low, swapped(one), two).astype(out_ref.dtype)
        out_ref[first_rows : first_rows + half, lanes] = first
        out_ref[second_rows : second_rows + half, lanes] = second


PADDED_COLUMNS = 48
FRAME, OWN, BACK, BACK_HALO, COT, UNPATCH, GRAD, GRAD_HALO, BY_ROW, BY_ROW_PATCH, SHIFT, STAY = range(12)


def place_table(lat_offset, lon_offset, rows, block, padded, n_mp):
    columns = block // WIN_W
    size = max(rows * block, 4 * padded, n_mp * PADDED_COLUMNS)
    token = np.arange(rows * block)
    window, spot = token // WIN, token % WIN
    row = (window // columns) * WIN_H + spot // WIN_W
    column = (window % columns) * WIN_W + spot % WIN_W
    patch, at = np.arange(4 * padded) // padded, np.arange(4 * padded) % padded
    real = at < rows * block // 4
    prow = 2 * (at // (block // 2)) + patch // 2
    pcolumn = 2 * (at % (block // 2)) + patch % 2
    side = np.arange(WIN_H * PADDED_COLUMNS) // PADDED_COLUMNS
    spot = np.arange(WIN_H * PADDED_COLUMNS) % PADDED_COLUMNS
    shown = spot < block
    group = np.arange(n_mp * PADDED_COLUMNS) // PADDED_COLUMNS
    place = np.arange(n_mp * PADDED_COLUMNS) % PADDED_COLUMNS
    inside = place < block
    unpatch = (2 * (row % 2) + column % 2) * padded + (row // 2) * (block // 2) + column // 2
    by_row = (spot // WIN_W) * WIN + side * WIN_W + spot % WIN_W
    by_row_patch = (spot % 2) * padded + side * (block // 2) + spot // 2
    lon = group * block + place
    wide = block + WIN_W
    source = {
        FRAME: (row, column, True, wide),
        OWN: (prow, pcolumn, real, wide),
        BACK: (prow, pcolumn, real, 0),
        BACK_HALO: (prow, pcolumn, real, 0),
        COT: (prow, pcolumn, real, block),
        UNPATCH: (0, unpatch, True, 0),
        GRAD: (row, column, True, 0),
        GRAD_HALO: (row, column, True, 0),
        BY_ROW: (0, by_row, shown, 0),
        BY_ROW_PATCH: (0, by_row_patch, shown, 0),
        SHIFT: (0, lon, inside, 0),
        STAY: (0, lon, inside, 0),
    }
    shape = (size, len(source))
    row_at, column_at, pitch = (np.zeros(shape, np.int32) for _ in range(3))
    valid = np.zeros(shape, bool)
    for key, (row_part, column_part, part, step) in source.items():
        count = column_part.shape[0]
        row_at[:count, key], column_at[:count, key], pitch[:, key] = row_part, column_part, step
        valid[:count, key] = part
    kind = np.arange(len(source))[None]
    back = np.isin(kind, (BACK, BACK_HALO))
    grad = np.isin(kind, (GRAD, GRAD_HALO))
    row_sign = np.where(back, -1, np.where(grad | (kind == FRAME), 1, 0)).astype(np.int32)
    column_sign = np.where(kind == SHIFT, 1, row_sign).astype(np.int32)
    row_at = row_at + row_sign * lat_offset
    column_at = column_at + column_sign * lon_offset
    straight = row_at * pitch + column_at
    full = n_mp * block
    straight = jnp.where((kind == SHIFT) & (straight >= full), straight - full, straight)
    down = jnp.where(back, row_at < 0, row_at >= rows)
    right = jnp.where(back, column_at < 0, column_at >= block)
    row_in = jnp.where(down, row_at + np.where(back, WIN_H, -rows).astype(np.int32), row_at)
    column_in = jnp.where(
        right, column_at + np.where(back, WIN_W, -block).astype(np.int32), column_at
    )
    band, slot = lax.div(row_in, jnp.int32(WIN_H)), lax.div(column_in, jnp.int32(WIN_W))
    halo_slot = jnp.where(down, jnp.where(right, 0, 3 + slot), 1 + band)
    outside = jnp.logical_or(down, right)
    halo = np.isin(kind, (BACK_HALO, GRAD_HALO))
    tile = jnp.where(halo, halo_slot, band * columns + slot)
    windowed = tile * WIN + (row_in - band * WIN_H) * WIN_W + column_in - slot * WIN_W
    result = jnp.where(back | grad, windowed, straight)
    hidden = (back | grad) & jnp.where(halo, jnp.logical_not(outside), outside)
    return jnp.where(valid & jnp.logical_not(hidden), result, -1).astype(jnp.int32)


def norm_stats(values, count):
    center = sum(jnp.sum(value, axis=1, keepdims=True) for value in values) / count
    second = sum(jnp.sum(value * value, axis=1, keepdims=True) for value in values) / count
    return (center, lax.rsqrt(second - center * center + EPSILON))


def norm_backward(grads, gains, units, scale_inv, count):
    scaled = [grad * gain for grad, gain in zip(grads, gains)]
    first = sum(jnp.sum(value, axis=1, keepdims=True) for value in scaled) / count
    second = (
        sum(jnp.sum(value * unit, axis=1, keepdims=True) for value, unit in zip(scaled, units))
        / count
    )
    return [scale_inv * (value - first - unit * second) for value, unit in zip(scaled, units)]


def pair_slabs(upper, lower, out_ref, first_rows):
    low = lax.broadcasted_iota(jnp.int32, (upper.shape[0], 2 * HDIM), 1) < HDIM
    rows = pl.ds(first_rows, upper.shape[0])
    for pair in range(upper.shape[1] // (2 * HDIM)):
        lanes = slice(2 * HDIM * pair, 2 * HDIM * (pair + 1))
        one, two = upper[:, lanes], lower[:, lanes]
        out_ref[2 * pair, rows, :] = jnp.where(low, one, swapped(two)).astype(BF16)
        out_ref[2 * pair + 1, rows, :] = jnp.where(low, swapped(one), two).astype(BF16)


WIN = WIN_H * WIN_W
FACTOR = HDIM ** (-0.5)


def heads_apart(values):
    low = lax.broadcasted_iota(jnp.int32, values.shape, 1) < HDIM
    zero = jnp.zeros_like(values)
    both = [jnp.where(low, values, zero), jnp.where(low, zero, values)]
    return jnp.concatenate(both, axis=0).astype(BF16)


def heads_together(values):
    low = lax.broadcasted_iota(jnp.int32, (WIN, 2 * HDIM), 1) < HDIM
    return jnp.where(low, values[:WIN], values[WIN:])


def window_probs(cut, window, query, keys):
    scores = dot_nt(query, keys) * FACTOR
    spot = lax.broadcasted_iota(jnp.int32, scores.shape, 0)
    spot = jnp.where(spot >= WIN, spot - WIN, spot)
    other = lax.broadcasted_iota(jnp.int32, scores.shape, 1)
    edge = cut * WIN_W - jnp.where(window >= 3, WIN, 0)
    same = (spot >= edge) == (other >= edge)
    scores = jnp.where(same, scores, MASKED)
    weights = jnp.exp(scores - jnp.max(scores, axis=1, keepdims=True))
    return weights / jnp.sum(weights, axis=1, keepdims=True)


def framed_packed(fields_ref, gain_ref, weights_ref, packed):
    values = fields_ref[...].astype(F32)
    center, scale_inv = norm_stats([values], values.shape[1])
    unit = (values - center) * scale_inv
    framed = (unit * gain_ref[...]).astype(BF16)
    for kind in range(3):
        packed[kind] = dot_nt(framed, weights_ref[kind]).astype(BF16).astype(F32)
    return (framed, unit, scale_inv)


def window_parts(refs, window, pair):
    rows = pl.ds(pl.multiple_of(window * WIN, 8), WIN)
    lanes = slice(2 * HDIM * pair, 2 * HDIM * (pair + 1))
    return [ref[rows, lanes] for ref in refs]


def attention_forward(
    cut_ref, body_ref, edge_ref, places_ref, gain_ref, weights_ref,
    out_ref, context_ref, fields_ref, own_ref, packed, held, grid,
):
    half, rest = body_ref.shape[1], edge_ref.shape[1]
    join_slabs(body_ref, grid, 0, half)
    join_slabs(edge_ref, grid, 2 * half, 2 * half + rest)
    tokens = fields_ref.shape[0]
    whole = grid[...]
    fields_ref[...] = picked(places_ref[:tokens, FRAME : FRAME + 1], whole).astype(BF16)
    padded = own_ref.shape[1]
    for patch in range(4):
        rows = slice(padded * patch, padded * (patch + 1))
        own_ref[patch] = picked(places_ref[rows, OWN : OWN + 1], whole).astype(BF16)
    framed_packed(fields_ref, gain_ref, weights_ref, packed)
    cut = cut_ref[0]
    windows = fields_ref.shape[0] // WIN

    def step(window, carry):
        rows = pl.ds(pl.multiple_of(window * WIN, 8), WIN)
        for pair in range(fields_ref.shape[1] // (2 * HDIM)):
            query, keys, values = window_parts([packed.at[kind] for kind in range(3)], window, pair)
            probs = window_probs(cut, window, heads_apart(query), keys.astype(BF16))
            joined = dot_nn(probs.astype(BF16), values.astype(BF16))
            held[rows, 2 * HDIM * pair : 2 * HDIM * (pair + 1)] = heads_together(joined)
        return carry

    lax.fori_loop(0, windows, step, 0)
    context = held[...].astype(BF16)
    context_ref[...] = context
    out_ref[...] = dot_nn(context, weights_ref[3]).astype(BF16)


def attention_backward(
    cut_ref, fields_ref, gain_ref, weights_ref, context_ref, grad_ref, halo_ref, places_ref,
    slab_ref, edge_ref, weight_ref, packed, grads, held,
):
    framed, unit, scale_inv = framed_packed(fields_ref, gain_ref, weights_ref, packed)
    cut = cut_ref[0]
    windows = fields_ref.shape[0] // WIN
    tokens = fields_ref.shape[0]
    grad_framed = (
        picked(places_ref[:tokens, GRAD : GRAD + 1], grad_ref[...])
        + picked(places_ref[:tokens, GRAD_HALO : GRAD_HALO + 1], halo_ref[...])
    ).astype(BF16)
    held[...] = dot_nt(grad_framed, weights_ref[3]).astype(BF16).astype(F32)

    def step(window, carry):
        rows = pl.ds(pl.multiple_of(window * WIN, 8), WIN)
        for pair in range(fields_ref.shape[1] // (2 * HDIM)):
            lanes = slice(2 * HDIM * pair, 2 * HDIM * (pair + 1))
            query, keys, values, grad = window_parts(
                [packed.at[kind] for kind in range(3)] + [held], window, pair
            )
            query, grad = heads_apart(query), heads_apart(grad)
            keys, values = keys.astype(BF16), values.astype(BF16)
            probs = window_probs(cut, window, query, keys)
            grad_probs = dot_nt(grad, values)
            inner = jnp.sum(grad_probs * probs, axis=1, keepdims=True)
            grad_scores = (probs * (grad_probs - inner) * FACTOR).astype(BF16)
            grads[0, rows, lanes] = heads_together(dot_nn(grad_scores, keys))
            grads[1, rows, lanes] = dot_tn(grad_scores, query)
            grads[2, rows, lanes] = dot_tn(probs.astype(BF16), grad)
        return carry

    lax.fori_loop(0, windows, step, 0)
    grad_normed = jnp.zeros(fields_ref.shape, F32)
    for kind in range(3):
        grad_kind = grads[kind].astype(BF16)
        weight_ref[kind] = dot_tn(grad_kind, framed).astype(BF16)
        grad_normed = grad_normed + dot_nn(grad_kind, weights_ref[kind])
    weight_ref[3] = dot_tn(context_ref[...], grad_framed).astype(BF16)
    (back,) = norm_backward([grad_normed], [gain_ref[...]], [unit], scale_inv, unit.shape[1])
    result = grad_framed.astype(F32) + back
    half = result.shape[0] // 2
    by_row = places_ref[: slab_ref.shape[1], BY_ROW : BY_ROW + 1]
    upper, lower = (picked(by_row, part.astype(BF16)) for part in (result[:half], result[half:]))
    pair_slabs(upper, lower, slab_ref, 0)
    half = edge_ref.shape[1]
    pair_slabs(lower[:half], lower[half:], edge_ref, 0)


def section_load(place_ref, own_ref, got_ref, weights, loaded):
    whole = pltpu.make_async_copy(got_ref, weights, loaded.at[0])
    whole.start()

    def wait():
        whole.wait()
        count = own_ref.shape[1]
        rows = pl.ds(pl.multiple_of(place_ref[0] * count, count), count)
        own = pltpu.make_async_copy(own_ref, weights.at[:, rows], loaded.at[1])
        own.start()
        own.wait()

    return wait


def merge_forward(
    place_ref, fields_ref, attention_ref, halo_ref, cot_got_ref, places_ref, gain_ref,
    mlp_gain_ref, own_ref, got_ref,
    pair_ref, hidden_ref, merged_ref, grad_ref, cot_ref, weights, loaded, joined,
):
    wait = section_load(place_ref, own_ref, got_ref, weights, loaded)
    width_two = merged_ref.shape[1]
    join_slabs(cot_got_ref, joined, 0, cot_got_ref.shape[1])
    cot = joined[...].astype(BF16)
    padded = merged_ref.shape[0]
    hidden = []
    for patch in range(4):
        rows = slice(padded * patch, padded * (patch + 1))
        cot_ref[patch] = picked(places_ref[rows, COT : COT + 1], cot).astype(BF16)
        attention = picked(places_ref[rows, BACK : BACK + 1], attention_ref[...])
        attention = attention + picked(
            places_ref[rows, BACK_HALO : BACK_HALO + 1], halo_ref[...]
        )
        value = fields_ref[patch].astype(F32) + attention
        hidden_ref[patch] = value.astype(BF16)
        hidden.append(value.astype(BF16).astype(F32))
    center, scale_inv = norm_stats(hidden, 4 * hidden[0].shape[1])
    merged = jnp.zeros(merged_ref.shape, F32)
    grad = jnp.zeros(merged_ref.shape, F32)
    wait()
    for patch in range(4):
        normed = (hidden[patch] - center) * scale_inv * gain_ref[patch : patch + 1, :]
        merged = merged + dot_nn(normed.astype(BF16), weights[patch])
        grad = grad + dot_nn(cot_ref[patch], weights[4 + patch])
    merged_ref[...] = merged.astype(BF16)
    merged = merged.astype(BF16).astype(F32)
    center, scale_inv = norm_stats([merged], width_two)
    mlp_in = (merged - center) * scale_inv * mlp_gain_ref[...]
    pair_ref[:, :width_two] = mlp_in.astype(BF16)
    pair_ref[:, width_two:] = grad.astype(BF16)
    grad_ref[...] = grad


def merge_backward(
    place_ref, parts_ref, merged_ref, grad_ref, hidden_ref, cot_ref, places_ref, gain_ref,
    mlp_gain_ref, own_ref, got_ref, slab_ref, out_ref, weights, loaded,
):
    wait = section_load(place_ref, own_ref, got_ref, weights, loaded)
    width_two = merged_ref.shape[1]
    total = parts_ref[0].astype(F32)
    for index in range(1, parts_ref.shape[0]):
        total = total + parts_ref[index].astype(F32)
    merged = merged_ref[...].astype(F32)
    bottom = (merged + total[:, :width_two]).astype(BF16)
    wait()
    decoded = [
        hidden_ref[patch].astype(F32) + dot_nt(bottom, weights[4 + patch])
        for patch in range(4)
    ]
    by_row = places_ref[: slab_ref.shape[1], BY_ROW_PATCH : BY_ROW_PATCH + 1]
    upper, lower = (
        picked(by_row, jnp.concatenate([decoded[at], decoded[at + 1]], axis=0).astype(BF16))
        for at in (0, 2)
    )
    pair_slabs(upper, lower, slab_ref, 0)
    center, scale_inv = norm_stats([merged], width_two)
    unit = (merged - center) * scale_inv
    (back,) = norm_backward(
        [total[:, width_two:]], [mlp_gain_ref[...]], [unit], scale_inv, width_two
    )
    grad_merged = (grad_ref[...] + back).astype(BF16)
    hidden = [hidden_ref[patch].astype(F32) for patch in range(4)]
    center, scale_inv = norm_stats(hidden, 4 * hidden[0].shape[1])
    units = [(value - center) * scale_inv for value in hidden]
    backs = norm_backward(
        [dot_nt(grad_merged, weights[patch]) for patch in range(4)],
        [gain_ref[patch : patch + 1, :] for patch in range(4)],
        units,
        scale_inv,
        4 * hidden[0].shape[1],
    )
    grads = [(cot_ref[patch].astype(F32) + backs[patch]) for patch in range(4)]
    grads = jnp.concatenate(grads, axis=0).astype(BF16)
    tokens = out_ref.shape[0]
    out_ref[...] = picked(places_ref[:tokens, UNPATCH : UNPATCH + 1], grads).astype(BF16)


def decoded_rows(got_ref, places_ref, out_ref):
    places = places_ref[: got_ref.shape[0] * PADDED_COLUMNS, STAY : STAY + 1]
    for side in range(WIN_H):
        rows = slice(side * PADDED_COLUMNS, (side + 1) * PADDED_COLUMNS)
        values = got_ref[:, rows, :].reshape(-1, 2 * HDIM)
        both = spread_over(places, values, out_ref.shape[2])
        for index in range(2):
            out_ref[2 * side + index] = both[HDIM * index : HDIM * (index + 1)].astype(BF16)


def input_rows(shift_ref, got_ref, edge_ref, places_ref, out_ref, framed):
    places = places_ref[: got_ref.shape[0] * PADDED_COLUMNS, SHIFT : SHIFT + 1]
    for side in range(WIN_H):
        rows = slice(side * PADDED_COLUMNS, (side + 1) * PADDED_COLUMNS)
        both = spread_over(places, got_ref[:, rows, :].reshape(-1, 2 * HDIM), out_ref.shape[2])
        framed[WIN_H + side] = both[:HDIM]
        framed[2 * WIN_H + side] = both[HDIM:]
    for side in range(WIN_H // 2):
        rows = slice(side * PADDED_COLUMNS, (side + 1) * PADDED_COLUMNS)
        both = spread_over(places, edge_ref[:, rows, :].reshape(-1, 2 * HDIM), out_ref.shape[2])
        framed[side] = both[:HDIM]
        framed[WIN_H // 2 + side] = both[HDIM:]
    first = WIN_H - shift_ref[0]
    for row in range(out_ref.shape[0]):
        out_ref[row] = framed[first + row]


def shards(
    fields,
    first_gain,
    qkv_weight,
    proj_weight,
    merge_gain,
    merge_weight,
    mlp_gain,
    up_weight,
    down_weight,
    expand_weight,
    lat_shift,
    lon_shift,
    cotangent,
):
    n_lat, n_mp = lax.axis_size("lat"), lax.axis_size("mp")
    lat, core = lax.axis_index("lat"), lax.rem(lax.axis_index("lat"), 2)
    lat_offset = lat_shift[0]
    lon_offset = lon_shift[0]
    rows, lon_count, group = fields.shape
    width = group * n_mp
    block = lon_count // n_mp
    wide = block + WIN_W
    bands, columns = rows // WIN_H, block // WIN_W
    tokens = rows * block
    width_two = merge_weight.shape[2]
    span = up_weight.shape[1]
    merged_count = tokens // 4
    padded = -(-merged_count // 16) * 16
    others = range(n_mp)

    section = jnp.concatenate([merge_weight, expand_weight.transpose(1, 2, 0)], axis=0)

    blocks = fields.reshape(rows, n_mp, block, group).transpose(1, 0, 2, 3)
    margin = jnp.roll(blocks[:, :, :WIN_W], -1, axis=0)
    field_blocks = jnp.concatenate([blocks, margin], axis=2)
    body_slab = halves_beside(field_blocks.reshape(n_mp, rows * wide, group))
    edge_slab = halves_beside(field_blocks[:, :WIN_H].reshape(n_mp, WIN_H * wide, group))
    cot_blocks = cotangent.reshape(rows, n_mp, block, group).transpose(1, 0, 2, 3)
    cot_slab = halves_beside(cot_blocks.reshape(n_mp, tokens, group))
    weights = jnp.concatenate(
        [qkv_weight.transpose(1, 2, 0), proj_weight.transpose(1, 0)[None]], axis=0
    )
    gains = jnp.pad(jnp.concatenate([first_gain[None], merge_gain], axis=0), ((0, 3), (0, 64)))

    def rows_at(here, step):
        return pl.ds(pl.multiple_of(lax.rem(here["mp"] + n_mp - step, n_mp) * group, group), group)

    def own_rows(ref, here, target):
        return ref.at[:, rows_at(here, 0)]

    def own_quarter(size):
        return lambda ref, here, target: ref.at[pl.ds(size * here["quarter"], size)]

    def quarter_rows(size, step, extra, half=None):
        def part(ref, here, target):
            first = size * lax.rem(here["quarter"] + extra, 4)
            if half is None:
                return ref.at[pl.ds(first, size), rows_at(here, step)]
            if size > 1:
                return ref.at[first + half, rows_at(here, step)]
            count = group // 2
            at = lax.rem(here["mp"] + n_mp - step, n_mp) * group + half * count
            return ref.at[first, pl.ds(pl.multiple_of(at, count), count)]

        return part

    nearest_first = (2, 6, 1, 7, 4, 3, 5)
    gather_moves = [
        (source, own_quarter(size), source, quarter_rows(size, 0, 0), 0, step)
        for source, size in ((0, 2), (1, 1))
        for step in nearest_first
    ]
    relays, last_relays = [], []
    for source, size, first in ((0, 2, 0), (1, 1, n_mp - 1)):
        for index, step in enumerate(nearest_first):
            after = first + index
            for half, down in ((0, 4), (1, -4)):
                part = quarter_rows(size, step, 0, half)
                relays.append((source, part, source, part, down, 0, after))
                part = quarter_rows(size, step, 2, half)
                last_relays.append((source, part, source, part, "sibling", 0, len(relays) - 1))
            part = quarter_rows(size, step, 0)
            relays.append((source, part, source, part, "sibling", 0, after))
    places = place_table(lat_offset, lon_offset, rows, block, padded, n_mp)
    moves = (
        gather_moves
        + [(4, None, 4, "mp", 0, step) for step in others]
        + [(2, "mp", 2, "mp", 0, step) for step in others]
        + [(3, "mp", 3, "mp", -1, step) for step in others]
        + [(1, None, 1, own_rows, 0, 0)]
    )
    last_relays = [move[:6] + (move[6] + len(moves),) for move in last_relays]
    section_got, weights_all, body_got, edge_got, gains_all = exchange(
        1,
        [section, weights, body_slab, edge_slab, gains],
        [
            ((8, width, width_two), BF16),
            ((4, width, width), BF16),
            (body_slab.shape, BF16),
            (edge_slab.shape, BF16),
            ((n_mp,) + gains.shape, F32),
        ],
        moves + relays + last_relays,
    )
    has_shard = lax.rem(lax.axis_index("mp"), 2) == core
    first_all = gains_all[:, 0, :group].reshape(1, width)
    merge_gain_all = gains_all[:, 1:5, :group].transpose(1, 0, 2).reshape(4, width)
    mlp_gain_row = mlp_gain.reshape(1, width_two)
    cut = (jnp.int32(rows) * (n_lat - lat) - lat_offset).reshape(1)
    attention_framed, context, framed_fields, own_fields = local_kernel(
        attention_forward,
        [cut, body_got, edge_got, places, first_all, weights_all],
        [((tokens, width), BF16)] * 3 + [((4, padded, width), BF16)],
        [
            pltpu.VMEM((3, tokens, width), F32),
            pltpu.VMEM((tokens, width), F32),
            pltpu.VMEM(((rows + WIN_H) * wide, width), BF16),
        ],
        scalars=1,
    )
    window_shape = (bands, columns, WIN, width)
    around = (2 * bands + 2, WIN, width)

    halo, cot_got = exchange(
        2,
        [attention_framed.reshape(window_shape), cot_slab],
        [(around, BF16), (cot_slab.shape, BF16)],
        [
            (0, (bands - 1, columns - 1), 0, (0,), 1, 1),
            (0, (slice(0, bands), columns - 1), 0, (slice(1, 1 + bands),), 0, 1),
            (0, (bands - 1,), 0, (slice(1 + bands, 1 + bands + columns),), 1, 0),
        ]
        + [(1, "mp", 1, "mp", 0, step) for step in others],
    )
    n_x = n_mp // 2
    section_scratch = [
        pltpu.VMEM(section_got.shape, BF16),
        pltpu.SemaphoreType.DMA((2,)),
    ]
    pair, hidden, merged, grad_bottom, cot_patches = local_kernel(
        merge_forward,
        [
            lax.axis_index("mp").reshape(1),
            own_fields,
            attention_framed,
            halo.reshape(-1, width),
            cot_got,
            places,
            merge_gain_all,
            mlp_gain_row,
            section,
            section_got,
        ],
        [
            ((padded, 2 * width_two), BF16),
            ((4, padded, width), BF16),
            ((padded, width_two), BF16),
            ((padded, width_two), F32),
            ((4, padded, width), BF16),
        ],
        section_scratch + [pltpu.VMEM((tokens, width), F32)],
        scalars=1,
        outside=2,
    )

    def chip_spot(step):
        def spot(ref, here, target):
            return ref.at[lax.rem(here["x"] + n_x + step, n_x), here["core"]]

        return spot

    pairs, up_other, down_other = exchange(
        3,
        [pair, up_weight, down_weight],
        [
            ((n_x, 2) + pair.shape, BF16),
            (up_weight.shape, BF16),
            (down_weight.shape, BF16),
        ],
        [
            (0, None, 0, chip_spot(0), 0, 4),
            (0, None, 0, chip_spot(0), 0, 2),
            (0, None, 0, chip_spot(0), 0, -2),
            (0, None, 0, chip_spot(0), "sibling", 0),
            (0, None, 0, chip_spot(0), 0, 0),
            (1, None, 1, None, "flip", 0),
            (2, None, 2, None, "flip", 0),
            (0, chip_spot(-1), 0, chip_spot(-1), "sibling", 0, 1),
            (0, chip_spot(1), 0, chip_spot(1), "sibling", 0, 2),
            (0, chip_spot(-2), 0, chip_spot(-2), "sibling", 0, 0),
        ],
    )
    up_shard = jnp.where(has_shard, up_weight, up_other)
    down_shard = jnp.where(has_shard, down_weight, down_other)
    pairs = pairs.reshape(n_mp * padded, 2 * width_two)
    mlp_in, bottom_grad = pairs[:, :width_two], pairs[:, width_two:]
    hidden_up = jnp.dot(mlp_in, up_shard, preferred_element_type=F32)
    activated = jax.nn.gelu(hidden_up).astype(BF16)
    grad_act = jnp.dot(bottom_grad, down_shard, preferred_element_type=F32)
    gelu_back = jax.vjp(jax.nn.gelu, hidden_up)[1]
    grad_pre = gelu_back(grad_act)[0].astype(BF16)
    terms = jnp.concatenate(
        [
            jnp.einsum("af,ef->ae", activated, down_shard, preferred_element_type=F32),
            jnp.einsum("af,ef->ae", grad_pre, up_shard, preferred_element_type=F32),
        ],
        axis=1,
    ).astype(BF16)
    large = (n_lat, width_two // n_lat, span)
    parts, up_got, down_got = terms_back(
        4,
        terms.reshape(n_x, 2, padded, 2 * width_two),
        jnp.einsum("ae,af->ef", mlp_in, grad_pre, preferred_element_type=F32)
        .astype(BF16)
        .reshape(large),
        jnp.einsum("ao,af->of", bottom_grad, activated, preferred_element_type=F32)
        .astype(BF16)
        .reshape(large),
    )
    row_slab = (n_mp, WIN_H * PADDED_COLUMNS, 2 * group)
    decoded_slab, grad_windows = local_kernel(
        merge_backward,
        [
            lax.axis_index("mp").reshape(1),
            parts,
            merged,
            grad_bottom,
            hidden,
            cot_patches,
            places,
            merge_gain_all,
            mlp_gain_row,
            section,
            section_got,
        ],
        [(row_slab, BF16), ((tokens, width), BF16)],
        section_scratch,
        scalars=1,
        outside=2,
    )
    halo, decoded_got = exchange(
        5,
        [grad_windows.reshape(window_shape), decoded_slab],
        [(around, BF16), (decoded_slab.shape, BF16)],
        [
            (0, (0, 0), 0, (0,), -1, -1),
            (0, (slice(0, bands), 0), 0, (slice(1, 1 + bands),), 0, -1),
            (0, (0,), 0, (slice(1 + bands, 1 + bands + columns),), -1, 0),
        ]
        + [(1, "mp", 1, "mp", 0, step) for step in others],
    )
    grad_up = jnp.sum(up_got.astype(F32), axis=0)
    grad_down = jnp.sum(down_got.astype(F32), axis=0)
    grad_slab, grad_edge, weight_grads = local_kernel(
        attention_backward,
        [
            cut,
            framed_fields,
            first_all,
            weights_all,
            context,
            grad_windows,
            halo.reshape(-1, width),
            places,
        ],
        [
            (row_slab, BF16),
            ((n_mp, WIN_H * PADDED_COLUMNS // 2, 2 * group), BF16),
            ((4, width, width), BF16),
        ],
        [
            pltpu.VMEM((3, tokens, width), F32),
            pltpu.VMEM((3, tokens, width), F32),
            pltpu.VMEM((tokens, width), F32),
        ],
        scalars=1,
    )
    weight_total, grad_got, edge_got = gradients_out(6, weight_grads, grad_slab, grad_edge)
    grad_qkv = weight_total[:, : 3 * group].reshape(width // n_lat, 3, group)
    grad_proj = weight_total[:, 3 * group :]
    (decoded,) = local_kernel(
        decoded_rows, [decoded_got, places], [((rows, group, lon_count), BF16)]
    )
    (grad_input,) = local_kernel(
        input_rows,
        [lat_shift, grad_got, edge_got, places],
        [((rows, group, lon_count), F32)],
        [pltpu.VMEM((rows + WIN_H, group, lon_count), F32)],
        scalars=1,
    )
    decoded, grad_input = decoded.transpose(0, 2, 1), grad_input.transpose(0, 2, 1)
    return (decoded, grad_input, grad_qkv, grad_proj, grad_up, grad_down)


def solution(mesh):
    return jax.shard_map(
        shards,
        mesh=mesh,
        in_specs=(
            P("lat", None, "mp"),
            P("mp"),
            P(None, None, "mp"),
            P(None, "mp"),
            P(None, "mp"),
            P(None, "mp", None),
            P(),
            P(None, "mp"),
            P(None, "mp"),
            P(None, None, "mp"),
            P(),
            P(),
            P("lat", None, "mp"),
        ),
        out_specs=(
            P("lat", None, "mp"),
            P("lat", None, "mp"),
            P("lat", None, "mp"),
            P("lat", "mp"),
            P("lat", "mp"),
            P("lat", "mp"),
        ),
        check_vma=False,
    )
```

```python
import jax
import jax.numpy as jnp
import numpy as np
from jax import lax
from jax.experimental import pallas as pl
from jax.experimental.pallas import tpu as pltpu
from jax.sharding import PartitionSpec as P

WIN_H = 6
WIN_W = 12
HDIM = 64
EPSILON = 1e-05
MASKED = -1e30
BF16 = jnp.bfloat16
F32 = jnp.float32


def space_of(shape):
    return pltpu.VMEM if int(np.prod(shape)) <= 2 * 1024 * 1024 else pl.ANY


def positions():
    lat, mp = lax.axis_index("lat"), lax.axis_index("mp")
    return {
        "lat": lat,
        "mp": mp,
        "core": lax.rem(lat, 2),
        "x": lax.div(mp, 2),
        "z": lax.rem(mp, 2),
        "quarter": 2 * lax.rem(lax.div(lat, 4), 2) + lax.rem(lat, 2),
    }


def reached(here, down, right):
    n_lat, n_mp = lax.axis_size("lat"), lax.axis_size("mp")
    if down == "sibling":
        return {"lat": here["lat"] + 1 - 2 * here["core"], "mp": here["mp"]}
    if down == "flip":
        return {"lat": here["lat"], "mp": 2 * here["x"] + 1 - here["z"]}
    return {
        "lat": lax.rem(here["lat"] + n_lat + down, n_lat),
        "mp": lax.rem(here["mp"] + n_mp + right, n_mp),
    }


def device_of(target):
    return {
        "device_id": (target["lat"], target["mp"]),
        "device_id_type": pl.DeviceIdType.MESH,
    }


def greet(here, steps, owned=False):
    barrier = pltpu.get_barrier_semaphore()
    count = len(steps)
    if owned:
        n_lat, x, z = lax.axis_size("lat"), here["x"], here["z"]
        owner = z == here["core"]
        mine = 2 * lax.div(here["lat"], 2) + z
        count = count + n_lat - jnp.where(owner, 1, 0)
        for source in range(n_lat):

            @pl.when(jnp.logical_or(jnp.logical_not(owner), mine != source))
            def _():
                target = {"lat": 2 * (source // 2) + z, "mp": 2 * x + source % 2}
                pl.semaphore_signal(barrier, inc=1, **device_of(target))

    for down, right in steps:
        source = reached(here, down if isinstance(down, str) else -down, -right)
        pl.semaphore_signal(barrier, inc=1, **device_of(source))
    pl.semaphore_wait(barrier, count)


def to_owners(here, source, landing, send, receive):
    n_lat = lax.axis_size("lat")
    lat, core, x, z = here["lat"], here["core"], here["x"], here["z"]
    mine = 2 * lax.div(lat, 2) + z
    owner = z == core

    def copy_at(step):
        target = {"lat": lax.rem(lat + step, n_lat), "mp": 2 * x + core}
        rows = target["lat"]
        return remote(source.at[rows], landing.at[mine], send.at[step], receive.at[mine], target)

    def start():
        for step in range(1, n_lat):
            copy_at(step).start()

        @pl.when(owner)
        def _():
            pltpu.make_async_copy(source.at[lat], landing.at[mine], receive.at[mine]).start()

        @pl.when(jnp.logical_not(owner))
        def _():
            copy_at(0).start()

    def wait():
        sibling = reached(here, "sibling", 0)
        for slot in range(n_lat):
            remote(
                source.at[slot], landing.at[slot], send.at[slot], receive.at[slot], sibling
            ).wait_recv()
        for step in range(1, n_lat):
            copy_at(step).wait_send()

        @pl.when(jnp.logical_not(owner))
        def _():
            copy_at(0).wait_send()

    return start, wait


def remote(source, landing, send, receive, target):
    return pltpu.make_async_remote_copy(
        src_ref=source, dst_ref=landing, send_sem=send, recv_sem=receive, **device_of(target)
    )


def exchange(collective, inputs, outputs, moves, owned=()):
    n_lat = lax.axis_size("lat")
    steps = []
    for move in moves:
        if move[4:6] != (0, 0) and move[4:6] not in steps:
            steps.append(move[4:6])

    def body(*refs):
        sources = refs[: len(inputs)]
        landings = refs[len(inputs) : len(inputs) + len(outputs)]
        send, receive, owned_send, owned_receive = refs[-4:]
        here = positions()

        def part_of(ref, part, place, target):
            if part is None:
                return ref
            if isinstance(part, str):
                return ref.at[place[part]]
            if callable(part):
                return part(ref, here, target)
            return ref.at[part]

        greet(here, steps, bool(owned))
        copies = []
        arrived = set()
        scatters = [
            to_owners(
                here, sources[one], landings[two], owned_send.at[index], owned_receive.at[index]
            )
            for index, (one, two) in enumerate(owned)
        ]
        for index, move in enumerate(moves):
            source, source_part, landing, landing_part, down, right = move[:6]
            target = reached(here, down, right)
            if len(move) > 6:
                if move[6] not in arrived:
                    copies[move[6]].wait_recv()
                    arrived.add(move[6])
                source_ref = part_of(landings[source], source_part, target, target)
            else:
                source_ref = part_of(sources[source], source_part, target, target)
            landing_ref = part_of(landings[landing], landing_part, here, target)
            if (down, right) == (0, 0):
                copy = pltpu.make_async_copy(source_ref, landing_ref, receive.at[index])
            else:
                copy = remote(
                    source_ref, landing_ref, send.at[index], receive.at[index], target
                )
            if down == "flip":
                pl.when(here["z"] == here["core"])(copy.start)
            else:
                copy.start()
            copies.append(copy)
        for start, _ in scatters:
            start()
        for _, wait in scatters:
            wait()
        for index, copy in enumerate(copies):
            if moves[index][4:6] == (0, 0):
                copy.wait()
            elif moves[index][4] == "flip":
                pl.when(here["z"] == here["core"])(copy.wait_send)
                pl.when(here["z"] != here["core"])(copy.wait_recv)
            else:
                copy.wait_send()
                if index not in arrived:
                    copy.wait_recv()

    return pl.pallas_call(
        body,
        out_shape=[jax.ShapeDtypeStruct(shape, dtype) for shape, dtype in outputs],
        in_specs=[pl.BlockSpec(memory_space=pl.ANY)] * len(inputs),
        out_specs=[pl.BlockSpec(memory_space=space_of(shape)) for shape, _ in outputs],
        scratch_shapes=[
            pltpu.SemaphoreType.DMA((len(moves),)),
            pltpu.SemaphoreType.DMA((len(moves),)),
            pltpu.SemaphoreType.DMA((max(len(owned), 1), n_lat)),
            pltpu.SemaphoreType.DMA((max(len(owned), 1), n_lat)),
        ],
        compiler_params=pltpu.CompilerParams(
            collective_id=collective, has_side_effects=True, vmem_limit_bytes=32 * 1024 * 1024
        ),
    )(*inputs)


X_STEPS = ((4, 2), (2, 1), (-2, 3))


def terms_back(collective, terms, backs, up_grads, down_grads):
    count, _, rows, width = terms.shape
    n_lat = lax.axis_size("lat")
    both = range(2)

    def body(
        terms_ref, backs_ref, up_ref, down_ref, parts_ref, up_got, down_got,
        other, own, total, send, receive, fetch, large_send, large_receive,
    ):
        here = positions()
        core, x = here["core"], here["x"]
        sibling = reached(here, "sibling", 0)
        greet(here, [("sibling", 0)] + [(0, right) for right, _ in X_STEPS], True)
        scatters = [
            to_owners(here, source, landing, large_send.at[index], large_receive.at[index])
            for index, (source, landing) in enumerate(((up_ref, up_got), (down_ref, down_got)))
        ]
        order = [lax.rem(x + step, count) for _, step in X_STEPS] + [x]
        swaps, loads = [], []
        for index, spot in enumerate(order):
            for which, source in enumerate((terms_ref, backs_ref)):
                swap = remote(
                    source.at[spot, 1 - core],
                    other.at[which, index],
                    send.at[2 * index + which],
                    receive.at[2 * index + which],
                    sibling,
                )
                load = pltpu.make_async_copy(
                    source.at[spot, core], own.at[which, index], fetch.at[2 * index + which]
                )
                swap.start()
                load.start()
                swaps.append(swap)
                loads.append(load)
        for start, _ in scatters:
            start()
        sends = []
        for index, spot in enumerate(order):
            for which in both:
                loads[2 * index + which].wait()
                swaps[2 * index + which].wait_recv()
                summed = own[which, index].astype(F32) + other[which, index].astype(F32)
                total[index, :, width * which : width * (which + 1)] = summed.astype(BF16)
            if index < len(X_STEPS):
                copy = remote(
                    total.at[index],
                    parts_ref.at[x],
                    send.at[2 * count + index],
                    receive.at[2 * count + index],
                    reached(here, 0, X_STEPS[index][0]),
                )
            else:
                copy = pltpu.make_async_copy(total.at[index], parts_ref.at[x], fetch.at[2 * count])
            copy.start()
            sends.append(copy)
        for swap in swaps:
            swap.wait_send()
        for copy in sends:
            copy.wait()
        for _, wait in scatters:
            wait()

    return pl.pallas_call(
        body,
        out_shape=[
            jax.ShapeDtypeStruct((count, rows, 2 * width), BF16),
            jax.ShapeDtypeStruct(up_grads.shape, BF16),
            jax.ShapeDtypeStruct(down_grads.shape, BF16),
        ],
        in_specs=[pl.BlockSpec(memory_space=pl.ANY)] * 4,
        out_specs=[
            pl.BlockSpec(memory_space=pltpu.VMEM),
            pl.BlockSpec(memory_space=pl.ANY),
            pl.BlockSpec(memory_space=pl.ANY),
        ],
        scratch_shapes=[
            pltpu.VMEM((2, count, rows, width), BF16),
            pltpu.VMEM((2, count, rows, width), BF16),
            pltpu.VMEM((count, rows, 2 * width), BF16),
            pltpu.SemaphoreType.DMA((3 * count,)),
            pltpu.SemaphoreType.DMA((3 * count,)),
            pltpu.SemaphoreType.DMA((2 * count + 1,)),
            pltpu.SemaphoreType.DMA((2, n_lat)),
            pltpu.SemaphoreType.DMA((2, n_lat)),
        ],
        compiler_params=pltpu.CompilerParams(
            collective_id=collective, has_side_effects=True, vmem_limit_bytes=48 * 1024 * 1024
        ),
    )(terms, backs, up_grads, down_grads)


def gradients_out(collective, weight_grads, slabs, edges, decoded_slabs):
    n_lat, n_mp = lax.axis_size("lat"), lax.axis_size("mp")
    kinds, width, _ = weight_grads.shape
    pair, group, share = kinds // 2, width // n_mp, width // n_lat

    def body(
        weight_ref, slab_ref, edge_ref, decoded_ref, out_ref, got_ref, edge_got, decoded_got,
        other, total, parts, turned, landed, send, receive,
    ):
        here = positions()
        lat, mp, core = here["lat"], here["mp"], here["core"]
        sibling = reached(here, "sibling", 0)
        barrier = pltpu.get_barrier_semaphore()
        greeted = [sibling]
        greeted += [reached(here, 0, -step) for step in range(1, n_mp)]
        greeted += [reached(here, -1, -step) for step in range(n_mp)]
        greeted += [reached(here, -step, 0) for step in range(1, n_lat)]
        for target in greeted:
            pl.semaphore_signal(barrier, inc=1, **device_of(target))
        pl.semaphore_wait(barrier, len(greeted))

        copies = []

        def sent(source, landing, target):
            index = len(copies)
            copy = remote(source, landing, send.at[index], receive.at[index], target)
            copy.start()
            copies.append(copy)
            return copy

        swap = sent(weight_ref.at[pl.ds(pair * (1 - core), pair)], other, sibling)
        for step in range(1, n_mp):
            target = reached(here, 0, step)
            sent(decoded_ref.at[target["mp"]], decoded_got.at[mp], target)
        own_slab = pltpu.make_async_copy(slab_ref.at[mp], got_ref.at[mp], send.at[60])
        own_slab.start()
        own_decoded = pltpu.make_async_copy(decoded_ref.at[mp], decoded_got.at[mp], send.at[61])
        own_decoded.start()

        swap.wait_recv()
        total[...] = (
            weight_ref[pl.ds(pair * core, pair)].astype(F32) + other[...].astype(F32)
        ).astype(BF16)
        scattered = []
        for step in range(1, n_mp):
            target = reached(here, 0, step)
            rows = pl.ds(pl.multiple_of(group * target["mp"], group), group)
            scattered.append(sent(total.at[:, rows], parts.at[mp], target))
        for step in range(1, n_mp):
            target = reached(here, 0, step)
            sent(slab_ref.at[target["mp"]], got_ref.at[mp], target)
        for step in range(n_mp):
            target = reached(here, 1, step)
            sent(edge_ref.at[target["mp"]], edge_got.at[mp], target)
        gathered = total[:, pl.ds(pl.multiple_of(group * mp, group), group), :].astype(F32)
        for step in range(1, n_mp):
            scattered[step - 1].wait_recv()
            gathered = gathered + parts[lax.rem(mp + n_mp - step, n_mp)].astype(F32)
        flat = gathered.reshape(pair * group, width).T.astype(BF16)
        for index in range(n_lat):
            turned[index] = flat[index * share : (index + 1) * share]
        spread = []
        for step in range(1, n_lat):
            target = reached(here, step, 0)
            spread.append(sent(turned.at[target["lat"]], landed.at[lat], target))
        landed[lat] = turned[lat]
        for copy in spread:
            copy.wait_recv()
        for half in range(2):
            result = landed[half].astype(F32)
            for index in range(half + 2, n_lat, 2):
                result = result + landed[index].astype(F32)
            out_ref[:, half * pair * group : (half + 1) * pair * group] = result

        done = [swap] + scattered + spread
        for copy in copies:
            copy.wait_send()
            if not any(copy is other_copy for other_copy in done):
                copy.wait_recv()
        own_slab.wait()
        own_decoded.wait()

    any_space = pl.BlockSpec(memory_space=pl.ANY)
    vmem = pl.BlockSpec(memory_space=pltpu.VMEM)
    return pl.pallas_call(
        body,
        out_shape=[
            jax.ShapeDtypeStruct((share, kinds * group), F32),
            jax.ShapeDtypeStruct(slabs.shape, BF16),
            jax.ShapeDtypeStruct(edges.shape, BF16),
            jax.ShapeDtypeStruct(decoded_slabs.shape, BF16),
        ],
        in_specs=[vmem, any_space, any_space, any_space],
        out_specs=[vmem, vmem, vmem, vmem],
        scratch_shapes=[
            pltpu.VMEM((pair, width, width), BF16),
            pltpu.VMEM((pair, width, width), BF16),
            pltpu.VMEM((n_mp, pair, group, width), BF16),
            pltpu.VMEM((n_lat, share, pair * group), BF16),
            pltpu.VMEM((n_lat, share, pair * group), BF16),
            pltpu.SemaphoreType.DMA((64,)),
            pltpu.SemaphoreType.DMA((64,)),
        ],
        compiler_params=pltpu.CompilerParams(
            collective_id=collective, has_side_effects=True, vmem_limit_bytes=48 * 1024 * 1024
        ),
    )(weight_grads, slabs, edges, decoded_slabs)


def local_kernel(body, operands, outputs, scratch=(), scalars=0, outside=0, grant=48):
    spaces = [pltpu.SMEM] * scalars + [pltpu.VMEM] * (len(operands) - scalars - outside)
    spaces += [pl.ANY] * outside
    return pl.pallas_call(
        body,
        out_shape=[jax.ShapeDtypeStruct(shape, dtype) for shape, dtype in outputs],
        in_specs=[pl.BlockSpec(memory_space=space) for space in spaces],
        out_specs=[pl.BlockSpec(memory_space=pltpu.VMEM)] * len(outputs),
        scratch_shapes=list(scratch),
        compiler_params=pltpu.CompilerParams(vmem_limit_bytes=grant * 1024 * 1024),
    )(*operands)


def dot_nn(left, right):
    return lax.dot_general(left, right, (((1,), (0,)), ((), ())), preferred_element_type=F32)


def dot_nt(left, right):
    return lax.dot_general(left, right, (((1,), (1,)), ((), ())), preferred_element_type=F32)


def dot_tn(left, right):
    return lax.dot_general(left, right, (((0,), (0,)), ((), ())), preferred_element_type=F32)


def halves_beside(values):
    half = values.shape[-2] // 2
    return jnp.concatenate([values[..., :half, :], values[..., half:, :]], axis=-1)


def picked(places, values):
    spots = lax.broadcasted_iota(jnp.int32, (places.shape[0], values.shape[0]), 1)
    return dot_nn(jnp.where(spots == places, 1.0, 0.0).astype(BF16), values)


def spread_over(places, values, count):
    spots = lax.broadcasted_iota(jnp.int32, (places.shape[0], count), 1)
    return dot_tn(values, jnp.where(spots == places, 1.0, 0.0).astype(BF16))


def swapped(values):
    return jnp.concatenate([values[:, HDIM:], values[:, :HDIM]], axis=1)


def join_slabs(slab_ref, out_ref, first_rows, second_rows):
    half = slab_ref.shape[1]
    low = lax.broadcasted_iota(jnp.int32, (half, 2 * HDIM), 1) < HDIM
    for pair in range(slab_ref.shape[0] // 2):
        lanes = slice(2 * HDIM * pair, 2 * HDIM * (pair + 1))
        one = slab_ref[2 * pair].astype(F32)
        two = slab_ref[2 * pair + 1].astype(F32)
        first = jnp.where(low, one, swapped(two)).astype(out_ref.dtype)
        second = jnp.where(low, swapped(one), two).astype(out_ref.dtype)
        out_ref[first_rows : first_rows + half, lanes] = first
        out_ref[second_rows : second_rows + half, lanes] = second


PADDED_COLUMNS = 48
FRAME, OWN, BACK, BACK_HALO, COT, UNPATCH, GRAD, GRAD_HALO, BY_ROW, BY_ROW_PATCH, SHIFT, STAY = range(12)


def place_table(lat_offset, lon_offset, rows, block, padded, n_mp):
    columns = block // WIN_W
    size = max(rows * block, 4 * padded, n_mp * PADDED_COLUMNS)
    token = np.arange(rows * block)
    window, spot = token // WIN, token % WIN
    row = (window // columns) * WIN_H + spot // WIN_W
    column = (window % columns) * WIN_W + spot % WIN_W
    patch, at = np.arange(4 * padded) // padded, np.arange(4 * padded) % padded
    real = at < rows * block // 4
    prow = 2 * (at // (block // 2)) + patch // 2
    pcolumn = 2 * (at % (block // 2)) + patch % 2
    side = np.arange(WIN_H * PADDED_COLUMNS) // PADDED_COLUMNS
    spot = np.arange(WIN_H * PADDED_COLUMNS) % PADDED_COLUMNS
    shown = spot < block
    group = np.arange(n_mp * PADDED_COLUMNS) // PADDED_COLUMNS
    place = np.arange(n_mp * PADDED_COLUMNS) % PADDED_COLUMNS
    inside = place < block
    unpatch = (2 * (row % 2) + column % 2) * padded + (row // 2) * (block // 2) + column // 2
    by_row = (spot // WIN_W) * WIN + side * WIN_W + spot % WIN_W
    by_row_patch = (spot % 2) * padded + side * (block // 2) + spot // 2
    lon = group * block + place
    wide = block + WIN_W
    source = {
        FRAME: (row, column, True, wide),
        OWN: (prow, pcolumn, real, wide),
        BACK: (prow, pcolumn, real, 0),
        BACK_HALO: (prow, pcolumn, real, 0),
        COT: (prow, pcolumn, real, block),
        UNPATCH: (0, unpatch, True, 0),
        GRAD: (row, column, True, 0),
        GRAD_HALO: (row, column, True, 0),
        BY_ROW: (0, by_row, shown, 0),
        BY_ROW_PATCH: (0, by_row_patch, shown, 0),
        SHIFT: (0, lon, inside, 0),
        STAY: (0, lon, inside, 0),
    }
    shape = (size, len(source))
    row_at, column_at, pitch = (np.zeros(shape, np.int32) for _ in range(3))
    valid = np.zeros(shape, bool)
    for key, (row_part, column_part, part, step) in source.items():
        count = column_part.shape[0]
        row_at[:count, key], column_at[:count, key], pitch[:, key] = row_part, column_part, step
        valid[:count, key] = part
    kind = np.arange(len(source))[None]
    back = np.isin(kind, (BACK, BACK_HALO))
    grad = np.isin(kind, (GRAD, GRAD_HALO))
    row_sign = np.where(back, -1, np.where(grad | (kind == FRAME), 1, 0)).astype(np.int32)
    column_sign = np.where(kind == SHIFT, 1, row_sign).astype(np.int32)
    row_at = row_at + row_sign * lat_offset
    column_at = column_at + column_sign * lon_offset
    straight = row_at * pitch + column_at
    full = n_mp * block
    straight = jnp.where((kind == SHIFT) & (straight >= full), straight - full, straight)
    down = jnp.where(back, row_at < 0, row_at >= rows)
    right = jnp.where(back, column_at < 0, column_at >= block)
    row_in = jnp.where(down, row_at + np.where(back, WIN_H, -rows).astype(np.int32), row_at)
    column_in = jnp.where(
        right, column_at + np.where(back, WIN_W, -block).astype(np.int32), column_at
    )
    band, slot = lax.div(row_in, jnp.int32(WIN_H)), lax.div(column_in, jnp.int32(WIN_W))
    halo_slot = jnp.where(down, jnp.where(right, 0, 3 + slot), 1 + band)
    outside = jnp.logical_or(down, right)
    halo = np.isin(kind, (BACK_HALO, GRAD_HALO))
    tile = jnp.where(halo, halo_slot, band * columns + slot)
    windowed = tile * WIN + (row_in - band * WIN_H) * WIN_W + column_in - slot * WIN_W
    result = jnp.where(back | grad, windowed, straight)
    hidden = (back | grad) & jnp.where(halo, jnp.logical_not(outside), outside)
    return jnp.where(valid & jnp.logical_not(hidden), result, -1).astype(jnp.int32)


def norm_stats(values, count):
    center = sum(jnp.sum(value, axis=1, keepdims=True) for value in values) / count
    second = sum(jnp.sum(value * value, axis=1, keepdims=True) for value in values) / count
    return (center, lax.rsqrt(second - center * center + EPSILON))


def norm_backward(grads, gains, units, scale_inv, count):
    scaled = [grad * gain for grad, gain in zip(grads, gains)]
    first = sum(jnp.sum(value, axis=1, keepdims=True) for value in scaled) / count
    second = (
        sum(jnp.sum(value * unit, axis=1, keepdims=True) for value, unit in zip(scaled, units))
        / count
    )
    return [scale_inv * (value - first - unit * second) for value, unit in zip(scaled, units)]


def pair_slabs(upper, lower, out_ref, first_rows):
    low = lax.broadcasted_iota(jnp.int32, (upper.shape[0], 2 * HDIM), 1) < HDIM
    rows = pl.ds(first_rows, upper.shape[0])
    for pair in range(upper.shape[1] // (2 * HDIM)):
        lanes = slice(2 * HDIM * pair, 2 * HDIM * (pair + 1))
        one, two = upper[:, lanes], lower[:, lanes]
        out_ref[2 * pair, rows, :] = jnp.where(low, one, swapped(two)).astype(BF16)
        out_ref[2 * pair + 1, rows, :] = jnp.where(low, swapped(one), two).astype(BF16)


WIN = WIN_H * WIN_W
FACTOR = HDIM ** (-0.5)


def heads_apart(values):
    low = lax.broadcasted_iota(jnp.int32, values.shape, 1) < HDIM
    zero = jnp.zeros_like(values)
    both = [jnp.where(low, values, zero), jnp.where(low, zero, values)]
    return jnp.concatenate(both, axis=0).astype(BF16)


def heads_together(values):
    low = lax.broadcasted_iota(jnp.int32, (WIN, 2 * HDIM), 1) < HDIM
    return jnp.where(low, values[:WIN], values[WIN:])


def window_probs(cut, window, query, keys):
    scores = dot_nt(query, keys) * FACTOR
    spot = lax.broadcasted_iota(jnp.int32, scores.shape, 0)
    spot = jnp.where(spot >= WIN, spot - WIN, spot)
    other = lax.broadcasted_iota(jnp.int32, scores.shape, 1)
    edge = cut * WIN_W - jnp.where(window >= 3, WIN, 0)
    same = (spot >= edge) == (other >= edge)
    scores = jnp.where(same, scores, MASKED)
    weights = jnp.exp(scores - jnp.max(scores, axis=1, keepdims=True))
    return weights / jnp.sum(weights, axis=1, keepdims=True)


def framed_packed(fields_ref, gain_ref, weights_ref, packed):
    values = fields_ref[...].astype(F32)
    center, scale_inv = norm_stats([values], values.shape[1])
    unit = (values - center) * scale_inv
    framed = (unit * gain_ref[...]).astype(BF16)
    for kind in range(3):
        packed[kind] = dot_nt(framed, weights_ref[kind]).astype(BF16).astype(F32)
    return (framed, unit, scale_inv)


def window_parts(refs, window, pair):
    rows = pl.ds(pl.multiple_of(window * WIN, 8), WIN)
    lanes = slice(2 * HDIM * pair, 2 * HDIM * (pair + 1))
    return [ref[rows, lanes] for ref in refs]


def attention_forward(
    cut_ref, body_ref, edge_ref, places_ref, gain_ref, weights_ref,
    out_ref, context_ref, fields_ref, own_ref, packed, held, grid,
):
    half, rest = body_ref.shape[1], edge_ref.shape[1]
    join_slabs(body_ref, grid, 0, half)
    join_slabs(edge_ref, grid, 2 * half, 2 * half + rest)
    tokens = fields_ref.shape[0]
    whole = grid[...]
    fields_ref[...] = picked(places_ref[:tokens, FRAME : FRAME + 1], whole).astype(BF16)
    padded = own_ref.shape[1]
    for patch in range(4):
        rows = slice(padded * patch, padded * (patch + 1))
        own_ref[patch] = picked(places_ref[rows, OWN : OWN + 1], whole).astype(BF16)
    framed_packed(fields_ref, gain_ref, weights_ref, packed)
    cut = cut_ref[0]
    windows = fields_ref.shape[0] // WIN

    def step(window, carry):
        rows = pl.ds(pl.multiple_of(window * WIN, 8), WIN)
        for pair in range(fields_ref.shape[1] // (2 * HDIM)):
            query, keys, values = window_parts([packed.at[kind] for kind in range(3)], window, pair)
            probs = window_probs(cut, window, heads_apart(query), keys.astype(BF16))
            joined = dot_nn(probs.astype(BF16), values.astype(BF16))
            held[rows, 2 * HDIM * pair : 2 * HDIM * (pair + 1)] = heads_together(joined)
        return carry

    lax.fori_loop(0, windows, step, 0)
    context = held[...].astype(BF16)
    context_ref[...] = context
    out_ref[...] = dot_nn(context, weights_ref[3]).astype(BF16)


def attention_backward(
    cut_ref, fields_ref, gain_ref, weights_ref, context_ref, grad_ref, halo_ref, places_ref,
    slab_ref, edge_ref, weight_ref, packed, grads, held,
):
    framed, unit, scale_inv = framed_packed(fields_ref, gain_ref, weights_ref, packed)
    cut = cut_ref[0]
    windows = fields_ref.shape[0] // WIN
    tokens = fields_ref.shape[0]
    grad_framed = (
        picked(places_ref[:tokens, GRAD : GRAD + 1], grad_ref[...])
        + picked(places_ref[:tokens, GRAD_HALO : GRAD_HALO + 1], halo_ref[...])
    ).astype(BF16)
    held[...] = dot_nt(grad_framed, weights_ref[3]).astype(BF16).astype(F32)

    def step(window, carry):
        rows = pl.ds(pl.multiple_of(window * WIN, 8), WIN)
        for pair in range(fields_ref.shape[1] // (2 * HDIM)):
            lanes = slice(2 * HDIM * pair, 2 * HDIM * (pair + 1))
            query, keys, values, grad = window_parts(
                [packed.at[kind] for kind in range(3)] + [held], window, pair
            )
            query, grad = heads_apart(query), heads_apart(grad)
            keys, values = keys.astype(BF16), values.astype(BF16)
            probs = window_probs(cut, window, query, keys)
            grad_probs = dot_nt(grad, values)
            inner = jnp.sum(grad_probs * probs, axis=1, keepdims=True)
            grad_scores = (probs * (grad_probs - inner) * FACTOR).astype(BF16)
            grads[0, rows, lanes] = heads_together(dot_nn(grad_scores, keys))
            grads[1, rows, lanes] = dot_tn(grad_scores, query)
            grads[2, rows, lanes] = dot_tn(probs.astype(BF16), grad)
        return carry

    lax.fori_loop(0, windows, step, 0)
    grad_normed = jnp.zeros(fields_ref.shape, F32)
    for kind in range(3):
        grad_kind = grads[kind].astype(BF16)
        weight_ref[kind] = dot_tn(grad_kind, framed).astype(BF16)
        grad_normed = grad_normed + dot_nn(grad_kind, weights_ref[kind])
    weight_ref[3] = dot_tn(context_ref[...], grad_framed).astype(BF16)
    (back,) = norm_backward([grad_normed], [gain_ref[...]], [unit], scale_inv, unit.shape[1])
    result = grad_framed.astype(F32) + back
    half = result.shape[0] // 2
    by_row = places_ref[: slab_ref.shape[1], BY_ROW : BY_ROW + 1]
    upper, lower = (picked(by_row, part.astype(BF16)) for part in (result[:half], result[half:]))
    pair_slabs(upper, lower, slab_ref, 0)
    half = edge_ref.shape[1]
    pair_slabs(lower[:half], lower[half:], edge_ref, 0)


def section_load(place_ref, own_ref, got_ref, weights, loaded):
    whole = pltpu.make_async_copy(got_ref, weights, loaded.at[0])
    whole.start()

    def wait():
        whole.wait()
        count = own_ref.shape[1]
        rows = pl.ds(pl.multiple_of(place_ref[0] * count, count), count)
        own = pltpu.make_async_copy(own_ref, weights.at[:, rows], loaded.at[1])
        own.start()
        own.wait()

    return wait


def merge_forward(
    place_ref, fields_ref, attention_ref, halo_ref, cot_got_ref, places_ref, gain_ref,
    mlp_gain_ref, own_ref, got_ref,
    pair_ref, hidden_ref, merged_ref, grad_ref, cot_ref, weights, loaded, joined,
):
    wait = section_load(place_ref, own_ref, got_ref, weights, loaded)
    width_two = merged_ref.shape[1]
    join_slabs(cot_got_ref, joined, 0, cot_got_ref.shape[1])
    cot = joined[...].astype(BF16)
    padded = merged_ref.shape[0]
    hidden = []
    for patch in range(4):
        rows = slice(padded * patch, padded * (patch + 1))
        cot_ref[patch] = picked(places_ref[rows, COT : COT + 1], cot).astype(BF16)
        attention = picked(places_ref[rows, BACK : BACK + 1], attention_ref[...])
        attention = attention + picked(
            places_ref[rows, BACK_HALO : BACK_HALO + 1], halo_ref[...]
        )
        value = fields_ref[patch].astype(F32) + attention
        hidden_ref[patch] = value.astype(BF16)
        hidden.append(value.astype(BF16).astype(F32))
    center, scale_inv = norm_stats(hidden, 4 * hidden[0].shape[1])
    merged = jnp.zeros(merged_ref.shape, F32)
    grad = jnp.zeros(merged_ref.shape, F32)
    wait()
    for patch in range(4):
        normed = (hidden[patch] - center) * scale_inv * gain_ref[patch : patch + 1, :]
        merged = merged + dot_nn(normed.astype(BF16), weights[patch])
        grad = grad + dot_nn(cot_ref[patch], weights[4 + patch])
    merged_ref[...] = merged.astype(BF16)
    merged = merged.astype(BF16).astype(F32)
    center, scale_inv = norm_stats([merged], width_two)
    mlp_in = (merged - center) * scale_inv * mlp_gain_ref[...]
    pair_ref[:, :width_two] = mlp_in.astype(BF16)
    pair_ref[:, width_two:] = grad.astype(BF16)
    grad_ref[...] = grad


def merge_backward(
    place_ref, parts_ref, merged_ref, grad_ref, hidden_ref, cot_ref, places_ref, gain_ref,
    mlp_gain_ref, own_ref, got_ref, slab_ref, out_ref, weights, loaded,
):
    wait = section_load(place_ref, own_ref, got_ref, weights, loaded)
    width_two = merged_ref.shape[1]
    total = parts_ref[0].astype(F32)
    for index in range(1, parts_ref.shape[0]):
        total = total + parts_ref[index].astype(F32)
    merged = merged_ref[...].astype(F32)
    bottom = (merged + total[:, :width_two]).astype(BF16)
    wait()
    decoded = [
        hidden_ref[patch].astype(F32) + dot_nt(bottom, weights[4 + patch])
        for patch in range(4)
    ]
    by_row = places_ref[: slab_ref.shape[1], BY_ROW_PATCH : BY_ROW_PATCH + 1]
    upper, lower = (
        picked(by_row, jnp.concatenate([decoded[at], decoded[at + 1]], axis=0).astype(BF16))
        for at in (0, 2)
    )
    pair_slabs(upper, lower, slab_ref, 0)
    center, scale_inv = norm_stats([merged], width_two)
    unit = (merged - center) * scale_inv
    (back,) = norm_backward(
        [total[:, width_two:]], [mlp_gain_ref[...]], [unit], scale_inv, width_two
    )
    grad_merged = (grad_ref[...] + back).astype(BF16)
    hidden = [hidden_ref[patch].astype(F32) for patch in range(4)]
    center, scale_inv = norm_stats(hidden, 4 * hidden[0].shape[1])
    units = [(value - center) * scale_inv for value in hidden]
    backs = norm_backward(
        [dot_nt(grad_merged, weights[patch]) for patch in range(4)],
        [gain_ref[patch : patch + 1, :] for patch in range(4)],
        units,
        scale_inv,
        4 * hidden[0].shape[1],
    )
    grads = [(cot_ref[patch].astype(F32) + backs[patch]) for patch in range(4)]
    grads = jnp.concatenate(grads, axis=0).astype(BF16)
    tokens = out_ref.shape[0]
    out_ref[...] = picked(places_ref[:tokens, UNPATCH : UNPATCH + 1], grads).astype(BF16)


def decoded_rows(got_ref, places_ref, out_ref):
    places = places_ref[: got_ref.shape[0] * PADDED_COLUMNS, STAY : STAY + 1]
    for side in range(WIN_H):
        rows = slice(side * PADDED_COLUMNS, (side + 1) * PADDED_COLUMNS)
        values = got_ref[:, rows, :].reshape(-1, 2 * HDIM)
        both = spread_over(places, values, out_ref.shape[2])
        for index in range(2):
            out_ref[2 * side + index] = both[HDIM * index : HDIM * (index + 1)].astype(BF16)


def input_rows(shift_ref, got_ref, edge_ref, places_ref, out_ref, framed):
    places = places_ref[: got_ref.shape[0] * PADDED_COLUMNS, SHIFT : SHIFT + 1]
    for side in range(WIN_H):
        rows = slice(side * PADDED_COLUMNS, (side + 1) * PADDED_COLUMNS)
        both = spread_over(places, got_ref[:, rows, :].reshape(-1, 2 * HDIM), out_ref.shape[2])
        framed[WIN_H + side] = both[:HDIM]
        framed[2 * WIN_H + side] = both[HDIM:]
    for side in range(WIN_H // 2):
        rows = slice(side * PADDED_COLUMNS, (side + 1) * PADDED_COLUMNS)
        both = spread_over(places, edge_ref[:, rows, :].reshape(-1, 2 * HDIM), out_ref.shape[2])
        framed[side] = both[:HDIM]
        framed[WIN_H // 2 + side] = both[HDIM:]
    first = WIN_H - shift_ref[0]
    for row in range(out_ref.shape[0]):
        out_ref[row] = framed[first + row]


def shards(
    fields,
    first_gain,
    qkv_weight,
    proj_weight,
    merge_gain,
    merge_weight,
    mlp_gain,
    up_weight,
    down_weight,
    expand_weight,
    lat_shift,
    lon_shift,
    cotangent,
):
    n_lat, n_mp = lax.axis_size("lat"), lax.axis_size("mp")
    lat, core = lax.axis_index("lat"), lax.rem(lax.axis_index("lat"), 2)
    lat_offset = lat_shift[0]
    lon_offset = lon_shift[0]
    rows, lon_count, group = fields.shape
    width = group * n_mp
    block = lon_count // n_mp
    wide = block + WIN_W
    bands, columns = rows // WIN_H, block // WIN_W
    tokens = rows * block
    width_two = merge_weight.shape[2]
    span = up_weight.shape[1]
    merged_count = tokens // 4
    padded = -(-merged_count // 16) * 16
    others = range(n_mp)

    section = jnp.concatenate([merge_weight, expand_weight.transpose(1, 2, 0)], axis=0)

    blocks = fields.reshape(rows, n_mp, block, group).transpose(1, 0, 2, 3)
    margin = jnp.roll(blocks[:, :, :WIN_W], -1, axis=0)
    field_blocks = jnp.concatenate([blocks, margin], axis=2)
    body_slab = halves_beside(field_blocks.reshape(n_mp, rows * wide, group))
    edge_slab = halves_beside(field_blocks[:, :WIN_H].reshape(n_mp, WIN_H * wide, group))
    cot_blocks = cotangent.reshape(rows, n_mp, block, group).transpose(1, 0, 2, 3)
    cot_slab = halves_beside(cot_blocks.reshape(n_mp, tokens, group))
    weights = jnp.concatenate(
        [qkv_weight.transpose(1, 2, 0), proj_weight.transpose(1, 0)[None]], axis=0
    )
    gains = jnp.pad(jnp.concatenate([first_gain[None], merge_gain], axis=0), ((0, 3), (0, 64)))

    def rows_at(here, step):
        return pl.ds(pl.multiple_of(lax.rem(here["mp"] + n_mp - step, n_mp) * group, group), group)

    def own_rows(ref, here, target):
        return ref.at[:, rows_at(here, 0)]

    def own_quarter(size):
        return lambda ref, here, target: ref.at[pl.ds(size * here["quarter"], size)]

    def quarter_rows(size, step, extra, half=None):
        def part(ref, here, target):
            first = size * lax.rem(here["quarter"] + extra, 4)
            if half is None:
                return ref.at[pl.ds(first, size), rows_at(here, step)]
            if size > 1:
                return ref.at[first + half, rows_at(here, step)]
            count = group // 2
            at = lax.rem(here["mp"] + n_mp - step, n_mp) * group + half * count
            return ref.at[first, pl.ds(pl.multiple_of(at, count), count)]

        return part

    nearest_first = (2, 6, 1, 7, 4, 3, 5)
    gather_moves = [
        (source, own_quarter(size), source, quarter_rows(size, 0, 0), 0, step)
        for source, size in ((0, 2), (1, 1))
        for step in nearest_first
    ]
    relays, last_relays = [], []
    for source, size, first in ((0, 2, 0), (1, 1, n_mp - 1)):
        for index, step in enumerate(nearest_first):
            after = first + index
            for half, down in ((0, 4), (1, -4)):
                part = quarter_rows(size, step, 0, half)
                relays.append((source, part, source, part, down, 0, after))
                part = quarter_rows(size, step, 2, half)
                last_relays.append((source, part, source, part, "sibling", 0, len(relays) - 1))
            part = quarter_rows(size, step, 0)
            relays.append((source, part, source, part, "sibling", 0, after))
    places = place_table(lat_offset, lon_offset, rows, block, padded, n_mp)
    moves = (
        gather_moves
        + [(4, None, 4, "mp", 0, step) for step in others]
        + [(2, "mp", 2, "mp", 0, step) for step in others]
        + [(3, "mp", 3, "mp", -1, step) for step in others]
        + [(1, None, 1, own_rows, 0, 0)]
    )
    last_relays = [move[:6] + (move[6] + len(moves),) for move in last_relays]
    section_got, weights_all, body_got, edge_got, gains_all = exchange(
        1,
        [section, weights, body_slab, edge_slab, gains],
        [
            ((8, width, width_two), BF16),
            ((4, width, width), BF16),
            (body_slab.shape, BF16),
            (edge_slab.shape, BF16),
            ((n_mp,) + gains.shape, F32),
        ],
        moves + relays + last_relays,
    )
    has_shard = lax.rem(lax.axis_index("mp"), 2) == core
    first_all = gains_all[:, 0, :group].reshape(1, width)
    merge_gain_all = gains_all[:, 1:5, :group].transpose(1, 0, 2).reshape(4, width)
    mlp_gain_row = mlp_gain.reshape(1, width_two)
    cut = (jnp.int32(rows) * (n_lat - lat) - lat_offset).reshape(1)
    attention_framed, context, framed_fields, own_fields = local_kernel(
        attention_forward,
        [cut, body_got, edge_got, places, first_all, weights_all],
        [((tokens, width), BF16)] * 3 + [((4, padded, width), BF16)],
        [
            pltpu.VMEM((3, tokens, width), F32),
            pltpu.VMEM((tokens, width), F32),
            pltpu.VMEM(((rows + WIN_H) * wide, width), BF16),
        ],
        scalars=1,
    )
    window_shape = (bands, columns, WIN, width)
    around = (2 * bands + 2, WIN, width)

    halo, cot_got = exchange(
        2,
        [attention_framed.reshape(window_shape), cot_slab],
        [(around, BF16), (cot_slab.shape, BF16)],
        [
            (0, (bands - 1, columns - 1), 0, (0,), 1, 1),
            (0, (slice(0, bands), columns - 1), 0, (slice(1, 1 + bands),), 0, 1),
            (0, (bands - 1,), 0, (slice(1 + bands, 1 + bands + columns),), 1, 0),
        ]
        + [(1, "mp", 1, "mp", 0, step) for step in others],
    )
    n_x = n_mp // 2
    section_scratch = [
        pltpu.VMEM(section_got.shape, BF16),
        pltpu.SemaphoreType.DMA((2,)),
    ]
    pair, hidden, merged, grad_bottom, cot_patches = local_kernel(
        merge_forward,
        [
            lax.axis_index("mp").reshape(1),
            own_fields,
            attention_framed,
            halo.reshape(-1, width),
            cot_got,
            places,
            merge_gain_all,
            mlp_gain_row,
            section,
            section_got,
        ],
        [
            ((padded, 2 * width_two), BF16),
            ((4, padded, width), BF16),
            ((padded, width_two), BF16),
            ((padded, width_two), F32),
            ((4, padded, width), BF16),
        ],
        section_scratch + [pltpu.VMEM((tokens, width), F32)],
        scalars=1,
        outside=2,
        grant=56,
    )

    def chip_spot(step):
        def spot(ref, here, target):
            return ref.at[lax.rem(here["x"] + n_x + step, n_x), here["core"]]

        return spot

    pairs, up_other, down_other = exchange(
        3,
        [pair, up_weight, down_weight],
        [
            ((n_x, 2) + pair.shape, BF16),
            (up_weight.shape, BF16),
            (down_weight.shape, BF16),
        ],
        [
            (0, None, 0, chip_spot(0), 0, 4),
            (0, None, 0, chip_spot(0), 0, 2),
            (0, None, 0, chip_spot(0), 0, -2),
            (0, None, 0, chip_spot(0), "sibling", 0),
            (0, None, 0, chip_spot(0), 0, 0),
            (1, None, 1, None, "flip", 0),
            (2, None, 2, None, "flip", 0),
            (0, chip_spot(-1), 0, chip_spot(-1), "sibling", 0, 1),
            (0, chip_spot(1), 0, chip_spot(1), "sibling", 0, 2),
            (0, chip_spot(-2), 0, chip_spot(-2), "sibling", 0, 0),
        ],
    )
    up_shard = jnp.where(has_shard, up_weight, up_other)
    down_shard = jnp.where(has_shard, down_weight, down_other)
    pairs = pairs.reshape(n_mp * padded, 2 * width_two)
    mlp_in, bottom_grad = pairs[:, :width_two], pairs[:, width_two:]
    hidden_up = jnp.dot(mlp_in, up_shard, preferred_element_type=F32)
    activated = jax.nn.gelu(hidden_up).astype(BF16)
    grad_act = jnp.dot(bottom_grad, down_shard, preferred_element_type=F32)
    gelu_back = jax.vjp(jax.nn.gelu, hidden_up)[1]
    grad_pre = gelu_back(grad_act)[0].astype(BF16)
    terms, backs = (
        jnp.einsum("af,ef->ae", part, weight, preferred_element_type=F32)
        .astype(BF16)
        .reshape(n_x, 2, padded, width_two)
        for part, weight in ((activated, down_shard), (grad_pre, up_shard))
    )
    large = (n_lat, width_two // n_lat, span)
    parts, up_got, down_got = terms_back(
        4,
        terms,
        backs,
        jnp.einsum("ae,af->ef", mlp_in, grad_pre, preferred_element_type=F32)
        .astype(BF16)
        .reshape(large),
        jnp.einsum("ao,af->of", bottom_grad, activated, preferred_element_type=F32)
        .astype(BF16)
        .reshape(large),
    )
    row_slab = (n_mp, WIN_H * PADDED_COLUMNS, 2 * group)
    decoded_slab, grad_windows = local_kernel(
        merge_backward,
        [
            lax.axis_index("mp").reshape(1),
            parts,
            merged,
            grad_bottom,
            hidden,
            cot_patches,
            places,
            merge_gain_all,
            mlp_gain_row,
            section,
            section_got,
        ],
        [(row_slab, BF16), ((tokens, width), BF16)],
        section_scratch,
        scalars=1,
        outside=2,
        grant=56,
    )
    (halo,) = exchange(
        5,
        [grad_windows.reshape(window_shape)],
        [(around, BF16)],
        [
            (0, (0, 0), 0, (0,), -1, -1),
            (0, (slice(0, bands), 0), 0, (slice(1, 1 + bands),), 0, -1),
            (0, (0,), 0, (slice(1 + bands, 1 + bands + columns),), -1, 0),
        ],
    )
    grad_up = jnp.sum(up_got.astype(F32), axis=0)
    grad_down = jnp.sum(down_got.astype(F32), axis=0)
    grad_slab, grad_edge, weight_grads = local_kernel(
        attention_backward,
        [
            cut,
            framed_fields,
            first_all,
            weights_all,
            context,
            grad_windows,
            halo.reshape(-1, width),
            places,
        ],
        [
            (row_slab, BF16),
            ((n_mp, WIN_H * PADDED_COLUMNS // 2, 2 * group), BF16),
            ((4, width, width), BF16),
        ],
        [
            pltpu.VMEM((3, tokens, width), F32),
            pltpu.VMEM((3, tokens, width), F32),
            pltpu.VMEM((tokens, width), F32),
        ],
        scalars=1,
    )
    weight_total, grad_got, edge_got, decoded_got = gradients_out(
        6, weight_grads, grad_slab, grad_edge, decoded_slab
    )
    grad_qkv = weight_total[:, : 3 * group].reshape(width // n_lat, 3, group)
    grad_proj = weight_total[:, 3 * group :]
    (decoded,) = local_kernel(
        decoded_rows, [decoded_got, places], [((rows, group, lon_count), BF16)]
    )
    (grad_input,) = local_kernel(
        input_rows,
        [lat_shift, grad_got, edge_got, places],
        [((rows, group, lon_count), F32)],
        [pltpu.VMEM((rows + WIN_H, group, lon_count), F32)],
        scalars=1,
    )
    decoded, grad_input = decoded.transpose(0, 2, 1), grad_input.transpose(0, 2, 1)
    return (decoded, grad_input, grad_qkv, grad_proj, grad_up, grad_down)


def solution(mesh):
    return jax.shard_map(
        shards,
        mesh=mesh,
        in_specs=(
            P("lat", None, "mp"),
            P("mp"),
            P(None, None, "mp"),
            P(None, "mp"),
            P(None, "mp"),
            P(None, "mp", None),
            P(),
            P(None, "mp"),
            P(None, "mp"),
            P(None, None, "mp"),
            P(),
            P(),
            P("lat", None, "mp"),
        ),
        out_specs=(
            P("lat", None, "mp"),
            P("lat", None, "mp"),
            P("lat", None, "mp"),
            P("lat", "mp"),
            P("lat", "mp"),
            P("lat", "mp"),
        ),
        check_vma=False,
    )
```

```python
import jax
import jax.numpy as jnp
import numpy as np
from jax import lax
from jax.experimental import pallas as pl
from jax.experimental.pallas import tpu as pltpu
from jax.sharding import PartitionSpec as P

WIN_H = 6
WIN_W = 12
HDIM = 64
EPSILON = 1e-05
MASKED = -1e30
BF16 = jnp.bfloat16
F32 = jnp.float32


def space_of(shape):
    return pltpu.VMEM if int(np.prod(shape)) <= 2 * 1024 * 1024 else pl.ANY


def positions():
    lat, mp = lax.axis_index("lat"), lax.axis_index("mp")
    return {
        "lat": lat,
        "mp": mp,
        "core": lax.rem(lat, 2),
        "x": lax.div(mp, 2),
        "z": lax.rem(mp, 2),
        "quarter": 2 * lax.rem(lax.div(lat, 4), 2) + lax.rem(lat, 2),
    }


def reached(here, down, right):
    n_lat, n_mp = lax.axis_size("lat"), lax.axis_size("mp")
    if down == "sibling":
        return {"lat": here["lat"] + 1 - 2 * here["core"], "mp": here["mp"]}
    if down == "flip":
        return {"lat": here["lat"], "mp": 2 * here["x"] + 1 - here["z"]}
    return {
        "lat": lax.rem(here["lat"] + n_lat + down, n_lat),
        "mp": lax.rem(here["mp"] + n_mp + right, n_mp),
    }


def device_of(target):
    return {
        "device_id": (target["lat"], target["mp"]),
        "device_id_type": pl.DeviceIdType.MESH,
    }


def greet(here, steps, owned=False):
    barrier = pltpu.get_barrier_semaphore()
    count = len(steps)
    if owned:
        n_lat, x, z = lax.axis_size("lat"), here["x"], here["z"]
        owner = z == here["core"]
        mine = 2 * lax.div(here["lat"], 2) + z
        count = count + n_lat - jnp.where(owner, 1, 0)
        for source in range(n_lat):

            @pl.when(jnp.logical_or(jnp.logical_not(owner), mine != source))
            def _():
                target = {"lat": 2 * (source // 2) + z, "mp": 2 * x + source % 2}
                pl.semaphore_signal(barrier, inc=1, **device_of(target))

    for down, right in steps:
        source = reached(here, down if isinstance(down, str) else -down, -right)
        pl.semaphore_signal(barrier, inc=1, **device_of(source))
    pl.semaphore_wait(barrier, count)


def to_owners(here, source, landing, send, receive):
    n_lat = lax.axis_size("lat")
    lat, core, x, z = here["lat"], here["core"], here["x"], here["z"]
    mine = 2 * lax.div(lat, 2) + z
    owner = z == core

    def copy_at(step):
        target = {"lat": lax.rem(lat + step, n_lat), "mp": 2 * x + core}
        rows = target["lat"]
        return remote(source.at[rows], landing.at[mine], send.at[step], receive.at[mine], target)

    def start():
        for step in range(1, n_lat):
            copy_at(step).start()

        @pl.when(owner)
        def _():
            pltpu.make_async_copy(source.at[lat], landing.at[mine], receive.at[mine]).start()

        @pl.when(jnp.logical_not(owner))
        def _():
            copy_at(0).start()

    def wait():
        sibling = reached(here, "sibling", 0)
        for slot in range(n_lat):
            remote(
                source.at[slot], landing.at[slot], send.at[slot], receive.at[slot], sibling
            ).wait_recv()
        for step in range(1, n_lat):
            copy_at(step).wait_send()

        @pl.when(jnp.logical_not(owner))
        def _():
            copy_at(0).wait_send()

    return start, wait


def remote(source, landing, send, receive, target):
    return pltpu.make_async_remote_copy(
        src_ref=source, dst_ref=landing, send_sem=send, recv_sem=receive, **device_of(target)
    )


def exchange(collective, inputs, outputs, moves, owned=(), outside=()):
    n_lat = lax.axis_size("lat")
    steps = []
    for move in moves:
        if move[4:6] != (0, 0) and move[4:6] not in steps:
            steps.append(move[4:6])

    def body(*refs):
        sources = refs[: len(inputs)]
        landings = refs[len(inputs) : len(inputs) + len(outputs)]
        send, receive, owned_send, owned_receive = refs[-4:]
        here = positions()

        def part_of(ref, part, place, target):
            if part is None:
                return ref
            if isinstance(part, str):
                return ref.at[place[part]]
            if callable(part):
                return part(ref, here, target)
            return ref.at[part]

        greet(here, steps, bool(owned))
        copies = []
        arrived = set()
        scatters = [
            to_owners(
                here, sources[one], landings[two], owned_send.at[index], owned_receive.at[index]
            )
            for index, (one, two) in enumerate(owned)
        ]
        for index, move in enumerate(moves):
            source, source_part, landing, landing_part, down, right = move[:6]
            target = reached(here, down, right)
            if len(move) > 6:
                if move[6] not in arrived:
                    copies[move[6]].wait_recv()
                    arrived.add(move[6])
                source_ref = part_of(landings[source], source_part, target, target)
            else:
                source_ref = part_of(sources[source], source_part, target, target)
            landing_ref = part_of(landings[landing], landing_part, here, target)
            if (down, right) == (0, 0):
                copy = pltpu.make_async_copy(source_ref, landing_ref, receive.at[index])
            else:
                copy = remote(
                    source_ref, landing_ref, send.at[index], receive.at[index], target
                )
            if down == "flip":
                pl.when(here["z"] == here["core"])(copy.start)
            else:
                copy.start()
            copies.append(copy)
        for start, _ in scatters:
            start()
        for _, wait in scatters:
            wait()
        for index, copy in enumerate(copies):
            if moves[index][4:6] == (0, 0):
                copy.wait()
            elif moves[index][4] == "flip":
                pl.when(here["z"] == here["core"])(copy.wait_send)
                pl.when(here["z"] != here["core"])(copy.wait_recv)
            else:
                copy.wait_send()
                if index not in arrived:
                    copy.wait_recv()

    return pl.pallas_call(
        body,
        out_shape=[jax.ShapeDtypeStruct(shape, dtype) for shape, dtype in outputs],
        in_specs=[pl.BlockSpec(memory_space=pl.ANY)] * len(inputs),
        out_specs=[
            pl.BlockSpec(memory_space=pl.ANY if index in outside else space_of(shape))
            for index, (shape, _) in enumerate(outputs)
        ],
        scratch_shapes=[
            pltpu.SemaphoreType.DMA((len(moves),)),
            pltpu.SemaphoreType.DMA((len(moves),)),
            pltpu.SemaphoreType.DMA((max(len(owned), 1), n_lat)),
            pltpu.SemaphoreType.DMA((max(len(owned), 1), n_lat)),
        ],
        compiler_params=pltpu.CompilerParams(
            collective_id=collective, has_side_effects=True, vmem_limit_bytes=32 * 1024 * 1024
        ),
    )(*inputs)


X_STEPS = ((4, 2), (2, 1), (-2, 3))


def terms_back(collective, terms, up_grads, down_grads):
    count, _, rows, width = terms.shape
    n_lat = lax.axis_size("lat")

    def body(
        terms_ref, up_ref, down_ref, parts_ref, up_got, down_got,
        other, own, total, send, receive, fetch, large_send, large_receive,
    ):
        here = positions()
        core, x = here["core"], here["x"]
        sibling = reached(here, "sibling", 0)
        greet(here, [("sibling", 0)] + [(0, right) for right, _ in X_STEPS], True)
        scatters = [
            to_owners(here, source, landing, large_send.at[index], large_receive.at[index])
            for index, (source, landing) in enumerate(((up_ref, up_got), (down_ref, down_got)))
        ]
        order = [lax.rem(x + step, count) for _, step in X_STEPS] + [x]
        swaps, loads = [], []
        for index, spot in enumerate(order):
            swap = remote(
                terms_ref.at[spot, 1 - core],
                other.at[index],
                send.at[index],
                receive.at[index],
                sibling,
            )
            load = pltpu.make_async_copy(terms_ref.at[spot, core], own.at[index], fetch.at[index])
            swap.start()
            load.start()
            swaps.append(swap)
            loads.append(load)
        for start, _ in scatters:
            start()
        sends = []
        for index, spot in enumerate(order):
            loads[index].wait()
            swaps[index].wait_recv()
            total[index] = (own[index].astype(F32) + other[index].astype(F32)).astype(BF16)
            if index < len(X_STEPS):
                copy = remote(
                    total.at[index],
                    parts_ref.at[x],
                    send.at[count + index],
                    receive.at[count + index],
                    reached(here, 0, X_STEPS[index][0]),
                )
            else:
                copy = pltpu.make_async_copy(total.at[index], parts_ref.at[x], fetch.at[count])
            copy.start()
            sends.append(copy)
        for swap in swaps:
            swap.wait_send()
        for copy in sends:
            copy.wait()
        for _, wait in scatters:
            wait()

    return pl.pallas_call(
        body,
        out_shape=[
            jax.ShapeDtypeStruct((count, rows, width), BF16),
            jax.ShapeDtypeStruct(up_grads.shape, BF16),
            jax.ShapeDtypeStruct(down_grads.shape, BF16),
        ],
        in_specs=[pl.BlockSpec(memory_space=pl.ANY)] * 3,
        out_specs=[
            pl.BlockSpec(memory_space=pltpu.VMEM),
            pl.BlockSpec(memory_space=pl.ANY),
            pl.BlockSpec(memory_space=pl.ANY),
        ],
        scratch_shapes=[
            pltpu.VMEM((count, rows, width), BF16),
            pltpu.VMEM((count, rows, width), BF16),
            pltpu.VMEM((count, rows, width), BF16),
            pltpu.SemaphoreType.DMA((2 * count,)),
            pltpu.SemaphoreType.DMA((2 * count,)),
            pltpu.SemaphoreType.DMA((count + 1,)),
            pltpu.SemaphoreType.DMA((2, n_lat)),
            pltpu.SemaphoreType.DMA((2, n_lat)),
        ],
        compiler_params=pltpu.CompilerParams(
            collective_id=collective, has_side_effects=True, vmem_limit_bytes=48 * 1024 * 1024
        ),
    )(terms, up_grads, down_grads)


def gradients_out(collective, weight_grads, slabs, edges, decoded_slabs):
    n_lat, n_mp = lax.axis_size("lat"), lax.axis_size("mp")
    kinds, width, _ = weight_grads.shape
    pair, group, share = kinds // 2, width // n_mp, width // n_lat

    def body(
        weight_ref, slab_ref, edge_ref, decoded_ref, out_ref, got_ref, edge_got, decoded_got,
        other, total, parts, turned, landed, send, receive,
    ):
        here = positions()
        lat, mp, core = here["lat"], here["mp"], here["core"]
        sibling = reached(here, "sibling", 0)
        barrier = pltpu.get_barrier_semaphore()
        greeted = [sibling]
        greeted += [reached(here, 0, -step) for step in range(1, n_mp)]
        greeted += [reached(here, -1, -step) for step in range(n_mp)]
        greeted += [reached(here, -step, 0) for step in range(1, n_lat)]
        for target in greeted:
            pl.semaphore_signal(barrier, inc=1, **device_of(target))
        pl.semaphore_wait(barrier, len(greeted))

        copies = []

        def sent(source, landing, target):
            index = len(copies)
            copy = remote(source, landing, send.at[index], receive.at[index], target)
            copy.start()
            copies.append(copy)
            return copy

        swap = sent(weight_ref.at[pl.ds(pair * (1 - core), pair)], other, sibling)
        for step in range(1, n_mp):
            target = reached(here, 0, step)
            sent(decoded_ref.at[target["mp"]], decoded_got.at[mp], target)
        own_slab = pltpu.make_async_copy(slab_ref.at[mp], got_ref.at[mp], send.at[60])
        own_slab.start()
        own_decoded = pltpu.make_async_copy(decoded_ref.at[mp], decoded_got.at[mp], send.at[61])
        own_decoded.start()

        swap.wait_recv()
        total[...] = (
            weight_ref[pl.ds(pair * core, pair)].astype(F32) + other[...].astype(F32)
        ).astype(BF16)
        scattered = []
        for step in range(1, n_mp):
            target = reached(here, 0, step)
            rows = pl.ds(pl.multiple_of(group * target["mp"], group), group)
            scattered.append(sent(total.at[:, rows], parts.at[mp], target))
        for step in range(1, n_mp):
            target = reached(here, 0, step)
            sent(slab_ref.at[target["mp"]], got_ref.at[mp], target)
        for step in range(n_mp):
            target = reached(here, 1, step)
            sent(edge_ref.at[target["mp"]], edge_got.at[mp], target)
        gathered = total[:, pl.ds(pl.multiple_of(group * mp, group), group), :].astype(F32)
        for step in range(1, n_mp):
            scattered[step - 1].wait_recv()
            gathered = gathered + parts[lax.rem(mp + n_mp - step, n_mp)].astype(F32)
        flat = gathered.reshape(pair * group, width).T.astype(BF16)
        for index in range(n_lat):
            turned[index] = flat[index * share : (index + 1) * share]
        spread = []
        for step in range(1, n_lat):
            target = reached(here, step, 0)
            spread.append(sent(turned.at[target["lat"]], landed.at[lat], target))
        landed[lat] = turned[lat]
        for copy in spread:
            copy.wait_recv()
        for half in range(2):
            result = landed[half].astype(F32)
            for index in range(half + 2, n_lat, 2):
                result = result + landed[index].astype(F32)
            out_ref[:, half * pair * group : (half + 1) * pair * group] = result

        done = [swap] + scattered + spread
        for copy in copies:
            copy.wait_send()
            if not any(copy is other_copy for other_copy in done):
                copy.wait_recv()
        own_slab.wait()
        own_decoded.wait()

    any_space = pl.BlockSpec(memory_space=pl.ANY)
    vmem = pl.BlockSpec(memory_space=pltpu.VMEM)
    return pl.pallas_call(
        body,
        out_shape=[
            jax.ShapeDtypeStruct((share, kinds * group), F32),
            jax.ShapeDtypeStruct(slabs.shape, BF16),
            jax.ShapeDtypeStruct(edges.shape, BF16),
            jax.ShapeDtypeStruct(decoded_slabs.shape, BF16),
        ],
        in_specs=[vmem, any_space, any_space, any_space],
        out_specs=[vmem, vmem, vmem, vmem],
        scratch_shapes=[
            pltpu.VMEM((pair, width, width), BF16),
            pltpu.VMEM((pair, width, width), BF16),
            pltpu.VMEM((n_mp, pair, group, width), BF16),
            pltpu.VMEM((n_lat, share, pair * group), BF16),
            pltpu.VMEM((n_lat, share, pair * group), BF16),
            pltpu.SemaphoreType.DMA((64,)),
            pltpu.SemaphoreType.DMA((64,)),
        ],
        compiler_params=pltpu.CompilerParams(
            collective_id=collective, has_side_effects=True, vmem_limit_bytes=48 * 1024 * 1024
        ),
    )(weight_grads, slabs, edges, decoded_slabs)


def local_kernel(body, operands, outputs, scratch=(), scalars=0, outside=0):
    spaces = [pltpu.SMEM] * scalars + [pltpu.VMEM] * (len(operands) - scalars - outside)
    spaces += [pl.ANY] * outside
    return pl.pallas_call(
        body,
        out_shape=[jax.ShapeDtypeStruct(shape, dtype) for shape, dtype in outputs],
        in_specs=[pl.BlockSpec(memory_space=space) for space in spaces],
        out_specs=[pl.BlockSpec(memory_space=pltpu.VMEM)] * len(outputs),
        scratch_shapes=list(scratch),
        compiler_params=pltpu.CompilerParams(vmem_limit_bytes=48 * 1024 * 1024),
    )(*operands)


def dot_nn(left, right):
    return lax.dot_general(left, right, (((1,), (0,)), ((), ())), preferred_element_type=F32)


def dot_nt(left, right):
    return lax.dot_general(left, right, (((1,), (1,)), ((), ())), preferred_element_type=F32)


def dot_tn(left, right):
    return lax.dot_general(left, right, (((0,), (0,)), ((), ())), preferred_element_type=F32)


def halves_beside(values):
    half = values.shape[-2] // 2
    return jnp.concatenate([values[..., :half, :], values[..., half:, :]], axis=-1)


def picked(places, values):
    spots = lax.broadcasted_iota(jnp.int32, (places.shape[0], values.shape[0]), 1)
    return dot_nn(jnp.where(spots == places, 1.0, 0.0).astype(BF16), values)


def spread_over(places, values, count):
    spots = lax.broadcasted_iota(jnp.int32, (places.shape[0], count), 1)
    return dot_tn(values, jnp.where(spots == places, 1.0, 0.0).astype(BF16))


def swapped(values):
    return jnp.concatenate([values[:, HDIM:], values[:, :HDIM]], axis=1)


def join_slabs(slab_ref, out_ref, first_rows, second_rows):
    half = slab_ref.shape[1]
    low = lax.broadcasted_iota(jnp.int32, (half, 2 * HDIM), 1) < HDIM
    for pair in range(slab_ref.shape[0] // 2):
        lanes = slice(2 * HDIM * pair, 2 * HDIM * (pair + 1))
        one = slab_ref[2 * pair].astype(F32)
        two = slab_ref[2 * pair + 1].astype(F32)
        first = jnp.where(low, one, swapped(two)).astype(out_ref.dtype)
        second = jnp.where(low, swapped(one), two).astype(out_ref.dtype)
        out_ref[first_rows : first_rows + half, lanes] = first
        out_ref[second_rows : second_rows + half, lanes] = second


PADDED_COLUMNS = 48
FRAME, OWN, BACK, BACK_HALO, COT, UNPATCH, GRAD, GRAD_HALO, BY_ROW, BY_ROW_PATCH, SHIFT, STAY = range(12)


def place_table(lat_offset, lon_offset, rows, block, padded, n_mp):
    columns = block // WIN_W
    size = max(rows * block, 4 * padded, n_mp * PADDED_COLUMNS)
    token = np.arange(rows * block)
    window, spot = token // WIN, token % WIN
    row = (window // columns) * WIN_H + spot // WIN_W
    column = (window % columns) * WIN_W + spot % WIN_W
    patch, at = np.arange(4 * padded) // padded, np.arange(4 * padded) % padded
    real = at < rows * block // 4
    prow = 2 * (at // (block // 2)) + patch // 2
    pcolumn = 2 * (at % (block // 2)) + patch % 2
    side = np.arange(WIN_H * PADDED_COLUMNS) // PADDED_COLUMNS
    spot = np.arange(WIN_H * PADDED_COLUMNS) % PADDED_COLUMNS
    shown = spot < block
    group = np.arange(n_mp * PADDED_COLUMNS) // PADDED_COLUMNS
    place = np.arange(n_mp * PADDED_COLUMNS) % PADDED_COLUMNS
    inside = place < block
    unpatch = (2 * (row % 2) + column % 2) * padded + (row // 2) * (block // 2) + column // 2
    by_row = (spot // WIN_W) * WIN + side * WIN_W + spot % WIN_W
    by_row_patch = (spot % 2) * padded + side * (block // 2) + spot // 2
    lon = group * block + place
    wide = block + WIN_W
    source = {
        FRAME: (row, column, True, wide),
        OWN: (prow, pcolumn, real, wide),
        BACK: (prow, pcolumn, real, 0),
        BACK_HALO: (prow, pcolumn, real, 0),
        COT: (prow, pcolumn, real, block),
        UNPATCH: (0, unpatch, True, 0),
        GRAD: (row, column, True, 0),
        GRAD_HALO: (row, column, True, 0),
        BY_ROW: (0, by_row, shown, 0),
        BY_ROW_PATCH: (0, by_row_patch, shown, 0),
        SHIFT: (0, lon, inside, 0),
        STAY: (0, lon, inside, 0),
    }
    shape = (size, len(source))
    row_at, column_at, pitch = (np.zeros(shape, np.int32) for _ in range(3))
    valid = np.zeros(shape, bool)
    for key, (row_part, column_part, part, step) in source.items():
        count = column_part.shape[0]
        row_at[:count, key], column_at[:count, key], pitch[:, key] = row_part, column_part, step
        valid[:count, key] = part
    kind = np.arange(len(source))[None]
    back = np.isin(kind, (BACK, BACK_HALO))
    grad = np.isin(kind, (GRAD, GRAD_HALO))
    row_sign = np.where(back, -1, np.where(grad | (kind == FRAME), 1, 0)).astype(np.int32)
    column_sign = np.where(kind == SHIFT, 1, row_sign).astype(np.int32)
    row_at = row_at + row_sign * lat_offset
    column_at = column_at + column_sign * lon_offset
    straight = row_at * pitch + column_at
    full = n_mp * block
    straight = jnp.where((kind == SHIFT) & (straight >= full), straight - full, straight)
    down = jnp.where(back, row_at < 0, row_at >= rows)
    right = jnp.where(back, column_at < 0, column_at >= block)
    row_in = jnp.where(down, row_at + np.where(back, WIN_H, -rows).astype(np.int32), row_at)
    column_in = jnp.where(
        right, column_at + np.where(back, WIN_W, -block).astype(np.int32), column_at
    )
    band, slot = lax.div(row_in, jnp.int32(WIN_H)), lax.div(column_in, jnp.int32(WIN_W))
    halo_slot = jnp.where(down, jnp.where(right, 0, 3 + slot), 1 + band)
    outside = jnp.logical_or(down, right)
    halo = np.isin(kind, (BACK_HALO, GRAD_HALO))
    tile = jnp.where(halo, halo_slot, band * columns + slot)
    windowed = tile * WIN + (row_in - band * WIN_H) * WIN_W + column_in - slot * WIN_W
    result = jnp.where(back | grad, windowed, straight)
    hidden = (back | grad) & jnp.where(halo, jnp.logical_not(outside), outside)
    return jnp.where(valid & jnp.logical_not(hidden), result, -1).astype(jnp.int32)


def norm_stats(values, count):
    center = sum(jnp.sum(value, axis=1, keepdims=True) for value in values) / count
    second = sum(jnp.sum(value * value, axis=1, keepdims=True) for value in values) / count
    return (center, lax.rsqrt(second - center * center + EPSILON))


def norm_backward(grads, gains, units, scale_inv, count):
    scaled = [grad * gain for grad, gain in zip(grads, gains)]
    first = sum(jnp.sum(value, axis=1, keepdims=True) for value in scaled) / count
    second = (
        sum(jnp.sum(value * unit, axis=1, keepdims=True) for value, unit in zip(scaled, units))
        / count
    )
    return [scale_inv * (value - first - unit * second) for value, unit in zip(scaled, units)]


def pair_slabs(upper, lower, out_ref, first_rows):
    low = lax.broadcasted_iota(jnp.int32, (upper.shape[0], 2 * HDIM), 1) < HDIM
    rows = pl.ds(first_rows, upper.shape[0])
    for pair in range(upper.shape[1] // (2 * HDIM)):
        lanes = slice(2 * HDIM * pair, 2 * HDIM * (pair + 1))
        one, two = upper[:, lanes], lower[:, lanes]
        out_ref[2 * pair, rows, :] = jnp.where(low, one, swapped(two)).astype(BF16)
        out_ref[2 * pair + 1, rows, :] = jnp.where(low, swapped(one), two).astype(BF16)


WIN = WIN_H * WIN_W
FACTOR = HDIM ** (-0.5)


def heads_apart(values):
    low = lax.broadcasted_iota(jnp.int32, values.shape, 1) < HDIM
    zero = jnp.zeros_like(values)
    both = [jnp.where(low, values, zero), jnp.where(low, zero, values)]
    return jnp.concatenate(both, axis=0).astype(BF16)


def heads_together(values):
    low = lax.broadcasted_iota(jnp.int32, (WIN, 2 * HDIM), 1) < HDIM
    return jnp.where(low, values[:WIN], values[WIN:])


def window_probs(cut, window, query, keys):
    scores = dot_nt(query, keys) * FACTOR
    spot = lax.broadcasted_iota(jnp.int32, scores.shape, 0)
    spot = jnp.where(spot >= WIN, spot - WIN, spot)
    other = lax.broadcasted_iota(jnp.int32, scores.shape, 1)
    edge = cut * WIN_W - jnp.where(window >= 3, WIN, 0)
    same = (spot >= edge) == (other >= edge)
    scores = jnp.where(same, scores, MASKED)
    weights = jnp.exp(scores - jnp.max(scores, axis=1, keepdims=True))
    return weights / jnp.sum(weights, axis=1, keepdims=True)


def framed_packed(fields_ref, gain_ref, weights_ref, packed):
    values = fields_ref[...].astype(F32)
    center, scale_inv = norm_stats([values], values.shape[1])
    unit = (values - center) * scale_inv
    framed = (unit * gain_ref[...]).astype(BF16)
    for kind in range(3):
        packed[kind] = dot_nt(framed, weights_ref[kind]).astype(BF16).astype(F32)
    return (framed, unit, scale_inv)


def window_parts(refs, window, pair):
    rows = pl.ds(pl.multiple_of(window * WIN, 8), WIN)
    lanes = slice(2 * HDIM * pair, 2 * HDIM * (pair + 1))
    return [ref[rows, lanes] for ref in refs]


def attention_forward(
    cut_ref, body_ref, edge_ref, places_ref, gain_ref, weights_ref,
    out_ref, context_ref, fields_ref, own_ref, packed, held, grid,
):
    half, rest = body_ref.shape[1], edge_ref.shape[1]
    join_slabs(body_ref, grid, 0, half)
    join_slabs(edge_ref, grid, 2 * half, 2 * half + rest)
    tokens = fields_ref.shape[0]
    whole = grid[...]
    fields_ref[...] = picked(places_ref[:tokens, FRAME : FRAME + 1], whole).astype(BF16)
    padded = own_ref.shape[1]
    for patch in range(4):
        rows = slice(padded * patch, padded * (patch + 1))
        own_ref[patch] = picked(places_ref[rows, OWN : OWN + 1], whole).astype(BF16)
    framed_packed(fields_ref, gain_ref, weights_ref, packed)
    cut = cut_ref[0]
    windows = fields_ref.shape[0] // WIN

    def step(window, carry):
        rows = pl.ds(pl.multiple_of(window * WIN, 8), WIN)
        for pair in range(fields_ref.shape[1] // (2 * HDIM)):
            query, keys, values = window_parts([packed.at[kind] for kind in range(3)], window, pair)
            probs = window_probs(cut, window, heads_apart(query), keys.astype(BF16))
            joined = dot_nn(probs.astype(BF16), values.astype(BF16))
            held[rows, 2 * HDIM * pair : 2 * HDIM * (pair + 1)] = heads_together(joined)
        return carry

    lax.fori_loop(0, windows, step, 0)
    context = held[...].astype(BF16)
    context_ref[...] = context
    out_ref[...] = dot_nn(context, weights_ref[3]).astype(BF16)


def attention_backward(
    cut_ref, fields_ref, gain_ref, weights_ref, context_ref, grad_ref, halo_ref, places_ref,
    slab_ref, edge_ref, weight_ref, packed, grads, held,
):
    framed, unit, scale_inv = framed_packed(fields_ref, gain_ref, weights_ref, packed)
    cut = cut_ref[0]
    windows = fields_ref.shape[0] // WIN
    tokens = fields_ref.shape[0]
    grad_framed = (
        picked(places_ref[:tokens, GRAD : GRAD + 1], grad_ref[...])
        + picked(places_ref[:tokens, GRAD_HALO : GRAD_HALO + 1], halo_ref[...])
    ).astype(BF16)
    held[...] = dot_nt(grad_framed, weights_ref[3]).astype(BF16).astype(F32)

    def step(window, carry):
        rows = pl.ds(pl.multiple_of(window * WIN, 8), WIN)
        for pair in range(fields_ref.shape[1] // (2 * HDIM)):
            lanes = slice(2 * HDIM * pair, 2 * HDIM * (pair + 1))
            query, keys, values, grad = window_parts(
                [packed.at[kind] for kind in range(3)] + [held], window, pair
            )
            query, grad = heads_apart(query), heads_apart(grad)
            keys, values = keys.astype(BF16), values.astype(BF16)
            probs = window_probs(cut, window, query, keys)
            grad_probs = dot_nt(grad, values)
            inner = jnp.sum(grad_probs * probs, axis=1, keepdims=True)
            grad_scores = (probs * (grad_probs - inner) * FACTOR).astype(BF16)
            grads[0, rows, lanes] = heads_together(dot_nn(grad_scores, keys))
            grads[1, rows, lanes] = dot_tn(grad_scores, query)
            grads[2, rows, lanes] = dot_tn(probs.astype(BF16), grad)
        return carry

    lax.fori_loop(0, windows, step, 0)
    grad_normed = jnp.zeros(fields_ref.shape, F32)
    for kind in range(3):
        grad_kind = grads[kind].astype(BF16)
        weight_ref[kind] = dot_tn(grad_kind, framed).astype(BF16)
        grad_normed = grad_normed + dot_nn(grad_kind, weights_ref[kind])
    weight_ref[3] = dot_tn(context_ref[...], grad_framed).astype(BF16)
    (back,) = norm_backward([grad_normed], [gain_ref[...]], [unit], scale_inv, unit.shape[1])
    result = grad_framed.astype(F32) + back
    half = result.shape[0] // 2
    by_row = places_ref[: slab_ref.shape[1], BY_ROW : BY_ROW + 1]
    upper, lower = (picked(by_row, part.astype(BF16)) for part in (result[:half], result[half:]))
    pair_slabs(upper, lower, slab_ref, 0)
    half = edge_ref.shape[1]
    pair_slabs(lower[:half], lower[half:], edge_ref, 0)


def section_load(place_ref, own_ref, got_ref, weights, loaded):
    whole = pltpu.make_async_copy(got_ref, weights, loaded.at[0])
    whole.start()

    def wait():
        whole.wait()
        count = own_ref.shape[1]
        rows = pl.ds(pl.multiple_of(place_ref[0] * count, count), count)
        own = pltpu.make_async_copy(own_ref, weights.at[:, rows], loaded.at[1])
        own.start()
        own.wait()

    return wait


def merge_forward(
    place_ref, fields_ref, attention_ref, halo_ref, cot_got_ref, places_ref, gain_ref,
    mlp_gain_ref, own_ref, got_ref,
    pair_ref, hidden_ref, merged_ref, grad_ref, cot_ref, weights, loaded, joined,
):
    wait = section_load(place_ref, own_ref, got_ref, weights, loaded)
    width_two = merged_ref.shape[1]
    join_slabs(cot_got_ref, joined, 0, cot_got_ref.shape[1])
    cot = joined[...].astype(BF16)
    padded = merged_ref.shape[0]
    hidden = []
    for patch in range(4):
        rows = slice(padded * patch, padded * (patch + 1))
        cot_ref[patch] = picked(places_ref[rows, COT : COT + 1], cot).astype(BF16)
        attention = picked(places_ref[rows, BACK : BACK + 1], attention_ref[...])
        attention = attention + picked(
            places_ref[rows, BACK_HALO : BACK_HALO + 1], halo_ref[...]
        )
        value = fields_ref[patch].astype(F32) + attention
        hidden_ref[patch] = value.astype(BF16)
        hidden.append(value.astype(BF16).astype(F32))
    center, scale_inv = norm_stats(hidden, 4 * hidden[0].shape[1])
    merged = jnp.zeros(merged_ref.shape, F32)
    grad = jnp.zeros(merged_ref.shape, F32)
    wait()
    for patch in range(4):
        normed = (hidden[patch] - center) * scale_inv * gain_ref[patch : patch + 1, :]
        merged = merged + dot_nn(normed.astype(BF16), weights[patch])
        grad = grad + dot_nn(cot_ref[patch], weights[4 + patch])
    merged_ref[...] = merged.astype(BF16)
    merged = merged.astype(BF16).astype(F32)
    center, scale_inv = norm_stats([merged], width_two)
    mlp_in = (merged - center) * scale_inv * mlp_gain_ref[...]
    pair_ref[:, :width_two] = mlp_in.astype(BF16)
    pair_ref[:, width_two:] = grad.astype(BF16)
    grad_ref[...] = grad


def merge_backward(
    place_ref, parts_ref, merged_ref, grad_ref, hidden_ref, cot_ref, places_ref, gain_ref,
    mlp_gain_ref, own_ref, got_ref, slab_ref, out_ref, weights, loaded,
):
    wait = section_load(place_ref, own_ref, got_ref, weights, loaded)
    width_two = merged_ref.shape[1]
    total = parts_ref[0].astype(F32)
    for index in range(1, parts_ref.shape[0]):
        total = total + parts_ref[index].astype(F32)
    merged = merged_ref[...].astype(F32)
    bottom = (merged + total[:, :width_two]).astype(BF16)
    wait()
    decoded = [
        hidden_ref[patch].astype(F32) + dot_nt(bottom, weights[4 + patch])
        for patch in range(4)
    ]
    by_row = places_ref[: slab_ref.shape[1], BY_ROW_PATCH : BY_ROW_PATCH + 1]
    upper, lower = (
        picked(by_row, jnp.concatenate([decoded[at], decoded[at + 1]], axis=0).astype(BF16))
        for at in (0, 2)
    )
    pair_slabs(upper, lower, slab_ref, 0)
    center, scale_inv = norm_stats([merged], width_two)
    unit = (merged - center) * scale_inv
    (back,) = norm_backward(
        [total[:, width_two:]], [mlp_gain_ref[...]], [unit], scale_inv, width_two
    )
    grad_merged = (grad_ref[...] + back).astype(BF16)
    hidden = [hidden_ref[patch].astype(F32) for patch in range(4)]
    center, scale_inv = norm_stats(hidden, 4 * hidden[0].shape[1])
    units = [(value - center) * scale_inv for value in hidden]
    backs = norm_backward(
        [dot_nt(grad_merged, weights[patch]) for patch in range(4)],
        [gain_ref[patch : patch + 1, :] for patch in range(4)],
        units,
        scale_inv,
        4 * hidden[0].shape[1],
    )
    grads = [(cot_ref[patch].astype(F32) + backs[patch]) for patch in range(4)]
    grads = jnp.concatenate(grads, axis=0).astype(BF16)
    tokens = out_ref.shape[0]
    out_ref[...] = picked(places_ref[:tokens, UNPATCH : UNPATCH + 1], grads).astype(BF16)


def decoded_rows(got_ref, places_ref, out_ref):
    places = places_ref[: got_ref.shape[0] * PADDED_COLUMNS, STAY : STAY + 1]
    for side in range(WIN_H):
        rows = slice(side * PADDED_COLUMNS, (side + 1) * PADDED_COLUMNS)
        values = got_ref[:, rows, :].reshape(-1, 2 * HDIM)
        both = spread_over(places, values, out_ref.shape[2])
        for index in range(2):
            out_ref[2 * side + index] = both[HDIM * index : HDIM * (index + 1)].astype(BF16)


def input_rows(shift_ref, got_ref, edge_ref, places_ref, out_ref, framed):
    places = places_ref[: got_ref.shape[0] * PADDED_COLUMNS, SHIFT : SHIFT + 1]
    for side in range(WIN_H):
        rows = slice(side * PADDED_COLUMNS, (side + 1) * PADDED_COLUMNS)
        both = spread_over(places, got_ref[:, rows, :].reshape(-1, 2 * HDIM), out_ref.shape[2])
        framed[WIN_H + side] = both[:HDIM]
        framed[2 * WIN_H + side] = both[HDIM:]
    for side in range(WIN_H // 2):
        rows = slice(side * PADDED_COLUMNS, (side + 1) * PADDED_COLUMNS)
        both = spread_over(places, edge_ref[:, rows, :].reshape(-1, 2 * HDIM), out_ref.shape[2])
        framed[side] = both[:HDIM]
        framed[WIN_H // 2 + side] = both[HDIM:]
    first = WIN_H - shift_ref[0]
    for row in range(out_ref.shape[0]):
        out_ref[row] = framed[first + row]


def shards(
    fields,
    first_gain,
    qkv_weight,
    proj_weight,
    merge_gain,
    merge_weight,
    mlp_gain,
    up_weight,
    down_weight,
    expand_weight,
    lat_shift,
    lon_shift,
    cotangent,
):
    n_lat, n_mp = lax.axis_size("lat"), lax.axis_size("mp")
    lat, core = lax.axis_index("lat"), lax.rem(lax.axis_index("lat"), 2)
    lat_offset = lat_shift[0]
    lon_offset = lon_shift[0]
    rows, lon_count, group = fields.shape
    width = group * n_mp
    block = lon_count // n_mp
    wide = block + WIN_W
    bands, columns = rows // WIN_H, block // WIN_W
    tokens = rows * block
    width_two = merge_weight.shape[2]
    span = up_weight.shape[1]
    merged_count = tokens // 4
    padded = -(-merged_count // 16) * 16
    others = range(n_mp)

    section = jnp.concatenate([merge_weight, expand_weight.transpose(1, 2, 0)], axis=0)

    blocks = fields.reshape(rows, n_mp, block, group).transpose(1, 0, 2, 3)
    margin = jnp.roll(blocks[:, :, :WIN_W], -1, axis=0)
    field_blocks = jnp.concatenate([blocks, margin], axis=2)
    body_slab = halves_beside(field_blocks.reshape(n_mp, rows * wide, group))
    edge_slab = halves_beside(field_blocks[:, :WIN_H].reshape(n_mp, WIN_H * wide, group))
    cot_blocks = cotangent.reshape(rows, n_mp, block, group).transpose(1, 0, 2, 3)
    cot_slab = halves_beside(cot_blocks.reshape(n_mp, tokens, group))
    weights = jnp.concatenate(
        [qkv_weight.transpose(1, 2, 0), proj_weight.transpose(1, 0)[None]], axis=0
    )
    gains = jnp.pad(jnp.concatenate([first_gain[None], merge_gain], axis=0), ((0, 3), (0, 64)))

    def rows_at(here, step):
        return pl.ds(pl.multiple_of(lax.rem(here["mp"] + n_mp - step, n_mp) * group, group), group)

    def own_rows(ref, here, target):
        return ref.at[:, rows_at(here, 0)]

    def own_quarter(size):
        return lambda ref, here, target: ref.at[pl.ds(size * here["quarter"], size)]

    def quarter_rows(size, step, extra, half=None):
        def part(ref, here, target):
            first = size * lax.rem(here["quarter"] + extra, 4)
            if half is None:
                return ref.at[pl.ds(first, size), rows_at(here, step)]
            if size > 1:
                return ref.at[first + half, rows_at(here, step)]
            count = group // 2
            at = lax.rem(here["mp"] + n_mp - step, n_mp) * group + half * count
            return ref.at[first, pl.ds(pl.multiple_of(at, count), count)]

        return part

    nearest_first = (2, 6, 1, 7, 4, 3, 5)
    gather_moves = [
        (source, own_quarter(size), source, quarter_rows(size, 0, 0), 0, step)
        for source, size in ((0, 2), (1, 1))
        for step in nearest_first
    ]
    relays, last_relays = [], []
    for source, size, first in ((0, 2, 0), (1, 1, n_mp - 1)):
        for index, step in enumerate(nearest_first):
            after = first + index
            for half, down in ((0, 4), (1, -4)):
                part = quarter_rows(size, step, 0, half)
                relays.append((source, part, source, part, down, 0, after))
                part = quarter_rows(size, step, 2, half)
                last_relays.append((source, part, source, part, "sibling", 0, len(relays) - 1))
            part = quarter_rows(size, step, 0)
            relays.append((source, part, source, part, "sibling", 0, after))
    places = place_table(lat_offset, lon_offset, rows, block, padded, n_mp)
    moves = (
        gather_moves
        + [(4, None, 4, "mp", 0, step) for step in others]
        + [(2, "mp", 2, "mp", 0, step) for step in others]
        + [(3, "mp", 3, "mp", -1, step) for step in others]
        + [(1, None, 1, own_rows, 0, 0)]
    )
    last_relays = [move[:6] + (move[6] + len(moves),) for move in last_relays]
    section_got, weights_all, body_got, edge_got, gains_all = exchange(
        1,
        [section, weights, body_slab, edge_slab, gains],
        [
            ((8, width, width_two), BF16),
            ((4, width, width), BF16),
            (body_slab.shape, BF16),
            (edge_slab.shape, BF16),
            ((n_mp,) + gains.shape, F32),
        ],
        moves + relays + last_relays,
        outside=(2, 3),
    )
    has_shard = lax.rem(lax.axis_index("mp"), 2) == core
    first_all = gains_all[:, 0, :group].reshape(1, width)
    merge_gain_all = gains_all[:, 1:5, :group].transpose(1, 0, 2).reshape(4, width)
    mlp_gain_row = mlp_gain.reshape(1, width_two)
    cut = (jnp.int32(rows) * (n_lat - lat) - lat_offset).reshape(1)
    attention_framed, context, framed_fields, own_fields = local_kernel(
        attention_forward,
        [cut, body_got, edge_got, places, first_all, weights_all],
        [((tokens, width), BF16)] * 3 + [((4, padded, width), BF16)],
        [
            pltpu.VMEM((3, tokens, width), F32),
            pltpu.VMEM((tokens, width), F32),
            pltpu.VMEM(((rows + WIN_H) * wide, width), BF16),
        ],
        scalars=1,
    )
    window_shape = (bands, columns, WIN, width)
    around = (2 * bands + 2, WIN, width)

    halo, cot_got = exchange(
        2,
        [attention_framed.reshape(window_shape), cot_slab],
        [(around, BF16), (cot_slab.shape, BF16)],
        [
            (0, (bands - 1, columns - 1), 0, (0,), 1, 1),
            (0, (slice(0, bands), columns - 1), 0, (slice(1, 1 + bands),), 0, 1),
            (0, (bands - 1,), 0, (slice(1 + bands, 1 + bands + columns),), 1, 0),
        ]
        + [(1, "mp", 1, "mp", 0, step) for step in others],
    )
    n_x = n_mp // 2
    section_scratch = [
        pltpu.VMEM(section_got.shape, BF16),
        pltpu.SemaphoreType.DMA((2,)),
    ]
    pair, hidden, merged, grad_bottom, cot_patches = local_kernel(
        merge_forward,
        [
            lax.axis_index("mp").reshape(1),
            own_fields,
            attention_framed,
            halo.reshape(-1, width),
            cot_got,
            places,
            merge_gain_all,
            mlp_gain_row,
            section,
            section_got,
        ],
        [
            ((padded, 2 * width_two), BF16),
            ((4, padded, width), BF16),
            ((padded, width_two), BF16),
            ((padded, width_two), F32),
            ((4, padded, width), BF16),
        ],
        section_scratch + [pltpu.VMEM((tokens, width), F32)],
        scalars=1,
        outside=2,
    )

    def chip_spot(step):
        def spot(ref, here, target):
            return ref.at[lax.rem(here["x"] + n_x + step, n_x), here["core"]]

        return spot

    pairs, up_other, down_other = exchange(
        3,
        [pair, up_weight, down_weight],
        [
            ((n_x, 2) + pair.shape, BF16),
            (up_weight.shape, BF16),
            (down_weight.shape, BF16),
        ],
        [
            (0, None, 0, chip_spot(0), 0, 4),
            (0, None, 0, chip_spot(0), 0, 2),
            (0, None, 0, chip_spot(0), 0, -2),
            (0, None, 0, chip_spot(0), "sibling", 0),
            (0, None, 0, chip_spot(0), 0, 0),
            (1, None, 1, None, "flip", 0),
            (2, None, 2, None, "flip", 0),
            (0, chip_spot(-1), 0, chip_spot(-1), "sibling", 0, 1),
            (0, chip_spot(1), 0, chip_spot(1), "sibling", 0, 2),
            (0, chip_spot(-2), 0, chip_spot(-2), "sibling", 0, 0),
        ],
    )
    up_shard = jnp.where(has_shard, up_weight, up_other)
    down_shard = jnp.where(has_shard, down_weight, down_other)
    pairs = pairs.reshape(n_mp * padded, 2 * width_two)
    mlp_in, bottom_grad = pairs[:, :width_two], pairs[:, width_two:]
    hidden_up = jnp.dot(mlp_in, up_shard, preferred_element_type=F32)
    activated = jax.nn.gelu(hidden_up).astype(BF16)
    grad_act = jnp.dot(bottom_grad, down_shard, preferred_element_type=F32)
    gelu_back = jax.vjp(jax.nn.gelu, hidden_up)[1]
    grad_pre = gelu_back(grad_act)[0].astype(BF16)
    terms = jnp.concatenate(
        [
            jnp.einsum("af,ef->ae", activated, down_shard, preferred_element_type=F32),
            jnp.einsum("af,ef->ae", grad_pre, up_shard, preferred_element_type=F32),
        ],
        axis=1,
    ).astype(BF16)
    large = (n_lat, width_two // n_lat, span)
    parts, up_got, down_got = terms_back(
        4,
        terms.reshape(n_x, 2, padded, 2 * width_two),
        jnp.einsum("ae,af->ef", mlp_in, grad_pre, preferred_element_type=F32)
        .astype(BF16)
        .reshape(large),
        jnp.einsum("ao,af->of", bottom_grad, activated, preferred_element_type=F32)
        .astype(BF16)
        .reshape(large),
    )
    row_slab = (n_mp, WIN_H * PADDED_COLUMNS, 2 * group)
    decoded_slab, grad_windows = local_kernel(
        merge_backward,
        [
            lax.axis_index("mp").reshape(1),
            parts,
            merged,
            grad_bottom,
            hidden,
            cot_patches,
            places,
            merge_gain_all,
            mlp_gain_row,
            section,
            section_got,
        ],
        [(row_slab, BF16), ((tokens, width), BF16)],
        section_scratch,
        scalars=1,
        outside=2,
    )
    (halo,) = exchange(
        5,
        [grad_windows.reshape(window_shape)],
        [(around, BF16)],
        [
            (0, (0, 0), 0, (0,), -1, -1),
            (0, (slice(0, bands), 0), 0, (slice(1, 1 + bands),), 0, -1),
            (0, (0,), 0, (slice(1 + bands, 1 + bands + columns),), -1, 0),
        ],
    )
    grad_up = jnp.sum(up_got.astype(F32), axis=0)
    grad_down = jnp.sum(down_got.astype(F32), axis=0)
    grad_slab, grad_edge, weight_grads = local_kernel(
        attention_backward,
        [
            cut,
            framed_fields,
            first_all,
            weights_all,
            context,
            grad_windows,
            halo.reshape(-1, width),
            places,
        ],
        [
            (row_slab, BF16),
            ((n_mp, WIN_H * PADDED_COLUMNS // 2, 2 * group), BF16),
            ((4, width, width), BF16),
        ],
        [
            pltpu.VMEM((3, tokens, width), F32),
            pltpu.VMEM((3, tokens, width), F32),
            pltpu.VMEM((tokens, width), F32),
        ],
        scalars=1,
    )
    weight_total, grad_got, edge_got, decoded_got = gradients_out(
        6, weight_grads, grad_slab, grad_edge, decoded_slab
    )
    grad_qkv = weight_total[:, : 3 * group].reshape(width // n_lat, 3, group)
    grad_proj = weight_total[:, 3 * group :]
    (decoded,) = local_kernel(
        decoded_rows, [decoded_got, places], [((rows, group, lon_count), BF16)]
    )
    (grad_input,) = local_kernel(
        input_rows,
        [lat_shift, grad_got, edge_got, places],
        [((rows, group, lon_count), F32)],
        [pltpu.VMEM((rows + WIN_H, group, lon_count), F32)],
        scalars=1,
    )
    decoded, grad_input = decoded.transpose(0, 2, 1), grad_input.transpose(0, 2, 1)
    return (decoded, grad_input, grad_qkv, grad_proj, grad_up, grad_down)


def solution(mesh):
    return jax.shard_map(
        shards,
        mesh=mesh,
        in_specs=(
            P("lat", None, "mp"),
            P("mp"),
            P(None, None, "mp"),
            P(None, "mp"),
            P(None, "mp"),
            P(None, "mp", None),
            P(),
            P(None, "mp"),
            P(None, "mp"),
            P(None, None, "mp"),
            P(),
            P(),
            P("lat", None, "mp"),
        ),
        out_specs=(
            P("lat", None, "mp"),
            P("lat", None, "mp"),
            P("lat", None, "mp"),
            P("lat", "mp"),
            P("lat", "mp"),
            P("lat", "mp"),
        ),
        check_vma=False,
    )
```
